128 devices in a mesh: section: 2 (over y_lo), dp: 2 (over core), shard: 32 (over x, z, y_hi).
Axes of the slice: x: 4, y: 4 (y_hi: 2, y_lo: 2; y = y_hi * 2 + y_lo), z: 4, core: 2. Of those that a mesh axis runs over, the one named last changes fastest.
Arguments:
- inputs: bfloat16 [2, 2, 2048, 1536], P('dp', None, 'shard'), may hold values from -6 to 6
- cotangent: bfloat16 [2, 2, 2048, 1536], P('dp', None, 'shard'), may hold values from -6 to 6
- routes: int32 [2, 2, 2, 2048, 6], P('section', 'dp', None, 'shard'), may hold values from 0 to 63, all different within a row; in each aligned block of 64 rows (0 to 63, 64 to 127, ..., all dimensions but the last counted through in order) at most 8 rows name the same one
- norm_attn: bfloat16 [2, 1536], P('section', 'shard'), may hold values from 0.5 to 1.5
- w_query: bfloat16 [2, 1536, 1536], P('section', 'shard'), may hold values from -0.15625 to 0.15625
- w_key: bfloat16 [2, 1536, 512], P('section', 'shard'), may hold values from -0.15625 to 0.15625
- w_value: bfloat16 [2, 1536, 512], P('section', 'shard'), may hold values from -0.15625 to 0.15625
- w_output: bfloat16 [2, 1536, 1536], P('section', 'shard'), may hold values from -3.5 to 3.5
- norm_ffn: bfloat16 [2, 1536], P('section', 'shard'), may hold values from 0.5 to 1.5
- w_router: bfloat16 [2, 1536, 64], P('section', 'shard'), may hold values from -0.078125 to 0.078125
- shared_gate: bfloat16 [2, 1536, 1024], P('section', 'shard'), may hold values from -0.15625 to 0.15625
- shared_up: bfloat16 [2, 1536, 1024], P('section', 'shard'), may hold values from -0.15625 to 0.15625
- shared_down: bfloat16 [2, 1024, 1536], P('section', 'shard'), may hold values from -0.1875 to 0.1875
- expert_gate: bfloat16 [2, 64, 1536, 512], P('section', 'shard'), may hold values from -0.15625 to 0.15625
- expert_up: bfloat16 [2, 64, 1536, 512], P('section', 'shard'), may hold values from -0.15625 to 0.15625
- expert_down: bfloat16 [2, 64, 512, 1536], P('section', 'shard'), may hold values from -0.5 to 0.5
Outputs:
- section_out: bfloat16 [2, 2, 2, 2048, 1536], P('section', 'dp', None, 'shard')
- section_in_grad: bfloat16 [2, 2, 2, 2048, 1536], P('section', 'dp', None, 'shard')
- grad_norm_attn: float32 [2, 1536], P('section', 'shard')
- grad_query: float32 [2, 1536, 1536], P('section', 'shard')
- grad_key: float32 [2, 1536, 512], P('section', 'shard')
- grad_value: float32 [2, 1536, 512], P('section', 'shard')
- grad_output: float32 [2, 1536, 1536], P('section', 'shard')
- grad_norm_ffn: float32 [2, 1536], P('section', 'shard')
- grad_router: float32 [2, 1536, 64], P('section', 'shard')
- grad_shared_gate: float32 [2, 1536, 1024], P('section', 'shard')
- grad_shared_up: float32 [2, 1536, 1024], P('section', 'shard')
- grad_shared_down: float32 [2, 1024, 1536], P('section', 'shard')
- grad_expert_gate: float32 [2, 64, 1536, 512], P('section', 'shard')
- grad_expert_up: float32 [2, 64, 1536, 512], P('section', 'shard')
- grad_expert_down: float32 [2, 64, 512, 1536], P('section', 'shard')
The draws below stay inside these ranges and needn't reach their ends.
Inputs may be any that keep to these rules, and one draw needn't show every extreme that they name: `routes`: each row names 6 different experts. In each aligned block of 64 rows (one index of shard in one micro-batch) no expert is named by more than 8 rows.
All inputs are finite; a program needn't handle non-finite values.
Results may differ from the reference program's by a relative error of at most 0.035.
Values may be sent and summed in bfloat16 or wider, within the bound.
No kernel may reach another device: no remote copies, remote signals or barrier semaphores. Data moves between devices by JAX's collectives and lax.ppermute only.
A program may use at most 320 MiB of HBM per device.

```python
import math
import jax
import jax.numpy as jnp
import numpy as np
from jax import lax

D = 1536
H = 12
KVH = 4
HD = 128
FE = 512
FS = 1024
TOPK = 6
MICRO = 2
BLOCK_ROWS = 64
EXPERTS = 64
BATCH_ROWS = 2048
LENGTH = 4096
SEQS = 2
CAP = 8
N_SHARD = 32


def shard_levels(stream_key, extent, pieces, least, high):
    def one(axis_at, blocks):
        steps = jax.random.uniform(jax.random.fold_in(jax.random.fold_in(stream_key, 6), axis_at), (blocks,), jnp.float32, least / len(pieces), high / len(pieces))
        return jnp.repeat(jnp.exp(steps), extent[axis_at] // blocks).reshape((-1,) + (1,) * (len(extent) - axis_at - 1))

    loudness = one(*pieces[0])
    for cut in pieces[1:]:
        loudness = loudness * one(*cut)
    return loudness


def assign_block(own_key, own, number, rows, amount, top, limit, slope):
    order = jax.random.permutation(own_key, amount)
    packed, ordinary = portions_of(amount, rows * top, limit, slope, True), portions_of(amount, rows * top, limit, slope, False)
    places = jnp.arange(amount)

    def named(sizes, turn):
        used = int((sizes > 0).sum())
        fixed = max(1, used // 4)
        passed = fixed + (places - fixed + turn * (used - fixed)) % max(1, amount - fixed)
        return jnp.zeros((amount,), jnp.int32).at[order[jnp.where(places < fixed, places, passed)]].set(jnp.asarray(sizes, jnp.int32))

    sizes = jnp.where(number % 4 == 0, named(packed, number // 4), named(ordinary, number - number // 4 - 1))
    mixed = jax.random.permutation(jax.random.fold_in(own, 3), amount)
    giver, receiver = mixed[0:amount // 2 * 2:2], mixed[1:amount // 2 * 2:2]
    slack = jnp.minimum(sizes[giver] - 1, limit - sizes[receiver]) // 2
    slack = jnp.where((giver == order[0]) | (receiver == order[0]) | (sizes[receiver] == 0), 0, jnp.maximum(slack, 0))
    passed = jax.random.randint(jax.random.fold_in(own, 4), (amount // 2,), 0, 1 << 20) % (slack + 1)
    sizes = sizes.at[giver].add(-passed).at[receiver].add(passed)
    items = jnp.searchsorted(jnp.cumsum(sizes), jnp.arange(rows * top), side="right").astype(jnp.int32)
    table = items.reshape(top, rows).T
    table = table[jax.random.permutation(jax.random.fold_in(own, 1), rows)]
    turn = jax.random.randint(jax.random.fold_in(own, 2), (rows, 1), 0, top)
    return jnp.take_along_axis(table, (jnp.arange(top)[None, :] + turn) % top, axis=1)


def portions_of(amount, total, reach, lean, full):
    loads = [(1 << 20) // math.isqrt(standing ** lean) + 1 for standing in range(1, amount + 1)]
    largest = reach if full else min(reach, max(-(-total // amount), total * loads[0] // sum(loads)))
    least = 1 if total - largest >= amount - 1 else 0
    holding, spare = [largest] + [least] * (amount - 1), total - largest - least * (amount - 1)
    while spare > 0:
        candidates = [i for i in range(1, amount) if holding[i] < largest] or [i for i in range(1, amount) if holding[i] < reach]
        pool, left = sum([loads[i] for i in candidates]), spare
        for i in candidates:
            addition = min(reach - holding[i], max(1, left * loads[i] // pool), spare)
            holding[i] = holding[i] + addition
            spare = spare - addition
    return np.array(holding)


def centred(key, extent, spread, limit, shards=(), held_as=jnp.bfloat16):
    entries = spread * jax.random.normal(key, extent, jnp.float32)
    if shards:
        entries = entries * shard_levels(key, extent, shards, -0.22, 0.18)
    return jnp.clip(entries, -limit, limit).astype(held_as)


def setup_inputs(seed: int = 0) -> dict:
    seeds = jax.random.split(jax.random.key(seed), 17)
    inputs = centred(seeds[0], (SEQS, MICRO, BATCH_ROWS, D), 1.0, 6.0, ((0, 2), (2, 32)))
    cotangent = centred(seeds[1], (SEQS, MICRO, BATCH_ROWS, D), 1.0, 6.0, ((0, 2), (2, 32)))
    routes_keys = jax.random.split(jax.random.fold_in(seeds[2], 1), 2 * SEQS * MICRO * BATCH_ROWS // BLOCK_ROWS)
    routes_turns = jax.random.permutation(jax.random.fold_in(seeds[2], 3), 2 * SEQS * MICRO * BATCH_ROWS // BLOCK_ROWS)
    routes = jax.vmap(lambda own, number: assign_block(jax.random.fold_in(seeds[2], 2), own, number, BLOCK_ROWS, EXPERTS, TOPK, CAP, 0))(routes_keys, routes_turns).reshape((2, SEQS, MICRO, BATCH_ROWS, TOPK))
    norm_attn = jnp.clip(1.0 + 0.1 * jax.random.normal(seeds[3], (2, D), jnp.float32), 0.5, 1.5).astype(jnp.bfloat16)
    w_query = centred(seeds[4], (2, D, H * HD), D ** -0.5, 0.15625, ((0, 2), (1, 32)))
    w_key = centred(seeds[5], (2, D, KVH * HD), D ** -0.5, 0.15625, ((0, 2), (1, 32)))
    w_value = centred(seeds[6], (2, D, KVH * HD), D ** -0.5, 0.15625, ((0, 2), (1, 32)))
    w_output = centred(seeds[7], (2, H * HD, D), (max(1, H * HD * 8 // LENGTH)) ** -0.5, 3.5, ((0, 2), (1, 32)))
    norm_ffn = jnp.clip(1.0 + 0.1 * jax.random.normal(seeds[8], (2, D), jnp.float32), 0.5, 1.5).astype(jnp.bfloat16)
    w_router = centred(seeds[9], (2, D, EXPERTS), (4 * D) ** -0.5, 0.078125, ((0, 2), (1, 32)))
    shared_gate = centred(seeds[10], (2, D, FS), D ** -0.5, 0.15625, ((0, 2), (1, 32)))
    shared_up = centred(seeds[11], (2, D, FS), D ** -0.5, 0.15625, ((0, 2), (1, 32)))
    shared_down = centred(seeds[12], (2, FS, D), FS ** -0.5, 0.1875, ((0, 2), (1, 32)))
    expert_gate = centred(seeds[13], (2, EXPERTS, D, FE), D ** -0.5, 0.15625, ((0, 2), (1, 32)))
    expert_up = centred(seeds[14], (2, EXPERTS, D, FE), D ** -0.5, 0.15625, ((0, 2), (1, 32)))
    expert_down = centred(seeds[15], (2, EXPERTS, FE, D), (FE // 4) ** -0.5, 0.5, ((0, 2), (1, 32)))
    return dict(inputs=inputs, cotangent=cotangent, routes=routes, norm_attn=norm_attn, w_query=w_query, w_key=w_key, w_value=w_value, w_output=w_output, norm_ffn=norm_ffn, w_router=w_router, shared_gate=shared_gate, shared_up=shared_up, shared_down=shared_down, expert_gate=expert_gate, expert_up=expert_up, expert_down=expert_down)


@jax.custom_vjp
def low(v):
    return lax.optimization_barrier(v.astype(jnp.bfloat16)).astype(jnp.float32)

@jax.custom_vjp
def low_back(v):
    return v

def low_keep(v):
    return (low(v), None)

def low_pass(kept, grad):
    return (grad,)

def back_keep(v):
    return (v, None)

def back_low(kept, grad):
    return (low(grad),)
low.defvjp(low_keep, low_pass)
low_back.defvjp(back_keep, back_low)
epsilon = 1e-05
masked_score = -1e+30

def product(left_side, right_side):
    return jnp.dot(left_side, right_side, precision=lax.Precision.HIGHEST)

def einsum_high(formula, left_side, right_side):
    return jnp.einsum(formula, left_side, right_side, precision=lax.Precision.HIGHEST)

def normed(layer_in):
    return layer_in * lax.rsqrt(lax.optimization_barrier(jnp.mean(layer_in * layer_in, axis=-1, keepdims=True)) + epsilon)

def silu_of(argument):
    return argument * jax.nn.sigmoid(argument)

def slot_rows(route_seq):
    blocks = route_seq.reshape(MICRO * N_SHARD, BLOCK_ROWS * TOPK)
    one_hot = (blocks[:, :, None] == jnp.arange(EXPERTS, dtype=jnp.int32)[None, None, :]).astype(jnp.int32)
    before = jnp.cumsum(one_hot, axis=1) - one_hot
    slot_ids = lax.optimization_barrier(jnp.sum(before * one_hot, axis=2))
    anchor = jnp.arange(MICRO * N_SHARD, dtype=jnp.int32)[:, None] * CAP
    return (anchor + slot_ids).reshape(LENGTH, TOPK)

def attention(queries, keys, values):
    group_size = H // KVH
    scaling = HD ** (-0.5)
    query_blocks = queries.reshape(MICRO, BATCH_ROWS, KVH, group_size, HD)
    key_heads = keys.reshape(LENGTH, KVH, HD)
    value_heads = values.reshape(LENGTH, KVH, HD)
    key_pos = jnp.arange(LENGTH, dtype=jnp.int32)

    def one_block(block_pair):
        query_block, first_row = block_pair
        scores = low_back(einsum_high('cghd,lgd->ghcl', query_block, key_heads) * scaling)
        query_pos = first_row + jnp.arange(BATCH_ROWS, dtype=jnp.int32)
        allowed = key_pos[None, :] <= query_pos[:, None]
        scores = jnp.where(allowed, scores, masked_score)
        probs_rounded = low(jax.nn.softmax(scores, axis=-1))
        mixed_rows = einsum_high('ghcl,lgd->cghd', probs_rounded, value_heads)
        return mixed_rows.reshape(BATCH_ROWS, H * HD)
    starts = jnp.arange(MICRO, dtype=jnp.int32) * BATCH_ROWS
    blocks = lax.map(jax.checkpoint(one_block), (query_blocks, starts))
    return blocks.reshape(LENGTH, H * HD)

def layer(layer_in, params, route_seq):
    gain_attn, query_w, key_w, value_w, output_w, gain_ffn, router_w, shared_g, shared_u, shared_d, expert_g, expert_u, expert_d = params
    normed_one = low(normed(layer_in) * gain_attn)
    queries = low(low_back(product(normed_one, query_w)))
    keys = low(low_back(product(normed_one, key_w)))
    values = low(low_back(product(normed_one, value_w)))
    attended = low(low_back(attention(queries, keys, values)))
    hidden = layer_in + low_back(product(attended, output_w))
    normed_two = low(normed(hidden) * gain_ffn)
    logits = low_back(product(normed_two, router_w))
    chosen = (route_seq[:, :, None] == jnp.arange(EXPERTS, dtype=jnp.int32)[None, None, :]).astype(jnp.float32)
    picked = lax.optimization_barrier(jnp.sum(chosen * logits[:, None, :], axis=2))
    gate_weights = jax.nn.softmax(picked, axis=-1)
    expert_rows = MICRO * N_SHARD * CAP
    flat_experts = route_seq.reshape(-1)
    flat_rows = slot_rows(route_seq).reshape(-1)
    token_ids = jnp.repeat(jnp.arange(LENGTH, dtype=jnp.int32), TOPK)
    table = jnp.full((EXPERTS, expert_rows), LENGTH, dtype=jnp.int32).at[flat_experts, flat_rows].set(token_ids)
    padded = jnp.concatenate([normed_two, jnp.zeros((1, D), jnp.float32)], axis=0)
    expert_in = low_back(padded[table])
    gate_pre = low_back(einsum_high('erd,edf->erf', expert_in, expert_g))
    up_pre = low_back(einsum_high('erd,edf->erf', expert_in, expert_u))
    activated = low(silu_of(gate_pre) * up_pre)
    expert_out = low(low_back(einsum_high('erf,efd->erd', activated, expert_d)))
    selected = expert_out.reshape(EXPERTS * expert_rows, D)[flat_experts * expert_rows + flat_rows]
    selected = selected.reshape(LENGTH, TOPK, D)
    routed = lax.optimization_barrier(jnp.sum(gate_weights[:, :, None] * selected, axis=1))
    shared_gate_pre = low_back(product(normed_two, shared_g))
    shared_up_pre = low_back(product(normed_two, shared_u))
    shared_act = low(silu_of(shared_gate_pre) * shared_up_pre)
    shared_out = low_back(product(shared_act, shared_d))
    return hidden + routed + shared_out

def reference(inputs, cotangent, routes, norm_attn, w_query, w_key, w_value, w_output, norm_ffn, w_router, shared_gate, shared_up, shared_down, expert_gate, expert_up, expert_down):
    params = tuple((array.astype(jnp.float32) for array in (norm_attn, w_query, w_key, w_value, w_output, norm_ffn, w_router, shared_gate, shared_up, shared_down, expert_gate, expert_up, expert_down)))
    seq_inputs = inputs.astype(jnp.float32).reshape(SEQS, LENGTH, D)
    seq_cots = cotangent.astype(jnp.float32).reshape(SEQS, LENGTH, D)
    seq_routes = jnp.transpose(routes.reshape(2, SEQS, LENGTH, TOPK), (1, 0, 2, 3))

    def one_sequence(totals, data):
        seq_in, seq_cot, route_pair = data
        first_params = tuple((array[0] for array in params))
        second_params = tuple((array[1] for array in params))

        def first_layer(layer_in, weights):
            return layer(layer_in, weights, route_pair[0])

        def second_layer(layer_in, weights):
            return layer(layer_in, weights, route_pair[1])
        first_out, first_back = jax.vjp(first_layer, seq_in, first_params)
        sent = first_out.astype(jnp.bfloat16).astype(jnp.float32)
        second_out, second_back = jax.vjp(second_layer, sent, second_params)
        sent_grad, second_grads = second_back(seq_cot)
        sent_grad = sent_grad.astype(jnp.bfloat16)
        input_grad, first_grads = first_back(sent_grad.astype(jnp.float32))
        totals = tuple((total + jnp.stack([first, second]) for total, first, second in zip(totals, first_grads, second_grads)))
        outputs = jnp.stack([first_out.astype(jnp.bfloat16), second_out.astype(jnp.bfloat16)])
        gradients = jnp.stack([input_grad.astype(jnp.bfloat16), sent_grad])
        return (totals, (outputs, gradients))
    start_totals = tuple((jnp.zeros_like(array) for array in params))
    totals, (outputs, gradients) = lax.scan(one_sequence, start_totals, (seq_inputs, seq_cots, seq_routes))
    section_out = jnp.transpose(outputs, (1, 0, 2, 3)).reshape(2, SEQS, MICRO, BATCH_ROWS, D)
    section_in_grad = jnp.transpose(gradients, (1, 0, 2, 3)).reshape(2, SEQS, MICRO, BATCH_ROWS, D)
    return (section_out, section_in_grad, totals[0], totals[1], totals[2], totals[3], totals[4], totals[5], totals[6], totals[7], totals[8], totals[9], totals[10], totals[11], totals[12])
```

```python
import functools

import jax
import jax.numpy as jnp
from jax import lax
from jax.experimental import pallas as pl
from jax.experimental.pallas import tpu as pltpu
from jax.sharding import PartitionSpec as P

H = 12
KVH = 4
HD = 128
GROUP = H // KVH
TOPK = 6
CAP = 8

epsilon = 1e-05
masked_score = -1e30
scaling = HD ** (-0.5)
log2_scale = scaling * 1.4426950408889634
bf = jnp.bfloat16
f32 = jnp.float32


def inverse_rms(rows):
    return lax.rsqrt(jnp.mean(rows * rows, axis=-1, keepdims=True) + epsilon)


def norm_back(layer_in, gain, upstream):
    inverse = inverse_rms(layer_in)
    unit_rows = layer_in * inverse
    gain_grad = jnp.sum(upstream * unit_rows, axis=0)
    scaled = upstream * gain
    in_grad = inverse * (scaled - unit_rows * jnp.mean(scaled * unit_rows, axis=-1, keepdims=True))
    return (in_grad, gain_grad)


def silu_parts(argument):
    sigmoid = jax.nn.sigmoid(argument)
    return argument * sigmoid, sigmoid * (1.0 + argument * (1.0 - sigmoid))


def dot(left_side, right_side):
    return jnp.dot(left_side, right_side, preferred_element_type=f32)


def dot_nt(left_side, right_side):
    return lax.dot_general(
        left_side, right_side, (((1,), (1,)), ((), ())), preferred_element_type=f32
    )


def dot_tn(left_side, right_side):
    return lax.dot_general(
        left_side, right_side, (((0,), (0,)), ((), ())), preferred_element_type=f32
    )


def wide_einsum(formula, left_side, right_side):
    return jnp.einsum(formula, left_side, right_side, preferred_element_type=f32)


def stacked_heads(ref, part):
    return jnp.concatenate(
        [ref[part, :, g * HD : (g + 1) * HD] for g in range(GROUP)], axis=0
    )


def diagonal_mask(rows, chunk, block, zy):
    key_at = lax.broadcasted_iota(jnp.int32, (rows, chunk), 1)
    row_at = lax.broadcasted_iota(jnp.int32, (rows, chunk), 0)
    return key_at <= zy * block + lax.rem(row_at, block)


def attention_forward_kernel(chunk, has_prev, info_ref, q_ref, *refs):
    if has_prev:
        prev_ref, cur_ref, o_ref, log_ref = refs
    else:
        cur_ref, o_ref, log_ref = refs
    parts, block, _ = q_ref.shape
    zy = info_ref[0]
    mask = diagonal_mask(GROUP * block, chunk, block, zy)
    for part in range(parts):
        queries = stacked_heads(q_ref, part)
        pieces = []
        if has_prev:
            bias = jnp.where(info_ref[1] > 0, 0.0, masked_score).astype(f32)
            pieces.append((dot_nt(queries, prev_ref[:, :HD]) + bias, prev_ref, 0, prev_ref.shape[0]))
        if part > 0:
            pieces.append((dot_nt(queries, cur_ref[: part * chunk, :HD]), cur_ref, 0, part * chunk))
        last = dot_nt(queries, cur_ref[part * chunk : (part + 1) * chunk, :HD])
        pieces.append(
            (jnp.where(mask, last, masked_score), cur_ref, part * chunk, (part + 1) * chunk)
        )
        peak = functools.reduce(
            jnp.maximum, [jnp.max(s, axis=-1, keepdims=True) for s, _, _, _ in pieces]
        )
        peak = peak * log2_scale
        total = jnp.zeros((GROUP * block, 1), f32)
        mixed = jnp.zeros((GROUP * block, HD), f32)
        for s, ref, start, stop in pieces:
            probs = jnp.exp2(s * log2_scale - peak)
            total = total + jnp.sum(probs, axis=-1, keepdims=True)
            mixed = mixed + dot(probs.astype(bf), ref[start:stop, HD:])
        out = (mixed / total).astype(bf)
        for g in range(GROUP):
            o_ref[part, :, g * HD : (g + 1) * HD] = out[g * block : (g + 1) * block]
        log_ref[part] = jnp.broadcast_to(peak + jnp.log2(total), (GROUP * block, HD))


def attention_backward_kernel(chunk, has_prev, info_ref, q_ref, do_ref, o_ref, log_ref, *refs):
    if has_prev:
        prev_ref, cur_ref, dq_ref, dcur_ref, dprev_ref = refs
        dprev_ref[...] = jnp.zeros(dprev_ref.shape, f32)
    else:
        cur_ref, dq_ref, dcur_ref = refs
    dcur_ref[...] = jnp.zeros(dcur_ref.shape, f32)
    parts, block, _ = q_ref.shape
    zy = info_ref[0]
    mask = diagonal_mask(GROUP * block, chunk, block, zy)
    for part in range(parts):
        queries = stacked_heads(q_ref, part)
        out_grad = stacked_heads(do_ref, part)
        out = stacked_heads(o_ref, part)
        inner = jnp.sum(out_grad.astype(f32) * out.astype(f32), axis=-1, keepdims=True)
        log_total = log_ref[part][:, :1]
        query_grad = jnp.zeros((GROUP * block, HD), f32)
        pieces = []
        if has_prev:
            log_prev = log_total + jnp.where(info_ref[1] > 0, 0.0, -masked_score).astype(f32)
            for start in range(0, prev_ref.shape[0], chunk):
                pieces.append((prev_ref, dprev_ref, start, log_prev, False))
        for start in range(0, (part + 1) * chunk, chunk):
            pieces.append((cur_ref, dcur_ref, start, log_total, start == part * chunk))
        for ref, grad_ref, start, log_row, on_diagonal in pieces:
            keys = ref[start : start + chunk, :HD]
            scores = dot_nt(queries, keys)
            probs = jnp.exp2(scores * log2_scale - log_row)
            if on_diagonal:
                probs = jnp.where(mask, probs, 0.0)
            probs_grad = dot_nt(out_grad, ref[start : start + chunk, HD:])
            score_grad = (probs * (probs_grad - inner)).astype(bf)
            query_grad = query_grad + dot(score_grad, keys)
            grad_ref[start : start + chunk, :HD] += dot_tn(score_grad, queries) * scaling
            grad_ref[start : start + chunk, HD:] += dot_tn(probs.astype(bf), out_grad)
        out_rows = (query_grad * scaling).astype(bf)
        for g in range(GROUP):
            dq_ref[part, :, g * HD : (g + 1) * HD] = out_rows[g * block : (g + 1) * block]


def vmem_specs(count):
    return [pl.BlockSpec(memory_space=pltpu.VMEM)] * count


def kernel_params():
    return pltpu.CompilerParams(vmem_limit_bytes=50 * 1024 * 1024)


def attention_forward(info, queries, prev, cur):
    parts, block, _ = queries.shape
    chunk = cur.shape[0] // parts
    kvs = (cur,) if prev is None else (prev, cur)
    keys = sum(kv.shape[0] for kv in kvs)
    rows = parts * GROUP * block
    return pl.pallas_call(
        functools.partial(attention_forward_kernel, chunk, prev is not None),
        out_shape=(
            jax.ShapeDtypeStruct(queries.shape, bf),
            jax.ShapeDtypeStruct((parts, GROUP * block, HD), f32),
        ),
        in_specs=[pl.BlockSpec(memory_space=pltpu.SMEM)] + vmem_specs(1 + len(kvs)),
        out_specs=tuple(vmem_specs(2)),
        compiler_params=kernel_params(),
        cost_estimate=pl.CostEstimate(
            flops=4 * rows * keys * HD,
            bytes_accessed=keys * 512 + rows * 1024,
            transcendentals=rows * keys,
        ),
    )(info, queries, *kvs)


def attention_backward(info, queries, out_grad, out, logs, prev, cur):
    parts, block, _ = queries.shape
    chunk = cur.shape[0] // parts
    kvs = (cur,) if prev is None else (prev, cur)
    keys = sum(kv.shape[0] for kv in kvs)
    rows = parts * GROUP * block
    return pl.pallas_call(
        functools.partial(attention_backward_kernel, chunk, prev is not None),
        out_shape=(jax.ShapeDtypeStruct(queries.shape, bf),)
        + tuple(jax.ShapeDtypeStruct(kv.shape, f32) for kv in reversed(kvs)),
        in_specs=[pl.BlockSpec(memory_space=pltpu.SMEM)] + vmem_specs(4 + len(kvs)),
        out_specs=tuple(vmem_specs(1 + len(kvs))),
        compiler_params=kernel_params(),
        cost_estimate=pl.CostEstimate(
            flops=10 * rows * keys * HD,
            bytes_accessed=keys * 1536 + rows * 1536,
            transcendentals=rows * keys,
        ),
    )(info, queries, out_grad, out, logs, *kvs)


def body(
    inputs,
    cotangent,
    routes,
    norm_attn,
    w_query,
    w_key,
    w_value,
    w_output,
    norm_ffn,
    w_router,
    shared_gate,
    shared_up,
    shared_down,
    expert_gate,
    expert_up,
    expert_down,
):
    micro_count, block, width = inputs.shape[1:]
    shards = lax.axis_size("shard")
    section = lax.axis_index("section")
    core = lax.axis_index("dp")
    position = lax.axis_index("shard")
    ring = shards // KVH
    local_experts = expert_gate.shape[1]
    experts = local_experts * shards
    slots = experts * CAP
    rows_per = w_query.shape[1]
    head_width = H * HD
    key_width = KVH * HD
    qkv_width = head_width + 2 * key_width
    shared_width = shared_gate.shape[2]
    down_rows = shared_down.shape[1]
    is_first = section == 0
    low_core = core == 0
    rings = [[x * ring + zy for x in range(KVH)] for zy in range(ring)]

    def exchange(value):
        return lax.all_to_all(value, "shard", split_axis=0, concat_axis=0, tiled=True)

    def exchange_x(value):
        return lax.all_to_all(
            value, "shard", split_axis=0, concat_axis=0, tiled=True, axis_index_groups=rings
        )

    def twin(value):
        return lax.ppermute(value, "dp", [(0, 1), (1, 0)])

    def mine_of(low_half, high_half):
        return jnp.where(low_core, low_half, high_half)

    def halves(value):
        half = value.shape[-1] // 2
        return value[..., :half], value[..., half:]

    down_flat = (rows_per, down_rows * width // 2 // rows_per)
    tail = jnp.concatenate(
        [
            w_router[0],
            norm_attn[0][:, None],
            norm_ffn[0][:, None],
            jnp.zeros((rows_per, 128 - experts - 2), bf),
        ],
        axis=1,
    )
    qkv_rows = jnp.concatenate([w_query[0], w_key[0], w_value[0]], axis=1)
    packed = jnp.concatenate(
        [
            mine_of(*halves(qkv_rows)),
            mine_of(*halves(w_output[0])),
            mine_of(shared_gate[0], shared_up[0]),
            mine_of(*halves(shared_down[0])).reshape(down_flat),
        ],
        axis=1,
    )
    sizes = [qkv_width // 2, width // 2, shared_width, down_flat[1]]
    gathered = lax.all_gather(
        jnp.concatenate([packed, tail], axis=1), "shard", axis=0, tiled=True
    )
    own_half, tail = gathered[:, : sum(sizes)], gathered[:, sum(sizes) :]
    other_half = twin(own_half)

    def cut(value):
        starts = [sum(sizes[:i]) for i in range(len(sizes))]
        qkv, out, gate_up, down = [
            value[:, start : start + size] for start, size in zip(starts, sizes)
        ]
        return qkv, out, gate_up, down.reshape(down_rows * shards, width // 2)

    qkv_w, output_w, gate_up_w, down_w = zip(cut(own_half), cut(other_half))
    router_w = tail[:, :experts]
    gains = tail[:, experts : experts + 2].T.astype(f32)
    gain_one, gain_two = gains[0][None], gains[1][None]

    def project(rows, pair):
        own, other = dot(rows, pair[0]), dot(rows, pair[1])
        return jnp.concatenate(
            [jnp.where(low_core, own, other), jnp.where(low_core, other, own)], axis=1
        )

    def project_back(low_half, high_half, pair):
        own = jnp.where(low_core, low_half, high_half)
        other = jnp.where(low_core, high_half, low_half)
        return dot_nt(own, pair[0]) + dot_nt(other, pair[1])

    expert_g, expert_u, expert_d = expert_gate[0], expert_up[0], expert_down[0]
    local_routes = routes[0, 0]
    slot_of = jnp.arange(slots, dtype=jnp.int32)
    spread = (jnp.arange(experts, dtype=jnp.int32)[:, None] == slot_of[None, :] // CAP).astype(bf)
    router_slots = dot(router_w, spread).astype(bf)
    row_index = jnp.arange(block, dtype=jnp.int32)
    earlier = (row_index[:, None] > row_index[None, :]).astype(bf)

    def slot_table(route_rows):
        named = jnp.any(
            route_rows[:, :, None] == jnp.arange(experts, dtype=jnp.int32)[None, None, :], axis=1
        ).astype(bf)
        slot_ids = dot(earlier, named).astype(bf)
        return (dot(named, spread) > 0.5) & (
            dot(slot_ids, spread).astype(jnp.int32) == (slot_of % CAP)[None, :]
        )

    tables = [slot_table(local_routes[m]) for m in range(micro_count)]
    info = jnp.stack([position % ring, (section == 0).astype(jnp.int32)]).astype(jnp.int32)
    info_all = jnp.stack([position % ring, jnp.ones_like(position)]).astype(jnp.int32)

    def gate_values(normed_two, table):
        logits = jnp.where(table, dot(normed_two, router_slots), masked_score)
        weights = jnp.exp(logits - jnp.max(logits, axis=-1, keepdims=True))
        weights = jnp.where(table, weights, 0.0)
        return weights / jnp.sum(weights, axis=-1, keepdims=True)

    def high_low(value):
        high = value.astype(bf)
        return high, (value - high.astype(f32)).astype(bf)

    def to_experts(rows):
        return (
            exchange(rows.reshape(shards, local_experts, CAP, width))
            .transpose(1, 0, 2, 3)
            .reshape(local_experts, shards * CAP, width)
        )

    def from_experts(rows):
        return exchange(
            rows.reshape(local_experts, shards, CAP, width).transpose(1, 0, 2, 3)
        ).reshape(slots, width)

    def forward(moment, received, previous):
        first_micro = min(moment, micro_count - 1)
        second_micro = max(moment - 1, 0)
        layer_b = jnp.where(is_first, inputs[0, first_micro], received)
        table = jnp.where(is_first, tables[first_micro], tables[second_micro])
        layer_in = layer_b.astype(f32)
        normed_one = (layer_in * inverse_rms(layer_in) * gain_one).astype(bf)
        qkv = project(normed_one, qkv_w).astype(bf)
        queries = qkv[:, :head_width].reshape(block, KVH, GROUP * HD).transpose(1, 0, 2)
        pairs = jnp.concatenate(
            [
                qkv[:, head_width : head_width + key_width].reshape(block, KVH, HD),
                qkv[:, head_width + key_width :].reshape(block, KVH, HD),
            ],
            axis=2,
        ).transpose(1, 0, 2)
        pairs = jnp.broadcast_to(pairs[:, None], (KVH, ring, block, 2 * HD))
        cache = exchange(pairs.reshape(shards, block, 2 * HD)).reshape(shards * block, 2 * HD)
        queries = exchange_x(queries)
        attn_info = info if moment == 1 else info_all
        out_rows, logs = attention_forward(attn_info, queries, previous, cache)
        attended = exchange_x(out_rows).transpose(1, 0, 2).reshape(block, head_width)
        hidden = layer_in + project(attended, output_w)
        normed_two = (hidden * inverse_rms(hidden) * gain_two).astype(bf)
        gates = gate_values(normed_two, table)
        pick = table.astype(bf)
        expert_in = to_experts(dot_tn(pick, normed_two).astype(bf))
        gate_pre = wide_einsum("erd,edf->erf", expert_in, expert_g)
        up_pre = wide_einsum("erd,edf->erf", expert_in, expert_u)
        activated = (silu_parts(gate_pre)[0] * up_pre).astype(bf)
        returned = from_experts(wide_einsum("erf,efd->erd", activated, expert_d).astype(bf))
        high, low = high_low(gates)
        routed = dot(high, returned) + dot(low, returned)
        shared_pre = project(normed_two, gate_up_w)
        shared_gate_pre, shared_up_pre = halves(shared_pre)
        shared_act = (silu_parts(shared_gate_pre)[0] * shared_up_pre).astype(bf)
        output_b = (hidden + routed + project(shared_act, down_w)).astype(bf)
        kept = dict(
            layer_b=layer_b,
            pick=pick,
            table=table,
            normed_one=normed_one,
            queries=queries,
            cache=cache,
            previous=previous,
            info=attn_info,
            out_rows=out_rows,
            logs=logs,
            attended=attended,
            hidden=hidden,
            normed_two=normed_two,
            gates=gates,
            expert_in=expert_in,
            gate_pre=gate_pre,
            up_pre=up_pre,
            activated=activated,
            returned=returned,
            shared_gate_pre=shared_gate_pre,
            shared_up_pre=shared_up_pre,
            shared_act=shared_act,
            output_b=output_b,
        )
        return output_b, kept

    saved = []
    received = jnp.zeros((block, width), bf)
    previous = None
    for moment in range(micro_count + 1):
        output_b, kept = forward(moment, received, previous)
        saved.append(kept)
        previous = kept["cache"]
        if moment < micro_count:
            received = lax.ppermute(output_b, "section", [(0, 1)])

    def ffn_backward(kept, upstream_b):
        upstream = upstream_b.astype(f32)
        gates, hidden = kept["gates"], kept["hidden"]
        high, low = high_low(gates)
        outgoing = dot_tn(high, upstream_b) + dot_tn(low, upstream_b)
        expert_grad = to_experts(outgoing.astype(bf))
        act_silu, act_slope = silu_parts(kept["gate_pre"])
        act_grad = wide_einsum("erd,efd->erf", expert_grad, expert_d)
        gate_pre_grad = (act_grad * kept["up_pre"] * act_slope).astype(bf)
        up_pre_grad = (act_grad * act_silu).astype(bf)
        expert_in_grad = (
            wide_einsum("erf,edf->erd", gate_pre_grad, expert_g)
            + wide_einsum("erf,edf->erd", up_pre_grad, expert_u)
        ).astype(bf)
        returned_grad = from_experts(expert_in_grad)
        shared_act_grad = project_back(*halves(upstream_b), down_w)
        shared_silu, shared_slope = silu_parts(kept["shared_gate_pre"])
        shared_gate_grad = (shared_act_grad * kept["shared_up_pre"] * shared_slope).astype(bf)
        shared_up_grad = (shared_act_grad * shared_silu).astype(bf)
        normed_two_grad = project_back(shared_gate_grad, shared_up_grad, gate_up_w)
        gate_grad = dot_nt(upstream_b, kept["returned"])
        picked_grad = gates * (gate_grad - jnp.sum(gates * gate_grad, axis=1, keepdims=True))
        picked_b = picked_grad.astype(bf)
        normed_two_grad = normed_two_grad + dot_nt(picked_b, router_slots)
        normed_two_grad = normed_two_grad + dot(kept["pick"], returned_grad)
        logit_grad = dot_nt(picked_b, spread).astype(bf)
        hidden_norm_grad, gain_two_grad = norm_back(hidden, gain_two, normed_two_grad)
        hidden_grad = upstream + hidden_norm_grad
        return dict(
            hidden_grad=hidden_grad,
            hidden_grad_b=hidden_grad.astype(bf),
            upstream_b=upstream_b,
            expert_grad=expert_grad,
            gate_pre_grad=gate_pre_grad,
            up_pre_grad=up_pre_grad,
            shared_gate_grad=shared_gate_grad,
            shared_up_grad=shared_up_grad,
            logit_grad=logit_grad,
            gain_two_grad=gain_two_grad,
        )

    def attention_back(kept, grads, carried):
        attended_grad = output_back(grads["hidden_grad_b"]).astype(bf)
        out_grad = exchange_x(
            attended_grad.reshape(block, KVH, GROUP * HD).transpose(1, 0, 2)
        )
        results = attention_backward(
            kept["info"],
            kept["queries"],
            out_grad,
            kept["out_rows"],
            kept["logs"],
            kept["previous"],
            kept["cache"],
        )
        cache_grad = results[1] if carried is None else results[1] + carried
        carried = results[2] if len(results) > 2 else None
        query_grad = exchange_x(results[0]).transpose(1, 0, 2).reshape(block, head_width)
        parts = exchange(cache_grad.astype(bf).reshape(shards, block, 2 * HD))
        own = jnp.sum(parts.reshape(KVH, ring, block, 2 * HD).astype(f32), axis=1).astype(bf)
        own = own.transpose(1, 0, 2)
        qkv_grad = jnp.concatenate(
            [
                query_grad,
                own[:, :, :HD].reshape(block, key_width),
                own[:, :, HD:].reshape(block, key_width),
            ],
            axis=1,
        )
        normed_one_grad = project_back(*halves(qkv_grad), qkv_w)
        in_norm_grad, gain_one_grad = norm_back(
            kept["layer_b"].astype(f32), gain_one, normed_one_grad
        )
        layer_grad = (grads["hidden_grad"] + in_norm_grad).astype(bf)
        grads = dict(grads, qkv_grad=qkv_grad, gain_one_grad=gain_one_grad, layer_grad=layer_grad)
        return grads, carried

    def output_back(rows):
        return project_back(*halves(rows), output_w)

    backs = [None] * (micro_count + 1)
    received = jnp.zeros((block, width), bf)
    carried = None
    for moment in range(micro_count + 1):
        source = micro_count - moment
        raw_second = source - 1
        if raw_second >= 0:
            second = cotangent[0, raw_second]
        else:
            second = jnp.zeros((block, width), bf)
        first = received if moment > 0 else jnp.zeros((block, width), bf)
        upstream_b = jnp.where(is_first, first, second)
        grads = ffn_backward(saved[source], upstream_b)
        grads, carried = attention_back(saved[source], grads, carried)
        backs[source] = grads
        if moment < micro_count:
            received = lax.ppermute(grads["layer_grad"], "section", [(1, 0)])

    def live(name, store, axis):
        ends = jnp.where(is_first, store[0][name], store[micro_count][name])
        return jnp.concatenate([ends, store[1][name]], axis=axis)

    def kept_rows(name, axis=0):
        return live(name, saved, axis)

    def back_rows(name, axis=0):
        return live(name, backs, axis)

    expert_parts = [
        wide_einsum("erd,erf->edf", kept_rows("expert_in", 1), back_rows("gate_pre_grad", 1)),
        wide_einsum("erd,erf->edf", kept_rows("expert_in", 1), back_rows("up_pre_grad", 1)),
        wide_einsum("erf,erd->efd", kept_rows("activated", 1), back_rows("expert_grad", 1)),
    ]
    expert_parts = [part.astype(bf) for part in expert_parts]
    expert_grads = [part.astype(f32) + twin(part).astype(f32) for part in expert_parts]

    def both(value):
        return jnp.concatenate([value, twin(value)], axis=0)

    def both_halves(low_half, high_half):
        own = jnp.where(low_core, low_half, high_half)
        other = jnp.where(low_core, high_half, low_half)
        return jnp.concatenate([own, twin(other)], axis=0)

    normed_one, normed_two = kept_rows("normed_one"), kept_rows("normed_two")
    grad_gate_up = dot_tn(
        both(normed_two), both_halves(back_rows("shared_gate_grad"), back_rows("shared_up_grad"))
    )
    grad_out = dot_tn(
        both(kept_rows("attended")), both_halves(*halves(back_rows("hidden_grad_b")))
    )
    grad_down = dot_tn(
        both(kept_rows("shared_act")), both_halves(*halves(back_rows("upstream_b")))
    )
    grad_qkv = dot_tn(both(normed_one), both_halves(*halves(back_rows("qkv_grad"))))
    grad_router = dot_tn(normed_two, back_rows("logit_grad"))
    gain_sums = jnp.stack(
        [
            sum(grads["gain_one_grad"] for grads in backs),
            sum(grads["gain_two_grad"] for grads in backs),
        ]
    )
    grad_tail = jnp.concatenate(
        [grad_router, gain_sums.T, jnp.zeros((width, 128 - experts - 2), f32)], axis=1
    )

    def scattered(value):
        pieces = value.astype(bf).reshape(shards, value.shape[0] // shards, value.shape[1])
        return jnp.sum(exchange(pieces).astype(f32), axis=0)

    share_rows = scattered(jnp.concatenate([grad_gate_up, grad_out], axis=1))
    share_down = scattered(grad_down)
    share_last = scattered(jnp.concatenate([grad_qkv, grad_tail], axis=1))

    def joined(own):
        other = twin(own)
        return jnp.where(low_core, own, other), jnp.where(low_core, other, own)

    low_rows, high_rows = joined(share_rows)
    low_down, high_down = joined(share_down)
    low_last, high_last = joined(share_last)
    half_qkv = qkv_width // 2
    qkv_out = jnp.concatenate([low_last[:, :half_qkv], high_last[:, :half_qkv]], axis=1)
    tail_out = low_last[:, half_qkv:] + high_last[:, half_qkv:]
    output_out = jnp.concatenate([low_rows[:, shared_width:], high_rows[:, shared_width:]], axis=1)
    down_out = jnp.concatenate([low_down, high_down], axis=1)

    out_store = jnp.stack(
        [
            jnp.where(is_first, saved[m]["output_b"], saved[m + 1]["output_b"])
            for m in range(micro_count)
        ]
    )
    grad_store = jnp.stack(
        [
            jnp.where(is_first, backs[m]["layer_grad"], backs[m + 1]["layer_grad"])
            for m in range(micro_count)
        ]
    )
    return (
        out_store[None, None],
        grad_store[None, None],
        tail_out[:, experts][None],
        qkv_out[:, :head_width][None],
        qkv_out[:, head_width : head_width + key_width][None],
        qkv_out[:, head_width + key_width :][None],
        output_out[None],
        tail_out[:, experts + 1][None],
        tail_out[:, :experts][None],
        low_rows[:, :shared_width][None],
        high_rows[:, :shared_width][None],
        down_out[None],
        expert_grads[0][None],
        expert_grads[1][None],
        expert_grads[2][None],
    )


def solution(mesh):
    rows = P("section", "shard", None)
    vector = P("section", "shard")
    expert = P("section", "shard", None, None)
    tokens = P("dp", None, "shard", None)
    section_tokens = P("section", "dp", None, "shard", None)
    weights = (vector, rows, rows, rows, rows, vector, rows, rows, rows, rows) + (expert,) * 3
    return jax.shard_map(
        body,
        mesh=mesh,
        in_specs=(tokens, tokens, section_tokens) + weights,
        out_specs=(section_tokens, section_tokens) + weights,
        check_vma=False,
    )
```

```python
import functools

import jax
import jax.numpy as jnp
from jax import lax
from jax.experimental import pallas as pl
from jax.experimental.pallas import tpu as pltpu
from jax.sharding import PartitionSpec as P

H = 12
KVH = 4
HD = 128
GROUP = H // KVH
TOPK = 6
CAP = 8

epsilon = 1e-05
masked_score = -1e30
scaling = HD ** (-0.5)
log2_scale = scaling * 1.4426950408889634
bf = jnp.bfloat16
f32 = jnp.float32
VMEM_LIMIT = 32 * 1024 * 1024
KEPT = ("ring_one", "attended", "normed_two", "shared_act", "expert_in", "activated")
BACK = (
    "qkv_grad",
    "ring_hidden",
    "gain_one_grad",
    "gain_two_grad",
    "logit_grad",
    "upstream_b",
    "shared_gate_grad",
    "shared_up_grad",
    "expert_grad",
    "gate_pre_grad",
    "up_pre_grad",
)


def inverse_rms(rows):
    return lax.rsqrt(jnp.mean(rows * rows, axis=-1, keepdims=True) + epsilon)


def norm_back(layer_in, gain, upstream):
    inverse = inverse_rms(layer_in)
    unit_rows = layer_in * inverse
    gain_grad = jnp.sum(upstream * unit_rows, axis=0)
    scaled = upstream * gain
    in_grad = inverse * (scaled - unit_rows * jnp.mean(scaled * unit_rows, axis=-1, keepdims=True))
    return (in_grad, gain_grad)


def silu_parts(argument):
    sigmoid = jax.nn.sigmoid(argument)
    return argument * sigmoid, sigmoid * (1.0 + argument * (1.0 - sigmoid))


def dot(left_side, right_side):
    return jnp.dot(left_side, right_side, preferred_element_type=f32)


def dot_nt(left_side, right_side):
    return lax.dot_general(
        left_side, right_side, (((1,), (1,)), ((), ())), preferred_element_type=f32
    )


def dot_tn(left_side, right_side):
    return lax.dot_general(
        left_side, right_side, (((0,), (0,)), ((), ())), preferred_element_type=f32
    )


def wide_einsum(formula, left_side, right_side):
    return jnp.einsum(formula, left_side, right_side, preferred_element_type=f32)


def stacked_heads(ref, part, micro):
    return jnp.concatenate(
        [ref[part, micro, :, g * HD : (g + 1) * HD] for g in range(GROUP)], axis=0
    )


def store_heads(ref, part, micro, rows):
    block = ref.shape[2]
    for g in range(GROUP):
        ref[part, micro, :, g * HD : (g + 1) * HD] = rows[g * block : (g + 1) * block]


def diagonal_mask(rows, chunk, block, zy):
    key_at = lax.broadcasted_iota(jnp.int32, (rows, chunk), 1)
    row_at = lax.broadcasted_iota(jnp.int32, (rows, chunk), 0)
    return key_at <= zy * block + lax.rem(row_at, block)


def attention_forward_kernel(info_ref, q_ref, kv_ref, o_ref, log_ref):
    parts, micros, block, _ = q_ref.shape
    span = kv_ref.shape[1]
    chunk = span // parts
    rows = GROUP * block
    mask = diagonal_mask(rows, chunk, block, info_ref[0])
    for part in range(parts):
        for micro in range(micros):
            queries = stacked_heads(q_ref, part, micro)
            pieces = [(m, 0, span) for m in range(micro)]
            if part > 0:
                pieces.append((micro, 0, part * chunk))
            pieces.append((micro, part * chunk, (part + 1) * chunk))
            scores = [dot_nt(queries, kv_ref[m, start:stop, :HD]) for m, start, stop in pieces]
            scores[-1] = jnp.where(mask, scores[-1], masked_score)
            peak = functools.reduce(
                jnp.maximum, [jnp.max(s, axis=-1, keepdims=True) for s in scores]
            )
            peak = peak * log2_scale
            total = jnp.zeros((rows, 1), f32)
            mixed = jnp.zeros((rows, HD), f32)
            for s, (m, start, stop) in zip(scores, pieces):
                probs = jnp.exp2(s * log2_scale - peak)
                total = total + jnp.sum(probs, axis=-1, keepdims=True)
                mixed = mixed + dot(probs.astype(bf), kv_ref[m, start:stop, HD:])
            store_heads(o_ref, part, micro, (mixed / total).astype(bf))
            log_ref[part, micro] = jnp.broadcast_to(peak + jnp.log2(total), (rows, HD))


def attention_backward_kernel(
    info_ref, q_ref, do_ref, o_ref, log_ref, kv_ref, dq_ref, dkv_ref
):
    parts, micros, block, _ = q_ref.shape
    span = kv_ref.shape[1]
    chunk = span // parts
    rows = GROUP * block
    mask = diagonal_mask(rows, chunk, block, info_ref[0])
    dkv_ref[...] = jnp.zeros(dkv_ref.shape, f32)
    for part in range(parts):
        for micro in range(micros):
            queries = stacked_heads(q_ref, part, micro)
            out_grad = stacked_heads(do_ref, part, micro)
            out = stacked_heads(o_ref, part, micro)
            inner = jnp.sum(out_grad.astype(f32) * out.astype(f32), axis=-1, keepdims=True)
            log_total = log_ref[part, micro][:, :1]
            query_grad = jnp.zeros((rows, HD), f32)
            pieces = [(m, start) for m in range(micro) for start in range(0, span, chunk)]
            pieces += [(micro, start) for start in range(0, (part + 1) * chunk, chunk)]
            for m, start in pieces:
                keys = kv_ref[m, start : start + chunk, :HD]
                probs = jnp.exp2(dot_nt(queries, keys) * log2_scale - log_total)
                if (m, start) == (micro, part * chunk):
                    probs = jnp.where(mask, probs, 0.0)
                probs_grad = dot_nt(out_grad, kv_ref[m, start : start + chunk, HD:])
                score_grad = (probs * (probs_grad - inner)).astype(bf)
                query_grad = query_grad + dot(score_grad, keys)
                dkv_ref[m, start : start + chunk, :HD] += dot_tn(score_grad, queries) * scaling
                dkv_ref[m, start : start + chunk, HD:] += dot_tn(probs.astype(bf), out_grad)
            store_heads(dq_ref, part, micro, (query_grad * scaling).astype(bf))


def in_vmem(count):
    return [pl.BlockSpec(memory_space=pltpu.VMEM)] * count


def attention_call(kernel, factor, out_shape, info, queries, *rest):
    parts, micros, block, _ = queries.shape
    rows = parts * micros * GROUP * block
    keys = rest[-1].shape[0] * rest[-1].shape[1]
    return pl.pallas_call(
        kernel,
        out_shape=out_shape,
        in_specs=[pl.BlockSpec(memory_space=pltpu.SMEM)] + in_vmem(1 + len(rest)),
        out_specs=tuple(in_vmem(len(out_shape))),
        compiler_params=pltpu.CompilerParams(vmem_limit_bytes=VMEM_LIMIT),
        cost_estimate=pl.CostEstimate(
            flops=factor * rows * keys * HD,
            bytes_accessed=factor * (keys + rows) * HD,
            transcendentals=rows * keys // 2,
        ),
    )(info, queries, *rest)


def attention_forward(info, queries, kv):
    parts, micros, block, _ = queries.shape
    logs = jax.ShapeDtypeStruct((parts, micros, GROUP * block, HD), f32)
    out = jax.ShapeDtypeStruct(queries.shape, bf)
    return attention_call(attention_forward_kernel, 2, (out, logs), info, queries, kv)


def attention_backward(info, queries, out_grad, out, logs, kv):
    shapes = (jax.ShapeDtypeStruct(queries.shape, bf), jax.ShapeDtypeStruct(kv.shape, f32))
    return attention_call(
        attention_backward_kernel, 5, shapes, info, queries, out_grad, out, logs, kv
    )


def body(
    inputs,
    cotangent,
    routes,
    norm_attn,
    w_query,
    w_key,
    w_value,
    w_output,
    norm_ffn,
    w_router,
    shared_gate,
    shared_up,
    shared_down,
    expert_gate,
    expert_up,
    expert_down,
):
    micros, block, width = inputs.shape[1:]
    tokens = micros * block
    shards = lax.axis_size("shard")
    section = lax.axis_index("section")
    core = lax.axis_index("dp")
    position = lax.axis_index("shard")
    heads = KVH
    ring = shards // heads
    local_experts = expert_gate.shape[1]
    experts = local_experts * shards
    room = micros * CAP
    slots = experts * room
    rows_per = w_query.shape[1]
    half_rows = rows_per // 2
    group_width = GROUP * HD
    head_width = H * HD
    key_width = KVH * HD
    part_width = group_width + 2 * HD
    shared_width = shared_gate.shape[2]
    down_rows = shared_down.shape[1]
    is_first = section == 0
    low_core = core == 0
    x_groups = [[x * ring + zy for x in range(heads)] for zy in range(ring)]
    zy_groups = [[x * ring + zy for zy in range(ring)] for x in range(heads)]

    def exchange(value, groups=None):
        return lax.all_to_all(
            value, "shard", split_axis=0, concat_axis=0, tiled=True, axis_index_groups=groups
        )

    def copies(value, count):
        return jnp.broadcast_to(value[None], (count,) + value.shape)

    def twin(value):
        return lax.ppermute(value, "dp", [(0, 1), (1, 0)])

    def mine_of(low_half, high_half):
        return jnp.where(low_core, low_half, high_half)

    def ordered(own, other, axis):
        low_half, high_half = mine_of(own, other), mine_of(other, own)
        return jnp.concatenate([low_half, high_half], axis=axis)

    def halves(value):
        half = value.shape[-1] // 2
        return value[..., :half], value[..., half:]

    def my_rows(value):
        return mine_of(value[..., :half_rows, :], value[..., half_rows:, :])

    tail = jnp.concatenate(
        [
            w_router[0],
            norm_attn[0][:, None],
            norm_ffn[0][:, None],
            jnp.zeros((rows_per, 128 - experts - 2), bf),
        ],
        axis=1,
    )
    by_head = jnp.concatenate(
        [
            w_query[0].reshape(rows_per, heads, group_width),
            w_key[0].reshape(rows_per, heads, HD),
            w_value[0].reshape(rows_per, heads, HD),
            jnp.broadcast_to(tail[:, None], (rows_per, heads, 128)),
        ],
        axis=2,
    ).transpose(1, 0, 2)
    by_head = my_rows(by_head)
    by_head = jnp.broadcast_to(
        by_head[:, None], (heads, ring, half_rows, part_width + 128)
    ).reshape(shards, half_rows, part_width + 128)
    own_part = exchange(by_head)
    fetched = ordered(own_part, twin(own_part), 1).reshape(width, part_width + 128)
    qkv_w, tail = fetched[:, :part_width], fetched[:, part_width:]
    own_out = lax.all_gather(my_rows(w_output[0]), "shard", axis_index_groups=zy_groups)
    output_w = ordered(own_out, twin(own_out), 1).reshape(group_width, width)
    router_w = tail[:, :experts]
    gains = tail[:, experts : experts + 2].T.astype(f32)
    gain_one, gain_two = gains[0][None], gains[1][None]

    down_flat = (rows_per, down_rows * width // 2 // rows_per)
    shared_rows = jnp.concatenate(
        [
            mine_of(shared_gate[0], shared_up[0]),
            mine_of(*halves(shared_down[0])).reshape(down_flat),
        ],
        axis=1,
    )
    own_shared = lax.all_gather(shared_rows, "shard", axis=0, tiled=True)
    other_shared = twin(own_shared)

    def cut(value):
        down = value[:, shared_width:].reshape(down_rows * shards, width // 2)
        return value[:, :shared_width], down

    gate_up_w, down_w = zip(cut(own_shared), cut(other_shared))

    def project(rows, pair):
        return ordered(dot(rows, pair[0]), dot(rows, pair[1]), 1)

    def project_back(low_half, high_half, pair):
        own, other = mine_of(low_half, high_half), mine_of(high_half, low_half)
        return dot_nt(own, pair[0]) + dot_nt(other, pair[1])

    expert_g, expert_u, expert_d = expert_gate[0], expert_up[0], expert_down[0]
    local_routes = routes[0, 0].reshape(tokens, TOPK)
    slot_of = jnp.arange(slots, dtype=jnp.int32)
    expert_of = jnp.arange(experts, dtype=jnp.int32)
    token_of = jnp.arange(tokens, dtype=jnp.int32)
    spread = (expert_of[:, None] == slot_of[None, :] // room).astype(bf)
    router_slots = dot(router_w, spread).astype(bf)
    named = jnp.any(local_routes[:, :, None] == expert_of[None, None, :], axis=1).astype(bf)
    earlier = (token_of[:, None] > token_of[None, :]) & (
        token_of[:, None] // block == token_of[None, :] // block
    )
    slot_ids = dot(earlier.astype(bf), named).astype(jnp.int32) + CAP * (token_of // block)[:, None]
    table = (dot(named, spread) > 0.5) & (
        dot(slot_ids.astype(bf), spread).astype(jnp.int32) == (slot_of % room)[None, :]
    )
    pick = table.astype(bf)
    info = jnp.stack([position % ring]).astype(jnp.int32)

    def gate_values(normed_two):
        logits = jnp.where(table, dot(normed_two, router_slots), masked_score)
        weights = jnp.exp(logits - jnp.max(logits, axis=-1, keepdims=True))
        weights = jnp.where(table, weights, 0.0)
        return weights / jnp.sum(weights, axis=-1, keepdims=True)

    def high_low(value):
        high = value.astype(bf)
        return high, (value - high.astype(f32)).astype(bf)

    def to_experts(rows):
        return (
            exchange(rows.reshape(shards, local_experts, room, width))
            .transpose(1, 0, 2, 3)
            .reshape(local_experts, shards * room, width)
        )

    def from_experts(rows):
        return exchange(
            rows.reshape(local_experts, shards, room, width).transpose(1, 0, 2, 3)
        ).reshape(slots, width)

    def sum_over_x(rows):
        parts = exchange(rows.astype(bf).reshape(heads, tokens, width), x_groups)
        return jnp.sum(parts.astype(f32), axis=0)

    def ring_rows(rows):
        return exchange(copies(rows, heads), x_groups).reshape(heads * tokens, width)

    def forward(layer_b):
        layer_in = layer_b.astype(f32)
        normed_one = (layer_in * inverse_rms(layer_in) * gain_one).astype(bf)
        ring_one = ring_rows(normed_one)
        qkv = dot(ring_one, qkv_w).astype(bf)
        queries = qkv[:, :group_width].reshape(heads, micros, block, group_width)
        pairs = exchange(copies(qkv[:, group_width:], ring), zy_groups)
        pairs = pairs.reshape(ring, heads, micros, block, 2 * HD).transpose(2, 1, 0, 3, 4)
        cache = pairs.reshape(micros, shards * block, 2 * HD)
        attended, logs = attention_forward(info, queries, cache)
        hidden = layer_in + sum_over_x(
            dot(attended.reshape(heads * tokens, group_width), output_w)
        )
        normed_two = (hidden * inverse_rms(hidden) * gain_two).astype(bf)
        gates = gate_values(normed_two)
        expert_in = to_experts(dot_tn(pick, normed_two).astype(bf))
        gate_pre = wide_einsum("erd,edf->erf", expert_in, expert_g)
        up_pre = wide_einsum("erd,edf->erf", expert_in, expert_u)
        activated = (silu_parts(gate_pre)[0] * up_pre).astype(bf)
        returned = from_experts(wide_einsum("erf,efd->erd", activated, expert_d).astype(bf))
        high, low = high_low(gates)
        routed = dot(high, returned) + dot(low, returned)
        shared_gate_pre, shared_up_pre = halves(project(normed_two, gate_up_w))
        shared_act = (silu_parts(shared_gate_pre)[0] * shared_up_pre).astype(bf)
        output_b = (hidden + routed + project(shared_act, down_w)).astype(bf)
        return dict(
            layer_b=layer_b,
            ring_one=ring_one,
            queries=queries,
            cache=cache,
            attended=attended,
            logs=logs,
            hidden=hidden,
            normed_two=normed_two,
            gates=gates,
            expert_in=expert_in,
            gate_pre=gate_pre,
            up_pre=up_pre,
            activated=activated,
            returned=returned,
            shared_gate_pre=shared_gate_pre,
            shared_up_pre=shared_up_pre,
            shared_act=shared_act,
            output_b=output_b,
        )

    def ffn_backward(kept, upstream_b):
        upstream = upstream_b.astype(f32)
        gates, hidden = kept["gates"], kept["hidden"]
        high, low = high_low(gates)
        outgoing = dot_tn(high, upstream_b) + dot_tn(low, upstream_b)
        expert_grad = to_experts(outgoing.astype(bf))
        act_silu, act_slope = silu_parts(kept["gate_pre"])
        act_grad = wide_einsum("erd,efd->erf", expert_grad, expert_d)
        gate_pre_grad = (act_grad * kept["up_pre"] * act_slope).astype(bf)
        up_pre_grad = (act_grad * act_silu).astype(bf)
        expert_in_grad = (
            wide_einsum("erf,edf->erd", gate_pre_grad, expert_g)
            + wide_einsum("erf,edf->erd", up_pre_grad, expert_u)
        ).astype(bf)
        returned_grad = from_experts(expert_in_grad)
        shared_act_grad = project_back(*halves(upstream_b), down_w)
        shared_silu, shared_slope = silu_parts(kept["shared_gate_pre"])
        shared_gate_grad = (shared_act_grad * kept["shared_up_pre"] * shared_slope).astype(bf)
        shared_up_grad = (shared_act_grad * shared_silu).astype(bf)
        normed_two_grad = project_back(shared_gate_grad, shared_up_grad, gate_up_w)
        gate_grad = dot_nt(upstream_b, kept["returned"])
        picked_grad = gates * (gate_grad - jnp.sum(gates * gate_grad, axis=1, keepdims=True))
        picked_b = picked_grad.astype(bf)
        normed_two_grad = normed_two_grad + dot_nt(picked_b, router_slots)
        normed_two_grad = normed_two_grad + dot(pick, returned_grad)
        logit_grad = dot_nt(picked_b, spread).astype(bf)
        hidden_norm_grad, gain_two_grad = norm_back(hidden, gain_two, normed_two_grad)
        return dict(
            hidden_grad=upstream + hidden_norm_grad,
            upstream_b=upstream_b,
            expert_grad=expert_grad,
            gate_pre_grad=gate_pre_grad,
            up_pre_grad=up_pre_grad,
            shared_gate_grad=shared_gate_grad,
            shared_up_grad=shared_up_grad,
            logit_grad=logit_grad,
            gain_two_grad=gain_two_grad,
        )

    def attention_back(kept, grads):
        ring_hidden = ring_rows(grads["hidden_grad"].astype(bf))
        out_grad = dot_nt(ring_hidden, output_w).astype(bf)
        out_grad = out_grad.reshape(heads, micros, block, group_width)
        query_grad, cache_grad = attention_backward(
            info, kept["queries"], out_grad, kept["attended"], kept["logs"], kept["cache"]
        )
        parts = cache_grad.astype(bf).reshape(micros, heads, ring, block, 2 * HD)
        parts = parts.transpose(2, 1, 0, 3, 4).reshape(ring, heads * tokens, 2 * HD)
        pair_grad = jnp.sum(exchange(parts, zy_groups).astype(f32), axis=0).astype(bf)
        qkv_grad = jnp.concatenate(
            [query_grad.reshape(heads * tokens, group_width), pair_grad], axis=1
        )
        normed_one_grad = sum_over_x(dot_nt(qkv_grad, qkv_w))
        in_norm_grad, gain_one_grad = norm_back(
            kept["layer_b"].astype(f32), gain_one, normed_one_grad
        )
        return dict(
            grads,
            ring_hidden=ring_hidden,
            qkv_grad=qkv_grad,
            gain_one_grad=gain_one_grad,
            layer_grad=(grads["hidden_grad"] + in_norm_grad).astype(bf),
        )

    first = forward(inputs[0].reshape(tokens, width))
    second = forward(lax.ppermute(first["output_b"], "section", [(0, 1)]))
    second_back = ffn_backward(second, cotangent[0].reshape(tokens, width))
    second_back = attention_back(second, second_back)
    received = lax.ppermute(second_back["layer_grad"], "section", [(1, 0)])
    first_back = attention_back(first, ffn_backward(first, received))

    kept = {name: jnp.where(is_first, first[name], second[name]) for name in KEPT}
    back = {name: jnp.where(is_first, first_back[name], second_back[name]) for name in BACK}

    expert_parts = [
        wide_einsum("erd,erf->edf", kept["expert_in"], back["gate_pre_grad"]),
        wide_einsum("erd,erf->edf", kept["expert_in"], back["up_pre_grad"]),
        wide_einsum("erf,erd->efd", kept["activated"], back["expert_grad"]),
    ]
    expert_parts = [part.astype(bf) for part in expert_parts]
    expert_grads = [part.astype(f32) + twin(part).astype(f32) for part in expert_parts]

    def both(value):
        return jnp.concatenate([value, twin(value)], axis=0)

    def both_halves(low_half, high_half):
        own, other = mine_of(low_half, high_half), mine_of(high_half, low_half)
        return jnp.concatenate([own, twin(other)], axis=0)

    grad_gate_up = dot_tn(
        both(kept["normed_two"]), both_halves(back["shared_gate_grad"], back["shared_up_grad"])
    )
    grad_down = dot_tn(both(kept["shared_act"]), both_halves(*halves(back["upstream_b"])))
    shared_flat = (shards, down_rows * width // 2 // shared_width, shared_width)
    shared_pieces = jnp.concatenate(
        [
            grad_gate_up.astype(bf).reshape(shards, rows_per, shared_width),
            grad_down.astype(bf).reshape(shared_flat),
        ],
        axis=1,
    )
    share_shared = jnp.sum(exchange(shared_pieces).astype(f32), axis=0)
    other_shared = twin(share_shared)

    grad_out = dot_tn(
        kept["attended"].reshape(heads * tokens, group_width), back["ring_hidden"]
    )
    share_out = jnp.sum(
        exchange(grad_out.astype(bf).reshape(ring, rows_per, width), zy_groups).astype(f32), axis=0
    )
    grad_qkv = dot_tn(kept["ring_one"], back["qkv_grad"])
    grad_router = dot_tn(kept["normed_two"], back["logit_grad"])
    gain_sums = jnp.stack([back["gain_one_grad"], back["gain_two_grad"]])
    grad_tail = jnp.concatenate(
        [grad_router, gain_sums.T, jnp.zeros((width, 128 - experts - 2), f32)], axis=1
    )
    pieces = exchange(
        jnp.concatenate([grad_qkv, grad_tail], axis=1)
        .astype(bf)
        .reshape(shards, rows_per, part_width + 128)
    ).astype(f32)
    share_qkv = jnp.sum(
        pieces[:, :, :part_width].reshape(heads, ring, rows_per, part_width), axis=1
    )
    share_qkv = share_qkv.transpose(1, 0, 2)
    share_tail = jnp.sum(pieces[:, :, part_width:], axis=0)

    def total(share):
        return share + twin(share)

    out_total, qkv_total, tail_total = total(share_out), total(share_qkv), total(share_tail)
    low_shared, high_shared = (
        mine_of(share_shared, other_shared),
        mine_of(other_shared, share_shared),
    )
    down_shape = (down_rows, width // 2)
    down_total = jnp.concatenate(
        [low_shared[rows_per:].reshape(down_shape), high_shared[rows_per:].reshape(down_shape)],
        axis=1,
    )
    token_shape = (1, 1, micros, block, width)
    return (
        jnp.where(is_first, first["output_b"], second["output_b"]).reshape(token_shape),
        jnp.where(is_first, first_back["layer_grad"], second_back["layer_grad"]).reshape(
            token_shape
        ),
        tail_total[:, experts][None],
        qkv_total[:, :, :group_width].reshape(1, rows_per, head_width),
        qkv_total[:, :, group_width : group_width + HD].reshape(1, rows_per, key_width),
        qkv_total[:, :, group_width + HD :].reshape(1, rows_per, key_width),
        out_total[None],
        tail_total[:, experts + 1][None],
        tail_total[:, :experts][None],
        low_shared[:rows_per][None],
        high_shared[:rows_per][None],
        down_total[None],
        expert_grads[0][None],
        expert_grads[1][None],
        expert_grads[2][None],
    )


def solution(mesh):
    rows = P("section", "shard", None)
    vector = P("section", "shard")
    expert = P("section", "shard", None, None)
    tokens = P("dp", None, "shard", None)
    section_tokens = P("section", "dp", None, "shard", None)
    weights = (vector, rows, rows, rows, rows, vector, rows, rows, rows, rows) + (expert,) * 3
    return jax.shard_map(
        body,
        mesh=mesh,
        in_specs=(tokens, tokens, section_tokens) + weights,
        out_specs=(section_tokens, section_tokens) + weights,
        check_vma=False,
    )
```

```python
import functools

import jax
import jax.numpy as jnp
from jax import lax
from jax.experimental import pallas as pl
from jax.experimental.pallas import tpu as pltpu
from jax.sharding import PartitionSpec as P

H = 12
KVH = 4
HD = 128
GROUP = H // KVH
TOPK = 6
CAP = 8

epsilon = 1e-05
masked_score = -1e30
scaling = HD ** (-0.5)
log2_scale = scaling * 1.4426950408889634
bf = jnp.bfloat16
f32 = jnp.float32
VMEM_LIMIT = 32 * 1024 * 1024
KEPT = ("ring_one", "attended", "normed_two", "shared_act", "expert_in", "activated")
BACK = (
    "qkv_grad",
    "ring_hidden",
    "gain_one_grad",
    "gain_two_grad",
    "logit_grad",
    "upstream_b",
    "shared_gate_grad",
    "shared_up_grad",
    "expert_grad",
    "gate_pre_grad",
    "up_pre_grad",
)


def inverse_rms(rows):
    return lax.rsqrt(jnp.mean(rows * rows, axis=-1, keepdims=True) + epsilon)


def norm_back(layer_in, gain, upstream):
    inverse = inverse_rms(layer_in)
    unit_rows = layer_in * inverse
    gain_grad = jnp.sum(upstream * unit_rows, axis=0)
    scaled = upstream * gain
    in_grad = inverse * (scaled - unit_rows * jnp.mean(scaled * unit_rows, axis=-1, keepdims=True))
    return (in_grad, gain_grad)


def silu_parts(argument):
    sigmoid = jax.nn.sigmoid(argument)
    return argument * sigmoid, sigmoid * (1.0 + argument * (1.0 - sigmoid))


def dot(left_side, right_side):
    return jnp.dot(left_side, right_side, preferred_element_type=f32)


def dot_nt(left_side, right_side):
    return lax.dot_general(
        left_side, right_side, (((1,), (1,)), ((), ())), preferred_element_type=f32
    )


def dot_tn(left_side, right_side):
    return lax.dot_general(
        left_side, right_side, (((0,), (0,)), ((), ())), preferred_element_type=f32
    )


def wide_einsum(formula, left_side, right_side):
    return jnp.einsum(formula, left_side, right_side, preferred_element_type=f32)


def stacked_heads(ref, part, micro):
    return jnp.concatenate(
        [ref[part, micro, :, g * HD : (g + 1) * HD] for g in range(GROUP)], axis=0
    )


def store_heads(ref, part, micro, rows):
    block = ref.shape[2]
    for g in range(GROUP):
        ref[part, micro, :, g * HD : (g + 1) * HD] = rows[g * block : (g + 1) * block]


def diagonal_mask(rows, chunk, block, zy):
    key_at = lax.broadcasted_iota(jnp.int32, (rows, chunk), 1)
    row_at = lax.broadcasted_iota(jnp.int32, (rows, chunk), 0)
    return key_at <= zy * block + lax.rem(row_at, block)


def attention_forward_kernel(info_ref, q_ref, kv_ref, o_ref, log_ref):
    parts, micros, block, _ = q_ref.shape
    span = kv_ref.shape[1]
    chunk = span // parts
    rows = GROUP * block
    mask = diagonal_mask(rows, chunk, block, info_ref[0])
    for part in range(parts):
        for micro in range(micros):
            queries = stacked_heads(q_ref, part, micro)
            pieces = [(m, 0, span) for m in range(micro)]
            if part > 0:
                pieces.append((micro, 0, part * chunk))
            pieces.append((micro, part * chunk, (part + 1) * chunk))
            scores = [dot_nt(queries, kv_ref[m, start:stop, :HD]) for m, start, stop in pieces]
            scores[-1] = jnp.where(mask, scores[-1], masked_score)
            peak = functools.reduce(
                jnp.maximum, [jnp.max(s, axis=-1, keepdims=True) for s in scores]
            )
            peak = peak * log2_scale
            total = jnp.zeros((rows, 1), f32)
            mixed = jnp.zeros((rows, HD), f32)
            for s, (m, start, stop) in zip(scores, pieces):
                probs = jnp.exp2(s * log2_scale - peak)
                total = total + jnp.sum(probs, axis=-1, keepdims=True)
                mixed = mixed + dot(probs.astype(bf), kv_ref[m, start:stop, HD:])
            store_heads(o_ref, part, micro, (mixed / total).astype(bf))
            log_ref[part, micro] = jnp.broadcast_to(peak + jnp.log2(total), (rows, HD))


def attention_backward_kernel(
    info_ref, q_ref, do_ref, o_ref, log_ref, kv_ref, dq_ref, dkv_ref
):
    parts, micros, block, _ = q_ref.shape
    span = kv_ref.shape[1]
    chunk = span // parts
    rows = GROUP * block
    mask = diagonal_mask(rows, chunk, block, info_ref[0])
    dkv_ref[...] = jnp.zeros(dkv_ref.shape, f32)
    for part in range(parts):
        for micro in range(micros):
            queries = stacked_heads(q_ref, part, micro)
            out_grad = stacked_heads(do_ref, part, micro)
            out = stacked_heads(o_ref, part, micro)
            inner = jnp.sum(out_grad.astype(f32) * out.astype(f32), axis=-1, keepdims=True)
            log_total = log_ref[part, micro][:, :1]
            query_grad = jnp.zeros((rows, HD), f32)
            pieces = [(m, start) for m in range(micro) for start in range(0, span, chunk)]
            pieces += [(micro, start) for start in range(0, (part + 1) * chunk, chunk)]
            for m, start in pieces:
                keys = kv_ref[m, start : start + chunk, :HD]
                probs = jnp.exp2(dot_nt(queries, keys) * log2_scale - log_total)
                if (m, start) == (micro, part * chunk):
                    probs = jnp.where(mask, probs, 0.0)
                probs_grad = dot_nt(out_grad, kv_ref[m, start : start + chunk, HD:])
                score_grad = (probs * (probs_grad - inner)).astype(bf)
                query_grad = query_grad + dot(score_grad, keys)
                dkv_ref[m, start : start + chunk, :HD] += dot_tn(score_grad, queries) * scaling
                dkv_ref[m, start : start + chunk, HD:] += dot_tn(probs.astype(bf), out_grad)
            store_heads(dq_ref, part, micro, (query_grad * scaling).astype(bf))


def in_vmem(count):
    return [pl.BlockSpec(memory_space=pltpu.VMEM)] * count


def attention_call(kernel, factor, out_shape, info, queries, *rest):
    parts, micros, block, _ = queries.shape
    rows = parts * micros * GROUP * block
    keys = rest[-1].shape[0] * rest[-1].shape[1]
    return pl.pallas_call(
        kernel,
        out_shape=out_shape,
        in_specs=[pl.BlockSpec(memory_space=pltpu.SMEM)] + in_vmem(1 + len(rest)),
        out_specs=tuple(in_vmem(len(out_shape))),
        compiler_params=pltpu.CompilerParams(vmem_limit_bytes=VMEM_LIMIT),
        cost_estimate=pl.CostEstimate(
            flops=factor * rows * keys * HD,
            bytes_accessed=factor * (keys + rows) * HD,
            transcendentals=rows * keys // 2,
        ),
    )(info, queries, *rest)


def attention_forward(info, queries, kv):
    parts, micros, block, _ = queries.shape
    logs = jax.ShapeDtypeStruct((parts, micros, GROUP * block, HD), f32)
    out = jax.ShapeDtypeStruct(queries.shape, bf)
    return attention_call(attention_forward_kernel, 2, (out, logs), info, queries, kv)


def attention_backward(info, queries, out_grad, out, logs, kv):
    shapes = (jax.ShapeDtypeStruct(queries.shape, bf), jax.ShapeDtypeStruct(kv.shape, f32))
    return attention_call(
        attention_backward_kernel, 5, shapes, info, queries, out_grad, out, logs, kv
    )


def body(
    inputs,
    cotangent,
    routes,
    norm_attn,
    w_query,
    w_key,
    w_value,
    w_output,
    norm_ffn,
    w_router,
    shared_gate,
    shared_up,
    shared_down,
    expert_gate,
    expert_up,
    expert_down,
):
    micros, block, width = inputs.shape[1:]
    tokens = micros * block
    shards = lax.axis_size("shard")
    section = lax.axis_index("section")
    core = lax.axis_index("dp")
    position = lax.axis_index("shard")
    heads = KVH
    ring = shards // heads
    local_experts = expert_gate.shape[1]
    experts = local_experts * shards
    room = micros * CAP
    slots = experts * room
    rows_per = w_query.shape[1]
    half_rows = rows_per // 2
    group_width = GROUP * HD
    head_width = H * HD
    key_width = KVH * HD
    part_width = group_width + 2 * HD
    shared_width = shared_gate.shape[2]
    down_rows = shared_down.shape[1]
    is_first = section == 0
    low_core = core == 0
    x_groups = [[x * ring + zy for x in range(heads)] for zy in range(ring)]
    zy_groups = [[x * ring + zy for zy in range(ring)] for x in range(heads)]

    def exchange(value, groups=None):
        return lax.all_to_all(
            value, "shard", split_axis=0, concat_axis=0, tiled=True, axis_index_groups=groups
        )

    def copies(value, count):
        return jnp.broadcast_to(value[None], (count,) + value.shape)

    def twin(value):
        return lax.ppermute(value, "dp", [(0, 1), (1, 0)])

    def mine_of(low_half, high_half):
        return jnp.where(low_core, low_half, high_half)

    def ordered(own, other, axis):
        low_half, high_half = mine_of(own, other), mine_of(other, own)
        return jnp.concatenate([low_half, high_half], axis=axis)

    def halves(value):
        half = value.shape[-1] // 2
        return value[..., :half], value[..., half:]

    def my_rows(value):
        return mine_of(value[..., :half_rows, :], value[..., half_rows:, :])

    tail = jnp.concatenate(
        [
            w_router[0],
            norm_attn[0][:, None],
            norm_ffn[0][:, None],
            jnp.zeros((rows_per, 128 - experts - 2), bf),
        ],
        axis=1,
    )
    by_head = jnp.concatenate(
        [
            w_query[0].reshape(rows_per, heads, group_width),
            w_key[0].reshape(rows_per, heads, HD),
            w_value[0].reshape(rows_per, heads, HD),
            jnp.broadcast_to(tail[:, None], (rows_per, heads, 128)),
        ],
        axis=2,
    ).transpose(1, 0, 2)
    by_head = my_rows(by_head)
    by_head = jnp.broadcast_to(
        by_head[:, None], (heads, ring, half_rows, part_width + 128)
    ).reshape(shards, half_rows, part_width + 128)
    own_part = exchange(by_head)
    fetched = ordered(own_part, twin(own_part), 1).reshape(width, part_width + 128)
    qkv_w, tail = fetched[:, :part_width], fetched[:, part_width:]
    router_w = tail[:, :experts]
    gains = tail[:, experts : experts + 2].T.astype(f32)
    gain_one, gain_two = gains[0][None], gains[1][None]

    down_flat = (rows_per, down_rows * width // 2 // rows_per)
    shared_rows = jnp.concatenate(
        [
            mine_of(shared_gate[0], shared_up[0]),
            mine_of(*halves(shared_down[0])).reshape(down_flat),
        ],
        axis=1,
    )
    gathered = lax.all_gather(
        jnp.concatenate([shared_rows, my_rows(w_output[0])], axis=0), "shard"
    )
    own_shared = gathered[:, :rows_per].reshape(width, width)
    own_out = lax.dynamic_slice_in_dim(
        gathered[:, rows_per:], (position // ring) * ring, ring, axis=0
    )
    other_shared = twin(own_shared)
    output_w = ordered(own_out, twin(own_out), 1).reshape(group_width, width)

    def cut(value):
        down = value[:, shared_width:].reshape(down_rows * shards, width // 2)
        return value[:, :shared_width], down

    gate_up_w, down_w = zip(cut(own_shared), cut(other_shared))

    def project(rows, pair):
        return ordered(dot(rows, pair[0]), dot(rows, pair[1]), 1)

    def project_back(low_half, high_half, pair):
        own, other = mine_of(low_half, high_half), mine_of(high_half, low_half)
        return dot_nt(own, pair[0]) + dot_nt(other, pair[1])

    expert_g, expert_u, expert_d = expert_gate[0], expert_up[0], expert_down[0]
    local_routes = routes[0, 0].reshape(tokens, TOPK)
    slot_of = jnp.arange(slots, dtype=jnp.int32)
    expert_of = jnp.arange(experts, dtype=jnp.int32)
    token_of = jnp.arange(tokens, dtype=jnp.int32)
    spread = (expert_of[:, None] == slot_of[None, :] // room).astype(bf)
    router_slots = dot(router_w, spread).astype(bf)
    named = jnp.any(local_routes[:, :, None] == expert_of[None, None, :], axis=1).astype(bf)
    earlier = (token_of[:, None] > token_of[None, :]) & (
        token_of[:, None] // block == token_of[None, :] // block
    )
    slot_ids = dot(earlier.astype(bf), named).astype(jnp.int32) + CAP * (token_of // block)[:, None]
    table = (dot(named, spread) > 0.5) & (
        dot(slot_ids.astype(bf), spread).astype(jnp.int32) == (slot_of % room)[None, :]
    )
    pick = table.astype(bf)
    info = jnp.stack([position % ring]).astype(jnp.int32)

    def gate_values(normed_two):
        logits = jnp.where(table, dot(normed_two, router_slots), masked_score)
        weights = jnp.exp(logits - jnp.max(logits, axis=-1, keepdims=True))
        weights = jnp.where(table, weights, 0.0)
        return weights / jnp.sum(weights, axis=-1, keepdims=True)

    def high_low(value):
        high = value.astype(bf)
        return high, (value - high.astype(f32)).astype(bf)

    def to_experts(rows):
        return (
            exchange(rows.reshape(shards, local_experts, room, width))
            .transpose(1, 0, 2, 3)
            .reshape(local_experts, shards * room, width)
        )

    def from_experts(rows):
        return exchange(
            rows.reshape(local_experts, shards, room, width).transpose(1, 0, 2, 3)
        ).reshape(slots, width)

    def sum_over_x(rows):
        parts = exchange(rows.astype(bf).reshape(heads, tokens, width), x_groups)
        return jnp.sum(parts.astype(f32), axis=0)

    def ring_rows(rows):
        return exchange(copies(rows, heads), x_groups).reshape(heads * tokens, width)

    def attend(layer_b):
        layer_in = layer_b.astype(f32)
        normed_one = (layer_in * inverse_rms(layer_in) * gain_one).astype(bf)
        ring_one = ring_rows(normed_one)
        qkv = dot(ring_one, qkv_w).astype(bf)
        queries = qkv[:, :group_width].reshape(heads, micros, block, group_width)
        pairs = exchange(copies(qkv[:, group_width:], ring), zy_groups)
        pairs = pairs.reshape(ring, heads, micros, block, 2 * HD).transpose(2, 1, 0, 3, 4)
        cache = pairs.reshape(micros, shards * block, 2 * HD)
        attended, logs = attention_forward(info, queries, cache)
        return dict(
            layer_b=layer_b,
            ring_one=ring_one,
            queries=queries,
            cache=cache,
            attended=attended,
            logs=logs,
        )

    def feed(kept):
        attended = kept["attended"].reshape(heads * tokens, group_width)
        hidden = kept["layer_b"].astype(f32) + sum_over_x(dot(attended, output_w))
        normed_two = (hidden * inverse_rms(hidden) * gain_two).astype(bf)
        gates = gate_values(normed_two)
        expert_in = to_experts(dot_tn(pick, normed_two).astype(bf))
        gate_pre = wide_einsum("erd,edf->erf", expert_in, expert_g)
        up_pre = wide_einsum("erd,edf->erf", expert_in, expert_u)
        activated = (silu_parts(gate_pre)[0] * up_pre).astype(bf)
        returned = from_experts(wide_einsum("erf,efd->erd", activated, expert_d).astype(bf))
        high, low = high_low(gates)
        routed = dot(high, returned) + dot(low, returned)
        shared_gate_pre, shared_up_pre = halves(project(normed_two, gate_up_w))
        shared_act = (silu_parts(shared_gate_pre)[0] * shared_up_pre).astype(bf)
        output_b = (hidden + routed + project(shared_act, down_w)).astype(bf)
        return dict(
            hidden=hidden,
            normed_two=normed_two,
            gates=gates,
            expert_in=expert_in,
            gate_pre=gate_pre,
            up_pre=up_pre,
            activated=activated,
            returned=returned,
            shared_gate_pre=shared_gate_pre,
            shared_up_pre=shared_up_pre,
            shared_act=shared_act,
            output_b=output_b,
        )

    def ffn_backward(kept, upstream_b):
        upstream = upstream_b.astype(f32)
        gates, hidden = kept["gates"], kept["hidden"]
        high, low = high_low(gates)
        outgoing = dot_tn(high, upstream_b) + dot_tn(low, upstream_b)
        expert_grad = to_experts(outgoing.astype(bf))
        act_silu, act_slope = silu_parts(kept["gate_pre"])
        act_grad = wide_einsum("erd,efd->erf", expert_grad, expert_d)
        gate_pre_grad = (act_grad * kept["up_pre"] * act_slope).astype(bf)
        up_pre_grad = (act_grad * act_silu).astype(bf)
        expert_in_grad = (
            wide_einsum("erf,edf->erd", gate_pre_grad, expert_g)
            + wide_einsum("erf,edf->erd", up_pre_grad, expert_u)
        ).astype(bf)
        returned_grad = from_experts(expert_in_grad)
        shared_act_grad = project_back(*halves(upstream_b), down_w)
        shared_silu, shared_slope = silu_parts(kept["shared_gate_pre"])
        shared_gate_grad = (shared_act_grad * kept["shared_up_pre"] * shared_slope).astype(bf)
        shared_up_grad = (shared_act_grad * shared_silu).astype(bf)
        normed_two_grad = project_back(shared_gate_grad, shared_up_grad, gate_up_w)
        gate_grad = dot_nt(upstream_b, kept["returned"])
        picked_grad = gates * (gate_grad - jnp.sum(gates * gate_grad, axis=1, keepdims=True))
        picked_b = picked_grad.astype(bf)
        normed_two_grad = normed_two_grad + dot_nt(picked_b, router_slots)
        normed_two_grad = normed_two_grad + dot(pick, returned_grad)
        logit_grad = dot_nt(picked_b, spread).astype(bf)
        hidden_norm_grad, gain_two_grad = norm_back(hidden, gain_two, normed_two_grad)
        return dict(
            hidden_grad=upstream + hidden_norm_grad,
            upstream_b=upstream_b,
            expert_grad=expert_grad,
            gate_pre_grad=gate_pre_grad,
            up_pre_grad=up_pre_grad,
            shared_gate_grad=shared_gate_grad,
            shared_up_grad=shared_up_grad,
            logit_grad=logit_grad,
            gain_two_grad=gain_two_grad,
        )

    def attention_back(kept, grads):
        ring_hidden = ring_rows(grads["hidden_grad"].astype(bf))
        out_grad = dot_nt(ring_hidden, output_w).astype(bf)
        out_grad = out_grad.reshape(heads, micros, block, group_width)
        query_grad, cache_grad = attention_backward(
            info, kept["queries"], out_grad, kept["attended"], kept["logs"], kept["cache"]
        )
        parts = cache_grad.astype(bf).reshape(micros, heads, ring, block, 2 * HD)
        parts = parts.transpose(2, 1, 0, 3, 4).reshape(ring, heads * tokens, 2 * HD)
        pair_grad = jnp.sum(exchange(parts, zy_groups).astype(f32), axis=0).astype(bf)
        qkv_grad = jnp.concatenate(
            [query_grad.reshape(heads * tokens, group_width), pair_grad], axis=1
        )
        normed_one_grad = sum_over_x(dot_nt(qkv_grad, qkv_w))
        in_norm_grad, gain_one_grad = norm_back(
            kept["layer_b"].astype(f32), gain_one, normed_one_grad
        )
        return dict(
            grads,
            ring_hidden=ring_hidden,
            qkv_grad=qkv_grad,
            gain_one_grad=gain_one_grad,
            layer_grad=(grads["hidden_grad"] + in_norm_grad).astype(bf),
        )

    def only(wanted, live):
        def dead():
            return jax.tree.map(lambda leaf: jnp.zeros(leaf.shape, leaf.dtype), jax.eval_shape(live))

        return lax.cond(wanted, live, dead)

    def weight_grads(kept, back):
        expert_parts = [
            wide_einsum("erd,erf->edf", kept["expert_in"], back["gate_pre_grad"]),
            wide_einsum("erd,erf->edf", kept["expert_in"], back["up_pre_grad"]),
            wide_einsum("erf,erd->efd", kept["activated"], back["expert_grad"]),
        ]
        expert_parts = [part.astype(bf) for part in expert_parts]
        expert_grads = [part.astype(f32) + twin(part).astype(f32) for part in expert_parts]

        def both(value):
            return jnp.concatenate([value, twin(value)], axis=0)

        def both_halves(low_half, high_half):
            own, other = mine_of(low_half, high_half), mine_of(high_half, low_half)
            return jnp.concatenate([own, twin(other)], axis=0)

        grad_gate_up = dot_tn(
            both(kept["normed_two"]), both_halves(back["shared_gate_grad"], back["shared_up_grad"])
        )
        grad_down = dot_tn(both(kept["shared_act"]), both_halves(*halves(back["upstream_b"])))
        shared_flat = (shards, down_rows * width // 2 // shared_width, shared_width)
        shared_pieces = jnp.concatenate(
            [
                grad_gate_up.astype(bf).reshape(shards, rows_per, shared_width),
                grad_down.astype(bf).reshape(shared_flat),
            ],
            axis=1,
        )
        share_shared = jnp.sum(exchange(shared_pieces).astype(f32), axis=0)
        other_shared = twin(share_shared)

        grad_out = dot_tn(
            kept["attended"].reshape(heads * tokens, group_width), back["ring_hidden"]
        )
        share_out = jnp.sum(
            exchange(grad_out.astype(bf).reshape(ring, rows_per, width), zy_groups).astype(f32), axis=0
        )
        grad_qkv = dot_tn(kept["ring_one"], back["qkv_grad"])
        grad_router = dot_tn(kept["normed_two"], back["logit_grad"])
        gain_sums = jnp.stack([back["gain_one_grad"], back["gain_two_grad"]])
        grad_tail = jnp.concatenate(
            [grad_router, gain_sums.T, jnp.zeros((width, 128 - experts - 2), f32)], axis=1
        )
        pieces = exchange(
            jnp.concatenate([grad_qkv, grad_tail], axis=1)
            .astype(bf)
            .reshape(shards, rows_per, part_width + 128)
        ).astype(f32)
        share_qkv = jnp.sum(
            pieces[:, :, :part_width].reshape(heads, ring, rows_per, part_width), axis=1
        )
        share_qkv = share_qkv.transpose(1, 0, 2)
        share_tail = jnp.sum(pieces[:, :, part_width:], axis=0)

        def total(share):
            return share + twin(share)

        out_total, qkv_total, tail_total = total(share_out), total(share_qkv), total(share_tail)
        low_shared, high_shared = (
            mine_of(share_shared, other_shared),
            mine_of(other_shared, share_shared),
        )
        down_shape = (down_rows, width // 2)
        down_total = jnp.concatenate(
            [low_shared[rows_per:].reshape(down_shape), high_shared[rows_per:].reshape(down_shape)],
            axis=1,
        )
        return (
            tail_total[:, experts],
            qkv_total[:, :, :group_width].reshape(rows_per, head_width),
            qkv_total[:, :, group_width : group_width + HD].reshape(rows_per, key_width),
            qkv_total[:, :, group_width + HD :].reshape(rows_per, key_width),
            out_total,
            tail_total[:, experts + 1],
            tail_total[:, :experts],
            low_shared[:rows_per],
            high_shared[:rows_per],
            down_total,
        ) + tuple(expert_grads)

    def second_phase(layer_b):
        kept = attend(layer_b)
        kept = dict(kept, **feed(kept))
        back = ffn_backward(kept, cotangent[0].reshape(tokens, width))
        back = attention_back(kept, back)
        return (
            {name: kept[name] for name in KEPT + ("output_b",)},
            {name: back[name] for name in BACK + ("layer_grad",)},
        )

    def first_last(kept, received):
        back = attention_back(kept, ffn_backward(kept, received))
        return (back["layer_grad"], kept["output_b"]) + weight_grads(kept, back)

    def second_last(kept, back):
        return (back["layer_grad"], kept["output_b"]) + weight_grads(kept, back)

    first = attend(inputs[0].reshape(tokens, width))
    first = dict(first, **only(is_first, lambda: feed(first)))
    received = lax.ppermute(first["output_b"], "section", [(0, 1)])
    second, second_back = only(jnp.logical_not(is_first), lambda: second_phase(received))
    received_back = lax.ppermute(second_back["layer_grad"], "section", [(1, 0)])
    layer_grad, output_b, *weight_totals = lax.cond(
        is_first,
        lambda: first_last(first, received_back),
        lambda: second_last(second, second_back),
    )
    token_shape = (1, 1, micros, block, width)
    return (output_b.reshape(token_shape), layer_grad.reshape(token_shape)) + tuple(
        value[None] for value in weight_totals
    )


def solution(mesh):
    rows = P("section", "shard", None)
    vector = P("section", "shard")
    expert = P("section", "shard", None, None)
    tokens = P("dp", None, "shard", None)
    section_tokens = P("section", "dp", None, "shard", None)
    weights = (vector, rows, rows, rows, rows, vector, rows, rows, rows, rows) + (expert,) * 3
    return jax.shard_map(
        body,
        mesh=mesh,
        in_specs=(tokens, tokens, section_tokens) + weights,
        out_specs=(section_tokens, section_tokens) + weights,
        check_vma=False,
    )
```

```python
import functools

import jax
import jax.numpy as jnp
from jax import lax
from jax.experimental import pallas as pl
from jax.experimental.pallas import tpu as pltpu
from jax.sharding import PartitionSpec as P

H = 12
KVH = 4
HD = 128
GROUP = H // KVH
TOPK = 6
CAP = 8

epsilon = 1e-05
masked_score = -1e30
scaling = HD ** (-0.5)
log2_scale = scaling * 1.4426950408889634
bf = jnp.bfloat16
f32 = jnp.float32
VMEM_LIMIT = 32 * 1024 * 1024


def inverse_rms(rows):
    return lax.rsqrt(jnp.mean(rows * rows, axis=-1, keepdims=True) + epsilon)


def norm_back(layer_in, gain, upstream):
    inverse = inverse_rms(layer_in)
    unit_rows = layer_in * inverse
    gain_grad = jnp.sum(upstream * unit_rows, axis=0)
    scaled = upstream * gain
    in_grad = inverse * (scaled - unit_rows * jnp.mean(scaled * unit_rows, axis=-1, keepdims=True))
    return (in_grad, gain_grad)


def silu_parts(argument):
    sigmoid = jax.nn.sigmoid(argument)
    return argument * sigmoid, sigmoid * (1.0 + argument * (1.0 - sigmoid))


def dot(left_side, right_side):
    return jnp.dot(left_side, right_side, preferred_element_type=f32)


def dot_nt(left_side, right_side):
    return lax.dot_general(
        left_side, right_side, (((1,), (1,)), ((), ())), preferred_element_type=f32
    )


def dot_tn(left_side, right_side):
    return lax.dot_general(
        left_side, right_side, (((0,), (0,)), ((), ())), preferred_element_type=f32
    )


def wide_einsum(formula, left_side, right_side):
    return jnp.einsum(formula, left_side, right_side, preferred_element_type=f32)


def stacked_heads(ref, part):
    return jnp.concatenate(
        [ref[part, :, g * HD : (g + 1) * HD] for g in range(GROUP)], axis=0
    )


def store_heads(ref, part, rows):
    block = ref.shape[1]
    for g in range(GROUP):
        ref[part, :, g * HD : (g + 1) * HD] = rows[g * block : (g + 1) * block]


def cached(ref, start, stop, column):
    rows = ref[:, start:stop, column : column + HD]
    return rows.reshape(rows.shape[0] * rows.shape[1], HD)


def diagonal_mask(rows, chunk, block, zy):
    key_at = lax.broadcasted_iota(jnp.int32, (rows, chunk), 1)
    row_at = lax.broadcasted_iota(jnp.int32, (rows, chunk), 0)
    return key_at <= zy * block + lax.rem(row_at, block)


def attention_forward_kernel(has_prev, info_ref, q_ref, *refs):
    prev_ref = refs[0] if has_prev else None
    cur_ref, o_ref, log_ref = refs[-3:]
    parts, block, _ = q_ref.shape
    rows = GROUP * block
    mask = diagonal_mask(rows, cur_ref.shape[0] * block, block, info_ref[0])
    for part in range(parts):
        queries = stacked_heads(q_ref, part)
        pieces = [(prev_ref, 0, parts * block)] if has_prev else []
        if part > 0:
            pieces.append((cur_ref, 0, part * block))
        pieces.append((cur_ref, part * block, (part + 1) * block))
        scores = [dot_nt(queries, cached(ref, start, stop, 0)) for ref, start, stop in pieces]
        if has_prev:
            scores[0] = scores[0] + jnp.where(info_ref[1] > 0, 0.0, masked_score).astype(f32)
        scores[-1] = jnp.where(mask, scores[-1], masked_score)
        peak = functools.reduce(
            jnp.maximum, [jnp.max(s, axis=-1, keepdims=True) for s in scores]
        )
        peak = peak * log2_scale
        total = jnp.zeros((rows, 1), f32)
        mixed = jnp.zeros((rows, HD), f32)
        for s, (ref, start, stop) in zip(scores, pieces):
            probs = jnp.exp2(s * log2_scale - peak)
            total = total + jnp.sum(probs, axis=-1, keepdims=True)
            mixed = mixed + dot(probs.astype(bf), cached(ref, start, stop, HD))
        store_heads(o_ref, part, (mixed / total).astype(bf))
        log_ref[part] = jnp.broadcast_to(peak + jnp.log2(total), (rows, HD))


def attention_backward_kernel(has_prev, has_carry, info_ref, q_ref, do_ref, o_ref, log_ref, *refs):
    refs = list(refs)
    sum_ref = refs.pop()
    carry_ref = refs.pop(0) if has_carry else None
    prev_ref = refs.pop(0) if has_prev else None
    cur_ref, dq_ref, dcur_ref = refs[:3]
    dprev_ref = refs[3] if has_prev else None
    sum_ref[...] = carry_ref[...] if has_carry else jnp.zeros(sum_ref.shape, f32)
    if has_prev:
        dprev_ref[...] = jnp.zeros(dprev_ref.shape, f32)
    parts, block, _ = q_ref.shape
    ring = cur_ref.shape[0]
    rows = GROUP * block
    mask = diagonal_mask(rows, ring * block, block, info_ref[0])
    for part in range(parts):
        queries = stacked_heads(q_ref, part)
        out_grad = stacked_heads(do_ref, part)
        out = stacked_heads(o_ref, part)
        inner = jnp.sum(out_grad.astype(f32) * out.astype(f32), axis=-1, keepdims=True)
        log_total = log_ref[part][:, :1]
        query_grad = jnp.zeros((rows, HD), f32)
        pieces = []
        if has_prev:
            log_prev = log_total + jnp.where(info_ref[1] > 0, 0.0, -masked_score).astype(f32)
            pieces = [(prev_ref, dprev_ref, p, log_prev) for p in range(parts)]
        pieces += [(cur_ref, sum_ref, p, log_total) for p in range(part + 1)]
        for ref, grad_ref, at, log_row in pieces:
            start, stop = at * block, (at + 1) * block
            keys = cached(ref, start, stop, 0)
            probs = jnp.exp2(dot_nt(queries, keys) * log2_scale - log_row)
            if ref is cur_ref and at == part:
                probs = jnp.where(mask, probs, 0.0)
            probs_grad = dot_nt(out_grad, cached(ref, start, stop, HD))
            score_grad = (probs * (probs_grad - inner)).astype(bf)
            query_grad = query_grad + dot(score_grad, keys)
            key_grad = dot_tn(score_grad, queries) * scaling
            value_grad = dot_tn(probs.astype(bf), out_grad)
            grad_ref[:, start:stop, :HD] += key_grad.reshape(ring, block, HD)
            grad_ref[:, start:stop, HD:] += value_grad.reshape(ring, block, HD)
        store_heads(dq_ref, part, (query_grad * scaling).astype(bf))
    dcur_ref[...] = sum_ref[...].astype(bf)


def attention_call(kernel, factor, out_shape, scratch, info, queries, *rest):
    parts, block, _ = queries.shape
    rows = parts * GROUP * block
    keys = sum(ref.shape[0] * ref.shape[1] for ref in rest if ref.shape == rest[-1].shape)
    in_vmem = pl.BlockSpec(memory_space=pltpu.VMEM)
    return pl.pallas_call(
        kernel,
        out_shape=out_shape,
        in_specs=[pl.BlockSpec(memory_space=pltpu.SMEM)] + [in_vmem] * (1 + len(rest)),
        out_specs=(in_vmem,) * len(out_shape),
        scratch_shapes=scratch,
        compiler_params=pltpu.CompilerParams(vmem_limit_bytes=VMEM_LIMIT),
        cost_estimate=pl.CostEstimate(
            flops=factor * rows * keys * HD,
            bytes_accessed=factor * (keys + rows) * HD,
            transcendentals=rows * keys // 2,
        ),
    )(info, queries, *rest)


def attention_forward(info, qkv, prev, cur):
    parts, block, _ = qkv.shape
    shapes = (
        jax.ShapeDtypeStruct((parts, block, GROUP * HD), bf),
        jax.ShapeDtypeStruct((parts, GROUP * block, HD), f32),
    )
    caches = (cur,) if prev is None else (prev, cur)
    kernel = functools.partial(attention_forward_kernel, prev is not None)
    return attention_call(kernel, 2, shapes, [], info, qkv, *caches)


def attention_backward(info, qkv, out_grad, out, logs, carry, prev, cur):
    shapes = (jax.ShapeDtypeStruct(out.shape, bf), jax.ShapeDtypeStruct(cur.shape, bf))
    if prev is not None:
        shapes += (jax.ShapeDtypeStruct(cur.shape, f32),)
    extra = tuple(value for value in (carry, prev) if value is not None)
    kernel = functools.partial(attention_backward_kernel, prev is not None, carry is not None)
    scratch = [pltpu.VMEM(cur.shape, f32)]
    return attention_call(
        kernel, 5, shapes, scratch, info, qkv, out_grad, out, logs, *extra, cur
    )


def body(
    inputs,
    cotangent,
    routes,
    norm_attn,
    w_query,
    w_key,
    w_value,
    w_output,
    norm_ffn,
    w_router,
    shared_gate,
    shared_up,
    shared_down,
    expert_gate,
    expert_up,
    expert_down,
):
    micros, block, width = inputs.shape[1:]
    shards = lax.axis_size("shard")
    section = lax.axis_index("section")
    core = lax.axis_index("dp")
    position = lax.axis_index("shard")
    heads = KVH
    ring = shards // heads
    local_experts = expert_gate.shape[1]
    experts = local_experts * shards
    slots = experts * CAP
    rows_per = w_query.shape[1]
    half_rows = rows_per // 2
    group_width = GROUP * HD
    head_width = H * HD
    key_width = KVH * HD
    part_width = group_width + 2 * HD
    shared_width = shared_gate.shape[2]
    down_rows = shared_down.shape[1]
    is_first = section == 0
    low_core = core == 0
    x_groups = [[x * ring + zy for x in range(heads)] for zy in range(ring)]
    zy_groups = [[x * ring + zy for zy in range(ring)] for x in range(heads)]

    def exchange(value, groups=None):
        return lax.all_to_all(
            value, "shard", split_axis=0, concat_axis=0, tiled=True, axis_index_groups=groups
        )

    def copies(value, count):
        return jnp.broadcast_to(value[None], (count,) + value.shape)

    def twin(value):
        return lax.ppermute(value, "dp", [(0, 1), (1, 0)])

    def mine_of(low_half, high_half):
        return jnp.where(low_core, low_half, high_half)

    def ordered(own, other, axis):
        low_half, high_half = mine_of(own, other), mine_of(other, own)
        return jnp.concatenate([low_half, high_half], axis=axis)

    def halves(value):
        half = value.shape[-1] // 2
        return value[..., :half], value[..., half:]

    def my_rows(value):
        return mine_of(value[..., :half_rows, :], value[..., half_rows:, :])

    tail = jnp.concatenate(
        [
            w_router[0],
            norm_attn[0][:, None],
            norm_ffn[0][:, None],
            jnp.zeros((rows_per, 128 - experts - 2), bf),
        ],
        axis=1,
    )
    by_head = jnp.concatenate(
        [
            w_query[0].reshape(rows_per, heads, group_width),
            w_key[0].reshape(rows_per, heads, HD),
            w_value[0].reshape(rows_per, heads, HD),
            jnp.broadcast_to(tail[:, None], (rows_per, heads, 128)),
        ],
        axis=2,
    ).transpose(1, 0, 2)
    by_head = my_rows(by_head)
    by_head = jnp.broadcast_to(
        by_head[:, None], (heads, ring, half_rows, part_width + 128)
    ).reshape(shards, half_rows, part_width + 128)
    own_part = exchange(by_head)
    fetched = ordered(own_part, twin(own_part), 1).reshape(width, part_width + 128)
    qkv_w, tail = fetched[:, :part_width], fetched[:, part_width:]
    router_w = tail[:, :experts]
    gains = tail[:, experts : experts + 2].T.astype(f32)
    gain_one, gain_two = gains[0][None], gains[1][None]

    down_half = down_rows // 2
    down_flat = (half_rows, down_half * width // half_rows)
    packed = jnp.concatenate(
        [
            my_rows(jnp.concatenate([shared_gate[0], shared_up[0], w_output[0]], axis=1)),
            mine_of(shared_down[0][:down_half], shared_down[0][down_half:]).reshape(down_flat),
        ],
        axis=1,
    )
    gathered = lax.all_gather(packed, "shard")
    ends = (2 * shared_width, 2 * shared_width + width)
    own_gate_up = gathered[:, :, : ends[0]]
    own_down = gathered[:, :, ends[1] :].reshape(shards, down_half, width)
    own_out = lax.dynamic_slice_in_dim(
        gathered[:, :, ends[0] : ends[1]], (position // ring) * ring, ring, axis=0
    )
    output_w = ordered(own_out, twin(own_out), 1).reshape(group_width, width)
    gate_up_w = ordered(own_gate_up, twin(own_gate_up), 1).reshape(width, 2 * shared_width)
    down_w = ordered(own_down, twin(own_down), 1).reshape(shards * down_rows, width)

    expert_g, expert_u, expert_d = expert_gate[0], expert_up[0], expert_down[0]
    slot_of = jnp.arange(slots, dtype=jnp.int32)
    expert_of = jnp.arange(experts, dtype=jnp.int32)
    row_of = jnp.arange(block, dtype=jnp.int32)
    spread = (expert_of[:, None] == slot_of[None, :] // CAP).astype(bf)
    router_slots = dot(router_w, spread).astype(bf)
    earlier = (row_of[:, None] > row_of[None, :]).astype(bf)

    def slot_table(route_rows):
        named = jnp.any(route_rows[:, :, None] == expert_of[None, None, :], axis=1).astype(bf)
        slot_ids = dot(earlier, named).astype(bf)
        return (dot(named, spread) > 0.5) & (
            dot(slot_ids, spread).astype(jnp.int32) == (slot_of % CAP)[None, :]
        )

    info = jnp.stack([position % ring, is_first.astype(jnp.int32)]).astype(jnp.int32)
    info_all = jnp.stack([position % ring, jnp.ones_like(position)]).astype(jnp.int32)

    def gate_values(normed_two, table):
        logits = jnp.where(table, dot(normed_two, router_slots), masked_score)
        weights = jnp.exp(logits - jnp.max(logits, axis=-1, keepdims=True))
        weights = jnp.where(table, weights, 0.0)
        return weights / jnp.sum(weights, axis=-1, keepdims=True)

    def high_low(value):
        high = value.astype(bf)
        return high, (value - high.astype(f32)).astype(bf)

    def to_experts(rows):
        return (
            exchange(rows.reshape(shards, local_experts, CAP, width))
            .transpose(1, 0, 2, 3)
            .reshape(local_experts, shards * CAP, width)
        )

    def from_experts(rows):
        return exchange(
            rows.reshape(local_experts, shards, CAP, width).transpose(1, 0, 2, 3)
        ).reshape(slots, width)

    def sum_over_x(rows):
        parts = exchange(rows.astype(bf).reshape(heads, block, width), x_groups)
        return jnp.sum(parts.astype(f32), axis=0)

    def ring_rows(rows):
        return exchange(copies(rows, heads), x_groups).reshape(heads * block, width)

    def forward(moment, received, previous):
        first_micro = min(moment, micros - 1)
        second_micro = max(moment - 1, 0)
        layer_b = jnp.where(is_first, inputs[0, first_micro], received)
        table = slot_table(
            jnp.where(is_first, routes[0, 0, first_micro], routes[0, 0, second_micro])
        )
        pick = table.astype(bf)
        layer_in = layer_b.astype(f32)
        normed_one = (layer_in * inverse_rms(layer_in) * gain_one).astype(bf)
        ring_one = ring_rows(normed_one)
        qkv = dot(ring_one, qkv_w).astype(bf)
        cache = exchange(copies(qkv[:, group_width:], ring), zy_groups)
        qkv = qkv.reshape(heads, block, part_width)
        attn_info = info if moment == 1 else info_all
        attended, logs = attention_forward(attn_info, qkv, previous, cache)
        attended_rows = attended.reshape(heads * block, group_width)
        hidden = layer_in + sum_over_x(dot(attended_rows, output_w))
        normed_two = (hidden * inverse_rms(hidden) * gain_two).astype(bf)
        gates = gate_values(normed_two, table)
        expert_in = to_experts(dot_tn(pick, normed_two).astype(bf))
        gate_pre = wide_einsum("erd,edf->erf", expert_in, expert_g)
        up_pre = wide_einsum("erd,edf->erf", expert_in, expert_u)
        activated = (silu_parts(gate_pre)[0] * up_pre).astype(bf)
        returned = from_experts(wide_einsum("erf,efd->erd", activated, expert_d).astype(bf))
        high, low = high_low(gates)
        routed = dot(high, returned) + dot(low, returned)
        shared_gate_pre, shared_up_pre = halves(dot(normed_two, gate_up_w))
        shared_act = (silu_parts(shared_gate_pre)[0] * shared_up_pre).astype(bf)
        output_b = (hidden + routed + dot(shared_act, down_w)).astype(bf)
        return dict(
            layer_b=layer_b,
            pick=pick,
            ring_one=ring_one,
            qkv=qkv,
            cache=cache,
            previous=previous,
            info=attn_info,
            attended=attended,
            logs=logs,
            hidden=hidden,
            normed_two=normed_two,
            gates=gates,
            expert_in=expert_in,
            gate_pre=gate_pre,
            up_pre=up_pre,
            activated=activated,
            returned=returned,
            shared_gate_pre=shared_gate_pre,
            shared_up_pre=shared_up_pre,
            shared_act=shared_act,
            output_b=output_b,
        )

    def ffn_backward(kept, upstream_b):
        upstream = upstream_b.astype(f32)
        gates, hidden = kept["gates"], kept["hidden"]
        high, low = high_low(gates)
        outgoing = dot_tn(high, upstream_b) + dot_tn(low, upstream_b)
        expert_grad = to_experts(outgoing.astype(bf))
        act_silu, act_slope = silu_parts(kept["gate_pre"])
        act_grad = wide_einsum("erd,efd->erf", expert_grad, expert_d)
        gate_pre_grad = (act_grad * kept["up_pre"] * act_slope).astype(bf)
        up_pre_grad = (act_grad * act_silu).astype(bf)
        expert_in_grad = (
            wide_einsum("erf,edf->erd", gate_pre_grad, expert_g)
            + wide_einsum("erf,edf->erd", up_pre_grad, expert_u)
        ).astype(bf)
        returned_grad = from_experts(expert_in_grad)
        shared_act_grad = dot_nt(upstream_b, down_w)
        shared_silu, shared_slope = silu_parts(kept["shared_gate_pre"])
        shared_gate_grad = (shared_act_grad * kept["shared_up_pre"] * shared_slope).astype(bf)
        shared_up_grad = (shared_act_grad * shared_silu).astype(bf)
        normed_two_grad = dot_nt(
            jnp.concatenate([shared_gate_grad, shared_up_grad], axis=1), gate_up_w
        )
        gate_grad = dot_nt(upstream_b, kept["returned"])
        picked_grad = gates * (gate_grad - jnp.sum(gates * gate_grad, axis=1, keepdims=True))
        picked_b = picked_grad.astype(bf)
        normed_two_grad = normed_two_grad + dot_nt(picked_b, router_slots)
        normed_two_grad = normed_two_grad + dot(kept["pick"], returned_grad)
        logit_grad = dot_nt(picked_b, spread).astype(bf)
        hidden_norm_grad, gain_two_grad = norm_back(hidden, gain_two, normed_two_grad)
        return dict(
            hidden_grad=upstream + hidden_norm_grad,
            upstream_b=upstream_b,
            expert_grad=expert_grad,
            gate_pre_grad=gate_pre_grad,
            up_pre_grad=up_pre_grad,
            shared_gate_grad=shared_gate_grad,
            shared_up_grad=shared_up_grad,
            logit_grad=logit_grad,
            gain_two_grad=gain_two_grad,
        )

    def attention_back(kept, grads, carried):
        ring_hidden = ring_rows(grads["hidden_grad"].astype(bf))
        out_grad = dot_nt(ring_hidden, output_w).astype(bf)
        results = attention_backward(
            kept["info"],
            kept["qkv"],
            out_grad.reshape(heads, block, group_width),
            kept["attended"],
            kept["logs"],
            carried,
            kept["previous"],
            kept["cache"],
        )
        carried = results[2] if len(results) > 2 else None
        pair_grad = jnp.sum(exchange(results[1], zy_groups).astype(f32), axis=0).astype(bf)
        qkv_grad = jnp.concatenate(
            [results[0].reshape(heads * block, group_width), pair_grad], axis=1
        )
        normed_one_grad = sum_over_x(dot_nt(qkv_grad, qkv_w))
        in_norm_grad, gain_one_grad = norm_back(
            kept["layer_b"].astype(f32), gain_one, normed_one_grad
        )
        grads = dict(
            grads,
            ring_hidden=ring_hidden,
            qkv_grad=qkv_grad,
            gain_one_grad=gain_one_grad,
            layer_grad=(grads["hidden_grad"] + in_norm_grad).astype(bf),
        )
        return grads, carried

    nothing = jnp.zeros((block, width), bf)
    saved = []
    received, previous = nothing, None
    for moment in range(micros + 1):
        kept = forward(moment, received, previous)
        saved.append(kept)
        previous = kept["cache"]
        if moment < micros:
            received = lax.ppermute(kept["output_b"], "section", [(0, 1)])
    backs = [None] * (micros + 1)
    received, carried = nothing, None
    for source in range(micros, -1, -1):
        own = cotangent[0, source - 1] if source > 0 else nothing
        upstream_b = jnp.where(is_first, received, own)
        grads = ffn_backward(saved[source], upstream_b)
        backs[source], carried = attention_back(saved[source], grads, carried)
        if source > 0:
            received = lax.ppermute(backs[source]["layer_grad"], "section", [(1, 0)])

    def live(name, store, axis):
        ends = jnp.where(is_first, store[0][name], store[micros][name])
        return jnp.concatenate([ends, store[1][name]], axis=axis)

    def kept_rows(name, axis=0):
        return live(name, saved, axis)

    def back_rows(name, axis=0):
        return live(name, backs, axis)

    expert_parts = [
        wide_einsum("erd,erf->edf", kept_rows("expert_in", 1), back_rows("gate_pre_grad", 1)),
        wide_einsum("erd,erf->edf", kept_rows("expert_in", 1), back_rows("up_pre_grad", 1)),
        wide_einsum("erf,erd->efd", kept_rows("activated", 1), back_rows("expert_grad", 1)),
    ]
    expert_parts = [part.astype(bf) for part in expert_parts]
    expert_grads = [part.astype(f32) + twin(part).astype(f32) for part in expert_parts]

    def both(value):
        return jnp.concatenate([value, twin(value)], axis=0)

    def both_halves(low_half, high_half):
        own, other = mine_of(low_half, high_half), mine_of(high_half, low_half)
        return jnp.concatenate([own, twin(other)], axis=0)

    normed_two = kept_rows("normed_two")
    grad_gate_up = dot_tn(
        both(normed_two), both_halves(back_rows("shared_gate_grad"), back_rows("shared_up_grad"))
    )
    grad_down = dot_tn(both(kept_rows("shared_act")), both_halves(*halves(back_rows("upstream_b"))))
    shared_flat = (shards, down_rows * width // 2 // shared_width, shared_width)
    shared_pieces = jnp.concatenate(
        [
            grad_gate_up.astype(bf).reshape(shards, rows_per, shared_width),
            grad_down.astype(bf).reshape(shared_flat),
        ],
        axis=1,
    )
    share_shared = jnp.sum(exchange(shared_pieces).astype(f32), axis=0)
    other_shared = twin(share_shared)

    grad_out = dot_tn(
        kept_rows("attended").reshape(micros * heads * block, group_width),
        back_rows("ring_hidden"),
    )
    share_out = jnp.sum(
        exchange(grad_out.astype(bf).reshape(ring, rows_per, width), zy_groups).astype(f32), axis=0
    )
    grad_qkv = dot_tn(kept_rows("ring_one"), back_rows("qkv_grad"))
    grad_router = dot_tn(normed_two, back_rows("logit_grad"))
    gain_sums = jnp.stack(
        [sum(grads[name] for grads in backs) for name in ("gain_one_grad", "gain_two_grad")]
    )
    grad_tail = jnp.concatenate(
        [grad_router, gain_sums.T, jnp.zeros((width, 128 - experts - 2), f32)], axis=1
    )
    pieces = exchange(
        jnp.concatenate([grad_qkv, grad_tail], axis=1)
        .astype(bf)
        .reshape(shards, rows_per, part_width + 128)
    ).astype(f32)
    share_qkv = jnp.sum(
        pieces[:, :, :part_width].reshape(heads, ring, rows_per, part_width), axis=1
    )
    share_qkv = share_qkv.transpose(1, 0, 2)
    share_tail = jnp.sum(pieces[:, :, part_width:], axis=0)

    def total(share):
        return share + twin(share)

    out_total, qkv_total, tail_total = total(share_out), total(share_qkv), total(share_tail)
    low_shared, high_shared = (
        mine_of(share_shared, other_shared),
        mine_of(other_shared, share_shared),
    )
    down_shape = (down_rows, width // 2)
    down_total = jnp.concatenate(
        [low_shared[rows_per:].reshape(down_shape), high_shared[rows_per:].reshape(down_shape)],
        axis=1,
    )
    def by_micro(store, name):
        return jnp.stack(
            [jnp.where(is_first, store[m][name], store[m + 1][name]) for m in range(micros)]
        )[None, None]

    return (
        by_micro(saved, "output_b"),
        by_micro(backs, "layer_grad"),
        tail_total[:, experts][None],
        qkv_total[:, :, :group_width].reshape(1, rows_per, head_width),
        qkv_total[:, :, group_width : group_width + HD].reshape(1, rows_per, key_width),
        qkv_total[:, :, group_width + HD :].reshape(1, rows_per, key_width),
        out_total[None],
        tail_total[:, experts + 1][None],
        tail_total[:, :experts][None],
        low_shared[:rows_per][None],
        high_shared[:rows_per][None],
        down_total[None],
        expert_grads[0][None],
        expert_grads[1][None],
        expert_grads[2][None],
    )


def solution(mesh):
    rows = P("section", "shard", None)
    vector = P("section", "shard")
    expert = P("section", "shard", None, None)
    tokens = P("dp", None, "shard", None)
    section_tokens = P("section", "dp", None, "shard", None)
    weights = (vector, rows, rows, rows, rows, vector, rows, rows, rows, rows) + (expert,) * 3
    return jax.shard_map(
        body,
        mesh=mesh,
        in_specs=(tokens, tokens, section_tokens) + weights,
        out_specs=(section_tokens, section_tokens) + weights,
        check_vma=False,
    )
```

```python
import functools

import jax
import jax.numpy as jnp
from jax import lax
from jax.experimental import pallas as pl
from jax.experimental.pallas import tpu as pltpu
from jax.sharding import PartitionSpec as P

H = 12
KVH = 4
HD = 128
GROUP = H // KVH
TOPK = 6
CAP = 8

epsilon = 1e-05
masked_score = -1e30
scaling = HD ** (-0.5)
log2_scale = scaling * 1.4426950408889634
bf = jnp.bfloat16
f32 = jnp.float32
VMEM_LIMIT = 32 * 1024 * 1024


def inverse_rms(rows):
    return lax.rsqrt(jnp.mean(rows * rows, axis=-1, keepdims=True) + epsilon)


def norm_back(layer_in, gain, upstream):
    inverse = inverse_rms(layer_in)
    unit_rows = layer_in * inverse
    gain_grad = jnp.sum(upstream * unit_rows, axis=0)
    scaled = upstream * gain
    in_grad = inverse * (scaled - unit_rows * jnp.mean(scaled * unit_rows, axis=-1, keepdims=True))
    return (in_grad, gain_grad)


def silu_parts(argument):
    sigmoid = jax.nn.sigmoid(argument)
    return argument * sigmoid, sigmoid * (1.0 + argument * (1.0 - sigmoid))


def dot(left_side, right_side):
    return jnp.dot(left_side, right_side, preferred_element_type=f32)


def dot_nt(left_side, right_side):
    return lax.dot_general(
        left_side, right_side, (((1,), (1,)), ((), ())), preferred_element_type=f32
    )


def dot_tn(left_side, right_side):
    return lax.dot_general(
        left_side, right_side, (((0,), (0,)), ((), ())), preferred_element_type=f32
    )


def wide_einsum(formula, left_side, right_side):
    return jnp.einsum(formula, left_side, right_side, preferred_element_type=f32)


def arrival(info_ref, parts, part):
    return lax.rem(info_ref[2] + parts - part, parts)


def stacked_heads(ref, at):
    return jnp.concatenate([ref[at, :, g * HD : (g + 1) * HD] for g in range(GROUP)], axis=0)


def store_heads(ref, at, rows):
    block = ref.shape[1]
    for g in range(GROUP):
        ref[at, :, g * HD : (g + 1) * HD] = rows[g * block : (g + 1) * block]


def cached(ref, span, column):
    rows = ref[:, span, column : column + HD]
    return rows.reshape(rows.shape[0] * rows.shape[1], HD)


def block_span(at, block):
    return pl.ds(pl.multiple_of(at * block, block), block)


def diagonal_mask(rows, chunk, block, zy):
    key_at = lax.broadcasted_iota(jnp.int32, (rows, chunk), 1)
    row_at = lax.broadcasted_iota(jnp.int32, (rows, chunk), 0)
    return key_at <= zy * block + lax.rem(row_at, block)


def attention_forward_kernel(has_prev, info_ref, q_ref, *refs):
    prev_ref = refs[0] if has_prev else None
    cur_ref, o_ref, log_ref = refs[-3:]
    parts, block, _ = q_ref.shape
    rows = GROUP * block
    mask = diagonal_mask(rows, cur_ref.shape[0] * block, block, info_ref[0])
    spans = [block_span(arrival(info_ref, parts, part), block) for part in range(parts)]
    for part in range(parts):
        at = arrival(info_ref, parts, part)
        queries = stacked_heads(q_ref, at)
        pieces = [(prev_ref, slice(None))] if has_prev else []
        pieces += [(cur_ref, spans[p]) for p in range(part + 1)]
        scores = [dot_nt(queries, cached(ref, span, 0)) for ref, span in pieces]
        if has_prev:
            scores[0] = scores[0] + jnp.where(info_ref[1] > 0, 0.0, masked_score).astype(f32)
        scores[-1] = jnp.where(mask, scores[-1], masked_score)
        peak = functools.reduce(
            jnp.maximum, [jnp.max(s, axis=-1, keepdims=True) for s in scores]
        )
        peak = peak * log2_scale
        total = jnp.zeros((rows, 1), f32)
        mixed = jnp.zeros((rows, HD), f32)
        for s, (ref, span) in zip(scores, pieces):
            probs = jnp.exp2(s * log2_scale - peak)
            total = total + jnp.sum(probs, axis=-1, keepdims=True)
            mixed = mixed + dot(probs.astype(bf), cached(ref, span, HD))
        store_heads(o_ref, at, (mixed / total).astype(bf))
        log_ref[at] = jnp.broadcast_to(peak + jnp.log2(total), (rows, HD))


def attention_backward_kernel(has_prev, has_carry, info_ref, q_ref, do_ref, o_ref, log_ref, *refs):
    refs = list(refs)
    sum_ref = refs.pop()
    carry_ref = refs.pop(0) if has_carry else None
    prev_ref = refs.pop(0) if has_prev else None
    cur_ref, dq_ref, dcur_ref = refs[:3]
    dprev_ref = refs[3] if has_prev else None
    sum_ref[...] = carry_ref[...] if has_carry else jnp.zeros(sum_ref.shape, f32)
    if has_prev:
        dprev_ref[...] = jnp.zeros(dprev_ref.shape, f32)
    parts, block, _ = q_ref.shape
    ring = cur_ref.shape[0]
    rows = GROUP * block
    mask = diagonal_mask(rows, ring * block, block, info_ref[0])
    spans = [block_span(arrival(info_ref, parts, part), block) for part in range(parts)]
    for part in range(parts):
        at = arrival(info_ref, parts, part)
        queries = stacked_heads(q_ref, at)
        out_grad = stacked_heads(do_ref, at)
        out = stacked_heads(o_ref, at)
        inner = jnp.sum(out_grad.astype(f32) * out.astype(f32), axis=-1, keepdims=True)
        log_total = log_ref[at][:, :1]
        query_grad = jnp.zeros((rows, HD), f32)
        pieces = []
        if has_prev:
            log_prev = log_total + jnp.where(info_ref[1] > 0, 0.0, -masked_score).astype(f32)
            pieces = [
                (prev_ref, dprev_ref, slice(p * block, (p + 1) * block), log_prev, False)
                for p in range(parts)
            ]
        pieces += [(cur_ref, sum_ref, spans[p], log_total, p == part) for p in range(part + 1)]
        for ref, grad_ref, span, log_row, on_diagonal in pieces:
            keys = cached(ref, span, 0)
            probs = jnp.exp2(dot_nt(queries, keys) * log2_scale - log_row)
            if on_diagonal:
                probs = jnp.where(mask, probs, 0.0)
            probs_grad = dot_nt(out_grad, cached(ref, span, HD))
            score_grad = (probs * (probs_grad - inner)).astype(bf)
            query_grad = query_grad + dot(score_grad, keys)
            key_grad = dot_tn(score_grad, queries) * scaling
            value_grad = dot_tn(probs.astype(bf), out_grad)
            grad_ref[:, span, :HD] += key_grad.reshape(ring, block, HD)
            grad_ref[:, span, HD:] += value_grad.reshape(ring, block, HD)
        store_heads(dq_ref, at, (query_grad * scaling).astype(bf))
    dcur_ref[...] = sum_ref[...].astype(bf)


def attention_call(kernel, factor, out_shape, scratch, info, queries, *rest):
    parts, block, _ = queries.shape
    rows = parts * GROUP * block
    keys = sum(ref.shape[0] * ref.shape[1] for ref in rest if ref.shape == rest[-1].shape)
    in_vmem = pl.BlockSpec(memory_space=pltpu.VMEM)
    return pl.pallas_call(
        kernel,
        out_shape=out_shape,
        in_specs=[pl.BlockSpec(memory_space=pltpu.SMEM)] + [in_vmem] * (1 + len(rest)),
        out_specs=(in_vmem,) * len(out_shape),
        scratch_shapes=scratch,
        compiler_params=pltpu.CompilerParams(vmem_limit_bytes=VMEM_LIMIT),
        cost_estimate=pl.CostEstimate(
            flops=factor * rows * keys * HD,
            bytes_accessed=factor * (keys + rows) * HD,
            transcendentals=rows * keys // 2,
        ),
    )(info, queries, *rest)


def attention_forward(info, qkv, prev, cur):
    parts, block, _ = qkv.shape
    shapes = (
        jax.ShapeDtypeStruct((parts, block, GROUP * HD), bf),
        jax.ShapeDtypeStruct((parts, GROUP * block, HD), f32),
    )
    caches = (cur,) if prev is None else (prev, cur)
    kernel = functools.partial(attention_forward_kernel, prev is not None)
    return attention_call(kernel, 2, shapes, [], info, qkv, *caches)


def attention_backward(info, qkv, out_grad, out, logs, carry, prev, cur):
    shapes = (jax.ShapeDtypeStruct(out.shape, bf), jax.ShapeDtypeStruct(cur.shape, bf))
    if prev is not None:
        shapes += (jax.ShapeDtypeStruct(cur.shape, f32),)
    extra = tuple(value for value in (carry, prev) if value is not None)
    kernel = functools.partial(attention_backward_kernel, prev is not None, carry is not None)
    scratch = [pltpu.VMEM(cur.shape, f32)]
    return attention_call(
        kernel, 5, shapes, scratch, info, qkv, out_grad, out, logs, *extra, cur
    )


def body(
    inputs,
    cotangent,
    routes,
    norm_attn,
    w_query,
    w_key,
    w_value,
    w_output,
    norm_ffn,
    w_router,
    shared_gate,
    shared_up,
    shared_down,
    expert_gate,
    expert_up,
    expert_down,
):
    micros, block, width = inputs.shape[1:]
    shards = lax.axis_size("shard")
    section = lax.axis_index("section")
    core = lax.axis_index("dp")
    position = lax.axis_index("shard")
    heads = KVH
    ring = shards // heads
    local_experts = expert_gate.shape[1]
    experts = local_experts * shards
    slots = experts * CAP
    rows_per = w_query.shape[1]
    half_rows = rows_per // 2
    group_width = GROUP * HD
    head_width = H * HD
    key_width = KVH * HD
    part_width = group_width + 2 * HD
    shared_width = shared_gate.shape[2]
    down_rows = shared_down.shape[1]
    is_first = section == 0
    low_core = core == 0
    zy_groups = [[x * ring + zy for zy in range(ring)] for x in range(heads)]

    def exchange(value, groups=None):
        return lax.all_to_all(
            value, "shard", split_axis=0, concat_axis=0, tiled=True, axis_index_groups=groups
        )

    def copies(value, count):
        return jnp.broadcast_to(value[None], (count,) + value.shape)

    def twin(value):
        return lax.ppermute(value, "dp", [(0, 1), (1, 0)])

    def mine_of(low_half, high_half):
        return jnp.where(low_core, low_half, high_half)

    def ordered(own, other, axis):
        low_half, high_half = mine_of(own, other), mine_of(other, own)
        return jnp.concatenate([low_half, high_half], axis=axis)

    def halves(value):
        half = value.shape[-1] // 2
        return value[..., :half], value[..., half:]

    def my_rows(value):
        return mine_of(value[..., :half_rows, :], value[..., half_rows:, :])

    tail = jnp.concatenate(
        [
            w_router[0],
            norm_attn[0][:, None],
            norm_ffn[0][:, None],
            jnp.zeros((rows_per, 128 - experts - 2), bf),
        ],
        axis=1,
    )
    by_head = jnp.concatenate(
        [
            w_query[0].reshape(rows_per, heads, group_width),
            w_key[0].reshape(rows_per, heads, HD),
            w_value[0].reshape(rows_per, heads, HD),
            jnp.broadcast_to(tail[:, None], (rows_per, heads, 128)),
        ],
        axis=2,
    ).transpose(1, 0, 2)
    by_head = my_rows(by_head)
    by_head = jnp.broadcast_to(
        by_head[:, None], (heads, ring, half_rows, part_width + 128)
    ).reshape(shards, half_rows, part_width + 128)
    own_part = exchange(by_head)
    fetched = ordered(own_part, twin(own_part), 1).reshape(width, part_width + 128)
    qkv_w, tail = fetched[:, :part_width], fetched[:, part_width:]
    router_w = tail[:, :experts]
    gains = tail[:, experts : experts + 2].T.astype(f32)
    gain_one, gain_two = gains[0][None], gains[1][None]

    all_out = lax.all_gather(my_rows(w_output[0]), "shard")
    own_out = lax.dynamic_slice_in_dim(all_out, (position // ring) * ring, ring, axis=0)
    output_w = ordered(own_out, twin(own_out), 1).reshape(group_width, width)
    down_half = down_rows // 2
    down_flat = (half_rows, down_half * width // half_rows)
    packed = jnp.concatenate(
        [
            my_rows(jnp.concatenate([shared_gate[0], shared_up[0]], axis=1)),
            mine_of(shared_down[0][:down_half], shared_down[0][down_half:]).reshape(down_flat),
        ],
        axis=1,
    )
    gathered = lax.all_gather(packed, "shard")
    own_gate_up = gathered[:, :, : 2 * shared_width]
    own_down = gathered[:, :, 2 * shared_width :].reshape(shards, down_half, width)
    gate_up_w = ordered(own_gate_up, twin(own_gate_up), 1).reshape(width, 2 * shared_width)
    down_w = ordered(own_down, twin(own_down), 1).reshape(shards * down_rows, width)

    expert_g, expert_u, expert_d = expert_gate[0], expert_up[0], expert_down[0]
    slot_of = jnp.arange(slots, dtype=jnp.int32)
    expert_of = jnp.arange(experts, dtype=jnp.int32)
    row_of = jnp.arange(block, dtype=jnp.int32)
    spread = (expert_of[:, None] == slot_of[None, :] // CAP).astype(bf)
    router_slots = dot(router_w, spread).astype(bf)
    earlier = (row_of[:, None] > row_of[None, :]).astype(bf)

    def slot_table(route_rows):
        named = jnp.any(route_rows[:, :, None] == expert_of[None, None, :], axis=1).astype(bf)
        slot_ids = dot(earlier, named).astype(bf)
        return (dot(named, spread) > 0.5) & (
            dot(slot_ids, spread).astype(jnp.int32) == (slot_of % CAP)[None, :]
        )

    here = [position % ring, jnp.ones_like(position), position // ring]
    info_all = jnp.stack(here).astype(jnp.int32)
    info = jnp.stack([here[0], is_first.astype(here[0].dtype), here[2]]).astype(jnp.int32)

    def gate_values(normed_two, table):
        logits = jnp.where(table, dot(normed_two, router_slots), masked_score)
        weights = jnp.exp(logits - jnp.max(logits, axis=-1, keepdims=True))
        weights = jnp.where(table, weights, 0.0)
        return weights / jnp.sum(weights, axis=-1, keepdims=True)

    def high_low(value):
        high = value.astype(bf)
        return high, (value - high.astype(f32)).astype(bf)

    def to_experts(rows):
        return (
            exchange(rows.reshape(shards, local_experts, CAP, width))
            .transpose(1, 0, 2, 3)
            .reshape(local_experts, shards * CAP, width)
        )

    def from_experts(rows):
        return exchange(
            rows.reshape(local_experts, shards, CAP, width).transpose(1, 0, 2, 3)
        ).reshape(slots, width)

    def shift_x(value, steps):
        pairs = [(p, (p // ring + steps) % heads * ring + p % ring) for p in range(shards)]
        return lax.ppermute(value, "shard", pairs)

    def sum_over_x(rows):
        parts = rows.reshape(heads, block, width)
        away = [shift_x(parts[k].astype(bf), -k).astype(f32) for k in range(1, heads)]
        return sum(away, parts[0])

    def ring_rows(rows):
        return jnp.concatenate([rows] + [shift_x(rows, k) for k in range(1, heads)], axis=0)

    def forward(moment, received, previous):
        first_micro = min(moment, micros - 1)
        second_micro = max(moment - 1, 0)
        layer_b = jnp.where(is_first, inputs[0, first_micro], received)
        table = slot_table(
            jnp.where(is_first, routes[0, 0, first_micro], routes[0, 0, second_micro])
        )
        pick = table.astype(bf)
        layer_in = layer_b.astype(f32)
        normed_one = (layer_in * inverse_rms(layer_in) * gain_one).astype(bf)
        ring_one = ring_rows(normed_one)
        qkv = dot(ring_one, qkv_w).astype(bf)
        cache = exchange(copies(qkv[:, group_width:], ring), zy_groups)
        qkv = qkv.reshape(heads, block, part_width)
        attn_info = info if moment == 1 else info_all
        attended, logs = attention_forward(attn_info, qkv, previous, cache)
        attended_rows = attended.reshape(heads * block, group_width)
        hidden = layer_in + sum_over_x(dot(attended_rows, output_w))
        normed_two = (hidden * inverse_rms(hidden) * gain_two).astype(bf)
        gates = gate_values(normed_two, table)
        expert_in = to_experts(dot_tn(pick, normed_two).astype(bf))
        gate_pre = wide_einsum("erd,edf->erf", expert_in, expert_g)
        up_pre = wide_einsum("erd,edf->erf", expert_in, expert_u)
        activated = (silu_parts(gate_pre)[0] * up_pre).astype(bf)
        returned = from_experts(wide_einsum("erf,efd->erd", activated, expert_d).astype(bf))
        high, low = high_low(gates)
        routed = dot(high, returned) + dot(low, returned)
        shared_gate_pre, shared_up_pre = halves(dot(normed_two, gate_up_w))
        shared_act = (silu_parts(shared_gate_pre)[0] * shared_up_pre).astype(bf)
        output_b = (hidden + routed + dot(shared_act, down_w)).astype(bf)
        return dict(
            layer_b=layer_b,
            pick=pick,
            ring_one=ring_one,
            qkv=qkv,
            cache=cache,
            previous=previous,
            info=attn_info,
            attended=attended,
            logs=logs,
            hidden=hidden,
            normed_two=normed_two,
            gates=gates,
            expert_in=expert_in,
            gate_pre=gate_pre,
            up_pre=up_pre,
            activated=activated,
            returned=returned,
            shared_gate_pre=shared_gate_pre,
            shared_up_pre=shared_up_pre,
            shared_act=shared_act,
            output_b=output_b,
        )

    def ffn_backward(kept, upstream_b):
        upstream = upstream_b.astype(f32)
        gates, hidden = kept["gates"], kept["hidden"]
        high, low = high_low(gates)
        outgoing = dot_tn(high, upstream_b) + dot_tn(low, upstream_b)
        expert_grad = to_experts(outgoing.astype(bf))
        act_silu, act_slope = silu_parts(kept["gate_pre"])
        act_grad = wide_einsum("erd,efd->erf", expert_grad, expert_d)
        gate_pre_grad = (act_grad * kept["up_pre"] * act_slope).astype(bf)
        up_pre_grad = (act_grad * act_silu).astype(bf)
        expert_in_grad = (
            wide_einsum("erf,edf->erd", gate_pre_grad, expert_g)
            + wide_einsum("erf,edf->erd", up_pre_grad, expert_u)
        ).astype(bf)
        returned_grad = from_experts(expert_in_grad)
        shared_act_grad = dot_nt(upstream_b, down_w)
        shared_silu, shared_slope = silu_parts(kept["shared_gate_pre"])
        shared_gate_grad = (shared_act_grad * kept["shared_up_pre"] * shared_slope).astype(bf)
        shared_up_grad = (shared_act_grad * shared_silu).astype(bf)
        normed_two_grad = dot_nt(
            jnp.concatenate([shared_gate_grad, shared_up_grad], axis=1), gate_up_w
        )
        gate_grad = dot_nt(upstream_b, kept["returned"])
        picked_grad = gates * (gate_grad - jnp.sum(gates * gate_grad, axis=1, keepdims=True))
        picked_b = picked_grad.astype(bf)
        normed_two_grad = normed_two_grad + dot_nt(picked_b, router_slots)
        normed_two_grad = normed_two_grad + dot(kept["pick"], returned_grad)
        logit_grad = dot_nt(picked_b, spread).astype(bf)
        hidden_norm_grad, gain_two_grad = norm_back(hidden, gain_two, normed_two_grad)
        return dict(
            hidden_grad=upstream + hidden_norm_grad,
            upstream_b=upstream_b,
            expert_grad=expert_grad,
            gate_pre_grad=gate_pre_grad,
            up_pre_grad=up_pre_grad,
            shared_gate_grad=shared_gate_grad,
            shared_up_grad=shared_up_grad,
            logit_grad=logit_grad,
            gain_two_grad=gain_two_grad,
        )

    def attention_back(kept, grads, carried):
        ring_hidden = ring_rows(grads["hidden_grad"].astype(bf))
        out_grad = dot_nt(ring_hidden, output_w).astype(bf)
        results = attention_backward(
            kept["info"],
            kept["qkv"],
            out_grad.reshape(heads, block, group_width),
            kept["attended"],
            kept["logs"],
            carried,
            kept["previous"],
            kept["cache"],
        )
        carried = results[2] if len(results) > 2 else None
        pair_grad = jnp.sum(exchange(results[1], zy_groups).astype(f32), axis=0).astype(bf)
        qkv_grad = jnp.concatenate(
            [results[0].reshape(heads * block, group_width), pair_grad], axis=1
        )
        normed_one_grad = sum_over_x(dot_nt(qkv_grad, qkv_w))
        in_norm_grad, gain_one_grad = norm_back(
            kept["layer_b"].astype(f32), gain_one, normed_one_grad
        )
        grads = dict(
            grads,
            ring_hidden=ring_hidden,
            qkv_grad=qkv_grad,
            gain_one_grad=gain_one_grad,
            layer_grad=(grads["hidden_grad"] + in_norm_grad).astype(bf),
        )
        return grads, carried

    nothing = jnp.zeros((block, width), bf)
    saved = []
    received, previous = nothing, None
    for moment in range(micros + 1):
        kept = forward(moment, received, previous)
        saved.append(kept)
        previous = kept["cache"]
        if moment < micros:
            received = lax.ppermute(kept["output_b"], "section", [(0, 1)])
    backs = [None] * (micros + 1)
    received, carried = nothing, None
    for source in range(micros, -1, -1):
        own = cotangent[0, source - 1] if source > 0 else nothing
        upstream_b = jnp.where(is_first, received, own)
        grads = ffn_backward(saved[source], upstream_b)
        backs[source], carried = attention_back(saved[source], grads, carried)
        if source > 0:
            received = lax.ppermute(backs[source]["layer_grad"], "section", [(1, 0)])

    def live(name, store, axis):
        ends = jnp.where(is_first, store[0][name], store[micros][name])
        return jnp.concatenate([ends, store[1][name]], axis=axis)

    def kept_rows(name, axis=0):
        return live(name, saved, axis)

    def back_rows(name, axis=0):
        return live(name, backs, axis)

    expert_parts = [
        wide_einsum("erd,erf->edf", kept_rows("expert_in", 1), back_rows("gate_pre_grad", 1)),
        wide_einsum("erd,erf->edf", kept_rows("expert_in", 1), back_rows("up_pre_grad", 1)),
        wide_einsum("erf,erd->efd", kept_rows("activated", 1), back_rows("expert_grad", 1)),
    ]
    expert_parts = [part.astype(bf) for part in expert_parts]
    expert_grads = [part.astype(f32) + twin(part).astype(f32) for part in expert_parts]

    def both(value):
        return jnp.concatenate([value, twin(value)], axis=0)

    def both_halves(low_half, high_half):
        own, other = mine_of(low_half, high_half), mine_of(high_half, low_half)
        return jnp.concatenate([own, twin(other)], axis=0)

    normed_two = kept_rows("normed_two")
    grad_gate_up = dot_tn(
        both(normed_two), both_halves(back_rows("shared_gate_grad"), back_rows("shared_up_grad"))
    )
    grad_down = dot_tn(both(kept_rows("shared_act")), both_halves(*halves(back_rows("upstream_b"))))

    def scattered(value, groups=None):
        count = shards if groups is None else len(groups[0])
        pieces = value.astype(bf).reshape(count, value.shape[0] // count, value.shape[1])
        return jnp.sum(exchange(pieces, groups).astype(f32), axis=0)

    share_gate_up, share_down = scattered(grad_gate_up), scattered(grad_down)

    grad_out = dot_tn(
        kept_rows("attended").reshape(micros * heads * block, group_width),
        back_rows("ring_hidden"),
    )
    share_out = scattered(grad_out, zy_groups)
    grad_qkv = dot_tn(kept_rows("ring_one"), back_rows("qkv_grad"))
    grad_router = dot_tn(normed_two, back_rows("logit_grad"))
    gain_sums = jnp.stack(
        [sum(grads[name] for grads in backs) for name in ("gain_one_grad", "gain_two_grad")]
    )
    grad_tail = jnp.concatenate(
        [grad_router, gain_sums.T, jnp.zeros((width, 128 - experts - 2), f32)], axis=1
    )
    pieces = exchange(
        jnp.concatenate([grad_qkv, grad_tail], axis=1)
        .astype(bf)
        .reshape(shards, rows_per, part_width + 128)
    ).astype(f32)
    share_qkv = jnp.sum(
        pieces[:, :, :part_width].reshape(heads, ring, rows_per, part_width), axis=1
    )
    share_qkv = share_qkv.transpose(1, 0, 2)
    share_tail = jnp.sum(pieces[:, :, part_width:], axis=0)

    def total(share):
        return share + twin(share)

    out_total, qkv_total, tail_total = total(share_out), total(share_qkv), total(share_tail)
    other_gate_up = twin(share_gate_up)
    down_total = ordered(share_down, twin(share_down), 1)

    def by_micro(store, name):
        return jnp.stack(
            [jnp.where(is_first, store[m][name], store[m + 1][name]) for m in range(micros)]
        )[None, None]

    return (
        by_micro(saved, "output_b"),
        by_micro(backs, "layer_grad"),
        tail_total[:, experts][None],
        qkv_total[:, :, :group_width].reshape(1, rows_per, head_width),
        qkv_total[:, :, group_width : group_width + HD].reshape(1, rows_per, key_width),
        qkv_total[:, :, group_width + HD :].reshape(1, rows_per, key_width),
        out_total[None],
        tail_total[:, experts + 1][None],
        tail_total[:, :experts][None],
        mine_of(share_gate_up, other_gate_up)[None],
        mine_of(other_gate_up, share_gate_up)[None],
        down_total[None],
        expert_grads[0][None],
        expert_grads[1][None],
        expert_grads[2][None],
    )


def solution(mesh):
    rows = P("section", "shard", None)
    vector = P("section", "shard")
    expert = P("section", "shard", None, None)
    tokens = P("dp", None, "shard", None)
    section_tokens = P("section", "dp", None, "shard", None)
    weights = (vector, rows, rows, rows, rows, vector, rows, rows, rows, rows) + (expert,) * 3
    return jax.shard_map(
        body,
        mesh=mesh,
        in_specs=(tokens, tokens, section_tokens) + weights,
        out_specs=(section_tokens, section_tokens) + weights,
        check_vma=False,
    )
```

```python
import functools

import jax
import jax.numpy as jnp
from jax import lax
from jax.experimental import pallas as pl
from jax.experimental.pallas import tpu as pltpu
from jax.sharding import PartitionSpec as P

H = 12
KVH = 4
HD = 128
GROUP = H // KVH
TOPK = 6
CAP = 8

epsilon = 1e-05
masked_score = -1e30
scaling = HD ** (-0.5)
log2_scale = scaling * 1.4426950408889634
bf = jnp.bfloat16
f32 = jnp.float32
VMEM_LIMIT = 32 * 1024 * 1024


def inverse_rms(rows):
    return lax.rsqrt(jnp.mean(rows * rows, axis=-1, keepdims=True) + epsilon)


def norm_back(layer_in, gain, upstream):
    inverse = inverse_rms(layer_in)
    unit_rows = layer_in * inverse
    gain_grad = jnp.sum(upstream * unit_rows, axis=0)
    scaled = upstream * gain
    in_grad = inverse * (scaled - unit_rows * jnp.mean(scaled * unit_rows, axis=-1, keepdims=True))
    return (in_grad, gain_grad)


def silu_parts(argument):
    sigmoid = jax.nn.sigmoid(argument)
    return argument * sigmoid, sigmoid * (1.0 + argument * (1.0 - sigmoid))


def dot(left_side, right_side):
    return jnp.dot(left_side, right_side, preferred_element_type=f32)


def dot_nt(left_side, right_side):
    return lax.dot_general(
        left_side, right_side, (((1,), (1,)), ((), ())), preferred_element_type=f32
    )


def dot_tn(left_side, right_side):
    return lax.dot_general(
        left_side, right_side, (((0,), (0,)), ((), ())), preferred_element_type=f32
    )


def wide_einsum(formula, left_side, right_side):
    return jnp.einsum(formula, left_side, right_side, preferred_element_type=f32)


def arrival(info_ref, parts, part):
    return lax.rem(info_ref[2] + parts - part, parts)


def stacked_heads(ref, at):
    return jnp.concatenate([ref[at, :, g * HD : (g + 1) * HD] for g in range(GROUP)], axis=0)


def store_heads(ref, at, rows):
    block = ref.shape[1]
    for g in range(GROUP):
        ref[at, :, g * HD : (g + 1) * HD] = rows[g * block : (g + 1) * block]


def cached(ref, span, column):
    rows = ref[:, span, column : column + HD]
    return rows.reshape(rows.shape[0] * rows.shape[1], HD)


def block_span(at, block):
    return pl.ds(pl.multiple_of(at * block, block), block)


def diagonal_mask(rows, chunk, block, zy):
    key_at = lax.broadcasted_iota(jnp.int32, (rows, chunk), 1)
    row_at = lax.broadcasted_iota(jnp.int32, (rows, chunk), 0)
    return key_at <= zy * block + lax.rem(row_at, block)


def attention_forward_kernel(has_prev, info_ref, q_ref, *refs):
    prev_ref = refs[0] if has_prev else None
    cur_ref, o_ref, log_ref = refs[-3:]
    parts, block, _ = q_ref.shape
    rows = GROUP * block
    mask = diagonal_mask(rows, cur_ref.shape[0] * block, block, info_ref[0])
    spans = [block_span(arrival(info_ref, parts, part), block) for part in range(parts)]
    for part in range(parts):
        at = arrival(info_ref, parts, part)
        queries = stacked_heads(q_ref, at)
        pieces = [(prev_ref, slice(None))] if has_prev else []
        pieces += [(cur_ref, spans[p]) for p in range(part + 1)]
        scores = [dot_nt(queries, cached(ref, span, 0)) for ref, span in pieces]
        if has_prev:
            scores[0] = scores[0] + jnp.where(info_ref[1] > 0, 0.0, masked_score).astype(f32)
        scores[-1] = jnp.where(mask, scores[-1], masked_score)
        peak = functools.reduce(
            jnp.maximum, [jnp.max(s, axis=-1, keepdims=True) for s in scores]
        )
        peak = peak * log2_scale
        total = jnp.zeros((rows, 1), f32)
        mixed = jnp.zeros((rows, HD), f32)
        for s, (ref, span) in zip(scores, pieces):
            probs = jnp.exp2(s * log2_scale - peak)
            total = total + jnp.sum(probs, axis=-1, keepdims=True)
            mixed = mixed + dot(probs.astype(bf), cached(ref, span, HD))
        store_heads(o_ref, at, (mixed / total).astype(bf))
        log_ref[at] = jnp.broadcast_to(peak + jnp.log2(total), (rows, HD))


def attention_backward_kernel(has_prev, has_carry, info_ref, q_ref, do_ref, o_ref, log_ref, *refs):
    refs = list(refs)
    sum_ref = refs.pop()
    carry_ref = refs.pop(0) if has_carry else None
    prev_ref = refs.pop(0) if has_prev else None
    cur_ref, dq_ref, dcur_ref = refs[:3]
    dprev_ref = refs[3] if has_prev else None
    sum_ref[...] = carry_ref[...] if has_carry else jnp.zeros(sum_ref.shape, f32)
    if has_prev:
        dprev_ref[...] = jnp.zeros(dprev_ref.shape, f32)
    parts, block, _ = q_ref.shape
    ring = cur_ref.shape[0]
    rows = GROUP * block
    mask = diagonal_mask(rows, ring * block, block, info_ref[0])
    spans = [block_span(arrival(info_ref, parts, part), block) for part in range(parts)]
    for part in range(parts):
        at = arrival(info_ref, parts, part)
        queries = stacked_heads(q_ref, at)
        out_grad = stacked_heads(do_ref, at)
        out = stacked_heads(o_ref, at)
        inner = jnp.sum(out_grad.astype(f32) * out.astype(f32), axis=-1, keepdims=True)
        log_total = log_ref[at][:, :1]
        query_grad = jnp.zeros((rows, HD), f32)
        pieces = []
        if has_prev:
            log_prev = log_total + jnp.where(info_ref[1] > 0, 0.0, -masked_score).astype(f32)
            pieces = [
                (prev_ref, dprev_ref, slice(p * block, (p + 1) * block), log_prev, False)
                for p in range(parts)
            ]
        pieces += [(cur_ref, sum_ref, spans[p], log_total, p == part) for p in range(part + 1)]
        for ref, grad_ref, span, log_row, on_diagonal in pieces:
            keys = cached(ref, span, 0)
            probs = jnp.exp2(dot_nt(queries, keys) * log2_scale - log_row)
            if on_diagonal:
                probs = jnp.where(mask, probs, 0.0)
            probs_grad = dot_nt(out_grad, cached(ref, span, HD))
            score_grad = (probs * (probs_grad - inner)).astype(bf)
            query_grad = query_grad + dot(score_grad, keys)
            key_grad = dot_tn(score_grad, queries) * scaling
            value_grad = dot_tn(probs.astype(bf), out_grad)
            grad_ref[:, span, :HD] += key_grad.reshape(ring, block, HD)
            grad_ref[:, span, HD:] += value_grad.reshape(ring, block, HD)
        store_heads(dq_ref, at, (query_grad * scaling).astype(bf))
    dcur_ref[...] = sum_ref[...].astype(bf)


def attention_call(kernel, factor, out_shape, scratch, info, queries, *rest):
    parts, block, _ = queries.shape
    rows = parts * GROUP * block
    keys = sum(ref.shape[0] * ref.shape[1] for ref in rest if ref.shape == rest[-1].shape)
    in_vmem = pl.BlockSpec(memory_space=pltpu.VMEM)
    return pl.pallas_call(
        kernel,
        out_shape=out_shape,
        in_specs=[pl.BlockSpec(memory_space=pltpu.SMEM)] + [in_vmem] * (1 + len(rest)),
        out_specs=(in_vmem,) * len(out_shape),
        scratch_shapes=scratch,
        compiler_params=pltpu.CompilerParams(vmem_limit_bytes=VMEM_LIMIT),
        cost_estimate=pl.CostEstimate(
            flops=factor * rows * keys * HD,
            bytes_accessed=factor * (keys + rows) * HD,
            transcendentals=rows * keys // 2,
        ),
    )(info, queries, *rest)


def attention_forward(info, qkv, prev, cur):
    parts, block, _ = qkv.shape
    shapes = (
        jax.ShapeDtypeStruct((parts, block, GROUP * HD), bf),
        jax.ShapeDtypeStruct((parts, GROUP * block, HD), f32),
    )
    caches = (cur,) if prev is None else (prev, cur)
    kernel = functools.partial(attention_forward_kernel, prev is not None)
    return attention_call(kernel, 2, shapes, [], info, qkv, *caches)


def attention_backward(info, qkv, out_grad, out, logs, carry, prev, cur):
    shapes = (jax.ShapeDtypeStruct(out.shape, bf), jax.ShapeDtypeStruct(cur.shape, bf))
    if prev is not None:
        shapes += (jax.ShapeDtypeStruct(cur.shape, f32),)
    extra = tuple(value for value in (carry, prev) if value is not None)
    kernel = functools.partial(attention_backward_kernel, prev is not None, carry is not None)
    scratch = [pltpu.VMEM(cur.shape, f32)]
    return attention_call(
        kernel, 5, shapes, scratch, info, qkv, out_grad, out, logs, *extra, cur
    )


def body(
    inputs,
    cotangent,
    routes,
    norm_attn,
    w_query,
    w_key,
    w_value,
    w_output,
    norm_ffn,
    w_router,
    shared_gate,
    shared_up,
    shared_down,
    expert_gate,
    expert_up,
    expert_down,
):
    micros, block, width = inputs.shape[1:]
    shards = lax.axis_size("shard")
    section = lax.axis_index("section")
    core = lax.axis_index("dp")
    position = lax.axis_index("shard")
    heads = KVH
    ring = shards // heads
    local_experts = expert_gate.shape[1]
    experts = local_experts * shards
    slots = experts * CAP
    rows_per = w_query.shape[1]
    half_rows = rows_per // 2
    group_width = GROUP * HD
    head_width = H * HD
    key_width = KVH * HD
    part_width = group_width + 2 * HD
    shared_width = shared_gate.shape[2]
    down_rows = shared_down.shape[1]
    is_first = section == 0
    low_core = core == 0
    zy_groups = [[x * ring + zy for zy in range(ring)] for x in range(heads)]

    def exchange(value, groups=None):
        return lax.all_to_all(
            value, "shard", split_axis=0, concat_axis=0, tiled=True, axis_index_groups=groups
        )

    def copies(value, count):
        return jnp.broadcast_to(value[None], (count,) + value.shape)

    def twin(value):
        return lax.ppermute(value, "dp", [(0, 1), (1, 0)])

    def mine_of(low_half, high_half):
        return jnp.where(low_core, low_half, high_half)

    def ordered(own, other, axis):
        low_half, high_half = mine_of(own, other), mine_of(other, own)
        return jnp.concatenate([low_half, high_half], axis=axis)

    def halves(value):
        half = value.shape[-1] // 2
        return value[..., :half], value[..., half:]

    def my_rows(value):
        return mine_of(value[..., :half_rows, :], value[..., half_rows:, :])

    tail = jnp.concatenate(
        [
            w_router[0],
            norm_attn[0][:, None],
            norm_ffn[0][:, None],
            jnp.zeros((rows_per, 128 - experts - 2), bf),
        ],
        axis=1,
    )
    by_head = jnp.concatenate(
        [
            w_query[0].reshape(rows_per, heads, group_width),
            w_key[0].reshape(rows_per, heads, HD),
            w_value[0].reshape(rows_per, heads, HD),
            jnp.broadcast_to(tail[:, None], (rows_per, heads, 128)),
        ],
        axis=2,
    ).transpose(1, 0, 2)
    by_head = my_rows(by_head)
    by_head = jnp.broadcast_to(
        by_head[:, None], (heads, ring, half_rows, part_width + 128)
    ).reshape(shards, half_rows, part_width + 128)
    down_half = down_rows // 2
    down_flat = (half_rows, down_half * width // half_rows)
    packed = jnp.concatenate(
        [
            my_rows(jnp.concatenate([shared_gate[0], shared_up[0]], axis=1)),
            mine_of(shared_down[0][:down_half], shared_down[0][down_half:]).reshape(down_flat),
        ],
        axis=1,
    )
    by_head, packed = lax.optimization_barrier((by_head, packed))
    gathered = lax.all_gather(packed, "shard")
    own_part = exchange(by_head)
    own_part, out_rows = lax.optimization_barrier(
        (own_part, copies(my_rows(w_output[0]), ring))
    )
    fetched = ordered(own_part, twin(own_part), 1).reshape(width, part_width + 128)
    qkv_w, tail = fetched[:, :part_width], fetched[:, part_width:]
    own_out = exchange(out_rows, zy_groups)
    output_w = ordered(own_out, twin(own_out), 1).reshape(group_width, width)
    own_gate_up = gathered[:, :, : 2 * shared_width]
    own_down = gathered[:, :, 2 * shared_width :].reshape(shards, down_half, width)
    gate_up_w = ordered(own_gate_up, twin(own_gate_up), 1).reshape(width, 2 * shared_width)
    down_w = ordered(own_down, twin(own_down), 1).reshape(shards * down_rows, width)
    router_w = tail[:, :experts]
    gains = tail[:, experts : experts + 2].T.astype(f32)
    gain_one, gain_two = gains[0][None], gains[1][None]

    expert_g, expert_u, expert_d = expert_gate[0], expert_up[0], expert_down[0]
    slot_of = jnp.arange(slots, dtype=jnp.int32)
    expert_of = jnp.arange(experts, dtype=jnp.int32)
    row_of = jnp.arange(block, dtype=jnp.int32)
    spread = (expert_of[:, None] == slot_of[None, :] // CAP).astype(bf)
    router_slots = dot(router_w, spread).astype(bf)
    earlier = (row_of[:, None] > row_of[None, :]).astype(bf)

    def slot_table(route_rows):
        named = jnp.any(route_rows[:, :, None] == expert_of[None, None, :], axis=1).astype(bf)
        slot_ids = dot(earlier, named).astype(bf)
        return (dot(named, spread) > 0.5) & (
            dot(slot_ids, spread).astype(jnp.int32) == (slot_of % CAP)[None, :]
        )

    here = [position % ring, jnp.ones_like(position), position // ring]
    info_all = jnp.stack(here).astype(jnp.int32)
    info = jnp.stack([here[0], is_first.astype(here[0].dtype), here[2]]).astype(jnp.int32)

    def gate_values(normed_two, table):
        logits = jnp.where(table, dot(normed_two, router_slots), masked_score)
        weights = jnp.exp(logits - jnp.max(logits, axis=-1, keepdims=True))
        weights = jnp.where(table, weights, 0.0)
        return weights / jnp.sum(weights, axis=-1, keepdims=True)

    def high_low(value):
        high = value.astype(bf)
        return high, (value - high.astype(f32)).astype(bf)

    def to_experts(rows):
        return (
            exchange(rows.reshape(shards, local_experts, CAP, width))
            .transpose(1, 0, 2, 3)
            .reshape(local_experts, shards * CAP, width)
        )

    def from_experts(rows):
        return exchange(
            rows.reshape(local_experts, shards, CAP, width).transpose(1, 0, 2, 3)
        ).reshape(slots, width)

    def moved(p, steps):
        return (p // ring + steps) % heads * ring + p % ring

    def shift_x(value, steps):
        return lax.ppermute(value, "shard", [(p, moved(p, steps)) for p in range(shards)])

    def next_ring(value):
        return jnp.stack(
            [
                lax.ppermute(
                    value,
                    ("section", "shard"),
                    [(p, shards + moved(p, steps)) for p in range(shards)],
                )
                for steps in range(heads)
            ]
        )

    def sum_over_x(rows):
        parts = rows.reshape(heads, block, width)
        away = [shift_x(parts[k].astype(bf), -k).astype(f32) for k in range(1, heads)]
        return sum(away, parts[0])

    def ring_rows(rows):
        return jnp.concatenate([rows] + [shift_x(rows, k) for k in range(1, heads)], axis=0)

    ring_inputs = [
        jnp.stack([inputs[0, m]] + [shift_x(inputs[0, m], k) for k in range(1, heads)])
        for m in range(micros)
    ]

    def forward(moment, received, previous):
        first_micro = min(moment, micros - 1)
        second_micro = max(moment - 1, 0)
        ring_b = jnp.where(is_first, ring_inputs[first_micro], received)
        layer_b = ring_b[0]
        table = slot_table(
            jnp.where(is_first, routes[0, 0, first_micro], routes[0, 0, second_micro])
        )
        pick = table.astype(bf)
        layer_in = layer_b.astype(f32)
        ring_in = ring_b.reshape(heads * block, width).astype(f32)
        ring_one = (ring_in * inverse_rms(ring_in) * gain_one).astype(bf)
        qkv = dot(ring_one, qkv_w).astype(bf)
        cache = exchange(copies(qkv[:, group_width:], ring), zy_groups)
        qkv = qkv.reshape(heads, block, part_width)
        attn_info = info if moment == 1 else info_all
        attended, logs = attention_forward(attn_info, qkv, previous, cache)
        attended_rows = attended.reshape(heads * block, group_width)
        hidden = layer_in + sum_over_x(dot(attended_rows, output_w))
        normed_two = (hidden * inverse_rms(hidden) * gain_two).astype(bf)
        gates = gate_values(normed_two, table)
        expert_in = to_experts(dot_tn(pick, normed_two).astype(bf))
        gate_pre = wide_einsum("erd,edf->erf", expert_in, expert_g)
        up_pre = wide_einsum("erd,edf->erf", expert_in, expert_u)
        activated = (silu_parts(gate_pre)[0] * up_pre).astype(bf)
        returned = from_experts(wide_einsum("erf,efd->erd", activated, expert_d).astype(bf))
        high, low = high_low(gates)
        routed = dot(high, returned) + dot(low, returned)
        shared_gate_pre, shared_up_pre = halves(dot(normed_two, gate_up_w))
        shared_act = (silu_parts(shared_gate_pre)[0] * shared_up_pre).astype(bf)
        beside = lax.optimization_barrier(hidden + dot(shared_act, down_w))
        output_b = (beside + routed).astype(bf)
        return dict(
            layer_b=layer_b,
            pick=pick,
            ring_one=ring_one,
            qkv=qkv,
            cache=cache,
            previous=previous,
            info=attn_info,
            attended=attended,
            logs=logs,
            hidden=hidden,
            normed_two=normed_two,
            gates=gates,
            expert_in=expert_in,
            gate_pre=gate_pre,
            up_pre=up_pre,
            activated=activated,
            returned=returned,
            shared_gate_pre=shared_gate_pre,
            shared_up_pre=shared_up_pre,
            shared_act=shared_act,
            output_b=output_b,
        )

    def ffn_backward(kept, upstream_b):
        upstream = upstream_b.astype(f32)
        gates, hidden = kept["gates"], kept["hidden"]
        high, low = high_low(gates)
        outgoing = dot_tn(high, upstream_b) + dot_tn(low, upstream_b)
        expert_grad = to_experts(outgoing.astype(bf))
        act_silu, act_slope = silu_parts(kept["gate_pre"])
        act_grad = wide_einsum("erd,efd->erf", expert_grad, expert_d)
        gate_pre_grad = (act_grad * kept["up_pre"] * act_slope).astype(bf)
        up_pre_grad = (act_grad * act_silu).astype(bf)
        expert_in_grad = (
            wide_einsum("erf,edf->erd", gate_pre_grad, expert_g)
            + wide_einsum("erf,edf->erd", up_pre_grad, expert_u)
        ).astype(bf)
        returned_grad = from_experts(expert_in_grad)
        shared_act_grad = dot_nt(upstream_b, down_w)
        shared_silu, shared_slope = silu_parts(kept["shared_gate_pre"])
        shared_gate_grad = (shared_act_grad * kept["shared_up_pre"] * shared_slope).astype(bf)
        shared_up_grad = (shared_act_grad * shared_silu).astype(bf)
        normed_two_grad = dot_nt(
            jnp.concatenate([shared_gate_grad, shared_up_grad], axis=1), gate_up_w
        )
        gate_grad = dot_nt(upstream_b, kept["returned"])
        picked_grad = gates * (gate_grad - jnp.sum(gates * gate_grad, axis=1, keepdims=True))
        picked_b = picked_grad.astype(bf)
        normed_two_grad = normed_two_grad + dot_nt(picked_b, router_slots)
        normed_two_grad = lax.optimization_barrier(normed_two_grad)
        normed_two_grad = normed_two_grad + dot(kept["pick"], returned_grad)
        logit_grad = dot_nt(picked_b, spread).astype(bf)
        hidden_norm_grad, gain_two_grad = norm_back(hidden, gain_two, normed_two_grad)
        return dict(
            hidden_grad=upstream + hidden_norm_grad,
            upstream_b=upstream_b,
            expert_grad=expert_grad,
            gate_pre_grad=gate_pre_grad,
            up_pre_grad=up_pre_grad,
            shared_gate_grad=shared_gate_grad,
            shared_up_grad=shared_up_grad,
            logit_grad=logit_grad,
            gain_two_grad=gain_two_grad,
        )

    def attention_back(kept, grads, carried):
        ring_hidden = ring_rows(grads["hidden_grad"].astype(bf))
        out_grad = dot_nt(ring_hidden, output_w).astype(bf)
        results = attention_backward(
            kept["info"],
            kept["qkv"],
            out_grad.reshape(heads, block, group_width),
            kept["attended"],
            kept["logs"],
            carried,
            kept["previous"],
            kept["cache"],
        )
        carried = results[2] if len(results) > 2 else None
        pair_grad = jnp.sum(exchange(results[1], zy_groups).astype(f32), axis=0).astype(bf)
        qkv_grad = jnp.concatenate(
            [results[0].reshape(heads * block, group_width), pair_grad], axis=1
        )
        normed_one_grad = sum_over_x(dot_nt(qkv_grad, qkv_w))
        in_norm_grad, gain_one_grad = norm_back(
            kept["layer_b"].astype(f32), gain_one, normed_one_grad
        )
        grads = dict(
            grads,
            ring_hidden=ring_hidden,
            qkv_grad=qkv_grad,
            gain_one_grad=gain_one_grad,
            layer_grad=(grads["hidden_grad"] + in_norm_grad).astype(bf),
        )
        return grads, carried

    nothing = jnp.zeros((block, width), bf)
    saved = []
    received, previous = jnp.zeros((heads, block, width), bf), None
    for moment in range(micros + 1):
        kept = forward(moment, received, previous)
        saved.append(kept)
        previous = kept["cache"]
        if moment < micros:
            received = next_ring(kept["output_b"])
    backs = [None] * (micros + 1)
    received, carried = nothing, None
    for source in range(micros, -1, -1):
        own = cotangent[0, source - 1] if source > 0 else nothing
        upstream_b = jnp.where(is_first, received, own)
        grads = ffn_backward(saved[source], upstream_b)
        backs[source], carried = attention_back(saved[source], grads, carried)
        if source > 0:
            received = lax.ppermute(backs[source]["layer_grad"], "section", [(1, 0)])

    def live(name, store, axis):
        ends = jnp.where(is_first, store[0][name], store[micros][name])
        return jnp.concatenate([ends, store[1][name]], axis=axis)

    def kept_rows(name, axis=0):
        return live(name, saved, axis)

    def back_rows(name, axis=0):
        return live(name, backs, axis)

    expert_parts = [
        wide_einsum("erd,erf->edf", kept_rows("expert_in", 1), back_rows("gate_pre_grad", 1)),
        wide_einsum("erd,erf->edf", kept_rows("expert_in", 1), back_rows("up_pre_grad", 1)),
        wide_einsum("erf,erd->efd", kept_rows("activated", 1), back_rows("expert_grad", 1)),
    ]
    expert_parts = [part.astype(bf) for part in expert_parts]
    expert_grads = [part.astype(f32) + twin(part).astype(f32) for part in expert_parts]

    def both(value):
        return jnp.concatenate([value, twin(value)], axis=0)

    def both_halves(low_half, high_half):
        own, other = mine_of(low_half, high_half), mine_of(high_half, low_half)
        return jnp.concatenate([own, twin(other)], axis=0)

    normed_two = kept_rows("normed_two")
    grad_gate_up = dot_tn(
        both(normed_two), both_halves(back_rows("shared_gate_grad"), back_rows("shared_up_grad"))
    )
    grad_down = dot_tn(both(kept_rows("shared_act")), both_halves(*halves(back_rows("upstream_b"))))

    def scattered(value, groups=None):
        count = shards if groups is None else len(groups[0])
        pieces = value.astype(bf).reshape(count, value.shape[0] // count, value.shape[1])
        return jnp.sum(exchange(pieces, groups).astype(f32), axis=0)

    share_gate_up, share_down = scattered(grad_gate_up), scattered(grad_down)

    grad_out = dot_tn(
        kept_rows("attended").reshape(micros * heads * block, group_width),
        back_rows("ring_hidden"),
    )
    share_out = scattered(grad_out, zy_groups)
    grad_qkv = dot_tn(kept_rows("ring_one"), back_rows("qkv_grad"))
    grad_router = dot_tn(normed_two, back_rows("logit_grad"))
    gain_sums = jnp.stack(
        [sum(grads[name] for grads in backs) for name in ("gain_one_grad", "gain_two_grad")]
    )
    grad_tail = jnp.concatenate(
        [grad_router, gain_sums.T, jnp.zeros((width, 128 - experts - 2), f32)], axis=1
    )
    pieces = exchange(
        jnp.concatenate([grad_qkv, grad_tail], axis=1)
        .astype(bf)
        .reshape(shards, rows_per, part_width + 128)
    ).astype(f32)
    share_qkv = jnp.sum(
        pieces[:, :, :part_width].reshape(heads, ring, rows_per, part_width), axis=1
    )
    share_qkv = share_qkv.transpose(1, 0, 2)
    share_tail = jnp.sum(pieces[:, :, part_width:], axis=0)

    def total(share):
        return share + twin(share)

    out_total, qkv_total, tail_total = total(share_out), total(share_qkv), total(share_tail)
    other_gate_up = twin(share_gate_up)
    down_total = ordered(share_down, twin(share_down), 1)

    def by_micro(store, name):
        return jnp.stack(
            [jnp.where(is_first, store[m][name], store[m + 1][name]) for m in range(micros)]
        )[None, None]

    return (
        by_micro(saved, "output_b"),
        by_micro(backs, "layer_grad"),
        tail_total[:, experts][None],
        qkv_total[:, :, :group_width].reshape(1, rows_per, head_width),
        qkv_total[:, :, group_width : group_width + HD].reshape(1, rows_per, key_width),
        qkv_total[:, :, group_width + HD :].reshape(1, rows_per, key_width),
        out_total[None],
        tail_total[:, experts + 1][None],
        tail_total[:, :experts][None],
        mine_of(share_gate_up, other_gate_up)[None],
        mine_of(other_gate_up, share_gate_up)[None],
        down_total[None],
        expert_grads[0][None],
        expert_grads[1][None],
        expert_grads[2][None],
    )


def solution(mesh):
    rows = P("section", "shard", None)
    vector = P("section", "shard")
    expert = P("section", "shard", None, None)
    tokens = P("dp", None, "shard", None)
    section_tokens = P("section", "dp", None, "shard", None)
    weights = (vector, rows, rows, rows, rows, vector, rows, rows, rows, rows) + (expert,) * 3
    return jax.shard_map(
        body,
        mesh=mesh,
        in_specs=(tokens, tokens, section_tokens) + weights,
        out_specs=(section_tokens, section_tokens) + weights,
        check_vma=False,
    )
```

```python
import functools

import jax
import jax.numpy as jnp
from jax import lax
from jax.experimental import pallas as pl
from jax.experimental.pallas import tpu as pltpu
from jax.sharding import PartitionSpec as P

H = 12
KVH = 4
HD = 128
GROUP = H // KVH
TOPK = 6
CAP = 8

epsilon = 1e-05
masked_score = -1e30
scaling = HD ** (-0.5)
log2_scale = scaling * 1.4426950408889634
bf = jnp.bfloat16
f32 = jnp.float32
VMEM_LIMIT = 32 * 1024 * 1024


def inverse_rms(rows):
    return lax.rsqrt(jnp.mean(rows * rows, axis=-1, keepdims=True) + epsilon)


def norm_back(layer_in, gain, upstream):
    inverse = inverse_rms(layer_in)
    unit_rows = layer_in * inverse
    gain_grad = jnp.sum(upstream * unit_rows, axis=0)
    scaled = upstream * gain
    in_grad = inverse * (scaled - unit_rows * jnp.mean(scaled * unit_rows, axis=-1, keepdims=True))
    return (in_grad, gain_grad)


def silu_parts(argument):
    sigmoid = jax.nn.sigmoid(argument)
    return argument * sigmoid, sigmoid * (1.0 + argument * (1.0 - sigmoid))


def dot(left_side, right_side):
    return jnp.dot(left_side, right_side, preferred_element_type=f32)


def dot_nt(left_side, right_side):
    return lax.dot_general(
        left_side, right_side, (((1,), (1,)), ((), ())), preferred_element_type=f32
    )


def dot_tn(left_side, right_side):
    return lax.dot_general(
        left_side, right_side, (((0,), (0,)), ((), ())), preferred_element_type=f32
    )


def wide_einsum(formula, left_side, right_side):
    return jnp.einsum(formula, left_side, right_side, preferred_element_type=f32)


def arrival(info_ref, parts, part):
    return lax.rem(info_ref[2] + parts - part, parts)


def stacked_heads(ref, at):
    return jnp.concatenate([ref[at, :, g * HD : (g + 1) * HD] for g in range(GROUP)], axis=0)


def store_heads(ref, at, rows):
    block = ref.shape[1]
    for g in range(GROUP):
        ref[at, :, g * HD : (g + 1) * HD] = rows[g * block : (g + 1) * block]


def cached(ref, span, column):
    rows = ref[:, span, column : column + HD]
    return rows.reshape(rows.shape[0] * rows.shape[1], HD)


def block_span(at, block):
    return pl.ds(pl.multiple_of(at * block, block), block)


def diagonal_mask(rows, chunk, block, zy):
    key_at = lax.broadcasted_iota(jnp.int32, (rows, chunk), 1)
    row_at = lax.broadcasted_iota(jnp.int32, (rows, chunk), 0)
    return key_at <= zy * block + lax.rem(row_at, block)


def attention_forward_kernel(has_prev, info_ref, q_ref, *refs):
    prev_ref = refs[0] if has_prev else None
    cur_ref, o_ref, log_ref = refs[-3:]
    parts, block, _ = q_ref.shape
    rows = GROUP * block
    mask = diagonal_mask(rows, cur_ref.shape[0] * block, block, info_ref[0])
    spans = [block_span(arrival(info_ref, parts, part), block) for part in range(parts)]
    for part in range(parts):
        at = arrival(info_ref, parts, part)
        queries = stacked_heads(q_ref, at)
        pieces = [(prev_ref, slice(None))] if has_prev else []
        pieces += [(cur_ref, spans[p]) for p in range(part + 1)]
        scores = [dot_nt(queries, cached(ref, span, 0)) for ref, span in pieces]
        if has_prev:
            scores[0] = scores[0] + jnp.where(info_ref[1] > 0, 0.0, masked_score).astype(f32)
        scores[-1] = jnp.where(mask, scores[-1], masked_score)
        peak = functools.reduce(
            jnp.maximum, [jnp.max(s, axis=-1, keepdims=True) for s in scores]
        )
        peak = peak * log2_scale
        total = jnp.zeros((rows, 1), f32)
        mixed = jnp.zeros((rows, HD), f32)
        for s, (ref, span) in zip(scores, pieces):
            probs = jnp.exp2(s * log2_scale - peak)
            total = total + jnp.sum(probs, axis=-1, keepdims=True)
            mixed = mixed + dot(probs.astype(bf), cached(ref, span, HD))
        store_heads(o_ref, at, (mixed / total).astype(bf))
        log_ref[at] = jnp.broadcast_to(peak + jnp.log2(total), (rows, HD))


def attention_backward_kernel(has_prev, has_carry, info_ref, q_ref, do_ref, o_ref, log_ref, *refs):
    refs = list(refs)
    sum_ref = refs.pop()
    carry_ref = refs.pop(0) if has_carry else None
    prev_ref = refs.pop(0) if has_prev else None
    cur_ref, dq_ref, dcur_ref = refs[:3]
    dprev_ref = refs[3] if has_prev else None
    sum_ref[...] = carry_ref[...] if has_carry else jnp.zeros(sum_ref.shape, f32)
    if has_prev:
        dprev_ref[...] = jnp.zeros(dprev_ref.shape, f32)
    parts, block, _ = q_ref.shape
    ring = cur_ref.shape[0]
    rows = GROUP * block
    mask = diagonal_mask(rows, ring * block, block, info_ref[0])
    spans = [block_span(arrival(info_ref, parts, part), block) for part in range(parts)]
    for part in range(parts):
        at = arrival(info_ref, parts, part)
        queries = stacked_heads(q_ref, at)
        out_grad = stacked_heads(do_ref, at)
        out = stacked_heads(o_ref, at)
        inner = jnp.sum(out_grad.astype(f32) * out.astype(f32), axis=-1, keepdims=True)
        log_total = log_ref[at][:, :1]
        query_grad = jnp.zeros((rows, HD), f32)
        pieces = []
        if has_prev:
            log_prev = log_total + jnp.where(info_ref[1] > 0, 0.0, -masked_score).astype(f32)
            pieces = [
                (prev_ref, dprev_ref, slice(p * block, (p + 1) * block), log_prev, False)
                for p in range(parts)
            ]
        pieces += [(cur_ref, sum_ref, spans[p], log_total, p == part) for p in range(part + 1)]
        for ref, grad_ref, span, log_row, on_diagonal in pieces:
            keys = cached(ref, span, 0)
            probs = jnp.exp2(dot_nt(queries, keys) * log2_scale - log_row)
            if on_diagonal:
                probs = jnp.where(mask, probs, 0.0)
            probs_grad = dot_nt(out_grad, cached(ref, span, HD))
            score_grad = (probs * (probs_grad - inner)).astype(bf)
            query_grad = query_grad + dot(score_grad, keys)
            key_grad = dot_tn(score_grad, queries) * scaling
            value_grad = dot_tn(probs.astype(bf), out_grad)
            grad_ref[:, span, :HD] += key_grad.reshape(ring, block, HD)
            grad_ref[:, span, HD:] += value_grad.reshape(ring, block, HD)
        store_heads(dq_ref, at, (query_grad * scaling).astype(bf))
    dcur_ref[...] = sum_ref[...].astype(bf)


def attention_call(kernel, factor, out_shape, scratch, info, queries, *rest):
    parts, block, _ = queries.shape
    rows = parts * GROUP * block
    keys = sum(ref.shape[0] * ref.shape[1] for ref in rest if ref.shape == rest[-1].shape)
    in_vmem = pl.BlockSpec(memory_space=pltpu.VMEM)
    return pl.pallas_call(
        kernel,
        out_shape=out_shape,
        in_specs=[pl.BlockSpec(memory_space=pltpu.SMEM)] + [in_vmem] * (1 + len(rest)),
        out_specs=(in_vmem,) * len(out_shape),
        scratch_shapes=scratch,
        compiler_params=pltpu.CompilerParams(vmem_limit_bytes=VMEM_LIMIT),
        cost_estimate=pl.CostEstimate(
            flops=factor * rows * keys * HD,
            bytes_accessed=factor * (keys + rows) * HD,
            transcendentals=rows * keys // 2,
        ),
    )(info, queries, *rest)


def attention_forward(info, qkv, prev, cur):
    parts, block, _ = qkv.shape
    shapes = (
        jax.ShapeDtypeStruct((parts, block, GROUP * HD), bf),
        jax.ShapeDtypeStruct((parts, GROUP * block, HD), f32),
    )
    caches = (cur,) if prev is None else (prev, cur)
    kernel = functools.partial(attention_forward_kernel, prev is not None)
    return attention_call(kernel, 2, shapes, [], info, qkv, *caches)


def attention_backward(info, qkv, out_grad, out, logs, carry, prev, cur):
    shapes = (jax.ShapeDtypeStruct(out.shape, bf), jax.ShapeDtypeStruct(cur.shape, bf))
    if prev is not None:
        shapes += (jax.ShapeDtypeStruct(cur.shape, f32),)
    extra = tuple(value for value in (carry, prev) if value is not None)
    kernel = functools.partial(attention_backward_kernel, prev is not None, carry is not None)
    scratch = [pltpu.VMEM(cur.shape, f32)]
    return attention_call(
        kernel, 5, shapes, scratch, info, qkv, out_grad, out, logs, *extra, cur
    )


def body(
    inputs,
    cotangent,
    routes,
    norm_attn,
    w_query,
    w_key,
    w_value,
    w_output,
    norm_ffn,
    w_router,
    shared_gate,
    shared_up,
    shared_down,
    expert_gate,
    expert_up,
    expert_down,
):
    micros, block, width = inputs.shape[1:]
    shards = lax.axis_size("shard")
    section = lax.axis_index("section")
    core = lax.axis_index("dp")
    position = lax.axis_index("shard")
    heads = KVH
    ring = shards // heads
    local_experts = expert_gate.shape[1]
    experts = local_experts * shards
    slots = experts * CAP
    rows_per = w_query.shape[1]
    half_rows = rows_per // 2
    group_width = GROUP * HD
    head_width = H * HD
    key_width = KVH * HD
    part_width = group_width + 2 * HD
    shared_width = shared_gate.shape[2]
    down_rows = shared_down.shape[1]
    is_first = section == 0
    low_core = core == 0
    zy_groups = [[x * ring + zy for zy in range(ring)] for x in range(heads)]

    def exchange(value, groups=None):
        return lax.all_to_all(
            value, "shard", split_axis=0, concat_axis=0, tiled=True, axis_index_groups=groups
        )

    def copies(value, count):
        return jnp.broadcast_to(value[None], (count,) + value.shape)

    def twin(value):
        return lax.ppermute(value, "dp", [(0, 1), (1, 0)])

    def mine_of(low_half, high_half):
        return jnp.where(low_core, low_half, high_half)

    def ordered(own, other, axis):
        low_half, high_half = mine_of(own, other), mine_of(other, own)
        return jnp.concatenate([low_half, high_half], axis=axis)

    def ordered_by(in_order, own, other):
        return jnp.stack([jnp.where(in_order, own, other), jnp.where(in_order, other, own)])

    def halves(value):
        half = value.shape[-1] // 2
        return value[..., :half], value[..., half:]

    def my_rows(value):
        return mine_of(value[..., :half_rows, :], value[..., half_rows:, :])

    tail = jnp.concatenate(
        [
            w_router[0],
            norm_attn[0][:, None],
            norm_ffn[0][:, None],
            jnp.zeros((rows_per, 128 - experts - 2), bf),
        ],
        axis=1,
    )
    by_head = jnp.concatenate(
        [
            w_query[0].reshape(rows_per, heads, group_width),
            w_key[0].reshape(rows_per, heads, HD),
            w_value[0].reshape(rows_per, heads, HD),
            jnp.broadcast_to(tail[:, None], (rows_per, heads, 128)),
        ],
        axis=2,
    ).transpose(1, 0, 2)
    by_head = my_rows(by_head)
    by_head = jnp.broadcast_to(
        by_head[:, None], (heads, ring, half_rows, part_width + 128)
    ).reshape(shards, half_rows, part_width + 128)
    packed = jnp.concatenate(
        [shared_gate[0], shared_up[0], shared_down[0].reshape(rows_per, shared_width)], axis=1
    )
    by_head, packed = lax.optimization_barrier((by_head, packed))
    gathered = lax.all_gather(packed, "shard", axis=0, tiled=True)
    gate_up_w = gathered[:, : 2 * shared_width]
    down_w = gathered[:, 2 * shared_width :].reshape(shared_width, width)
    own_part = exchange(by_head)
    out_rows = my_rows(w_output[0])
    out_rows = ordered_by(
        position % 2 == 0, out_rows, lax.ppermute(out_rows, "shard", [(p, p ^ 1) for p in range(shards)])
    )
    out_parts = [out_rows] + [
        lax.ppermute(
            out_rows,
            "shard",
            [(p, p // ring * ring + (p % ring - 2 * k) % ring) for p in range(shards)],
        )
        for k in range(1, ring // 2)
    ]
    own_part, *out_parts = lax.optimization_barrier((own_part, *out_parts))
    own_out = lax.dynamic_slice_in_dim(
        jnp.concatenate(out_parts + out_parts), ring - position % ring // 2 * 2, ring, axis=0
    )
    output_w = ordered(own_out, twin(own_out), 1).reshape(group_width, width)
    fetched = ordered(own_part, twin(own_part), 1).reshape(width, part_width + 128)
    qkv_w, tail = fetched[:, :part_width], fetched[:, part_width:]
    router_w = tail[:, :experts]
    gains = tail[:, experts : experts + 2].T.astype(f32)
    gain_one, gain_two = gains[0][None], gains[1][None]

    expert_g, expert_u, expert_d = expert_gate[0], expert_up[0], expert_down[0]
    slot_of = jnp.arange(slots, dtype=jnp.int32)
    expert_of = jnp.arange(experts, dtype=jnp.int32)
    row_of = jnp.arange(block, dtype=jnp.int32)
    spread = (expert_of[:, None] == slot_of[None, :] // CAP).astype(bf)
    router_slots = dot(router_w, spread).astype(bf)
    earlier = (row_of[:, None] > row_of[None, :]).astype(bf)

    def slot_table(route_rows):
        named = jnp.any(route_rows[:, :, None] == expert_of[None, None, :], axis=1).astype(bf)
        slot_ids = dot(earlier, named).astype(bf)
        return (dot(named, spread) > 0.5) & (
            dot(slot_ids, spread).astype(jnp.int32) == (slot_of % CAP)[None, :]
        )

    here = [position % ring, jnp.ones_like(position), position // ring]
    info_all = jnp.stack(here).astype(jnp.int32)
    info = jnp.stack([here[0], is_first.astype(here[0].dtype), here[2]]).astype(jnp.int32)

    def gate_values(normed_two, table):
        logits = jnp.where(table, dot(normed_two, router_slots), masked_score)
        weights = jnp.exp(logits - jnp.max(logits, axis=-1, keepdims=True))
        weights = jnp.where(table, weights, 0.0)
        return weights / jnp.sum(weights, axis=-1, keepdims=True)

    def high_low(value):
        high = value.astype(bf)
        return high, (value - high.astype(f32)).astype(bf)

    def to_experts(rows):
        return (
            exchange(rows.reshape(shards, local_experts, CAP, width))
            .transpose(1, 0, 2, 3)
            .reshape(local_experts, shards * CAP, width)
        )

    def from_experts(rows):
        return exchange(
            rows.reshape(local_experts, shards, CAP, width).transpose(1, 0, 2, 3)
        ).reshape(slots, width)

    def moved(p, steps):
        return (p // ring + steps) % heads * ring + p % ring

    def shift_x(value, steps):
        return lax.ppermute(value, "shard", [(p, moved(p, steps)) for p in range(shards)])

    def next_ring(value):
        return jnp.stack(
            [
                lax.ppermute(
                    value,
                    ("section", "shard"),
                    [(p, shards + moved(p, steps)) for p in range(shards)],
                )
                for steps in range(heads)
            ]
        )

    def sum_over_x(rows):
        parts = rows.reshape(heads, block, width)
        away = [shift_x(parts[k].astype(bf), -k).astype(f32) for k in range(1, heads)]
        return sum(away, parts[0])

    def ring_rows(rows):
        return jnp.concatenate([rows] + [shift_x(rows, k) for k in range(1, heads)], axis=0)

    ring_inputs = [
        jnp.stack([inputs[0, m]] + [shift_x(inputs[0, m], k) for k in range(1, heads)])
        for m in range(micros)
    ]

    def forward(moment, received, previous):
        first_micro = min(moment, micros - 1)
        second_micro = max(moment - 1, 0)
        ring_b = jnp.where(is_first, ring_inputs[first_micro], received)
        layer_b = ring_b[0]
        table = slot_table(
            jnp.where(is_first, routes[0, 0, first_micro], routes[0, 0, second_micro])
        )
        pick = table.astype(bf)
        layer_in = layer_b.astype(f32)
        ring_in = ring_b.reshape(heads * block, width).astype(f32)
        ring_one = (ring_in * inverse_rms(ring_in) * gain_one).astype(bf)
        qkv = dot(ring_one, qkv_w).astype(bf)
        cache = exchange(copies(qkv[:, group_width:], ring), zy_groups)
        qkv = qkv.reshape(heads, block, part_width)
        attn_info = info if moment == 1 else info_all
        attended, logs = attention_forward(attn_info, qkv, previous, cache)
        attended_rows = attended.reshape(heads * block, group_width)
        hidden = layer_in + sum_over_x(dot(attended_rows, output_w))
        normed_two = (hidden * inverse_rms(hidden) * gain_two).astype(bf)
        gates = gate_values(normed_two, table)
        expert_in = to_experts(dot_tn(pick, normed_two).astype(bf))
        gate_pre = wide_einsum("erd,edf->erf", expert_in, expert_g)
        up_pre = wide_einsum("erd,edf->erf", expert_in, expert_u)
        activated = (silu_parts(gate_pre)[0] * up_pre).astype(bf)
        returned = from_experts(wide_einsum("erf,efd->erd", activated, expert_d).astype(bf))
        high, low = high_low(gates)
        routed = dot(high, returned) + dot(low, returned)
        shared_gate_pre, shared_up_pre = halves(dot(normed_two, gate_up_w))
        shared_act = (silu_parts(shared_gate_pre)[0] * shared_up_pre).astype(bf)
        beside = lax.optimization_barrier(hidden + dot(shared_act, down_w))
        output_b = (beside + routed).astype(bf)
        return dict(
            layer_b=layer_b,
            pick=pick,
            ring_one=ring_one,
            qkv=qkv,
            cache=cache,
            previous=previous,
            info=attn_info,
            attended=attended,
            logs=logs,
            hidden=hidden,
            normed_two=normed_two,
            gates=gates,
            expert_in=expert_in,
            gate_pre=gate_pre,
            up_pre=up_pre,
            activated=activated,
            returned=returned,
            shared_gate_pre=shared_gate_pre,
            shared_up_pre=shared_up_pre,
            shared_act=shared_act,
            output_b=output_b,
        )

    def ffn_backward(kept, upstream_b):
        upstream = upstream_b.astype(f32)
        gates, hidden = kept["gates"], kept["hidden"]
        high, low = high_low(gates)
        outgoing = dot_tn(high, upstream_b) + dot_tn(low, upstream_b)
        expert_grad = to_experts(outgoing.astype(bf))
        act_silu, act_slope = silu_parts(kept["gate_pre"])
        act_grad = wide_einsum("erd,efd->erf", expert_grad, expert_d)
        gate_pre_grad = (act_grad * kept["up_pre"] * act_slope).astype(bf)
        up_pre_grad = (act_grad * act_silu).astype(bf)
        expert_in_grad = (
            wide_einsum("erf,edf->erd", gate_pre_grad, expert_g)
            + wide_einsum("erf,edf->erd", up_pre_grad, expert_u)
        ).astype(bf)
        returned_grad = from_experts(expert_in_grad)
        shared_act_grad = dot_nt(upstream_b, down_w)
        shared_silu, shared_slope = silu_parts(kept["shared_gate_pre"])
        shared_gate_grad = (shared_act_grad * kept["shared_up_pre"] * shared_slope).astype(bf)
        shared_up_grad = (shared_act_grad * shared_silu).astype(bf)
        normed_two_grad = dot_nt(
            jnp.concatenate([shared_gate_grad, shared_up_grad], axis=1), gate_up_w
        )
        gate_grad = dot_nt(upstream_b, kept["returned"])
        picked_grad = gates * (gate_grad - jnp.sum(gates * gate_grad, axis=1, keepdims=True))
        picked_b = picked_grad.astype(bf)
        normed_two_grad = normed_two_grad + dot_nt(picked_b, router_slots)
        normed_two_grad = lax.optimization_barrier(normed_two_grad)
        normed_two_grad = normed_two_grad + dot(kept["pick"], returned_grad)
        logit_grad = dot_nt(picked_b, spread).astype(bf)
        hidden_norm_grad, gain_two_grad = norm_back(hidden, gain_two, normed_two_grad)
        return dict(
            hidden_grad=upstream + hidden_norm_grad,
            upstream_b=upstream_b,
            expert_grad=expert_grad,
            gate_pre_grad=gate_pre_grad,
            up_pre_grad=up_pre_grad,
            shared_gate_grad=shared_gate_grad,
            shared_up_grad=shared_up_grad,
            logit_grad=logit_grad,
            gain_two_grad=gain_two_grad,
        )

    def attention_back(kept, grads, carried):
        ring_hidden = ring_rows(grads["hidden_grad"].astype(bf))
        out_grad = dot_nt(ring_hidden, output_w).astype(bf)
        results = attention_backward(
            kept["info"],
            kept["qkv"],
            out_grad.reshape(heads, block, group_width),
            kept["attended"],
            kept["logs"],
            carried,
            kept["previous"],
            kept["cache"],
        )
        carried = results[2] if len(results) > 2 else None
        query_grad = results[0].reshape(heads * block, group_width)
        query_part = lax.optimization_barrier(dot_nt(query_grad, qkv_w[:, :group_width]))
        pair_grad = jnp.sum(exchange(results[1], zy_groups).astype(f32), axis=0).astype(bf)
        qkv_grad = jnp.concatenate([query_grad, pair_grad], axis=1)
        normed_one_grad = sum_over_x(query_part + dot_nt(pair_grad, qkv_w[:, group_width:]))
        in_norm_grad, gain_one_grad = norm_back(
            kept["layer_b"].astype(f32), gain_one, normed_one_grad
        )
        grads = dict(
            grads,
            ring_hidden=ring_hidden,
            qkv_grad=qkv_grad,
            gain_one_grad=gain_one_grad,
            layer_grad=(grads["hidden_grad"] + in_norm_grad).astype(bf),
        )
        return grads, carried

    nothing = jnp.zeros((block, width), bf)
    saved = []
    received, previous = jnp.zeros((heads, block, width), bf), None
    for moment in range(micros + 1):
        kept = forward(moment, received, previous)
        saved.append(kept)
        previous = kept["cache"]
        if moment < micros:
            received = next_ring(kept["output_b"])
    backs = [None] * (micros + 1)
    received, carried = nothing, None
    for source in range(micros, -1, -1):
        own = cotangent[0, source - 1] if source > 0 else nothing
        upstream_b = jnp.where(is_first, received, own)
        grads = ffn_backward(saved[source], upstream_b)
        backs[source], carried = attention_back(saved[source], grads, carried)
        if source > 0:
            received = lax.ppermute(backs[source]["layer_grad"], "section", [(1, 0)])

    def live(name, store, axis):
        ends = jnp.where(is_first, store[0][name], store[micros][name])
        return jnp.concatenate([ends, store[1][name]], axis=axis)

    def kept_rows(name, axis=0):
        return live(name, saved, axis)

    def back_rows(name, axis=0):
        return live(name, backs, axis)

    expert_parts = [
        wide_einsum("erd,erf->edf", kept_rows("expert_in", 1), back_rows("gate_pre_grad", 1)),
        wide_einsum("erd,erf->edf", kept_rows("expert_in", 1), back_rows("up_pre_grad", 1)),
        wide_einsum("erf,erd->efd", kept_rows("activated", 1), back_rows("expert_grad", 1)),
    ]
    expert_parts = [part.astype(bf) for part in expert_parts]
    expert_grads = [part.astype(f32) + twin(part).astype(f32) for part in expert_parts]

    def both(value):
        return jnp.concatenate([value, twin(value)], axis=0)

    def both_halves(low_half, high_half):
        own, other = mine_of(low_half, high_half), mine_of(high_half, low_half)
        return jnp.concatenate([own, twin(other)], axis=0)

    normed_two = kept_rows("normed_two")
    grad_gate_up = dot_tn(
        both(normed_two), both_halves(back_rows("shared_gate_grad"), back_rows("shared_up_grad"))
    )
    grad_down = dot_tn(both(kept_rows("shared_act")), both_halves(*halves(back_rows("upstream_b"))))

    def scattered(value, groups=None):
        count = shards if groups is None else len(groups[0])
        pieces = value.reshape(count, value.shape[0] // count, value.shape[1])
        return jnp.sum(exchange(pieces, groups).astype(f32), axis=0)


    grad_out = dot_tn(
        kept_rows("attended").reshape(micros * heads * block, group_width),
        back_rows("ring_hidden"),
    )
    grad_gate_up, grad_down, grad_out, last_grad = lax.optimization_barrier(
        (
            grad_gate_up.astype(bf),
            grad_down.astype(bf),
            grad_out.astype(bf),
            backs[0]["layer_grad"],
        )
    )
    backs[0]["layer_grad"] = last_grad
    share_gate_up, share_down = scattered(grad_gate_up), scattered(grad_down)
    share_out = scattered(grad_out, zy_groups)
    grad_qkv = dot_tn(kept_rows("ring_one"), back_rows("qkv_grad"))
    grad_router = dot_tn(normed_two, back_rows("logit_grad"))
    gain_sums = jnp.stack(
        [sum(grads[name] for grads in backs) for name in ("gain_one_grad", "gain_two_grad")]
    )
    grad_tail = jnp.concatenate(
        [grad_router, gain_sums.T, jnp.zeros((width, 128 - experts - 2), f32)], axis=1
    )
    pieces = exchange(
        jnp.concatenate([grad_qkv, grad_tail], axis=1)
        .astype(bf)
        .reshape(shards, rows_per, part_width + 128)
    ).astype(f32)
    share_qkv = jnp.sum(
        pieces[:, :, :part_width].reshape(heads, ring, rows_per, part_width), axis=1
    )
    share_qkv = share_qkv.transpose(1, 0, 2)
    share_tail = jnp.sum(pieces[:, :, part_width:], axis=0)

    def total(share):
        return share + twin(share)

    out_total, qkv_total, tail_total = total(share_out), total(share_qkv), total(share_tail)
    other_gate_up = twin(share_gate_up)
    down_total = ordered(share_down, twin(share_down), 1)

    def by_micro(store, name):
        return jnp.stack(
            [jnp.where(is_first, store[m][name], store[m + 1][name]) for m in range(micros)]
        )[None, None]

    return (
        by_micro(saved, "output_b"),
        by_micro(backs, "layer_grad"),
        tail_total[:, experts][None],
        qkv_total[:, :, :group_width].reshape(1, rows_per, head_width),
        qkv_total[:, :, group_width : group_width + HD].reshape(1, rows_per, key_width),
        qkv_total[:, :, group_width + HD :].reshape(1, rows_per, key_width),
        out_total[None],
        tail_total[:, experts + 1][None],
        tail_total[:, :experts][None],
        mine_of(share_gate_up, other_gate_up)[None],
        mine_of(other_gate_up, share_gate_up)[None],
        down_total[None],
        expert_grads[0][None],
        expert_grads[1][None],
        expert_grads[2][None],
    )


def solution(mesh):
    rows = P("section", "shard", None)
    vector = P("section", "shard")
    expert = P("section", "shard", None, None)
    tokens = P("dp", None, "shard", None)
    section_tokens = P("section", "dp", None, "shard", None)
    weights = (vector, rows, rows, rows, rows, vector, rows, rows, rows, rows) + (expert,) * 3
    return jax.shard_map(
        body,
        mesh=mesh,
        in_specs=(tokens, tokens, section_tokens) + weights,
        out_specs=(section_tokens, section_tokens) + weights,
        check_vma=False,
    )
```

```python
import functools

import jax
import jax.numpy as jnp
from jax import lax
from jax.experimental import pallas as pl
from jax.experimental.pallas import tpu as pltpu
from jax.sharding import PartitionSpec as P

H = 12
KVH = 4
HD = 128
GROUP = H // KVH
TOPK = 6
CAP = 8

epsilon = 1e-05
masked_score = -1e30
scaling = HD ** (-0.5)
log2_scale = scaling * 1.4426950408889634
bf = jnp.bfloat16
f32 = jnp.float32
VMEM_LIMIT = 32 * 1024 * 1024


def inverse_rms(rows):
    return lax.rsqrt(jnp.mean(rows * rows, axis=-1, keepdims=True) + epsilon)


def norm_back(layer_in, gain, upstream):
    inverse = inverse_rms(layer_in)
    unit_rows = layer_in * inverse
    gain_grad = jnp.sum(upstream * unit_rows, axis=0)
    scaled = upstream * gain
    in_grad = inverse * (scaled - unit_rows * jnp.mean(scaled * unit_rows, axis=-1, keepdims=True))
    return (in_grad, gain_grad)


def silu_parts(argument):
    sigmoid = jax.nn.sigmoid(argument)
    return argument * sigmoid, sigmoid * (1.0 + argument * (1.0 - sigmoid))


def dot(left_side, right_side):
    return jnp.dot(left_side, right_side, preferred_element_type=f32)


def dot_nt(left_side, right_side):
    return lax.dot_general(
        left_side, right_side, (((1,), (1,)), ((), ())), preferred_element_type=f32
    )


def dot_tn(left_side, right_side):
    return lax.dot_general(
        left_side, right_side, (((0,), (0,)), ((), ())), preferred_element_type=f32
    )


def wide_einsum(formula, left_side, right_side):
    return jnp.einsum(formula, left_side, right_side, preferred_element_type=f32)


def arrival(info_ref, parts, part):
    return lax.rem(info_ref[2] + parts - part, parts)


def stacked_heads(ref, at):
    return jnp.concatenate([ref[at, :, g * HD : (g + 1) * HD] for g in range(GROUP)], axis=0)


def store_heads(ref, at, rows):
    block = ref.shape[1]
    for g in range(GROUP):
        ref[at, :, g * HD : (g + 1) * HD] = rows[g * block : (g + 1) * block]


def cached(ref, span, column):
    rows = ref[:, span, column : column + HD]
    return rows.reshape(rows.shape[0] * rows.shape[1], HD)


def block_span(at, block):
    return pl.ds(pl.multiple_of(at * block, block), block)


def diagonal_mask(rows, chunk, block, zy):
    key_at = lax.broadcasted_iota(jnp.int32, (rows, chunk), 1)
    row_at = lax.broadcasted_iota(jnp.int32, (rows, chunk), 0)
    return key_at <= zy * block + lax.rem(row_at, block)


def attention_forward_kernel(has_prev, info_ref, q_ref, *refs):
    prev_ref = refs[0] if has_prev else None
    cur_ref, o_ref, log_ref = refs[-3:]
    parts, block, _ = q_ref.shape
    rows = GROUP * block
    mask = diagonal_mask(rows, cur_ref.shape[0] * block, block, info_ref[0])
    spans = [block_span(arrival(info_ref, parts, part), block) for part in range(parts)]
    for part in range(parts):
        at = arrival(info_ref, parts, part)
        queries = stacked_heads(q_ref, at)
        pieces = [(prev_ref, slice(None))] if has_prev else []
        pieces += [(cur_ref, spans[p]) for p in range(part + 1)]
        scores = [dot_nt(queries, cached(ref, span, 0)) for ref, span in pieces]
        if has_prev:
            scores[0] = scores[0] + jnp.where(info_ref[1] > 0, 0.0, masked_score).astype(f32)
        scores[-1] = jnp.where(mask, scores[-1], masked_score)
        peak = functools.reduce(
            jnp.maximum, [jnp.max(s, axis=-1, keepdims=True) for s in scores]
        )
        peak = peak * log2_scale
        total = jnp.zeros((rows, 1), f32)
        mixed = jnp.zeros((rows, HD), f32)
        for s, (ref, span) in zip(scores, pieces):
            probs = jnp.exp2(s * log2_scale - peak)
            total = total + jnp.sum(probs, axis=-1, keepdims=True)
            mixed = mixed + dot(probs.astype(bf), cached(ref, span, HD))
        store_heads(o_ref, at, (mixed / total).astype(bf))
        log_ref[at] = jnp.broadcast_to(peak + jnp.log2(total), (rows, HD))


def attention_backward_kernel(has_prev, has_carry, info_ref, q_ref, do_ref, o_ref, log_ref, *refs):
    refs = list(refs)
    sum_ref = refs.pop()
    carry_ref = refs.pop(0) if has_carry else None
    prev_ref = refs.pop(0) if has_prev else None
    cur_ref, dq_ref, dcur_ref = refs[:3]
    dprev_ref = refs[3] if has_prev else None
    sum_ref[...] = carry_ref[...] if has_carry else jnp.zeros(sum_ref.shape, f32)
    if has_prev:
        dprev_ref[...] = jnp.zeros(dprev_ref.shape, f32)
    parts, block, _ = q_ref.shape
    ring = cur_ref.shape[0]
    rows = GROUP * block
    mask = diagonal_mask(rows, ring * block, block, info_ref[0])
    spans = [block_span(arrival(info_ref, parts, part), block) for part in range(parts)]
    for part in range(parts):
        at = arrival(info_ref, parts, part)
        queries = stacked_heads(q_ref, at)
        out_grad = stacked_heads(do_ref, at)
        out = stacked_heads(o_ref, at)
        inner = jnp.sum(out_grad.astype(f32) * out.astype(f32), axis=-1, keepdims=True)
        log_total = log_ref[at][:, :1]
        query_grad = jnp.zeros((rows, HD), f32)
        pieces = []
        if has_prev:
            log_prev = log_total + jnp.where(info_ref[1] > 0, 0.0, -masked_score).astype(f32)
            pieces = [
                (prev_ref, dprev_ref, slice(p * block, (p + 1) * block), log_prev, False)
                for p in range(parts)
            ]
        pieces += [(cur_ref, sum_ref, spans[p], log_total, p == part) for p in range(part + 1)]
        for ref, grad_ref, span, log_row, on_diagonal in pieces:
            keys = cached(ref, span, 0)
            probs = jnp.exp2(dot_nt(queries, keys) * log2_scale - log_row)
            if on_diagonal:
                probs = jnp.where(mask, probs, 0.0)
            probs_grad = dot_nt(out_grad, cached(ref, span, HD))
            score_grad = (probs * (probs_grad - inner)).astype(bf)
            query_grad = query_grad + dot(score_grad, keys)
            key_grad = dot_tn(score_grad, queries) * scaling
            value_grad = dot_tn(probs.astype(bf), out_grad)
            grad_ref[:, span, :HD] += key_grad.reshape(ring, block, HD)
            grad_ref[:, span, HD:] += value_grad.reshape(ring, block, HD)
        store_heads(dq_ref, at, (query_grad * scaling).astype(bf))
    dcur_ref[...] = sum_ref[...].astype(bf)


def attention_call(kernel, factor, out_shape, scratch, info, queries, *rest):
    parts, block, _ = queries.shape
    rows = parts * GROUP * block
    keys = sum(ref.shape[0] * ref.shape[1] for ref in rest if ref.shape == rest[-1].shape)
    in_vmem = pl.BlockSpec(memory_space=pltpu.VMEM)
    return pl.pallas_call(
        kernel,
        out_shape=out_shape,
        in_specs=[pl.BlockSpec(memory_space=pltpu.SMEM)] + [in_vmem] * (1 + len(rest)),
        out_specs=(in_vmem,) * len(out_shape),
        scratch_shapes=scratch,
        compiler_params=pltpu.CompilerParams(vmem_limit_bytes=VMEM_LIMIT),
        cost_estimate=pl.CostEstimate(
            flops=factor * rows * keys * HD,
            bytes_accessed=factor * (keys + rows) * HD,
            transcendentals=rows * keys // 2,
        ),
    )(info, queries, *rest)


def attention_forward(info, qkv, prev, cur):
    parts, block, _ = qkv.shape
    shapes = (
        jax.ShapeDtypeStruct((parts, block, GROUP * HD), bf),
        jax.ShapeDtypeStruct((parts, GROUP * block, HD), f32),
    )
    caches = (cur,) if prev is None else (prev, cur)
    kernel = functools.partial(attention_forward_kernel, prev is not None)
    return attention_call(kernel, 2, shapes, [], info, qkv, *caches)


def attention_backward(info, qkv, out_grad, out, logs, carry, prev, cur):
    shapes = (jax.ShapeDtypeStruct(out.shape, bf), jax.ShapeDtypeStruct(cur.shape, bf))
    if prev is not None:
        shapes += (jax.ShapeDtypeStruct(cur.shape, f32),)
    extra = tuple(value for value in (carry, prev) if value is not None)
    kernel = functools.partial(attention_backward_kernel, prev is not None, carry is not None)
    scratch = [pltpu.VMEM(cur.shape, f32)]
    return attention_call(
        kernel, 5, shapes, scratch, info, qkv, out_grad, out, logs, *extra, cur
    )


def body(
    inputs,
    cotangent,
    routes,
    norm_attn,
    w_query,
    w_key,
    w_value,
    w_output,
    norm_ffn,
    w_router,
    shared_gate,
    shared_up,
    shared_down,
    expert_gate,
    expert_up,
    expert_down,
):
    micros, block, width = inputs.shape[1:]
    shards = lax.axis_size("shard")
    section = lax.axis_index("section")
    core = lax.axis_index("dp")
    position = lax.axis_index("shard")
    heads = KVH
    ring = shards // heads
    local_experts = expert_gate.shape[1]
    experts = local_experts * shards
    slots = experts * CAP
    rows_per = w_query.shape[1]
    half_rows = rows_per // 2
    group_width = GROUP * HD
    head_width = H * HD
    key_width = KVH * HD
    part_width = group_width + 2 * HD
    shared_width = shared_gate.shape[2]
    down_rows = shared_down.shape[1]
    is_first = section == 0
    low_core = core == 0
    zy_groups = [[x * ring + zy for zy in range(ring)] for x in range(heads)]

    def exchange(value, groups=None):
        return lax.all_to_all(
            value, "shard", split_axis=0, concat_axis=0, tiled=True, axis_index_groups=groups
        )

    def copies(value, count):
        return jnp.broadcast_to(value[None], (count,) + value.shape)

    def twin(value):
        return lax.ppermute(value, "dp", [(0, 1), (1, 0)])

    def mine_of(low_half, high_half):
        return jnp.where(low_core, low_half, high_half)

    def ordered(own, other, axis):
        low_half, high_half = mine_of(own, other), mine_of(other, own)
        return jnp.concatenate([low_half, high_half], axis=axis)

    def ordered_by(in_order, own, other):
        return jnp.stack([jnp.where(in_order, own, other), jnp.where(in_order, other, own)])

    def halves(value):
        half = value.shape[-1] // 2
        return value[..., :half], value[..., half:]

    def my_rows(value):
        return mine_of(value[..., :half_rows, :], value[..., half_rows:, :])

    tail = jnp.concatenate(
        [
            w_router[0],
            norm_attn[0][:, None],
            norm_ffn[0][:, None],
            jnp.zeros((rows_per, 128 - experts - 2), bf),
        ],
        axis=1,
    )
    by_head = jnp.concatenate(
        [
            w_query[0].reshape(rows_per, heads, group_width),
            w_key[0].reshape(rows_per, heads, HD),
            w_value[0].reshape(rows_per, heads, HD),
            jnp.broadcast_to(tail[:, None], (rows_per, heads, 128)),
        ],
        axis=2,
    ).transpose(1, 0, 2)
    by_head = my_rows(by_head)
    by_head = jnp.broadcast_to(
        by_head[:, None], (heads, ring, half_rows, part_width + 128)
    ).reshape(shards, half_rows, part_width + 128)
    down_half = down_rows // 2
    down_flat = (half_rows, down_half * width // half_rows)
    packed = jnp.concatenate(
        [
            my_rows(jnp.concatenate([shared_gate[0], shared_up[0]], axis=1)),
            mine_of(shared_down[0][:down_half], shared_down[0][down_half:]).reshape(down_flat),
        ],
        axis=1,
    )
    by_head, packed = lax.optimization_barrier((by_head, packed))
    gathered = lax.all_gather(packed, "shard")
    own_part = exchange(by_head)
    out_rows = my_rows(w_output[0])
    out_rows = ordered_by(
        position % 2 == 0, out_rows, lax.ppermute(out_rows, "shard", [(p, p ^ 1) for p in range(shards)])
    )
    out_parts = [out_rows] + [
        lax.ppermute(
            out_rows,
            "shard",
            [(p, p // ring * ring + (p % ring - 2 * k) % ring) for p in range(shards)],
        )
        for k in range(1, ring // 2)
    ]
    own_part, *out_parts = lax.optimization_barrier((own_part, *out_parts))
    own_out = lax.dynamic_slice_in_dim(
        jnp.concatenate(out_parts + out_parts), ring - position % ring // 2 * 2, ring, axis=0
    )
    output_w = ordered(own_out, twin(own_out), 1).reshape(group_width, width)
    fetched = ordered(own_part, twin(own_part), 1).reshape(width, part_width + 128)
    qkv_w, tail = fetched[:, :part_width], fetched[:, part_width:]
    router_w = tail[:, :experts]
    gains = tail[:, experts : experts + 2].T.astype(f32)
    gain_one, gain_two = gains[0][None], gains[1][None]

    expert_g, expert_u, expert_d = expert_gate[0], expert_up[0], expert_down[0]
    slot_of = jnp.arange(slots, dtype=jnp.int32)
    expert_of = jnp.arange(experts, dtype=jnp.int32)
    row_of = jnp.arange(block, dtype=jnp.int32)
    spread = (expert_of[:, None] == slot_of[None, :] // CAP).astype(bf)
    router_slots = dot(router_w, spread).astype(bf)
    earlier = (row_of[:, None] > row_of[None, :]).astype(bf)

    def slot_table(route_rows):
        named = jnp.any(route_rows[:, :, None] == expert_of[None, None, :], axis=1).astype(bf)
        slot_ids = dot(earlier, named).astype(bf)
        return (dot(named, spread) > 0.5) & (
            dot(slot_ids, spread).astype(jnp.int32) == (slot_of % CAP)[None, :]
        )

    here = [position % ring, jnp.ones_like(position), position // ring]
    info_all = jnp.stack(here).astype(jnp.int32)
    info = jnp.stack([here[0], is_first.astype(here[0].dtype), here[2]]).astype(jnp.int32)

    def gate_values(normed_two, table):
        logits = jnp.where(table, dot(normed_two, router_slots), masked_score)
        weights = jnp.exp(logits - jnp.max(logits, axis=-1, keepdims=True))
        weights = jnp.where(table, weights, 0.0)
        return weights / jnp.sum(weights, axis=-1, keepdims=True)

    def high_low(value):
        high = value.astype(bf)
        return high, (value - high.astype(f32)).astype(bf)

    def to_experts(rows):
        return (
            exchange(rows.reshape(shards, local_experts, CAP, width))
            .transpose(1, 0, 2, 3)
            .reshape(local_experts, shards * CAP, width)
        )

    def from_experts(rows):
        return exchange(
            rows.reshape(local_experts, shards, CAP, width).transpose(1, 0, 2, 3)
        ).reshape(slots, width)

    def moved(p, steps):
        return (p // ring + steps) % heads * ring + p % ring

    def shift_x(value, steps):
        return lax.ppermute(value, "shard", [(p, moved(p, steps)) for p in range(shards)])

    def next_ring(value):
        return jnp.stack(
            [
                lax.ppermute(
                    value,
                    ("section", "shard"),
                    [(p, shards + moved(p, steps)) for p in range(shards)],
                )
                for steps in range(heads)
            ]
        )

    def sum_over_x(rows):
        parts = rows.reshape(heads, block, width)
        away = [shift_x(parts[k].astype(bf), -k).astype(f32) for k in range(1, heads)]
        return sum(away, parts[0])

    def ring_rows(rows):
        return jnp.concatenate([rows] + [shift_x(rows, k) for k in range(1, heads)], axis=0)

    ring_inputs = [
        jnp.stack([inputs[0, m]] + [shift_x(inputs[0, m], k) for k in range(1, heads)])
        for m in range(micros)
    ]

    def shared_weights(gathered):
        gate_up = gathered[:, :, : 2 * shared_width]
        down = gathered[:, :, 2 * shared_width :].reshape(shards, down_half, width)
        return (
            ordered(gate_up, twin(gate_up), 1).reshape(width, 2 * shared_width),
            ordered(down, twin(down), 1).reshape(shards * down_rows, width),
        )

    def forward(moment, received, previous, shared_pair):
        first_micro = min(moment, micros - 1)
        second_micro = max(moment - 1, 0)
        ring_b = jnp.where(is_first, ring_inputs[first_micro], received)
        layer_b = ring_b[0]
        table = slot_table(
            jnp.where(is_first, routes[0, 0, first_micro], routes[0, 0, second_micro])
        )
        pick = table.astype(bf)
        layer_in = layer_b.astype(f32)
        ring_in = ring_b.reshape(heads * block, width).astype(f32)
        ring_one = (ring_in * inverse_rms(ring_in) * gain_one).astype(bf)
        qkv = dot(ring_one, qkv_w).astype(bf)
        cache = exchange(copies(qkv[:, group_width:], ring), zy_groups)
        qkv = qkv.reshape(heads, block, part_width)
        attn_info = info if moment == 1 else info_all
        attended, logs = attention_forward(attn_info, qkv, previous, cache)
        attended_rows = attended.reshape(heads * block, group_width)
        hidden = layer_in + sum_over_x(dot(attended_rows, output_w))
        if shared_pair is None:
            arrived, hidden = lax.optimization_barrier((gathered, hidden))
            shared_pair = shared_weights(arrived)
        gate_up_w, down_w = shared_pair
        normed_two = (hidden * inverse_rms(hidden) * gain_two).astype(bf)
        gates = gate_values(normed_two, table)
        expert_in = to_experts(dot_tn(pick, normed_two).astype(bf))
        gate_pre = wide_einsum("erd,edf->erf", expert_in, expert_g)
        up_pre = wide_einsum("erd,edf->erf", expert_in, expert_u)
        activated = (silu_parts(gate_pre)[0] * up_pre).astype(bf)
        returned = from_experts(wide_einsum("erf,efd->erd", activated, expert_d).astype(bf))
        high, low = high_low(gates)
        routed = dot(high, returned) + dot(low, returned)
        shared_gate_pre, shared_up_pre = halves(dot(normed_two, gate_up_w))
        shared_act = (silu_parts(shared_gate_pre)[0] * shared_up_pre).astype(bf)
        beside = lax.optimization_barrier(hidden + dot(shared_act, down_w))
        output_b = (beside + routed).astype(bf)
        return dict(
            layer_b=layer_b,
            pick=pick,
            ring_one=ring_one,
            qkv=qkv,
            cache=cache,
            previous=previous,
            info=attn_info,
            attended=attended,
            logs=logs,
            hidden=hidden,
            normed_two=normed_two,
            gates=gates,
            expert_in=expert_in,
            gate_pre=gate_pre,
            up_pre=up_pre,
            activated=activated,
            returned=returned,
            shared_gate_pre=shared_gate_pre,
            shared_up_pre=shared_up_pre,
            shared_act=shared_act,
            output_b=output_b,
            shared_pair=shared_pair,
        )

    def ffn_backward(kept, upstream_b):
        upstream = upstream_b.astype(f32)
        gates, hidden = kept["gates"], kept["hidden"]
        gate_up_w, down_w = kept["shared_pair"]
        high, low = high_low(gates)
        outgoing = dot_tn(high, upstream_b) + dot_tn(low, upstream_b)
        expert_grad = to_experts(outgoing.astype(bf))
        act_silu, act_slope = silu_parts(kept["gate_pre"])
        act_grad = wide_einsum("erd,efd->erf", expert_grad, expert_d)
        gate_pre_grad = (act_grad * kept["up_pre"] * act_slope).astype(bf)
        up_pre_grad = (act_grad * act_silu).astype(bf)
        expert_in_grad = (
            wide_einsum("erf,edf->erd", gate_pre_grad, expert_g)
            + wide_einsum("erf,edf->erd", up_pre_grad, expert_u)
        ).astype(bf)
        returned_grad = from_experts(expert_in_grad)
        shared_act_grad = dot_nt(upstream_b, down_w)
        shared_silu, shared_slope = silu_parts(kept["shared_gate_pre"])
        shared_gate_grad = (shared_act_grad * kept["shared_up_pre"] * shared_slope).astype(bf)
        shared_up_grad = (shared_act_grad * shared_silu).astype(bf)
        normed_two_grad = dot_nt(
            jnp.concatenate([shared_gate_grad, shared_up_grad], axis=1), gate_up_w
        )
        gate_grad = dot_nt(upstream_b, kept["returned"])
        picked_grad = gates * (gate_grad - jnp.sum(gates * gate_grad, axis=1, keepdims=True))
        picked_b = picked_grad.astype(bf)
        normed_two_grad = normed_two_grad + dot_nt(picked_b, router_slots)
        normed_two_grad = lax.optimization_barrier(normed_two_grad)
        normed_two_grad = normed_two_grad + dot(kept["pick"], returned_grad)
        logit_grad = dot_nt(picked_b, spread).astype(bf)
        hidden_norm_grad, gain_two_grad = norm_back(hidden, gain_two, normed_two_grad)
        return dict(
            hidden_grad=upstream + hidden_norm_grad,
            upstream_b=upstream_b,
            expert_grad=expert_grad,
            gate_pre_grad=gate_pre_grad,
            up_pre_grad=up_pre_grad,
            shared_gate_grad=shared_gate_grad,
            shared_up_grad=shared_up_grad,
            logit_grad=logit_grad,
            gain_two_grad=gain_two_grad,
        )

    def attention_back(kept, grads, carried):
        ring_hidden = ring_rows(grads["hidden_grad"].astype(bf))
        out_grad = dot_nt(ring_hidden, output_w).astype(bf)
        results = attention_backward(
            kept["info"],
            kept["qkv"],
            out_grad.reshape(heads, block, group_width),
            kept["attended"],
            kept["logs"],
            carried,
            kept["previous"],
            kept["cache"],
        )
        carried = results[2] if len(results) > 2 else None
        query_grad = results[0].reshape(heads * block, group_width)
        query_part = lax.optimization_barrier(dot_nt(query_grad, qkv_w[:, :group_width]))
        pair_grad = jnp.sum(exchange(results[1], zy_groups).astype(f32), axis=0).astype(bf)
        qkv_grad = jnp.concatenate([query_grad, pair_grad], axis=1)
        normed_one_grad = sum_over_x(query_part + dot_nt(pair_grad, qkv_w[:, group_width:]))
        in_norm_grad, gain_one_grad = norm_back(
            kept["layer_b"].astype(f32), gain_one, normed_one_grad
        )
        grads = dict(
            grads,
            ring_hidden=ring_hidden,
            qkv_grad=qkv_grad,
            gain_one_grad=gain_one_grad,
            layer_grad=(grads["hidden_grad"] + in_norm_grad).astype(bf),
        )
        return grads, carried

    nothing = jnp.zeros((block, width), bf)
    saved = []
    received, previous, shared_pair = jnp.zeros((heads, block, width), bf), None, None
    for moment in range(micros + 1):
        kept = forward(moment, received, previous, shared_pair)
        shared_pair = kept["shared_pair"]
        saved.append(kept)
        previous = kept["cache"]
        if moment < micros:
            received = next_ring(kept["output_b"])
    backs = [None] * (micros + 1)
    received, carried = nothing, None
    for source in range(micros, -1, -1):
        own = cotangent[0, source - 1] if source > 0 else nothing
        upstream_b = jnp.where(is_first, received, own)
        grads = ffn_backward(saved[source], upstream_b)
        backs[source], carried = attention_back(saved[source], grads, carried)
        if source > 0:
            received = lax.ppermute(backs[source]["layer_grad"], "section", [(1, 0)])

    def live(name, store, axis):
        ends = jnp.where(is_first, store[0][name], store[micros][name])
        return jnp.concatenate([ends, store[1][name]], axis=axis)

    def kept_rows(name, axis=0):
        return live(name, saved, axis)

    def back_rows(name, axis=0):
        return live(name, backs, axis)

    expert_parts = [
        wide_einsum("erd,erf->edf", kept_rows("expert_in", 1), back_rows("gate_pre_grad", 1)),
        wide_einsum("erd,erf->edf", kept_rows("expert_in", 1), back_rows("up_pre_grad", 1)),
        wide_einsum("erf,erd->efd", kept_rows("activated", 1), back_rows("expert_grad", 1)),
    ]
    expert_parts = [part.astype(bf) for part in expert_parts]
    expert_grads = [part.astype(f32) + twin(part).astype(f32) for part in expert_parts]

    def both(value):
        return jnp.concatenate([value, twin(value)], axis=0)

    def both_halves(low_half, high_half):
        own, other = mine_of(low_half, high_half), mine_of(high_half, low_half)
        return jnp.concatenate([own, twin(other)], axis=0)

    normed_two = kept_rows("normed_two")
    grad_gate_up = dot_tn(
        both(normed_two), both_halves(back_rows("shared_gate_grad"), back_rows("shared_up_grad"))
    )
    grad_down = dot_tn(both(kept_rows("shared_act")), both_halves(*halves(back_rows("upstream_b"))))


    def shift_z(value, steps):
        pairs = [(p, p // ring * ring + (p % ring + 2 * steps) % ring) for p in range(shards)]
        return lax.ppermute(value, "shard", pairs)

    def shift_y(value, steps):
        return lax.ppermute(value, "shard", [(p, p ^ 1) for p in range(shards)])

    along = dict(
        x=(shift_x, position // ring), z=(shift_z, position % ring // 2), y=(shift_y, position % 2)
    )

    def reduced(value, name, axis, held_as=bf):
        shift, here = along[name]
        count = value.shape[axis]

        def piece(steps):
            return lax.dynamic_index_in_dim(value, (here + steps) % count, axis, keepdims=False)

        total = piece(0).astype(f32)
        for steps in range(1, count):
            total = total + shift(piece(steps), steps).astype(f32)
        return total.astype(held_as)

    grad_gate_up, grad_down, ring_hidden = lax.optimization_barrier(
        (grad_gate_up.astype(bf), grad_down.astype(bf), backs[0]["ring_hidden"])
    )
    backs[0]["ring_hidden"] = ring_hidden
    pieces = grad_gate_up.reshape(heads, ring // 2, 2, rows_per, shared_width)
    share_gate_up = reduced(reduced(reduced(pieces, "x", 0), "z", 0), "y", 0, f32)
    pieces = grad_down.reshape(heads, ring // 2, 2, down_rows, width // 2)
    share_down = reduced(reduced(reduced(pieces, "z", 1), "x", 0), "y", 0, f32)

    grad_out = dot_tn(
        kept_rows("attended").reshape(micros * heads * block, group_width),
        back_rows("ring_hidden"),
    )

    def with_twin(value):
        value = value.astype(bf)
        own = my_rows(value)
        other = mine_of(value[..., half_rows:, :], value[..., :half_rows, :])
        return (own.astype(f32) + twin(other).astype(f32)).astype(bf)

    grad_out = with_twin(grad_out.reshape(ring, rows_per, width))
    grad_out, last_grad = lax.optimization_barrier((grad_out, backs[0]["layer_grad"]))
    backs[0]["layer_grad"] = last_grad
    share_out = jnp.sum(exchange(grad_out, zy_groups).astype(f32), axis=0)
    grad_qkv = dot_tn(kept_rows("ring_one"), back_rows("qkv_grad"))
    grad_router = dot_tn(normed_two, back_rows("logit_grad"))
    gain_sums = jnp.stack(
        [sum(grads[name] for grads in backs) for name in ("gain_one_grad", "gain_two_grad")]
    )
    grad_tail = jnp.concatenate(
        [grad_router, gain_sums.T, jnp.zeros((width, 128 - experts - 2), f32)], axis=1
    )
    grad_qkv = jnp.concatenate([grad_qkv, grad_tail], axis=1)
    pieces = exchange(
        with_twin(grad_qkv.reshape(shards, rows_per, part_width + 128))
    ).astype(f32)
    share_qkv = jnp.sum(
        pieces[:, :, :part_width].reshape(heads, ring, half_rows, part_width), axis=1
    )
    share_qkv = share_qkv.transpose(1, 0, 2)
    share_tail = jnp.sum(pieces[:, :, part_width:], axis=0)

    def total(share):
        return ordered(share, twin(share), 0)

    out_total, qkv_total, tail_total = total(share_out), total(share_qkv), total(share_tail)
    other_gate_up = twin(share_gate_up)
    down_total = ordered(share_down, twin(share_down), 1)

    def by_micro(store, name):
        return jnp.stack(
            [jnp.where(is_first, store[m][name], store[m + 1][name]) for m in range(micros)]
        )[None, None]

    return (
        by_micro(saved, "output_b"),
        by_micro(backs, "layer_grad"),
        tail_total[:, experts][None],
        qkv_total[:, :, :group_width].reshape(1, rows_per, head_width),
        qkv_total[:, :, group_width : group_width + HD].reshape(1, rows_per, key_width),
        qkv_total[:, :, group_width + HD :].reshape(1, rows_per, key_width),
        out_total[None],
        tail_total[:, experts + 1][None],
        tail_total[:, :experts][None],
        mine_of(share_gate_up, other_gate_up)[None],
        mine_of(other_gate_up, share_gate_up)[None],
        down_total[None],
        expert_grads[0][None],
        expert_grads[1][None],
        expert_grads[2][None],
    )


def solution(mesh):
    rows = P("section", "shard", None)
    vector = P("section", "shard")
    expert = P("section", "shard", None, None)
    tokens = P("dp", None, "shard", None)
    section_tokens = P("section", "dp", None, "shard", None)
    weights = (vector, rows, rows, rows, rows, vector, rows, rows, rows, rows) + (expert,) * 3
    return jax.shard_map(
        body,
        mesh=mesh,
        in_specs=(tokens, tokens, section_tokens) + weights,
        out_specs=(section_tokens, section_tokens) + weights,
        check_vma=False,
    )
```

```python
import functools

import jax
import jax.numpy as jnp
from jax import lax
from jax.experimental import pallas as pl
from jax.experimental.pallas import tpu as pltpu
from jax.sharding import PartitionSpec as P

H = 12
KVH = 4
HD = 128
GROUP = H // KVH
TOPK = 6
CAP = 8

epsilon = 1e-05
masked_score = -1e30
scaling = HD ** (-0.5)
log2_scale = scaling * 1.4426950408889634
bf = jnp.bfloat16
f32 = jnp.float32
VMEM_LIMIT = 32 * 1024 * 1024


def inverse_rms(rows):
    return lax.rsqrt(jnp.mean(rows * rows, axis=-1, keepdims=True) + epsilon)


def norm_back(layer_in, gain, upstream):
    inverse = inverse_rms(layer_in)
    unit_rows = layer_in * inverse
    gain_grad = jnp.sum(upstream * unit_rows, axis=0)
    scaled = upstream * gain
    in_grad = inverse * (scaled - unit_rows * jnp.mean(scaled * unit_rows, axis=-1, keepdims=True))
    return (in_grad, gain_grad)


def silu_parts(argument):
    sigmoid = jax.nn.sigmoid(argument)
    return argument * sigmoid, sigmoid * (1.0 + argument * (1.0 - sigmoid))


def dot(left_side, right_side):
    return jnp.dot(left_side, right_side, preferred_element_type=f32)


def dot_nt(left_side, right_side):
    return lax.dot_general(
        left_side, right_side, (((1,), (1,)), ((), ())), preferred_element_type=f32
    )


def dot_tn(left_side, right_side):
    return lax.dot_general(
        left_side, right_side, (((0,), (0,)), ((), ())), preferred_element_type=f32
    )


def wide_einsum(formula, left_side, right_side):
    return jnp.einsum(formula, left_side, right_side, preferred_element_type=f32)


def arrival(info_ref, parts, part):
    return lax.rem(info_ref[2] + parts - part, parts)


def stacked_heads(ref, at):
    return jnp.concatenate([ref[at, :, g * HD : (g + 1) * HD] for g in range(GROUP)], axis=0)


def store_heads(ref, at, rows):
    block = ref.shape[1]
    for g in range(GROUP):
        ref[at, :, g * HD : (g + 1) * HD] = rows[g * block : (g + 1) * block]


def cached(ref, span, column):
    rows = ref[:, span, column : column + HD]
    return rows.reshape(rows.shape[0] * rows.shape[1], HD)


def block_span(at, block):
    return pl.ds(pl.multiple_of(at * block, block), block)


def diagonal_mask(rows, chunk, block, zy):
    key_at = lax.broadcasted_iota(jnp.int32, (rows, chunk), 1)
    row_at = lax.broadcasted_iota(jnp.int32, (rows, chunk), 0)
    return key_at <= zy * block + lax.rem(row_at, block)


def attention_forward_kernel(has_prev, info_ref, q_ref, *refs):
    prev_ref = refs[0] if has_prev else None
    cur_ref, o_ref, log_ref = refs[-3:]
    parts, block, _ = q_ref.shape
    rows = GROUP * block
    mask = diagonal_mask(rows, cur_ref.shape[0] * block, block, info_ref[0])
    spans = [block_span(arrival(info_ref, parts, part), block) for part in range(parts)]
    for part in range(parts):
        at = arrival(info_ref, parts, part)
        queries = stacked_heads(q_ref, at)
        pieces = [(prev_ref, slice(None))] if has_prev else []
        pieces += [(cur_ref, spans[p]) for p in range(part + 1)]
        scores = [dot_nt(queries, cached(ref, span, 0)) for ref, span in pieces]
        if has_prev:
            scores[0] = scores[0] + jnp.where(info_ref[1] > 0, 0.0, masked_score).astype(f32)
        scores[-1] = jnp.where(mask, scores[-1], masked_score)
        peak = functools.reduce(
            jnp.maximum, [jnp.max(s, axis=-1, keepdims=True) for s in scores]
        )
        peak = peak * log2_scale
        total = jnp.zeros((rows, 1), f32)
        mixed = jnp.zeros((rows, HD), f32)
        for s, (ref, span) in zip(scores, pieces):
            probs = jnp.exp2(s * log2_scale - peak)
            total = total + jnp.sum(probs, axis=-1, keepdims=True)
            mixed = mixed + dot(probs.astype(bf), cached(ref, span, HD))
        store_heads(o_ref, at, (mixed / total).astype(bf))
        log_ref[at] = jnp.broadcast_to(peak + jnp.log2(total), (rows, HD))


def attention_backward_kernel(has_prev, has_carry, info_ref, q_ref, do_ref, o_ref, log_ref, *refs):
    refs = list(refs)
    sum_ref = refs.pop()
    carry_ref = refs.pop(0) if has_carry else None
    prev_ref = refs.pop(0) if has_prev else None
    cur_ref, dq_ref, dcur_ref = refs[:3]
    dprev_ref = refs[3] if has_prev else None
    sum_ref[...] = carry_ref[...] if has_carry else jnp.zeros(sum_ref.shape, f32)
    if has_prev:
        dprev_ref[...] = jnp.zeros(dprev_ref.shape, f32)
    parts, block, _ = q_ref.shape
    ring = cur_ref.shape[0]
    rows = GROUP * block
    mask = diagonal_mask(rows, ring * block, block, info_ref[0])
    spans = [block_span(arrival(info_ref, parts, part), block) for part in range(parts)]
    for part in range(parts):
        at = arrival(info_ref, parts, part)
        queries = stacked_heads(q_ref, at)
        out_grad = stacked_heads(do_ref, at)
        out = stacked_heads(o_ref, at)
        inner = jnp.sum(out_grad.astype(f32) * out.astype(f32), axis=-1, keepdims=True)
        log_total = log_ref[at][:, :1]
        query_grad = jnp.zeros((rows, HD), f32)
        pieces = []
        if has_prev:
            log_prev = log_total + jnp.where(info_ref[1] > 0, 0.0, -masked_score).astype(f32)
            pieces = [
                (prev_ref, dprev_ref, slice(p * block, (p + 1) * block), log_prev, False)
                for p in range(parts)
            ]
        pieces += [(cur_ref, sum_ref, spans[p], log_total, p == part) for p in range(part + 1)]
        for ref, grad_ref, span, log_row, on_diagonal in pieces:
            keys = cached(ref, span, 0)
            probs = jnp.exp2(dot_nt(queries, keys) * log2_scale - log_row)
            if on_diagonal:
                probs = jnp.where(mask, probs, 0.0)
            probs_grad = dot_nt(out_grad, cached(ref, span, HD))
            score_grad = (probs * (probs_grad - inner)).astype(bf)
            query_grad = query_grad + dot(score_grad, keys)
            key_grad = dot_tn(score_grad, queries) * scaling
            value_grad = dot_tn(probs.astype(bf), out_grad)
            grad_ref[:, span, :HD] += key_grad.reshape(ring, block, HD)
            grad_ref[:, span, HD:] += value_grad.reshape(ring, block, HD)
        store_heads(dq_ref, at, (query_grad * scaling).astype(bf))
    dcur_ref[...] = sum_ref[...].astype(bf)


def attention_call(kernel, factor, out_shape, scratch, info, queries, *rest):
    parts, block, _ = queries.shape
    rows = parts * GROUP * block
    keys = sum(ref.shape[0] * ref.shape[1] for ref in rest if ref.shape == rest[-1].shape)
    in_vmem = pl.BlockSpec(memory_space=pltpu.VMEM)
    return pl.pallas_call(
        kernel,
        out_shape=out_shape,
        in_specs=[pl.BlockSpec(memory_space=pltpu.SMEM)] + [in_vmem] * (1 + len(rest)),
        out_specs=(in_vmem,) * len(out_shape),
        scratch_shapes=scratch,
        compiler_params=pltpu.CompilerParams(vmem_limit_bytes=VMEM_LIMIT),
        cost_estimate=pl.CostEstimate(
            flops=factor * rows * keys * HD,
            bytes_accessed=factor * (keys + rows) * HD,
            transcendentals=rows * keys // 2,
        ),
    )(info, queries, *rest)


def attention_forward(info, qkv, prev, cur):
    parts, block, _ = qkv.shape
    shapes = (
        jax.ShapeDtypeStruct((parts, block, GROUP * HD), bf),
        jax.ShapeDtypeStruct((parts, GROUP * block, HD), f32),
    )
    caches = (cur,) if prev is None else (prev, cur)
    kernel = functools.partial(attention_forward_kernel, prev is not None)
    return attention_call(kernel, 2, shapes, [], info, qkv, *caches)


def attention_backward(info, qkv, out_grad, out, logs, carry, prev, cur):
    shapes = (jax.ShapeDtypeStruct(out.shape, bf), jax.ShapeDtypeStruct(cur.shape, bf))
    if prev is not None:
        shapes += (jax.ShapeDtypeStruct(cur.shape, f32),)
    extra = tuple(value for value in (carry, prev) if value is not None)
    kernel = functools.partial(attention_backward_kernel, prev is not None, carry is not None)
    scratch = [pltpu.VMEM(cur.shape, f32)]
    return attention_call(
        kernel, 5, shapes, scratch, info, qkv, out_grad, out, logs, *extra, cur
    )


def body(
    inputs,
    cotangent,
    routes,
    norm_attn,
    w_query,
    w_key,
    w_value,
    w_output,
    norm_ffn,
    w_router,
    shared_gate,
    shared_up,
    shared_down,
    expert_gate,
    expert_up,
    expert_down,
):
    micros, block, width = inputs.shape[1:]
    shards = lax.axis_size("shard")
    section = lax.axis_index("section")
    core = lax.axis_index("dp")
    position = lax.axis_index("shard")
    heads = KVH
    ring = shards // heads
    local_experts = expert_gate.shape[1]
    experts = local_experts * shards
    slots = experts * CAP
    rows_per = w_query.shape[1]
    half_rows = rows_per // 2
    group_width = GROUP * HD
    head_width = H * HD
    key_width = KVH * HD
    part_width = group_width + 2 * HD
    shared_width = shared_gate.shape[2]
    down_rows = shared_down.shape[1]
    is_first = section == 0
    low_core = core == 0
    zy_groups = [[x * ring + zy for zy in range(ring)] for x in range(heads)]

    def exchange(value, groups=None):
        return lax.all_to_all(
            value, "shard", split_axis=0, concat_axis=0, tiled=True, axis_index_groups=groups
        )

    def copies(value, count):
        return jnp.broadcast_to(value[None], (count,) + value.shape)

    def twin(value):
        return lax.ppermute(value, "dp", [(0, 1), (1, 0)])

    def mine_of(low_half, high_half):
        return jnp.where(low_core, low_half, high_half)

    def ordered(own, other, axis):
        low_half, high_half = mine_of(own, other), mine_of(other, own)
        return jnp.concatenate([low_half, high_half], axis=axis)

    def ordered_by(in_order, own, other):
        return jnp.stack([jnp.where(in_order, own, other), jnp.where(in_order, other, own)])

    def halves(value):
        half = value.shape[-1] // 2
        return value[..., :half], value[..., half:]

    def my_rows(value):
        return mine_of(value[..., :half_rows, :], value[..., half_rows:, :])

    tail = jnp.concatenate(
        [
            w_router[0],
            norm_attn[0][:, None],
            norm_ffn[0][:, None],
            jnp.zeros((rows_per, 128 - experts - 2), bf),
        ],
        axis=1,
    )
    by_head = jnp.concatenate(
        [
            w_query[0].reshape(rows_per, heads, group_width),
            w_key[0].reshape(rows_per, heads, HD),
            w_value[0].reshape(rows_per, heads, HD),
            jnp.broadcast_to(tail[:, None], (rows_per, heads, 128)),
        ],
        axis=2,
    ).transpose(1, 0, 2)
    by_head = my_rows(by_head)
    by_head = jnp.broadcast_to(
        by_head[:, None], (heads, ring, half_rows, part_width + 128)
    ).reshape(shards, half_rows, part_width + 128)
    down_half = down_rows // 2
    down_flat = (half_rows, down_half * width // half_rows)
    packed = jnp.concatenate(
        [
            my_rows(jnp.concatenate([shared_gate[0], shared_up[0]], axis=1)),
            mine_of(shared_down[0][:down_half], shared_down[0][down_half:]).reshape(down_flat),
        ],
        axis=1,
    )
    by_head, packed = lax.optimization_barrier((by_head, packed))
    gathered = lax.all_gather(packed, "shard")
    own_part = exchange(by_head)
    out_rows = my_rows(w_output[0])
    out_rows = ordered_by(
        position % 2 == 0, out_rows, lax.ppermute(out_rows, "shard", [(p, p ^ 1) for p in range(shards)])
    )
    out_parts = [out_rows] + [
        lax.ppermute(
            out_rows,
            "shard",
            [(p, p // ring * ring + (p % ring - 2 * k) % ring) for p in range(shards)],
        )
        for k in range(1, ring // 2)
    ]
    own_part, *out_parts = lax.optimization_barrier((own_part, *out_parts))
    own_out = lax.dynamic_slice_in_dim(
        jnp.concatenate(out_parts + out_parts), ring - position % ring // 2 * 2, ring, axis=0
    )
    output_w = ordered(own_out, twin(own_out), 1).reshape(group_width, width)
    fetched = ordered(own_part, twin(own_part), 1).reshape(width, part_width + 128)
    qkv_w, tail = fetched[:, :part_width], fetched[:, part_width:]
    router_w = tail[:, :experts]
    gains = tail[:, experts : experts + 2].T.astype(f32)
    gain_one, gain_two = gains[0][None], gains[1][None]

    expert_g, expert_u, expert_d = expert_gate[0], expert_up[0], expert_down[0]
    slot_of = jnp.arange(slots, dtype=jnp.int32)
    expert_of = jnp.arange(experts, dtype=jnp.int32)
    row_of = jnp.arange(block, dtype=jnp.int32)
    spread = (expert_of[:, None] == slot_of[None, :] // CAP).astype(bf)
    router_slots = dot(router_w, spread).astype(bf)
    earlier = (row_of[:, None] > row_of[None, :]).astype(bf)

    def slot_table(route_rows):
        named = jnp.any(route_rows[:, :, None] == expert_of[None, None, :], axis=1).astype(bf)
        slot_ids = dot(earlier, named).astype(bf)
        return (dot(named, spread) > 0.5) & (
            dot(slot_ids, spread).astype(jnp.int32) == (slot_of % CAP)[None, :]
        )

    here = [position % ring, jnp.ones_like(position), position // ring]
    info_all = jnp.stack(here).astype(jnp.int32)
    info = jnp.stack([here[0], is_first.astype(here[0].dtype), here[2]]).astype(jnp.int32)

    def gate_values(normed_two, table):
        logits = jnp.where(table, dot(normed_two, router_slots), masked_score)
        weights = jnp.exp(logits - jnp.max(logits, axis=-1, keepdims=True))
        weights = jnp.where(table, weights, 0.0)
        return weights / jnp.sum(weights, axis=-1, keepdims=True)

    def high_low(value):
        high = value.astype(bf)
        return high, (value - high.astype(f32)).astype(bf)

    def to_experts(rows):
        return (
            exchange(rows.reshape(shards, local_experts, CAP, width))
            .transpose(1, 0, 2, 3)
            .reshape(local_experts, shards * CAP, width)
        )

    def from_experts(rows):
        return exchange(
            rows.reshape(local_experts, shards, CAP, width).transpose(1, 0, 2, 3)
        ).reshape(slots, width)

    def moved(p, steps):
        return (p // ring + steps) % heads * ring + p % ring

    def shift_x(value, steps):
        return lax.ppermute(value, "shard", [(p, moved(p, steps)) for p in range(shards)])

    def next_ring(value):
        return jnp.stack(
            [
                lax.ppermute(
                    value,
                    ("section", "shard"),
                    [(p, shards + moved(p, steps)) for p in range(shards)],
                )
                for steps in range(heads)
            ]
        )

    def sum_over_x(rows):
        parts = rows.reshape(heads, block, width)
        away = [shift_x(parts[k].astype(bf), -k).astype(f32) for k in range(1, heads)]
        return sum(away, parts[0])

    def ring_rows(rows):
        return jnp.concatenate([rows] + [shift_x(rows, k) for k in range(1, heads)], axis=0)

    ring_inputs = [
        jnp.stack([inputs[0, m]] + [shift_x(inputs[0, m], k) for k in range(1, heads)])
        for m in range(micros)
    ]

    def shared_weights(gathered):
        gate_up = gathered[:, :, : 2 * shared_width]
        down = gathered[:, :, 2 * shared_width :].reshape(shards, down_half, width)
        return (
            ordered(gate_up, twin(gate_up), 1).reshape(width, 2 * shared_width),
            ordered(down, twin(down), 1).reshape(shards * down_rows, width),
        )

    def forward(moment, received, previous, shared_pair):
        first_micro = min(moment, micros - 1)
        second_micro = max(moment - 1, 0)
        ring_b = jnp.where(is_first, ring_inputs[first_micro], received)
        layer_b = ring_b[0]
        table = slot_table(
            jnp.where(is_first, routes[0, 0, first_micro], routes[0, 0, second_micro])
        )
        pick = table.astype(bf)
        layer_in = layer_b.astype(f32)
        ring_in = ring_b.reshape(heads * block, width).astype(f32)
        ring_one = (ring_in * inverse_rms(ring_in) * gain_one).astype(bf)
        qkv = dot(ring_one, qkv_w).astype(bf)
        cache = exchange(copies(qkv[:, group_width:], ring), zy_groups)
        qkv = qkv.reshape(heads, block, part_width)
        attn_info = info if moment == 1 else info_all
        attended, logs = attention_forward(attn_info, qkv, previous, cache)
        attended_rows = attended.reshape(heads * block, group_width)
        hidden = layer_in + sum_over_x(dot(attended_rows, output_w))
        if shared_pair is None:
            arrived, hidden = lax.optimization_barrier((gathered, hidden))
            shared_pair = shared_weights(arrived)
        gate_up_w, down_w = shared_pair
        normed_two = (hidden * inverse_rms(hidden) * gain_two).astype(bf)
        gates = gate_values(normed_two, table)
        expert_in = to_experts(dot_tn(pick, normed_two).astype(bf))
        gate_pre = wide_einsum("erd,edf->erf", expert_in, expert_g)
        up_pre = wide_einsum("erd,edf->erf", expert_in, expert_u)
        activated = (silu_parts(gate_pre)[0] * up_pre).astype(bf)
        returned = from_experts(wide_einsum("erf,efd->erd", activated, expert_d).astype(bf))
        high, low = high_low(gates)
        routed = dot(high, returned) + dot(low, returned)
        shared_gate_pre, shared_up_pre = halves(dot(normed_two, gate_up_w))
        shared_act = (silu_parts(shared_gate_pre)[0] * shared_up_pre).astype(bf)
        beside = lax.optimization_barrier(hidden + dot(shared_act, down_w))
        output_b = (beside + routed).astype(bf)
        return dict(
            layer_b=layer_b,
            pick=pick,
            ring_one=ring_one,
            qkv=qkv,
            cache=cache,
            previous=previous,
            info=attn_info,
            attended=attended,
            logs=logs,
            hidden=hidden,
            normed_two=normed_two,
            gates=gates,
            expert_in=expert_in,
            gate_pre=gate_pre,
            up_pre=up_pre,
            activated=activated,
            returned=returned,
            shared_gate_pre=shared_gate_pre,
            shared_up_pre=shared_up_pre,
            shared_act=shared_act,
            output_b=output_b,
            shared_pair=shared_pair,
        )

    def ffn_backward(kept, upstream_b):
        upstream = upstream_b.astype(f32)
        gates, hidden = kept["gates"], kept["hidden"]
        gate_up_w, down_w = kept["shared_pair"]
        high, low = high_low(gates)
        outgoing = dot_tn(high, upstream_b) + dot_tn(low, upstream_b)
        expert_grad = to_experts(outgoing.astype(bf))
        act_silu, act_slope = silu_parts(kept["gate_pre"])
        act_grad = wide_einsum("erd,efd->erf", expert_grad, expert_d)
        gate_pre_grad = (act_grad * kept["up_pre"] * act_slope).astype(bf)
        up_pre_grad = (act_grad * act_silu).astype(bf)
        expert_in_grad = (
            wide_einsum("erf,edf->erd", gate_pre_grad, expert_g)
            + wide_einsum("erf,edf->erd", up_pre_grad, expert_u)
        ).astype(bf)
        returned_grad = from_experts(expert_in_grad)
        shared_act_grad = dot_nt(upstream_b, down_w)
        shared_silu, shared_slope = silu_parts(kept["shared_gate_pre"])
        shared_gate_grad = (shared_act_grad * kept["shared_up_pre"] * shared_slope).astype(bf)
        shared_up_grad = (shared_act_grad * shared_silu).astype(bf)
        normed_two_grad = dot_nt(
            jnp.concatenate([shared_gate_grad, shared_up_grad], axis=1), gate_up_w
        )
        gate_grad = dot_nt(upstream_b, kept["returned"])
        picked_grad = gates * (gate_grad - jnp.sum(gates * gate_grad, axis=1, keepdims=True))
        picked_b = picked_grad.astype(bf)
        normed_two_grad = normed_two_grad + dot_nt(picked_b, router_slots)
        normed_two_grad = lax.optimization_barrier(normed_two_grad)
        normed_two_grad = normed_two_grad + dot(kept["pick"], returned_grad)
        logit_grad = dot_nt(picked_b, spread).astype(bf)
        hidden_norm_grad, gain_two_grad = norm_back(hidden, gain_two, normed_two_grad)
        return dict(
            hidden_grad=upstream + hidden_norm_grad,
            upstream_b=upstream_b,
            expert_grad=expert_grad,
            gate_pre_grad=gate_pre_grad,
            up_pre_grad=up_pre_grad,
            shared_gate_grad=shared_gate_grad,
            shared_up_grad=shared_up_grad,
            logit_grad=logit_grad,
            gain_two_grad=gain_two_grad,
        )

    def attention_back(kept, grads, carried):
        ring_hidden = ring_rows(grads["hidden_grad"].astype(bf))
        out_grad = dot_nt(ring_hidden, output_w).astype(bf)
        results = attention_backward(
            kept["info"],
            kept["qkv"],
            out_grad.reshape(heads, block, group_width),
            kept["attended"],
            kept["logs"],
            carried,
            kept["previous"],
            kept["cache"],
        )
        carried = results[2] if len(results) > 2 else None
        query_grad = results[0].reshape(heads * block, group_width)
        query_part = lax.optimization_barrier(dot_nt(query_grad, qkv_w[:, :group_width]))
        pair_grad = jnp.sum(exchange(results[1], zy_groups).astype(f32), axis=0).astype(bf)
        qkv_grad = jnp.concatenate([query_grad, pair_grad], axis=1)
        normed_one_grad = sum_over_x(query_part + dot_nt(pair_grad, qkv_w[:, group_width:]))
        in_norm_grad, gain_one_grad = norm_back(
            kept["layer_b"].astype(f32), gain_one, normed_one_grad
        )
        grads = dict(
            grads,
            ring_hidden=ring_hidden,
            qkv_grad=qkv_grad,
            gain_one_grad=gain_one_grad,
            layer_grad=(grads["hidden_grad"] + in_norm_grad).astype(bf),
        )
        return grads, carried

    nothing = jnp.zeros((block, width), bf)
    saved = []
    received, previous, shared_pair = jnp.zeros((heads, block, width), bf), None, None
    for moment in range(micros + 1):
        kept = forward(moment, received, previous, shared_pair)
        shared_pair = kept["shared_pair"]
        saved.append(kept)
        previous = kept["cache"]
        if moment < micros:
            received = next_ring(kept["output_b"])
    backs = [None] * (micros + 1)
    received, carried = nothing, None
    for source in range(micros, -1, -1):
        own = cotangent[0, source - 1] if source > 0 else nothing
        upstream_b = jnp.where(is_first, received, own)
        grads = ffn_backward(saved[source], upstream_b)
        backs[source], carried = attention_back(saved[source], grads, carried)
        if source > 0:
            received = lax.ppermute(backs[source]["layer_grad"], "section", [(1, 0)])

    def live(name, store, axis):
        ends = jnp.where(is_first, store[0][name], store[micros][name])
        return jnp.concatenate([ends, store[1][name]], axis=axis)

    def kept_rows(name, axis=0):
        return live(name, saved, axis)

    def back_rows(name, axis=0):
        return live(name, backs, axis)

    expert_parts = [
        wide_einsum("erd,erf->edf", kept_rows("expert_in", 1), back_rows("gate_pre_grad", 1)),
        wide_einsum("erd,erf->edf", kept_rows("expert_in", 1), back_rows("up_pre_grad", 1)),
        wide_einsum("erf,erd->efd", kept_rows("activated", 1), back_rows("expert_grad", 1)),
    ]
    expert_parts = [part.astype(bf) for part in expert_parts]
    expert_others = [twin(part) for part in expert_parts]

    def both(value):
        return jnp.concatenate([value, twin(value)], axis=0)

    def both_halves(low_half, high_half):
        own, other = mine_of(low_half, high_half), mine_of(high_half, low_half)
        return jnp.concatenate([own, twin(other)], axis=0)

    normed_two = kept_rows("normed_two")
    grad_gate_up = dot_tn(
        both(normed_two), both_halves(back_rows("shared_gate_grad"), back_rows("shared_up_grad"))
    )
    grad_down = dot_tn(both(kept_rows("shared_act")), both_halves(*halves(back_rows("upstream_b"))))


    def shift_z(value, steps):
        pairs = [(p, p // ring * ring + (p % ring + 2 * steps) % ring) for p in range(shards)]
        return lax.ppermute(value, "shard", pairs)

    def shift_y(value, steps):
        return lax.ppermute(value, "shard", [(p, p ^ 1) for p in range(shards)])

    along = dict(
        x=(shift_x, position // ring), z=(shift_z, position % ring // 2), y=(shift_y, position % 2)
    )

    def reduced(value, name, axis, held_as=bf):
        shift, here = along[name]
        count = value.shape[axis]

        def piece(steps):
            return lax.dynamic_index_in_dim(value, (here + steps) % count, axis, keepdims=False)

        total = piece(0).astype(f32)
        for steps in range(1, count):
            total = total + shift(piece(steps), steps).astype(f32)
        return total.astype(held_as)

    grad_out = dot_tn(
        kept_rows("attended").reshape(micros * heads * block, group_width),
        back_rows("ring_hidden"),
    )
    grad_gate_up, grad_down, grad_out, last_grad, *expert_others = lax.optimization_barrier(
        (
            grad_gate_up.astype(bf),
            grad_down.astype(bf),
            grad_out.astype(bf),
            backs[0]["layer_grad"],
            *expert_others,
        )
    )
    backs[0]["layer_grad"] = last_grad
    expert_grads = [
        part.astype(f32) + other.astype(f32) for part, other in zip(expert_parts, expert_others)
    ]
    pieces = grad_gate_up.reshape(heads, ring // 2, 2, rows_per, shared_width)
    share_gate_up = reduced(reduced(reduced(pieces, "x", 0), "z", 0), "y", 0, f32)
    pieces = grad_down.reshape(heads, ring // 2, 2, down_rows, width // 2)
    share_down = reduced(reduced(reduced(pieces, "z", 1), "x", 0), "y", 0, f32)

    share_out = jnp.sum(
        exchange(grad_out.reshape(ring, rows_per, width), zy_groups).astype(f32), axis=0
    )
    grad_qkv = dot_tn(kept_rows("ring_one"), back_rows("qkv_grad"))
    grad_router = dot_tn(normed_two, back_rows("logit_grad"))
    gain_sums = jnp.stack(
        [sum(grads[name] for grads in backs) for name in ("gain_one_grad", "gain_two_grad")]
    )
    grad_tail = jnp.concatenate(
        [grad_router, gain_sums.T, jnp.zeros((width, 128 - experts - 2), f32)], axis=1
    )
    grad_qkv = jnp.concatenate([grad_qkv, grad_tail], axis=1)
    pieces = exchange(
        grad_qkv.astype(bf).reshape(shards, rows_per, part_width + 128)
    ).astype(f32)
    share_qkv = jnp.sum(
        pieces[:, :, :part_width].reshape(heads, ring, rows_per, part_width), axis=1
    )
    share_qkv = share_qkv.transpose(1, 0, 2)
    share_tail = jnp.sum(pieces[:, :, part_width:], axis=0)

    def total(share):
        return share + twin(share)

    out_total, qkv_total, tail_total = total(share_out), total(share_qkv), total(share_tail)
    other_gate_up = twin(share_gate_up)
    down_total = ordered(share_down, twin(share_down), 1)

    def by_micro(store, name):
        return jnp.stack(
            [jnp.where(is_first, store[m][name], store[m + 1][name]) for m in range(micros)]
        )[None, None]

    return (
        by_micro(saved, "output_b"),
        by_micro(backs, "layer_grad"),
        tail_total[:, experts][None],
        qkv_total[:, :, :group_width].reshape(1, rows_per, head_width),
        qkv_total[:, :, group_width : group_width + HD].reshape(1, rows_per, key_width),
        qkv_total[:, :, group_width + HD :].reshape(1, rows_per, key_width),
        out_total[None],
        tail_total[:, experts + 1][None],
        tail_total[:, :experts][None],
        mine_of(share_gate_up, other_gate_up)[None],
        mine_of(other_gate_up, share_gate_up)[None],
        down_total[None],
        expert_grads[0][None],
        expert_grads[1][None],
        expert_grads[2][None],
    )


def solution(mesh):
    rows = P("section", "shard", None)
    vector = P("section", "shard")
    expert = P("section", "shard", None, None)
    tokens = P("dp", None, "shard", None)
    section_tokens = P("section", "dp", None, "shard", None)
    weights = (vector, rows, rows, rows, rows, vector, rows, rows, rows, rows) + (expert,) * 3
    return jax.shard_map(
        body,
        mesh=mesh,
        in_specs=(tokens, tokens, section_tokens) + weights,
        out_specs=(section_tokens, section_tokens) + weights,
        check_vma=False,
    )
```

```python
import functools

import jax
import jax.numpy as jnp
from jax import lax
from jax.experimental import pallas as pl
from jax.experimental.pallas import tpu as pltpu
from jax.sharding import PartitionSpec as P

H = 12
KVH = 4
HD = 128
GROUP = H // KVH
TOPK = 6
CAP = 8

epsilon = 1e-05
masked_score = -1e30
scaling = HD ** (-0.5)
log2_scale = scaling * 1.4426950408889634
bf = jnp.bfloat16
f32 = jnp.float32
VMEM_LIMIT = 32 * 1024 * 1024
KEPT = ("ring_one", "attended", "normed_two", "shared_act", "expert_in", "activated")
BACK = (
    "qkv_grad",
    "ring_hidden",
    "gain_one_grad",
    "gain_two_grad",
    "logit_grad",
    "upstream_b",
    "shared_gate_grad",
    "shared_up_grad",
    "expert_grad",
    "gate_pre_grad",
    "up_pre_grad",
)


def inverse_rms(rows):
    return lax.rsqrt(jnp.mean(rows * rows, axis=-1, keepdims=True) + epsilon)


def norm_back(layer_in, gain, upstream):
    inverse = inverse_rms(layer_in)
    unit_rows = layer_in * inverse
    gain_grad = jnp.sum(upstream * unit_rows, axis=0)
    scaled = upstream * gain
    in_grad = inverse * (scaled - unit_rows * jnp.mean(scaled * unit_rows, axis=-1, keepdims=True))
    return (in_grad, gain_grad)


def silu_parts(argument):
    sigmoid = jax.nn.sigmoid(argument)
    return argument * sigmoid, sigmoid * (1.0 + argument * (1.0 - sigmoid))


def dot(left_side, right_side):
    return jnp.dot(left_side, right_side, preferred_element_type=f32)


def dot_nt(left_side, right_side):
    return lax.dot_general(
        left_side, right_side, (((1,), (1,)), ((), ())), preferred_element_type=f32
    )


def dot_tn(left_side, right_side):
    return lax.dot_general(
        left_side, right_side, (((0,), (0,)), ((), ())), preferred_element_type=f32
    )


def wide_einsum(formula, left_side, right_side):
    return jnp.einsum(formula, left_side, right_side, preferred_element_type=f32)


def arrival(info_ref, parts, part):
    return lax.rem(info_ref[1] + parts - part, parts)


def stacked_heads(ref, at, micro):
    return jnp.concatenate(
        [ref[at, micro, :, g * HD : (g + 1) * HD] for g in range(GROUP)], axis=0
    )


def store_heads(ref, at, micro, rows):
    block = ref.shape[2]
    for g in range(GROUP):
        ref[at, micro, :, g * HD : (g + 1) * HD] = rows[g * block : (g + 1) * block]


def cached(ref, span, column):
    rows = ref[:, span, column : column + HD]
    return rows.reshape(rows.shape[0] * rows.shape[1], HD)


def key_spans(info_ref, parts, micros, block, part, micro):
    spans = [
        slice((at * micros + m) * block, (at * micros + m + 1) * block)
        for m in range(micro)
        for at in range(parts)
    ]
    for p in range(part + 1):
        start = (arrival(info_ref, parts, p) * micros + micro) * block
        spans.append(pl.ds(pl.multiple_of(start, block), block))
    return spans


def diagonal_mask(rows, chunk, block, zy):
    key_at = lax.broadcasted_iota(jnp.int32, (rows, chunk), 1)
    row_at = lax.broadcasted_iota(jnp.int32, (rows, chunk), 0)
    return key_at <= zy * block + lax.rem(row_at, block)


def attention_forward_kernel(info_ref, q_ref, kv_ref, o_ref, log_ref):
    parts, micros, block, _ = q_ref.shape
    rows = GROUP * block
    mask = diagonal_mask(rows, kv_ref.shape[0] * block, block, info_ref[0])
    for part in range(parts):
        at = arrival(info_ref, parts, part)
        for micro in range(micros):
            queries = stacked_heads(q_ref, at, micro)
            spans = key_spans(info_ref, parts, micros, block, part, micro)
            scores = [dot_nt(queries, cached(kv_ref, span, 0)) for span in spans]
            scores[-1] = jnp.where(mask, scores[-1], masked_score)
            peak = functools.reduce(
                jnp.maximum, [jnp.max(s, axis=-1, keepdims=True) for s in scores]
            )
            peak = peak * log2_scale
            total = jnp.zeros((rows, 1), f32)
            mixed = jnp.zeros((rows, HD), f32)
            for s, span in zip(scores, spans):
                probs = jnp.exp2(s * log2_scale - peak)
                total = total + jnp.sum(probs, axis=-1, keepdims=True)
                mixed = mixed + dot(probs.astype(bf), cached(kv_ref, span, HD))
            store_heads(o_ref, at, micro, (mixed / total).astype(bf))
            log_ref[at, micro] = jnp.broadcast_to(peak + jnp.log2(total), (rows, HD))


def attention_backward_kernel(
    info_ref, q_ref, do_ref, o_ref, log_ref, kv_ref, dq_ref, dkv_ref, sum_ref
):
    parts, micros, block, _ = q_ref.shape
    ring = kv_ref.shape[0]
    rows = GROUP * block
    mask = diagonal_mask(rows, ring * block, block, info_ref[0])
    sum_ref[...] = jnp.zeros(sum_ref.shape, f32)
    for part in range(parts):
        at = arrival(info_ref, parts, part)
        for micro in range(micros):
            queries = stacked_heads(q_ref, at, micro)
            out_grad = stacked_heads(do_ref, at, micro)
            out = stacked_heads(o_ref, at, micro)
            inner = jnp.sum(out_grad.astype(f32) * out.astype(f32), axis=-1, keepdims=True)
            log_total = log_ref[at, micro][:, :1]
            query_grad = jnp.zeros((rows, HD), f32)
            spans = key_spans(info_ref, parts, micros, block, part, micro)
            for i, span in enumerate(spans):
                keys = cached(kv_ref, span, 0)
                probs = jnp.exp2(dot_nt(queries, keys) * log2_scale - log_total)
                if i == len(spans) - 1:
                    probs = jnp.where(mask, probs, 0.0)
                probs_grad = dot_nt(out_grad, cached(kv_ref, span, HD))
                score_grad = (probs * (probs_grad - inner)).astype(bf)
                query_grad = query_grad + dot(score_grad, keys)
                key_grad = dot_tn(score_grad, queries) * scaling
                value_grad = dot_tn(probs.astype(bf), out_grad)
                sum_ref[:, span, :HD] += key_grad.reshape(ring, block, HD)
                sum_ref[:, span, HD:] += value_grad.reshape(ring, block, HD)
            store_heads(dq_ref, at, micro, (query_grad * scaling).astype(bf))
    dkv_ref[...] = sum_ref[...].astype(bf)


def attention_call(kernel, factor, out_shape, scratch, info, queries, *rest):
    parts, micros, block, _ = queries.shape
    rows = parts * micros * GROUP * block
    keys = rest[-1].shape[0] * rest[-1].shape[1]
    in_vmem = pl.BlockSpec(memory_space=pltpu.VMEM)
    return pl.pallas_call(
        kernel,
        out_shape=out_shape,
        in_specs=[pl.BlockSpec(memory_space=pltpu.SMEM)] + [in_vmem] * (1 + len(rest)),
        out_specs=(in_vmem,) * len(out_shape),
        scratch_shapes=scratch,
        compiler_params=pltpu.CompilerParams(vmem_limit_bytes=VMEM_LIMIT),
        cost_estimate=pl.CostEstimate(
            flops=factor * rows * keys * HD,
            bytes_accessed=factor * (keys + rows) * HD,
            transcendentals=rows * keys // 2,
        ),
    )(info, queries, *rest)


def attention_forward(info, qkv, cache):
    parts, micros, block, _ = qkv.shape
    shapes = (
        jax.ShapeDtypeStruct((parts, micros, block, GROUP * HD), bf),
        jax.ShapeDtypeStruct((parts, micros, GROUP * block, HD), f32),
    )
    return attention_call(attention_forward_kernel, 2, shapes, [], info, qkv, cache)


def attention_backward(info, qkv, out_grad, out, logs, cache):
    shapes = (jax.ShapeDtypeStruct(out.shape, bf), jax.ShapeDtypeStruct(cache.shape, bf))
    scratch = [pltpu.VMEM(cache.shape, f32)]
    return attention_call(
        attention_backward_kernel, 5, shapes, scratch, info, qkv, out_grad, out, logs, cache
    )


def body(
    inputs,
    cotangent,
    routes,
    norm_attn,
    w_query,
    w_key,
    w_value,
    w_output,
    norm_ffn,
    w_router,
    shared_gate,
    shared_up,
    shared_down,
    expert_gate,
    expert_up,
    expert_down,
):
    micros, block, width = inputs.shape[1:]
    tokens = micros * block
    shards = lax.axis_size("shard")
    section = lax.axis_index("section")
    core = lax.axis_index("dp")
    position = lax.axis_index("shard")
    heads = KVH
    ring = shards // heads
    local_experts = expert_gate.shape[1]
    experts = local_experts * shards
    room = micros * CAP
    slots = experts * room
    rows_per = w_query.shape[1]
    half_rows = rows_per // 2
    group_width = GROUP * HD
    head_width = H * HD
    key_width = KVH * HD
    part_width = group_width + 2 * HD
    shared_width = shared_gate.shape[2]
    down_rows = shared_down.shape[1]
    is_first = section == 0
    low_core = core == 0
    zy_groups = [[x * ring + zy for zy in range(ring)] for x in range(heads)]

    def exchange(value, groups=None):
        return lax.all_to_all(
            value, "shard", split_axis=0, concat_axis=0, tiled=True, axis_index_groups=groups
        )

    def copies(value, count):
        return jnp.broadcast_to(value[None], (count,) + value.shape)

    def twin(value):
        return lax.ppermute(value, "dp", [(0, 1), (1, 0)])

    def mine_of(low_half, high_half):
        return jnp.where(low_core, low_half, high_half)

    def ordered(own, other, axis):
        low_half, high_half = mine_of(own, other), mine_of(other, own)
        return jnp.concatenate([low_half, high_half], axis=axis)

    def ordered_by(in_order, own, other):
        return jnp.stack([jnp.where(in_order, own, other), jnp.where(in_order, other, own)])

    def halves(value):
        half = value.shape[-1] // 2
        return value[..., :half], value[..., half:]

    def my_rows(value):
        return mine_of(value[..., :half_rows, :], value[..., half_rows:, :])

    tail = jnp.concatenate(
        [
            w_router[0],
            norm_attn[0][:, None],
            norm_ffn[0][:, None],
            jnp.zeros((rows_per, 128 - experts - 2), bf),
        ],
        axis=1,
    )
    by_head = jnp.concatenate(
        [
            w_query[0].reshape(rows_per, heads, group_width),
            w_key[0].reshape(rows_per, heads, HD),
            w_value[0].reshape(rows_per, heads, HD),
            jnp.broadcast_to(tail[:, None], (rows_per, heads, 128)),
        ],
        axis=2,
    ).transpose(1, 0, 2)
    by_head = my_rows(by_head)
    by_head = jnp.broadcast_to(
        by_head[:, None], (heads, ring, half_rows, part_width + 128)
    ).reshape(shards, half_rows, part_width + 128)
    down_half = down_rows // 2
    down_flat = (half_rows, down_half * width // half_rows)
    packed = jnp.concatenate(
        [
            my_rows(jnp.concatenate([shared_gate[0], shared_up[0]], axis=1)),
            mine_of(shared_down[0][:down_half], shared_down[0][down_half:]).reshape(down_flat),
        ],
        axis=1,
    )
    by_head, packed = lax.optimization_barrier((by_head, packed))
    gathered = lax.all_gather(packed, "shard")
    own_part = exchange(by_head)
    out_rows = my_rows(w_output[0])
    out_rows = ordered_by(
        position % 2 == 0, out_rows, lax.ppermute(out_rows, "shard", [(p, p ^ 1) for p in range(shards)])
    )
    out_parts = [out_rows] + [
        lax.ppermute(
            out_rows,
            "shard",
            [(p, p // ring * ring + (p % ring - 2 * k) % ring) for p in range(shards)],
        )
        for k in range(1, ring // 2)
    ]
    own_part, *out_parts = lax.optimization_barrier((own_part, *out_parts))
    own_out = lax.dynamic_slice_in_dim(
        jnp.concatenate(out_parts + out_parts), ring - position % ring // 2 * 2, ring, axis=0
    )
    output_w = ordered(own_out, twin(own_out), 1).reshape(group_width, width)
    fetched = ordered(own_part, twin(own_part), 1).reshape(width, part_width + 128)
    qkv_w, tail = fetched[:, :part_width], fetched[:, part_width:]
    router_w = tail[:, :experts]
    gains = tail[:, experts : experts + 2].T.astype(f32)
    gain_one, gain_two = gains[0][None], gains[1][None]

    expert_g, expert_u, expert_d = expert_gate[0], expert_up[0], expert_down[0]
    slot_of = jnp.arange(slots, dtype=jnp.int32)
    expert_of = jnp.arange(experts, dtype=jnp.int32)
    token_of = jnp.arange(tokens, dtype=jnp.int32)
    micro_of = token_of // block
    spread = (expert_of[:, None] == slot_of[None, :] // room).astype(bf)
    router_slots = dot(router_w, spread).astype(bf)
    local_routes = routes[0, 0].reshape(tokens, TOPK)
    named = jnp.any(local_routes[:, :, None] == expert_of[None, None, :], axis=1).astype(bf)
    earlier = (token_of[:, None] > token_of[None, :]) & (micro_of[:, None] == micro_of[None, :])
    slot_ids = dot(earlier.astype(bf), named) + (CAP * micro_of)[:, None].astype(f32)
    table = (dot(named, spread) > 0.5) & (
        dot(slot_ids.astype(bf), spread).astype(jnp.int32) == (slot_of % room)[None, :]
    )
    pick = table.astype(bf)
    info = jnp.stack([position % ring, position // ring]).astype(jnp.int32)

    def gate_values(normed_two):
        logits = jnp.where(table, dot(normed_two, router_slots), masked_score)
        weights = jnp.exp(logits - jnp.max(logits, axis=-1, keepdims=True))
        weights = jnp.where(table, weights, 0.0)
        return weights / jnp.sum(weights, axis=-1, keepdims=True)

    def high_low(value):
        high = value.astype(bf)
        return high, (value - high.astype(f32)).astype(bf)

    def to_experts(rows):
        return (
            exchange(rows.reshape(shards, local_experts, room, width))
            .transpose(1, 0, 2, 3)
            .reshape(local_experts, shards * room, width)
        )

    def from_experts(rows):
        return exchange(
            rows.reshape(local_experts, shards, room, width).transpose(1, 0, 2, 3)
        ).reshape(slots, width)

    def moved(p, steps):
        return (p // ring + steps) % heads * ring + p % ring

    def shift_x(value, steps):
        return lax.ppermute(value, "shard", [(p, moved(p, steps)) for p in range(shards)])

    def next_ring(value):
        return jnp.stack(
            [
                lax.ppermute(
                    value,
                    ("section", "shard"),
                    [(p, shards + moved(p, steps)) for p in range(shards)],
                )
                for steps in range(heads)
            ]
        )

    def sum_over_x(rows):
        parts = rows.reshape(heads, tokens, width)
        away = [shift_x(parts[k].astype(bf), -k).astype(f32) for k in range(1, heads)]
        return sum(away, parts[0])

    def ring_rows(rows):
        return jnp.concatenate([rows] + [shift_x(rows, k) for k in range(1, heads)], axis=0)

    def shared_weights(gathered):
        gate_up = gathered[:, :, : 2 * shared_width]
        down = gathered[:, :, 2 * shared_width :].reshape(shards, down_half, width)
        return (
            ordered(gate_up, twin(gate_up), 1).reshape(width, 2 * shared_width),
            ordered(down, twin(down), 1).reshape(shards * down_rows, width),
        )

    def forward(ring_b, shared_pair):
        layer_b = ring_b[0]
        layer_in = layer_b.astype(f32)
        ring_in = ring_b.reshape(heads * tokens, width).astype(f32)
        ring_one = (ring_in * inverse_rms(ring_in) * gain_one).astype(bf)
        qkv = dot(ring_one, qkv_w).astype(bf)
        cache = exchange(copies(qkv[:, group_width:], ring), zy_groups)
        qkv = qkv.reshape(heads, micros, block, part_width)
        attended, logs = attention_forward(info, qkv, cache)
        attended_rows = attended.reshape(heads * tokens, group_width)
        hidden = layer_in + sum_over_x(dot(attended_rows, output_w))
        if shared_pair is None:
            arrived, hidden = lax.optimization_barrier((gathered, hidden))
            shared_pair = shared_weights(arrived)
        gate_up_w, down_w = shared_pair
        normed_two = (hidden * inverse_rms(hidden) * gain_two).astype(bf)
        gates = gate_values(normed_two)
        expert_in = to_experts(dot_tn(pick, normed_two).astype(bf))
        gate_pre = wide_einsum("erd,edf->erf", expert_in, expert_g)
        up_pre = wide_einsum("erd,edf->erf", expert_in, expert_u)
        activated = (silu_parts(gate_pre)[0] * up_pre).astype(bf)
        returned = from_experts(wide_einsum("erf,efd->erd", activated, expert_d).astype(bf))
        high, low = high_low(gates)
        routed = dot(high, returned) + dot(low, returned)
        shared_gate_pre, shared_up_pre = halves(dot(normed_two, gate_up_w))
        shared_act = (silu_parts(shared_gate_pre)[0] * shared_up_pre).astype(bf)
        beside = lax.optimization_barrier(hidden + dot(shared_act, down_w))
        output_b = (beside + routed).astype(bf)
        return dict(
            layer_b=layer_b,
            ring_one=ring_one,
            qkv=qkv,
            cache=cache,
            attended=attended,
            logs=logs,
            hidden=hidden,
            normed_two=normed_two,
            gates=gates,
            expert_in=expert_in,
            gate_pre=gate_pre,
            up_pre=up_pre,
            activated=activated,
            returned=returned,
            shared_gate_pre=shared_gate_pre,
            shared_up_pre=shared_up_pre,
            shared_act=shared_act,
            output_b=output_b,
            shared_pair=shared_pair,
        )

    def ffn_backward(kept, upstream_b):
        upstream = upstream_b.astype(f32)
        gates, hidden = kept["gates"], kept["hidden"]
        gate_up_w, down_w = kept["shared_pair"]
        high, low = high_low(gates)
        outgoing = dot_tn(high, upstream_b) + dot_tn(low, upstream_b)
        expert_grad = to_experts(outgoing.astype(bf))
        act_silu, act_slope = silu_parts(kept["gate_pre"])
        act_grad = wide_einsum("erd,efd->erf", expert_grad, expert_d)
        gate_pre_grad = (act_grad * kept["up_pre"] * act_slope).astype(bf)
        up_pre_grad = (act_grad * act_silu).astype(bf)
        expert_in_grad = (
            wide_einsum("erf,edf->erd", gate_pre_grad, expert_g)
            + wide_einsum("erf,edf->erd", up_pre_grad, expert_u)
        ).astype(bf)
        returned_grad = from_experts(expert_in_grad)
        shared_act_grad = dot_nt(upstream_b, down_w)
        shared_silu, shared_slope = silu_parts(kept["shared_gate_pre"])
        shared_gate_grad = (shared_act_grad * kept["shared_up_pre"] * shared_slope).astype(bf)
        shared_up_grad = (shared_act_grad * shared_silu).astype(bf)
        normed_two_grad = dot_nt(
            jnp.concatenate([shared_gate_grad, shared_up_grad], axis=1), gate_up_w
        )
        gate_grad = dot_nt(upstream_b, kept["returned"])
        picked_grad = gates * (gate_grad - jnp.sum(gates * gate_grad, axis=1, keepdims=True))
        picked_b = picked_grad.astype(bf)
        normed_two_grad = normed_two_grad + dot_nt(picked_b, router_slots)
        normed_two_grad = lax.optimization_barrier(normed_two_grad)
        normed_two_grad = normed_two_grad + dot(pick, returned_grad)
        logit_grad = dot_nt(picked_b, spread).astype(bf)
        hidden_norm_grad, gain_two_grad = norm_back(hidden, gain_two, normed_two_grad)
        return dict(
            hidden_grad=upstream + hidden_norm_grad,
            upstream_b=upstream_b,
            expert_grad=expert_grad,
            gate_pre_grad=gate_pre_grad,
            up_pre_grad=up_pre_grad,
            shared_gate_grad=shared_gate_grad,
            shared_up_grad=shared_up_grad,
            logit_grad=logit_grad,
            gain_two_grad=gain_two_grad,
        )

    def attention_back(kept, grads):
        ring_hidden = ring_rows(grads["hidden_grad"].astype(bf))
        out_grad = dot_nt(ring_hidden, output_w).astype(bf)
        results = attention_backward(
            info,
            kept["qkv"],
            out_grad.reshape(heads, micros, block, group_width),
            kept["attended"],
            kept["logs"],
            kept["cache"],
        )
        query_grad = results[0].reshape(heads * tokens, group_width)
        query_part = lax.optimization_barrier(dot_nt(query_grad, qkv_w[:, :group_width]))
        pair_grad = jnp.sum(exchange(results[1], zy_groups).astype(f32), axis=0).astype(bf)
        qkv_grad = jnp.concatenate([query_grad, pair_grad], axis=1)
        normed_one_grad = sum_over_x(query_part + dot_nt(pair_grad, qkv_w[:, group_width:]))
        in_norm_grad, gain_one_grad = norm_back(
            kept["layer_b"].astype(f32), gain_one, normed_one_grad
        )
        return dict(
            grads,
            ring_hidden=ring_hidden,
            qkv_grad=qkv_grad,
            gain_one_grad=gain_one_grad,
            layer_grad=(grads["hidden_grad"] + in_norm_grad).astype(bf),
        )

    own_rows = inputs[0].reshape(tokens, width)
    ring_inputs = jnp.stack([own_rows] + [shift_x(own_rows, k) for k in range(1, heads)])
    first = forward(ring_inputs, None)
    second = forward(next_ring(first["output_b"]), first["shared_pair"])
    second_back = ffn_backward(second, cotangent[0].reshape(tokens, width))
    second_back = attention_back(second, second_back)
    received = lax.ppermute(second_back["layer_grad"], "section", [(1, 0)])
    first_back = attention_back(first, ffn_backward(first, received))

    def live(name, stores):
        return jnp.where(is_first, stores[0][name], stores[1][name])

    kept = {name: live(name, (first, second)) for name in KEPT}
    back = {name: live(name, (first_back, second_back)) for name in BACK}

    expert_parts = [
        wide_einsum("erd,erf->edf", kept["expert_in"], back["gate_pre_grad"]),
        wide_einsum("erd,erf->edf", kept["expert_in"], back["up_pre_grad"]),
        wide_einsum("erf,erd->efd", kept["activated"], back["expert_grad"]),
    ]
    expert_parts = [part.astype(bf) for part in expert_parts]
    expert_others = [twin(part) for part in expert_parts]

    def both(value):
        return jnp.concatenate([value, twin(value)], axis=0)

    def both_halves(low_half, high_half):
        own, other = mine_of(low_half, high_half), mine_of(high_half, low_half)
        return jnp.concatenate([own, twin(other)], axis=0)

    normed_two = kept["normed_two"]
    grad_gate_up = dot_tn(
        both(normed_two), both_halves(back["shared_gate_grad"], back["shared_up_grad"])
    )
    grad_down = dot_tn(both(kept["shared_act"]), both_halves(*halves(back["upstream_b"])))


    def shift_z(value, steps):
        pairs = [(p, p // ring * ring + (p % ring + 2 * steps) % ring) for p in range(shards)]
        return lax.ppermute(value, "shard", pairs)

    def shift_y(value, steps):
        return lax.ppermute(value, "shard", [(p, p ^ 1) for p in range(shards)])

    along = dict(
        x=(shift_x, position // ring), z=(shift_z, position % ring // 2), y=(shift_y, position % 2)
    )

    def reduced(value, name, axis, held_as=bf):
        shift, here = along[name]
        count = value.shape[axis]

        def piece(steps):
            return lax.dynamic_index_in_dim(value, (here + steps) % count, axis, keepdims=False)

        total = piece(0).astype(f32)
        for steps in range(1, count):
            total = total + shift(piece(steps), steps).astype(f32)
        return total.astype(held_as)

    grad_out = dot_tn(
        kept["attended"].reshape(heads * tokens, group_width),
        back["ring_hidden"],
    )
    grad_gate_up, grad_down, grad_out, last_grad, *expert_others = lax.optimization_barrier(
        (
            grad_gate_up.astype(bf),
            grad_down.astype(bf),
            grad_out.astype(bf),
            first_back["layer_grad"],
            *expert_others,
        )
    )
    expert_grads = [
        part.astype(f32) + other.astype(f32) for part, other in zip(expert_parts, expert_others)
    ]
    pieces = grad_gate_up.reshape(heads, ring // 2, 2, rows_per, shared_width)
    share_gate_up = reduced(reduced(reduced(pieces, "x", 0), "z", 0), "y", 0, f32)
    pieces = grad_down.reshape(heads, ring // 2, 2, down_rows, width // 2)
    share_down = reduced(reduced(reduced(pieces, "z", 1), "x", 0), "y", 0, f32)

    share_out = jnp.sum(
        exchange(grad_out.reshape(ring, rows_per, width), zy_groups).astype(f32), axis=0
    )
    grad_qkv = dot_tn(kept["ring_one"], back["qkv_grad"])
    grad_router = dot_tn(normed_two, back["logit_grad"])
    gain_sums = jnp.stack([back["gain_one_grad"], back["gain_two_grad"]])
    grad_tail = jnp.concatenate(
        [grad_router, gain_sums.T, jnp.zeros((width, 128 - experts - 2), f32)], axis=1
    )
    grad_qkv = jnp.concatenate([grad_qkv, grad_tail], axis=1)
    pieces = exchange(
        grad_qkv.astype(bf).reshape(shards, rows_per, part_width + 128)
    ).astype(f32)
    share_qkv = jnp.sum(
        pieces[:, :, :part_width].reshape(heads, ring, rows_per, part_width), axis=1
    )
    share_qkv = share_qkv.transpose(1, 0, 2)
    share_tail = jnp.sum(pieces[:, :, part_width:], axis=0)

    def total(share):
        return share + twin(share)

    out_total, qkv_total, tail_total = total(share_out), total(share_qkv), total(share_tail)
    other_gate_up = twin(share_gate_up)
    down_total = ordered(share_down, twin(share_down), 1)

    token_shape = (1, 1, micros, block, width)
    layer_grad = jnp.where(is_first, last_grad, second_back["layer_grad"])
    return (
        jnp.where(is_first, first["output_b"], second["output_b"]).reshape(token_shape),
        layer_grad.reshape(token_shape),
        tail_total[:, experts][None],
        qkv_total[:, :, :group_width].reshape(1, rows_per, head_width),
        qkv_total[:, :, group_width : group_width + HD].reshape(1, rows_per, key_width),
        qkv_total[:, :, group_width + HD :].reshape(1, rows_per, key_width),
        out_total[None],
        tail_total[:, experts + 1][None],
        tail_total[:, :experts][None],
        mine_of(share_gate_up, other_gate_up)[None],
        mine_of(other_gate_up, share_gate_up)[None],
        down_total[None],
        expert_grads[0][None],
        expert_grads[1][None],
        expert_grads[2][None],
    )


def solution(mesh):
    rows = P("section", "shard", None)
    vector = P("section", "shard")
    expert = P("section", "shard", None, None)
    tokens = P("dp", None, "shard", None)
    section_tokens = P("section", "dp", None, "shard", None)
    weights = (vector, rows, rows, rows, rows, vector, rows, rows, rows, rows) + (expert,) * 3
    return jax.shard_map(
        body,
        mesh=mesh,
        in_specs=(tokens, tokens, section_tokens) + weights,
        out_specs=(section_tokens, section_tokens) + weights,
        check_vma=False,
    )
```

```python
import functools

import jax
import jax.numpy as jnp
from jax import lax
from jax.experimental import pallas as pl
from jax.experimental.pallas import tpu as pltpu
from jax.sharding import PartitionSpec as P

H = 12
KVH = 4
HD = 128
GROUP = H // KVH
TOPK = 6
CAP = 8

epsilon = 1e-05
masked_score = -1e30
scaling = HD ** (-0.5)
log2_scale = scaling * 1.4426950408889634
bf = jnp.bfloat16
f32 = jnp.float32
VMEM_LIMIT = 32 * 1024 * 1024


def inverse_rms(rows):
    return lax.rsqrt(jnp.mean(rows * rows, axis=-1, keepdims=True) + epsilon)


def norm_back(layer_in, gain, upstream):
    inverse = inverse_rms(layer_in)
    unit_rows = layer_in * inverse
    gain_grad = jnp.sum(upstream * unit_rows, axis=0)
    scaled = upstream * gain
    in_grad = inverse * (scaled - unit_rows * jnp.mean(scaled * unit_rows, axis=-1, keepdims=True))
    return (in_grad, gain_grad)


def silu_parts(argument):
    sigmoid = jax.nn.sigmoid(argument)
    return argument * sigmoid, sigmoid * (1.0 + argument * (1.0 - sigmoid))


def dot(left_side, right_side):
    return jnp.dot(left_side, right_side, preferred_element_type=f32)


def dot_nt(left_side, right_side):
    return lax.dot_general(
        left_side, right_side, (((1,), (1,)), ((), ())), preferred_element_type=f32
    )


def dot_tn(left_side, right_side):
    return lax.dot_general(
        left_side, right_side, (((0,), (0,)), ((), ())), preferred_element_type=f32
    )


def wide_einsum(formula, left_side, right_side):
    return jnp.einsum(formula, left_side, right_side, preferred_element_type=f32)


def arrival(info_ref, parts, part):
    return lax.rem(info_ref[2] + parts - part, parts)


def stacked_heads(ref, at):
    return jnp.concatenate([ref[at, :, g * HD : (g + 1) * HD] for g in range(GROUP)], axis=0)


def store_heads(ref, at, rows):
    block = ref.shape[1]
    for g in range(GROUP):
        ref[at, :, g * HD : (g + 1) * HD] = rows[g * block : (g + 1) * block]


def cached(ref, span, column):
    rows = ref[:, span, column : column + HD]
    return rows.reshape(rows.shape[0] * rows.shape[1], HD)


def block_span(at, block):
    return pl.ds(pl.multiple_of(at * block, block), block)


def diagonal_mask(rows, chunk, block, zy):
    key_at = lax.broadcasted_iota(jnp.int32, (rows, chunk), 1)
    row_at = lax.broadcasted_iota(jnp.int32, (rows, chunk), 0)
    return key_at <= zy * block + lax.rem(row_at, block)


def attention_forward_kernel(has_prev, info_ref, q_ref, *refs):
    prev_ref = refs[0] if has_prev else None
    cur_ref, o_ref, log_ref = refs[-3:]
    parts, block, _ = q_ref.shape
    rows = GROUP * block
    mask = diagonal_mask(rows, cur_ref.shape[0] * block, block, info_ref[0])
    spans = [block_span(arrival(info_ref, parts, part), block) for part in range(parts)]
    for part in range(parts):
        at = arrival(info_ref, parts, part)
        queries = stacked_heads(q_ref, at)
        pieces = [(prev_ref, slice(None))] if has_prev else []
        pieces += [(cur_ref, spans[p]) for p in range(part + 1)]
        scores = [dot_nt(queries, cached(ref, span, 0)) for ref, span in pieces]
        if has_prev:
            scores[0] = scores[0] + jnp.where(info_ref[1] > 0, 0.0, masked_score).astype(f32)
        scores[-1] = jnp.where(mask, scores[-1], masked_score)
        peak = functools.reduce(
            jnp.maximum, [jnp.max(s, axis=-1, keepdims=True) for s in scores]
        )
        peak = peak * log2_scale
        total = jnp.zeros((rows, 1), f32)
        mixed = jnp.zeros((rows, HD), f32)
        for s, (ref, span) in zip(scores, pieces):
            probs = jnp.exp2(s * log2_scale - peak)
            total = total + jnp.sum(probs, axis=-1, keepdims=True)
            mixed = mixed + dot(probs.astype(bf), cached(ref, span, HD))
        store_heads(o_ref, at, (mixed / total).astype(bf))
        log_ref[at] = jnp.broadcast_to(peak + jnp.log2(total), (rows, HD))


def attention_backward_kernel(has_prev, has_carry, info_ref, q_ref, do_ref, o_ref, log_ref, *refs):
    refs = list(refs)
    sum_ref = refs.pop()
    carry_ref = refs.pop(0) if has_carry else None
    prev_ref = refs.pop(0) if has_prev else None
    cur_ref, dq_ref, dcur_ref = refs[:3]
    dprev_ref = refs[3] if has_prev else None
    sum_ref[...] = carry_ref[...] if has_carry else jnp.zeros(sum_ref.shape, f32)
    if has_prev:
        dprev_ref[...] = jnp.zeros(dprev_ref.shape, f32)
    parts, block, _ = q_ref.shape
    ring = cur_ref.shape[0]
    rows = GROUP * block
    mask = diagonal_mask(rows, ring * block, block, info_ref[0])
    spans = [block_span(arrival(info_ref, parts, part), block) for part in range(parts)]
    for part in range(parts):
        at = arrival(info_ref, parts, part)
        queries = stacked_heads(q_ref, at)
        out_grad = stacked_heads(do_ref, at)
        out = stacked_heads(o_ref, at)
        inner = jnp.sum(out_grad.astype(f32) * out.astype(f32), axis=-1, keepdims=True)
        log_total = log_ref[at][:, :1]
        query_grad = jnp.zeros((rows, HD), f32)
        pieces = []
        if has_prev:
            log_prev = log_total + jnp.where(info_ref[1] > 0, 0.0, -masked_score).astype(f32)
            pieces = [
                (prev_ref, dprev_ref, slice(p * block, (p + 1) * block), log_prev, False)
                for p in range(parts)
            ]
        pieces += [(cur_ref, sum_ref, spans[p], log_total, p == part) for p in range(part + 1)]
        for ref, grad_ref, span, log_row, on_diagonal in pieces:
            keys = cached(ref, span, 0)
            probs = jnp.exp2(dot_nt(queries, keys) * log2_scale - log_row)
            if on_diagonal:
                probs = jnp.where(mask, probs, 0.0)
            probs_grad = dot_nt(out_grad, cached(ref, span, HD))
            score_grad = (probs * (probs_grad - inner)).astype(bf)
            query_grad = query_grad + dot(score_grad, keys)
            key_grad = dot_tn(score_grad, queries) * scaling
            value_grad = dot_tn(probs.astype(bf), out_grad)
            grad_ref[:, span, :HD] += key_grad.reshape(ring, block, HD)
            grad_ref[:, span, HD:] += value_grad.reshape(ring, block, HD)
        store_heads(dq_ref, at, (query_grad * scaling).astype(bf))
    dcur_ref[...] = sum_ref[...].astype(bf)


def attention_call(kernel, factor, out_shape, scratch, info, queries, *rest):
    parts, block, _ = queries.shape
    rows = parts * GROUP * block
    keys = sum(ref.shape[0] * ref.shape[1] for ref in rest if ref.shape == rest[-1].shape)
    in_vmem = pl.BlockSpec(memory_space=pltpu.VMEM)
    return pl.pallas_call(
        kernel,
        out_shape=out_shape,
        in_specs=[pl.BlockSpec(memory_space=pltpu.SMEM)] + [in_vmem] * (1 + len(rest)),
        out_specs=(in_vmem,) * len(out_shape),
        scratch_shapes=scratch,
        compiler_params=pltpu.CompilerParams(vmem_limit_bytes=VMEM_LIMIT),
        cost_estimate=pl.CostEstimate(
            flops=factor * rows * keys * HD,
            bytes_accessed=factor * (keys + rows) * HD,
            transcendentals=rows * keys // 2,
        ),
    )(info, queries, *rest)


def attention_forward(info, qkv, prev, cur):
    parts, block, _ = qkv.shape
    shapes = (
        jax.ShapeDtypeStruct((parts, block, GROUP * HD), bf),
        jax.ShapeDtypeStruct((parts, GROUP * block, HD), f32),
    )
    caches = (cur,) if prev is None else (prev, cur)
    kernel = functools.partial(attention_forward_kernel, prev is not None)
    return attention_call(kernel, 2, shapes, [], info, qkv, *caches)


def attention_backward(info, qkv, out_grad, out, logs, carry, prev, cur):
    shapes = (jax.ShapeDtypeStruct(out.shape, bf), jax.ShapeDtypeStruct(cur.shape, bf))
    if prev is not None:
        shapes += (jax.ShapeDtypeStruct(cur.shape, f32),)
    extra = tuple(value for value in (carry, prev) if value is not None)
    kernel = functools.partial(attention_backward_kernel, prev is not None, carry is not None)
    scratch = [pltpu.VMEM(cur.shape, f32)]
    return attention_call(
        kernel, 5, shapes, scratch, info, qkv, out_grad, out, logs, *extra, cur
    )


def body(
    inputs,
    cotangent,
    routes,
    norm_attn,
    w_query,
    w_key,
    w_value,
    w_output,
    norm_ffn,
    w_router,
    shared_gate,
    shared_up,
    shared_down,
    expert_gate,
    expert_up,
    expert_down,
):
    micros, block, width = inputs.shape[1:]
    shards = lax.axis_size("shard")
    section = lax.axis_index("section")
    core = lax.axis_index("dp")
    position = lax.axis_index("shard")
    heads = KVH
    ring = shards // heads
    local_experts = expert_gate.shape[1]
    experts = local_experts * shards
    slots = experts * CAP
    rows_per = w_query.shape[1]
    half_rows = rows_per // 2
    group_width = GROUP * HD
    head_width = H * HD
    key_width = KVH * HD
    part_width = group_width + 2 * HD
    shared_width = shared_gate.shape[2]
    down_rows = shared_down.shape[1]
    is_first = section == 0
    low_core = core == 0
    zy_groups = [[x * ring + zy for zy in range(ring)] for x in range(heads)]

    def exchange(value, groups=None):
        return lax.all_to_all(
            value, "shard", split_axis=0, concat_axis=0, tiled=True, axis_index_groups=groups
        )

    def copies(value, count):
        return jnp.broadcast_to(value[None], (count,) + value.shape)

    def twin(value):
        return lax.ppermute(value, "dp", [(0, 1), (1, 0)])

    def mine_of(low_half, high_half):
        return jnp.where(low_core, low_half, high_half)

    def ordered(own, other, axis):
        low_half, high_half = mine_of(own, other), mine_of(other, own)
        return jnp.concatenate([low_half, high_half], axis=axis)

    def ordered_by(in_order, own, other):
        return jnp.stack([jnp.where(in_order, own, other), jnp.where(in_order, other, own)])

    def halves(value):
        half = value.shape[-1] // 2
        return value[..., :half], value[..., half:]

    def my_rows(value):
        return mine_of(value[..., :half_rows, :], value[..., half_rows:, :])

    tail = jnp.concatenate(
        [
            w_router[0],
            norm_attn[0][:, None],
            norm_ffn[0][:, None],
            jnp.zeros((rows_per, 128 - experts - 2), bf),
        ],
        axis=1,
    )
    by_head = jnp.concatenate(
        [
            w_query[0].reshape(rows_per, heads, group_width),
            w_key[0].reshape(rows_per, heads, HD),
            w_value[0].reshape(rows_per, heads, HD),
            jnp.broadcast_to(tail[:, None], (rows_per, heads, 128)),
        ],
        axis=2,
    ).transpose(1, 0, 2)
    by_head = my_rows(by_head)
    by_head = jnp.broadcast_to(
        by_head[:, None], (heads, ring, half_rows, part_width + 128)
    ).reshape(shards, half_rows, part_width + 128)
    down_half = down_rows // 2
    down_flat = (half_rows, down_half * width // half_rows)
    packed = jnp.concatenate(
        [
            my_rows(jnp.concatenate([shared_gate[0], shared_up[0]], axis=1)),
            mine_of(shared_down[0][:down_half], shared_down[0][down_half:]).reshape(down_flat),
        ],
        axis=1,
    )
    by_head, packed = lax.optimization_barrier((by_head, packed))
    gathered = lax.all_gather(packed, "shard")
    own_part = exchange(by_head)
    out_rows = my_rows(w_output[0])
    out_rows = ordered_by(
        position % 2 == 0, out_rows, lax.ppermute(out_rows, "shard", [(p, p ^ 1) for p in range(shards)])
    )
    out_parts = [out_rows] + [
        lax.ppermute(
            out_rows,
            "shard",
            [(p, p // ring * ring + (p % ring - 2 * k) % ring) for p in range(shards)],
        )
        for k in range(1, ring // 2)
    ]
    own_part, *out_parts = lax.optimization_barrier((own_part, *out_parts))
    own_out = lax.dynamic_slice_in_dim(
        jnp.concatenate(out_parts + out_parts), ring - position % ring // 2 * 2, ring, axis=0
    )
    output_w = ordered(own_out, twin(own_out), 1).reshape(group_width, width)
    fetched = ordered(own_part, twin(own_part), 1).reshape(width, part_width + 128)
    qkv_w, tail = fetched[:, :part_width], fetched[:, part_width:]
    router_w = tail[:, :experts]
    gains = tail[:, experts : experts + 2].T.astype(f32)
    gain_one, gain_two = gains[0][None], gains[1][None]

    expert_g, expert_u, expert_d = expert_gate[0], expert_up[0], expert_down[0]
    slot_of = jnp.arange(slots, dtype=jnp.int32)
    expert_of = jnp.arange(experts, dtype=jnp.int32)
    row_of = jnp.arange(block, dtype=jnp.int32)
    spread = (expert_of[:, None] == slot_of[None, :] // CAP).astype(bf)
    router_slots = dot(router_w, spread).astype(bf)
    earlier = (row_of[:, None] > row_of[None, :]).astype(bf)

    def slot_table(route_rows):
        named = jnp.any(route_rows[:, :, None] == expert_of[None, None, :], axis=1).astype(bf)
        slot_ids = dot(earlier, named).astype(bf)
        return (dot(named, spread) > 0.5) & (
            dot(slot_ids, spread).astype(jnp.int32) == (slot_of % CAP)[None, :]
        )

    here = [position % ring, jnp.ones_like(position), position // ring]
    info_all = jnp.stack(here).astype(jnp.int32)
    info = jnp.stack([here[0], is_first.astype(here[0].dtype), here[2]]).astype(jnp.int32)

    def gate_values(normed_two, table):
        logits = jnp.where(table, dot(normed_two, router_slots), masked_score)
        weights = jnp.exp(logits - jnp.max(logits, axis=-1, keepdims=True))
        weights = jnp.where(table, weights, 0.0)
        return weights / jnp.sum(weights, axis=-1, keepdims=True)

    def high_low(value):
        high = value.astype(bf)
        return high, (value - high.astype(f32)).astype(bf)

    def to_experts(rows):
        return (
            exchange(rows.reshape(shards, local_experts, CAP, width))
            .transpose(1, 0, 2, 3)
            .reshape(local_experts, shards * CAP, width)
        )

    def from_experts(rows):
        return exchange(
            rows.reshape(local_experts, shards, CAP, width).transpose(1, 0, 2, 3)
        ).reshape(slots, width)

    def moved(p, steps):
        return (p // ring + steps) % heads * ring + p % ring

    def shift_x(value, steps):
        return lax.ppermute(value, "shard", [(p, moved(p, steps)) for p in range(shards)])

    def next_ring(value):
        return jnp.stack(
            [
                lax.ppermute(
                    value,
                    ("section", "shard"),
                    [(p, shards + moved(p, steps)) for p in range(shards)],
                )
                for steps in range(heads)
            ]
        )

    def sum_over_x(rows):
        parts = rows.reshape(heads, block, width)
        away = [shift_x(parts[k].astype(bf), -k).astype(f32) for k in range(1, heads)]
        return sum(away, parts[0])

    def ring_rows(rows):
        return jnp.concatenate([rows] + [shift_x(rows, k) for k in range(1, heads)], axis=0)

    ring_inputs = [
        jnp.stack([inputs[0, m]] + [shift_x(inputs[0, m], k) for k in range(1, heads)])
        for m in range(micros)
    ]

    def shared_weights(gathered):
        gate_up = gathered[:, :, : 2 * shared_width]
        down = gathered[:, :, 2 * shared_width :].reshape(shards, down_half, width)
        return (
            ordered(gate_up, twin(gate_up), 1).reshape(width, 2 * shared_width),
            ordered(down, twin(down), 1).reshape(shards * down_rows, width),
        )

    def forward(moment, received, previous, shared_pair):
        first_micro = min(moment, micros - 1)
        second_micro = max(moment - 1, 0)
        ring_b = jnp.where(is_first, ring_inputs[first_micro], received)
        layer_b = ring_b[0]
        table = slot_table(
            jnp.where(is_first, routes[0, 0, first_micro], routes[0, 0, second_micro])
        )
        pick = table.astype(bf)
        if moment == micros:
            last_rows = cotangent[0, micros - 1]
            last_rows = jnp.where(is_first, jnp.zeros_like(last_rows), last_rows)
            cotangent_rows = dot_tn(pick, last_rows).astype(bf)
        layer_in = layer_b.astype(f32)
        ring_in = ring_b.reshape(heads * block, width).astype(f32)
        ring_one = (ring_in * inverse_rms(ring_in) * gain_one).astype(bf)
        qkv = dot(ring_one, qkv_w).astype(bf)
        cache = exchange(copies(qkv[:, group_width:], ring), zy_groups)
        qkv = qkv.reshape(heads, block, part_width)
        attn_info = info if moment == 1 else info_all
        early = None
        if moment == micros:
            sent, cache = lax.optimization_barrier((cotangent_rows, cache))
            early = to_experts(sent)
        attended, logs = attention_forward(attn_info, qkv, previous, cache)
        attended_rows = attended.reshape(heads * block, group_width)
        hidden = layer_in + sum_over_x(dot(attended_rows, output_w))
        if shared_pair is None:
            arrived, hidden = lax.optimization_barrier((gathered, hidden))
            shared_pair = shared_weights(arrived)
        gate_up_w, down_w = shared_pair
        normed_two = (hidden * inverse_rms(hidden) * gain_two).astype(bf)
        gates = gate_values(normed_two, table)
        expert_in = to_experts(dot_tn(pick, normed_two).astype(bf))
        gate_pre = wide_einsum("erd,edf->erf", expert_in, expert_g)
        up_pre = wide_einsum("erd,edf->erf", expert_in, expert_u)
        activated = (silu_parts(gate_pre)[0] * up_pre).astype(bf)
        returned = from_experts(wide_einsum("erf,efd->erd", activated, expert_d).astype(bf))
        high, low = high_low(gates)
        routed = dot(high, returned) + dot(low, returned)
        shared_gate_pre, shared_up_pre = halves(dot(normed_two, gate_up_w))
        shared_act = (silu_parts(shared_gate_pre)[0] * shared_up_pre).astype(bf)
        beside = lax.optimization_barrier(hidden + dot(shared_act, down_w))
        output_b = (beside + routed).astype(bf)
        return dict(
            layer_b=layer_b,
            pick=pick,
            ring_one=ring_one,
            qkv=qkv,
            cache=cache,
            previous=previous,
            info=attn_info,
            attended=attended,
            logs=logs,
            hidden=hidden,
            normed_two=normed_two,
            gates=gates,
            expert_in=expert_in,
            gate_pre=gate_pre,
            up_pre=up_pre,
            activated=activated,
            returned=returned,
            shared_gate_pre=shared_gate_pre,
            shared_up_pre=shared_up_pre,
            shared_act=shared_act,
            output_b=output_b,
            shared_pair=shared_pair,
            expert_grad=early,
        )

    def ffn_backward(kept, upstream_b):
        upstream = upstream_b.astype(f32)
        gates, hidden = kept["gates"], kept["hidden"]
        gate_up_w, down_w = kept["shared_pair"]
        expert_grad = kept["expert_grad"]
        if expert_grad is None:
            expert_grad = to_experts(dot_tn(kept["pick"], upstream_b).astype(bf))
        act_silu, act_slope = silu_parts(kept["gate_pre"])
        act_grad = wide_einsum("erd,efd->erf", expert_grad, expert_d)
        gate_pre_grad = (act_grad * kept["up_pre"] * act_slope).astype(bf)
        up_pre_grad = (act_grad * act_silu).astype(bf)
        expert_in_grad = (
            wide_einsum("erf,edf->erd", gate_pre_grad, expert_g)
            + wide_einsum("erf,edf->erd", up_pre_grad, expert_u)
        ).astype(bf)
        returned_grad = from_experts(expert_in_grad)
        shared_act_grad = dot_nt(upstream_b, down_w)
        shared_silu, shared_slope = silu_parts(kept["shared_gate_pre"])
        shared_gate_grad = (shared_act_grad * kept["shared_up_pre"] * shared_slope).astype(bf)
        shared_up_grad = (shared_act_grad * shared_silu).astype(bf)
        normed_two_grad = dot_nt(
            jnp.concatenate([shared_gate_grad, shared_up_grad], axis=1), gate_up_w
        )
        gate_grad = dot_nt(upstream_b, kept["returned"])
        picked_grad = gates * (gate_grad - jnp.sum(gates * gate_grad, axis=1, keepdims=True))
        picked_b = picked_grad.astype(bf)
        normed_two_grad = normed_two_grad + dot_nt(picked_b, router_slots)
        normed_two_grad = lax.optimization_barrier(normed_two_grad)
        high, low = high_low(gates)
        normed_two_grad = normed_two_grad + (dot(high, returned_grad) + dot(low, returned_grad))
        logit_grad = dot_nt(picked_b, spread).astype(bf)
        hidden_norm_grad, gain_two_grad = norm_back(hidden, gain_two, normed_two_grad)
        return dict(
            hidden_grad=upstream + hidden_norm_grad,
            upstream_b=upstream_b,
            expert_grad=expert_grad,
            gate_pre_grad=gate_pre_grad,
            up_pre_grad=up_pre_grad,
            shared_gate_grad=shared_gate_grad,
            shared_up_grad=shared_up_grad,
            logit_grad=logit_grad,
            gain_two_grad=gain_two_grad,
        )

    def attention_back(kept, grads, carried):
        ring_hidden = ring_rows(grads["hidden_grad"].astype(bf))
        if not sent_gates:
            flat, ring_hidden = lax.optimization_barrier((gate_rows, ring_hidden))
            sent_gates.append(exchange(flat))
        out_grad = dot_nt(ring_hidden, output_w).astype(bf)
        results = attention_backward(
            kept["info"],
            kept["qkv"],
            out_grad.reshape(heads, block, group_width),
            kept["attended"],
            kept["logs"],
            carried,
            kept["previous"],
            kept["cache"],
        )
        carried = results[2] if len(results) > 2 else None
        query_grad = results[0].reshape(heads * block, group_width)
        query_part = lax.optimization_barrier(dot_nt(query_grad, qkv_w[:, :group_width]))
        pair_grad = jnp.sum(exchange(results[1], zy_groups).astype(f32), axis=0).astype(bf)
        qkv_grad = jnp.concatenate([query_grad, pair_grad], axis=1)
        normed_one_grad = sum_over_x(query_part + dot_nt(pair_grad, qkv_w[:, group_width:]))
        in_norm_grad, gain_one_grad = norm_back(
            kept["layer_b"].astype(f32), gain_one, normed_one_grad
        )
        grads = dict(
            grads,
            ring_hidden=ring_hidden,
            qkv_grad=qkv_grad,
            gain_one_grad=gain_one_grad,
            layer_grad=(grads["hidden_grad"] + in_norm_grad).astype(bf),
        )
        return grads, carried

    nothing = jnp.zeros((block, width), bf)
    saved = []
    received, previous, shared_pair = jnp.zeros((heads, block, width), bf), None, None
    for moment in range(micros + 1):
        kept = forward(moment, received, previous, shared_pair)
        shared_pair = kept["shared_pair"]
        saved.append(kept)
        previous = kept["cache"]
        if moment < micros:
            received = next_ring(kept["output_b"])
    gate_rows = jnp.stack([jnp.sum(kept["gates"], axis=0) for kept in saved])
    gate_rows = gate_rows.reshape(micros + 1, shards, local_experts * CAP).transpose(1, 0, 2)
    sent_gates = []
    backs = [None] * (micros + 1)
    received, carried = nothing, None
    for source in range(micros, -1, -1):
        own = cotangent[0, source - 1] if source > 0 else nothing
        upstream_b = jnp.where(is_first, received, own)
        grads = ffn_backward(saved[source], upstream_b)
        backs[source], carried = attention_back(saved[source], grads, carried)
        if source > 0:
            received = lax.ppermute(backs[source]["layer_grad"], "section", [(1, 0)])

    def live(name, store, axis):
        ends = jnp.where(is_first, store[0][name], store[micros][name])
        return jnp.concatenate([ends, store[1][name]], axis=axis)

    def kept_rows(name, axis=0):
        return live(name, saved, axis)

    def back_rows(name, axis=0):
        return live(name, backs, axis)

    expert_gates = sent_gates[0].reshape(shards, micros + 1, local_experts, CAP)
    expert_gates = expert_gates.transpose(1, 2, 0, 3).reshape(
        micros + 1, local_experts, shards * CAP, 1
    )
    for source, grads in enumerate(backs):
        for name in ("expert_grad", "gate_pre_grad", "up_pre_grad"):
            grads[name] = (grads[name].astype(f32) * expert_gates[source]).astype(bf)

    expert_parts = [
        wide_einsum("erd,erf->edf", kept_rows("expert_in", 1), back_rows("gate_pre_grad", 1)),
        wide_einsum("erd,erf->edf", kept_rows("expert_in", 1), back_rows("up_pre_grad", 1)),
        wide_einsum("erf,erd->efd", kept_rows("activated", 1), back_rows("expert_grad", 1)),
    ]
    expert_parts = [part.astype(bf) for part in expert_parts]
    expert_others = [twin(part) for part in expert_parts]

    def both(value):
        return jnp.concatenate([value, twin(value)], axis=0)

    def both_halves(low_half, high_half):
        own, other = mine_of(low_half, high_half), mine_of(high_half, low_half)
        return jnp.concatenate([own, twin(other)], axis=0)

    normed_two = kept_rows("normed_two")
    grad_gate_up = dot_tn(
        both(normed_two), both_halves(back_rows("shared_gate_grad"), back_rows("shared_up_grad"))
    )
    grad_down = dot_tn(both(kept_rows("shared_act")), both_halves(*halves(back_rows("upstream_b"))))


    def shift_z(value, steps):
        pairs = [(p, p // ring * ring + (p % ring + 2 * steps) % ring) for p in range(shards)]
        return lax.ppermute(value, "shard", pairs)

    def shift_y(value, steps):
        return lax.ppermute(value, "shard", [(p, p ^ 1) for p in range(shards)])

    along = dict(
        x=(shift_x, position // ring), z=(shift_z, position % ring // 2), y=(shift_y, position % 2)
    )

    def reduced(value, name, axis, held_as=bf):
        shift, here = along[name]
        count = value.shape[axis]

        def piece(steps):
            return lax.dynamic_index_in_dim(value, (here + steps) % count, axis, keepdims=False)

        total = piece(0).astype(f32)
        for steps in range(1, count):
            total = total + shift(piece(steps), steps).astype(f32)
        return total.astype(held_as)

    grad_out = dot_tn(
        kept_rows("attended").reshape(micros * heads * block, group_width),
        back_rows("ring_hidden"),
    )
    grad_gate_up, grad_down, grad_out, last_grad, *expert_others = lax.optimization_barrier(
        (
            grad_gate_up.astype(bf),
            grad_down.astype(bf),
            grad_out.astype(bf),
            backs[0]["layer_grad"],
            *expert_others,
        )
    )
    backs[0]["layer_grad"] = last_grad
    expert_grads = [
        part.astype(f32) + other.astype(f32) for part, other in zip(expert_parts, expert_others)
    ]
    pieces = grad_gate_up.reshape(heads, ring // 2, 2, rows_per, shared_width)
    share_gate_up = reduced(reduced(reduced(pieces, "x", 0), "z", 0), "y", 0, f32)
    pieces = grad_down.reshape(heads, ring // 2, 2, down_rows, width // 2)
    share_down = reduced(reduced(reduced(pieces, "z", 1), "x", 0), "y", 0, f32)

    share_out = jnp.sum(
        exchange(grad_out.reshape(ring, rows_per, width), zy_groups).astype(f32), axis=0
    )
    grad_qkv = dot_tn(kept_rows("ring_one"), back_rows("qkv_grad"))
    grad_router = dot_tn(normed_two, back_rows("logit_grad"))
    gain_sums = jnp.stack(
        [sum(grads[name] for grads in backs) for name in ("gain_one_grad", "gain_two_grad")]
    )
    grad_tail = jnp.concatenate(
        [grad_router, gain_sums.T, jnp.zeros((width, 128 - experts - 2), f32)], axis=1
    )
    grad_qkv = jnp.concatenate([grad_qkv, grad_tail], axis=1)
    pieces = exchange(
        grad_qkv.astype(bf).reshape(shards, rows_per, part_width + 128)
    ).astype(f32)
    share_qkv = jnp.sum(
        pieces[:, :, :part_width].reshape(heads, ring, rows_per, part_width), axis=1
    )
    share_qkv = share_qkv.transpose(1, 0, 2)
    share_tail = jnp.sum(pieces[:, :, part_width:], axis=0)

    def total(share):
        return share + twin(share)

    out_total, qkv_total, tail_total = total(share_out), total(share_qkv), total(share_tail)
    other_gate_up = twin(share_gate_up)
    down_total = ordered(share_down, twin(share_down), 1)

    def by_micro(store, name):
        return jnp.stack(
            [jnp.where(is_first, store[m][name], store[m + 1][name]) for m in range(micros)]
        )[None, None]

    return (
        by_micro(saved, "output_b"),
        by_micro(backs, "layer_grad"),
        tail_total[:, experts][None],
        qkv_total[:, :, :group_width].reshape(1, rows_per, head_width),
        qkv_total[:, :, group_width : group_width + HD].reshape(1, rows_per, key_width),
        qkv_total[:, :, group_width + HD :].reshape(1, rows_per, key_width),
        out_total[None],
        tail_total[:, experts + 1][None],
        tail_total[:, :experts][None],
        mine_of(share_gate_up, other_gate_up)[None],
        mine_of(other_gate_up, share_gate_up)[None],
        down_total[None],
        expert_grads[0][None],
        expert_grads[1][None],
        expert_grads[2][None],
    )


def solution(mesh):
    rows = P("section", "shard", None)
    vector = P("section", "shard")
    expert = P("section", "shard", None, None)
    tokens = P("dp", None, "shard", None)
    section_tokens = P("section", "dp", None, "shard", None)
    weights = (vector, rows, rows, rows, rows, vector, rows, rows, rows, rows) + (expert,) * 3
    return jax.shard_map(
        body,
        mesh=mesh,
        in_specs=(tokens, tokens, section_tokens) + weights,
        out_specs=(section_tokens, section_tokens) + weights,
        check_vma=False,
    )
```

```python
import functools

import jax
import jax.numpy as jnp
from jax import lax
from jax.experimental import pallas as pl
from jax.experimental.pallas import tpu as pltpu
from jax.sharding import PartitionSpec as P

H = 12
KVH = 4
HD = 128
GROUP = H // KVH
TOPK = 6
CAP = 8

epsilon = 1e-05
masked_score = -1e30
scaling = HD ** (-0.5)
log2_scale = scaling * 1.4426950408889634
bf = jnp.bfloat16
f32 = jnp.float32
VMEM_LIMIT = 32 * 1024 * 1024


def inverse_rms(rows):
    return lax.rsqrt(jnp.mean(rows * rows, axis=-1, keepdims=True) + epsilon)


def norm_back(layer_in, gain, upstream):
    inverse = inverse_rms(layer_in)
    unit_rows = layer_in * inverse
    gain_grad = jnp.sum(upstream * unit_rows, axis=0)
    scaled = upstream * gain
    in_grad = inverse * (scaled - unit_rows * jnp.mean(scaled * unit_rows, axis=-1, keepdims=True))
    return (in_grad, gain_grad)


def silu_parts(argument):
    sigmoid = jax.nn.sigmoid(argument)
    return argument * sigmoid, sigmoid * (1.0 + argument * (1.0 - sigmoid))


def dot(left_side, right_side):
    return jnp.dot(left_side, right_side, preferred_element_type=f32)


def dot_nt(left_side, right_side):
    return lax.dot_general(
        left_side, right_side, (((1,), (1,)), ((), ())), preferred_element_type=f32
    )


def dot_tn(left_side, right_side):
    return lax.dot_general(
        left_side, right_side, (((0,), (0,)), ((), ())), preferred_element_type=f32
    )


def wide_einsum(formula, left_side, right_side):
    return jnp.einsum(formula, left_side, right_side, preferred_element_type=f32)


def arrival(info_ref, parts, part):
    return lax.rem(info_ref[2] + parts - part, parts)


def stacked_heads(ref, at):
    return jnp.concatenate([ref[at, :, g * HD : (g + 1) * HD] for g in range(GROUP)], axis=0)


def store_heads(ref, at, rows):
    block = ref.shape[1]
    for g in range(GROUP):
        ref[at, :, g * HD : (g + 1) * HD] = rows[g * block : (g + 1) * block]


def cached(ref, span, column):
    rows = ref[:, span, column : column + HD]
    return rows.reshape(rows.shape[0] * rows.shape[1], HD)


def block_span(at, block):
    return pl.ds(pl.multiple_of(at * block, block), block)


def diagonal_mask(rows, chunk, block, zy):
    key_at = lax.broadcasted_iota(jnp.int32, (rows, chunk), 1)
    row_at = lax.broadcasted_iota(jnp.int32, (rows, chunk), 0)
    return key_at <= zy * block + lax.rem(row_at, block)


def all_heads(ref, ats):
    return jnp.concatenate([stacked_heads(ref, at) for at in ats], axis=0)


def added_from(total, first, value):
    if first == 0:
        return total + value
    return jnp.concatenate([total[:first], total[first:] + value], axis=0)


def masked_first(mask, value, fill):
    count = mask.shape[0]
    own = jnp.where(mask, value[:count], fill)
    return own if value.shape[0] == count else jnp.concatenate([own, value[count:]], axis=0)


def attention_forward_kernel(has_prev, info_ref, q_ref, *refs):
    prev_ref = refs[0] if has_prev else None
    cur_ref, o_ref, log_ref = refs[-3:]
    parts, block, _ = q_ref.shape
    rows = GROUP * block
    mask = diagonal_mask(rows, cur_ref.shape[0] * block, block, info_ref[0])
    ats = [arrival(info_ref, parts, part) for part in range(parts)]
    queries = all_heads(q_ref, ats)
    pieces = []
    if has_prev:
        bias = jnp.where(info_ref[1] > 0, 0.0, masked_score).astype(f32)
        everything = slice(None)
        scores = dot_nt(queries, cached(prev_ref, everything, 0)) + bias
        pieces.append((scores, prev_ref, everything, 0))
    for part in range(parts):
        span, first = block_span(ats[part], block), part * rows
        scores = dot_nt(queries[first:], cached(cur_ref, span, 0))
        pieces.append((masked_first(mask, scores, masked_score), cur_ref, span, first))
    peaks = []
    for part in range(parts):
        at = part * rows
        tops = [
            jnp.max(scores[at - first : at - first + rows], axis=-1, keepdims=True)
            for scores, _, _, first in pieces
            if first <= at
        ]
        peaks.append(functools.reduce(jnp.maximum, tops))
    peak = jnp.concatenate(peaks, axis=0) * log2_scale
    total = jnp.zeros((parts * rows, 1), f32)
    mixed = jnp.zeros((parts * rows, HD), f32)
    for scores, ref, span, first in pieces:
        probs = jnp.exp2(scores * log2_scale - peak[first:])
        total = added_from(total, first, jnp.sum(probs, axis=-1, keepdims=True))
        mixed = added_from(mixed, first, dot(probs.astype(bf), cached(ref, span, HD)))
    out = (mixed / total).astype(bf)
    log_total = peak + jnp.log2(total)
    for part, at in enumerate(ats):
        store_heads(o_ref, at, out[part * rows : (part + 1) * rows])
        log_ref[at] = jnp.broadcast_to(log_total[part * rows : (part + 1) * rows], (rows, HD))


def attention_backward_kernel(has_prev, has_carry, info_ref, q_ref, do_ref, o_ref, log_ref, *refs):
    refs = list(refs)
    carry_ref = refs.pop(0) if has_carry else None
    prev_ref = refs.pop(0) if has_prev else None
    cur_ref, dq_ref, dcur_ref = refs[:3]
    dprev_ref = refs[3] if has_prev else None
    parts, block, _ = q_ref.shape
    ring = cur_ref.shape[0]
    rows = GROUP * block
    mask = diagonal_mask(rows, ring * block, block, info_ref[0])
    ats = [arrival(info_ref, parts, part) for part in range(parts)]
    queries, out_grad = all_heads(q_ref, ats), all_heads(do_ref, ats)
    out = all_heads(o_ref, ats)
    inner = jnp.sum(out_grad.astype(f32) * out.astype(f32), axis=-1, keepdims=True)
    log_total = jnp.concatenate([log_ref[at][:, :1] for at in ats], axis=0)

    def one_block(ref, span, first, log_rows, own_block):
        keys, values = cached(ref, span, 0), cached(ref, span, HD)
        some, some_grad = queries[first:], out_grad[first:]
        probs = jnp.exp2(dot_nt(some, keys) * log2_scale - log_rows[first:])
        if own_block:
            probs = masked_first(mask, probs, 0.0)
        score_grad = (probs * (dot_nt(some_grad, values) - inner[first:])).astype(bf)
        key_grad = dot_tn(score_grad, some) * scaling
        value_grad = dot_tn(probs.astype(bf), some_grad)
        shape = (ring, block, HD)
        return dot(score_grad, keys), key_grad.reshape(shape), value_grad.reshape(shape)

    query_grad = jnp.zeros((parts * rows, HD), f32)
    if has_prev:
        log_prev = log_total + jnp.where(info_ref[1] > 0, 0.0, -masked_score).astype(f32)
        for part in range(parts):
            span = slice(part * block, (part + 1) * block)
            more, key_grad, value_grad = one_block(prev_ref, span, 0, log_prev, False)
            query_grad = query_grad + more
            dprev_ref[:, span, :HD] = key_grad
            dprev_ref[:, span, HD:] = value_grad
    for part in range(parts):
        span = block_span(ats[part], block)
        more, key_grad, value_grad = one_block(cur_ref, span, part * rows, log_total, True)
        query_grad = added_from(query_grad, part * rows, more)
        if has_carry:
            key_grad = key_grad + carry_ref[:, span, :HD]
            value_grad = value_grad + carry_ref[:, span, HD:]
        dcur_ref[:, span, :HD] = key_grad.astype(bf)
        dcur_ref[:, span, HD:] = value_grad.astype(bf)
    query_grad = (query_grad * scaling).astype(bf)
    for part, at in enumerate(ats):
        store_heads(dq_ref, at, query_grad[part * rows : (part + 1) * rows])


def attention_call(kernel, factor, out_shape, info, queries, *rest):
    parts, block, _ = queries.shape
    rows = parts * GROUP * block
    keys = sum(ref.shape[0] * ref.shape[1] for ref in rest if ref.shape == rest[-1].shape)
    in_vmem = pl.BlockSpec(memory_space=pltpu.VMEM)
    return pl.pallas_call(
        kernel,
        out_shape=out_shape,
        in_specs=[pl.BlockSpec(memory_space=pltpu.SMEM)] + [in_vmem] * (1 + len(rest)),
        out_specs=(in_vmem,) * len(out_shape),
        compiler_params=pltpu.CompilerParams(vmem_limit_bytes=VMEM_LIMIT),
        cost_estimate=pl.CostEstimate(
            flops=factor * rows * keys * HD,
            bytes_accessed=factor * (keys + rows) * HD,
            transcendentals=rows * keys // 2,
        ),
    )(info, queries, *rest)


def attention_forward(info, qkv, prev, cur):
    parts, block, _ = qkv.shape
    shapes = (
        jax.ShapeDtypeStruct((parts, block, GROUP * HD), bf),
        jax.ShapeDtypeStruct((parts, GROUP * block, HD), f32),
    )
    caches = (cur,) if prev is None else (prev, cur)
    kernel = functools.partial(attention_forward_kernel, prev is not None)
    return attention_call(kernel, 2, shapes, info, qkv, *caches)


def attention_backward(info, qkv, out_grad, out, logs, carry, prev, cur):
    shapes = (jax.ShapeDtypeStruct(out.shape, bf), jax.ShapeDtypeStruct(cur.shape, bf))
    if prev is not None:
        shapes += (jax.ShapeDtypeStruct(cur.shape, f32),)
    extra = tuple(value for value in (carry, prev) if value is not None)
    kernel = functools.partial(attention_backward_kernel, prev is not None, carry is not None)
    return attention_call(kernel, 5, shapes, info, qkv, out_grad, out, logs, *extra, cur)


def body(
    inputs,
    cotangent,
    routes,
    norm_attn,
    w_query,
    w_key,
    w_value,
    w_output,
    norm_ffn,
    w_router,
    shared_gate,
    shared_up,
    shared_down,
    expert_gate,
    expert_up,
    expert_down,
):
    micros, block, width = inputs.shape[1:]
    shards = lax.axis_size("shard")
    section = lax.axis_index("section")
    core = lax.axis_index("dp")
    position = lax.axis_index("shard")
    heads = KVH
    ring = shards // heads
    local_experts = expert_gate.shape[1]
    experts = local_experts * shards
    slots = experts * CAP
    rows_per = w_query.shape[1]
    half_rows = rows_per // 2
    group_width = GROUP * HD
    head_width = H * HD
    key_width = KVH * HD
    part_width = group_width + 2 * HD
    shared_width = shared_gate.shape[2]
    down_rows = shared_down.shape[1]
    is_first = section == 0
    low_core = core == 0
    zy_groups = [[x * ring + zy for zy in range(ring)] for x in range(heads)]

    def exchange(value, groups=None):
        return lax.all_to_all(
            value, "shard", split_axis=0, concat_axis=0, tiled=True, axis_index_groups=groups
        )

    def copies(value, count):
        return jnp.broadcast_to(value[None], (count,) + value.shape)

    def twin(value):
        return lax.ppermute(value, "dp", [(0, 1), (1, 0)])

    def mine_of(low_half, high_half):
        return jnp.where(low_core, low_half, high_half)

    def ordered(own, other, axis):
        low_half, high_half = mine_of(own, other), mine_of(other, own)
        return jnp.concatenate([low_half, high_half], axis=axis)

    def ordered_by(in_order, own, other):
        return jnp.stack([jnp.where(in_order, own, other), jnp.where(in_order, other, own)])

    def halves(value):
        half = value.shape[-1] // 2
        return value[..., :half], value[..., half:]

    def my_rows(value):
        return mine_of(value[..., :half_rows, :], value[..., half_rows:, :])

    tail = jnp.concatenate(
        [
            w_router[0],
            norm_attn[0][:, None],
            norm_ffn[0][:, None],
            jnp.zeros((rows_per, 128 - experts - 2), bf),
        ],
        axis=1,
    )
    by_head = jnp.concatenate(
        [
            w_query[0].reshape(rows_per, heads, group_width),
            w_key[0].reshape(rows_per, heads, HD),
            w_value[0].reshape(rows_per, heads, HD),
            jnp.broadcast_to(tail[:, None], (rows_per, heads, 128)),
        ],
        axis=2,
    ).transpose(1, 0, 2)
    by_head = my_rows(by_head)
    by_head = jnp.broadcast_to(
        by_head[:, None], (heads, ring, half_rows, part_width + 128)
    ).reshape(shards, half_rows, part_width + 128)
    down_half = down_rows // 2
    down_flat = (half_rows, down_half * width // half_rows)
    packed = jnp.concatenate(
        [
            my_rows(jnp.concatenate([shared_gate[0], shared_up[0]], axis=1)),
            mine_of(shared_down[0][:down_half], shared_down[0][down_half:]).reshape(down_flat),
        ],
        axis=1,
    )
    by_head, packed = lax.optimization_barrier((by_head, packed))
    gathered = lax.all_gather(packed, "shard")
    own_part = exchange(by_head)
    out_rows = my_rows(w_output[0])
    out_rows = ordered_by(
        position % 2 == 0, out_rows, lax.ppermute(out_rows, "shard", [(p, p ^ 1) for p in range(shards)])
    )
    out_parts = [out_rows] + [
        lax.ppermute(
            out_rows,
            "shard",
            [(p, p // ring * ring + (p % ring - 2 * k) % ring) for p in range(shards)],
        )
        for k in range(1, ring // 2)
    ]
    own_part, *out_parts = lax.optimization_barrier((own_part, *out_parts))
    own_out = lax.dynamic_slice_in_dim(
        jnp.concatenate(out_parts + out_parts), ring - position % ring // 2 * 2, ring, axis=0
    )
    output_w = ordered(own_out, twin(own_out), 1).reshape(group_width, width)
    fetched = ordered(own_part, twin(own_part), 1).reshape(width, part_width + 128)
    qkv_w, tail = fetched[:, :part_width], fetched[:, part_width:]
    router_w = tail[:, :experts]
    gains = tail[:, experts : experts + 2].T.astype(f32)
    gain_one, gain_two = gains[0][None], gains[1][None]

    expert_g, expert_u, expert_d = expert_gate[0], expert_up[0], expert_down[0]
    slot_of = jnp.arange(slots, dtype=jnp.int32)
    expert_of = jnp.arange(experts, dtype=jnp.int32)
    row_of = jnp.arange(block, dtype=jnp.int32)
    spread = (expert_of[:, None] == slot_of[None, :] // CAP).astype(bf)
    router_slots = dot(router_w, spread).astype(bf)
    earlier = (row_of[:, None] > row_of[None, :]).astype(bf)

    def slot_table(route_rows):
        named = jnp.any(route_rows[:, :, None] == expert_of[None, None, :], axis=1).astype(bf)
        slot_ids = dot(earlier, named).astype(bf)
        return (dot(named, spread) > 0.5) & (
            dot(slot_ids, spread).astype(jnp.int32) == (slot_of % CAP)[None, :]
        )

    here = [position % ring, jnp.ones_like(position), position // ring]
    info_all = jnp.stack(here).astype(jnp.int32)
    info = jnp.stack([here[0], is_first.astype(here[0].dtype), here[2]]).astype(jnp.int32)

    def gate_values(normed_two, table):
        logits = jnp.where(table, dot(normed_two, router_slots), masked_score)
        weights = jnp.exp(logits - jnp.max(logits, axis=-1, keepdims=True))
        weights = jnp.where(table, weights, 0.0)
        return weights / jnp.sum(weights, axis=-1, keepdims=True)

    def high_low(value):
        high = value.astype(bf)
        return high, (value - high.astype(f32)).astype(bf)

    def to_experts(rows):
        return (
            exchange(rows.reshape(shards, local_experts, CAP, width))
            .transpose(1, 0, 2, 3)
            .reshape(local_experts, shards * CAP, width)
        )

    def from_experts(rows):
        return exchange(
            rows.reshape(local_experts, shards, CAP, width).transpose(1, 0, 2, 3)
        ).reshape(slots, width)

    def moved(p, steps):
        return (p // ring + steps) % heads * ring + p % ring

    def shift_x(value, steps):
        return lax.ppermute(value, "shard", [(p, moved(p, steps)) for p in range(shards)])

    def next_ring(value):
        return jnp.stack(
            [
                lax.ppermute(
                    value,
                    ("section", "shard"),
                    [(p, shards + moved(p, steps)) for p in range(shards)],
                )
                for steps in range(heads)
            ]
        )

    def sum_over_x(rows):
        parts = rows.reshape(heads, block, width)
        away = [shift_x(parts[k].astype(bf), -k).astype(f32) for k in range(1, heads)]
        return sum(away, parts[0])

    def ring_rows(rows):
        return jnp.concatenate([rows] + [shift_x(rows, k) for k in range(1, heads)], axis=0)

    ring_inputs = [
        jnp.stack([inputs[0, m]] + [shift_x(inputs[0, m], k) for k in range(1, heads)])
        for m in range(micros)
    ]

    def shared_weights(gathered):
        gate_up = gathered[:, :, : 2 * shared_width]
        down = gathered[:, :, 2 * shared_width :].reshape(shards, down_half, width)
        return (
            ordered(gate_up, twin(gate_up), 1).reshape(width, 2 * shared_width),
            ordered(down, twin(down), 1).reshape(shards * down_rows, width),
        )

    def forward(moment, received, previous, shared_pair):
        first_micro = min(moment, micros - 1)
        second_micro = max(moment - 1, 0)
        ring_b = jnp.where(is_first, ring_inputs[first_micro], received)
        layer_b = ring_b[0]
        table = slot_table(
            jnp.where(is_first, routes[0, 0, first_micro], routes[0, 0, second_micro])
        )
        pick = table.astype(bf)
        layer_in = layer_b.astype(f32)
        ring_in = ring_b.reshape(heads * block, width).astype(f32)
        ring_one = (ring_in * inverse_rms(ring_in) * gain_one).astype(bf)
        qkv = dot(ring_one, qkv_w).astype(bf)
        cache = exchange(copies(qkv[:, group_width:], ring), zy_groups)
        qkv = qkv.reshape(heads, block, part_width)
        attn_info = info if moment == 1 else info_all
        attended, logs = attention_forward(attn_info, qkv, previous, cache)
        attended_rows = attended.reshape(heads * block, group_width)
        hidden = layer_in + sum_over_x(dot(attended_rows, output_w))
        if shared_pair is None:
            arrived, hidden = lax.optimization_barrier((gathered, hidden))
            shared_pair = shared_weights(arrived)
        gate_up_w, down_w = shared_pair
        normed_two = (hidden * inverse_rms(hidden) * gain_two).astype(bf)
        gates = gate_values(normed_two, table)
        expert_in = to_experts(dot_tn(pick, normed_two).astype(bf))
        gate_pre = wide_einsum("erd,edf->erf", expert_in, expert_g)
        up_pre = wide_einsum("erd,edf->erf", expert_in, expert_u)
        activated = (silu_parts(gate_pre)[0] * up_pre).astype(bf)
        returned = from_experts(wide_einsum("erf,efd->erd", activated, expert_d).astype(bf))
        high, low = high_low(gates)
        routed = dot(high, returned) + dot(low, returned)
        shared_gate_pre, shared_up_pre = halves(dot(normed_two, gate_up_w))
        shared_act = (silu_parts(shared_gate_pre)[0] * shared_up_pre).astype(bf)
        beside = lax.optimization_barrier(hidden + dot(shared_act, down_w))
        output_b = (beside + routed).astype(bf)
        return dict(
            layer_b=layer_b,
            pick=pick,
            ring_one=ring_one,
            qkv=qkv,
            cache=cache,
            previous=previous,
            info=attn_info,
            attended=attended,
            logs=logs,
            hidden=hidden,
            normed_two=normed_two,
            gates=gates,
            expert_in=expert_in,
            gate_pre=gate_pre,
            up_pre=up_pre,
            activated=activated,
            returned=returned,
            shared_gate_pre=shared_gate_pre,
            shared_up_pre=shared_up_pre,
            shared_act=shared_act,
            output_b=output_b,
            shared_pair=shared_pair,
        )

    def ffn_backward(kept, upstream_b):
        upstream = upstream_b.astype(f32)
        gates, hidden = kept["gates"], kept["hidden"]
        gate_up_w, down_w = kept["shared_pair"]
        high, low = high_low(gates)
        outgoing = dot_tn(high, upstream_b) + dot_tn(low, upstream_b)
        expert_grad = to_experts(outgoing.astype(bf))
        act_silu, act_slope = silu_parts(kept["gate_pre"])
        act_grad = wide_einsum("erd,efd->erf", expert_grad, expert_d)
        gate_pre_grad = (act_grad * kept["up_pre"] * act_slope).astype(bf)
        up_pre_grad = (act_grad * act_silu).astype(bf)
        expert_in_grad = (
            wide_einsum("erf,edf->erd", gate_pre_grad, expert_g)
            + wide_einsum("erf,edf->erd", up_pre_grad, expert_u)
        ).astype(bf)
        returned_grad = from_experts(expert_in_grad)
        shared_act_grad = dot_nt(upstream_b, down_w)
        shared_silu, shared_slope = silu_parts(kept["shared_gate_pre"])
        shared_gate_grad = (shared_act_grad * kept["shared_up_pre"] * shared_slope).astype(bf)
        shared_up_grad = (shared_act_grad * shared_silu).astype(bf)
        normed_two_grad = dot_nt(
            jnp.concatenate([shared_gate_grad, shared_up_grad], axis=1), gate_up_w
        )
        gate_grad = dot_nt(upstream_b, kept["returned"])
        picked_grad = gates * (gate_grad - jnp.sum(gates * gate_grad, axis=1, keepdims=True))
        picked_b = picked_grad.astype(bf)
        normed_two_grad = normed_two_grad + dot_nt(picked_b, router_slots)
        normed_two_grad = lax.optimization_barrier(normed_two_grad)
        normed_two_grad = normed_two_grad + dot(kept["pick"], returned_grad)
        logit_grad = dot_nt(picked_b, spread).astype(bf)
        hidden_norm_grad, gain_two_grad = norm_back(hidden, gain_two, normed_two_grad)
        return dict(
            hidden_grad=upstream + hidden_norm_grad,
            upstream_b=upstream_b,
            expert_grad=expert_grad,
            gate_pre_grad=gate_pre_grad,
            up_pre_grad=up_pre_grad,
            shared_gate_grad=shared_gate_grad,
            shared_up_grad=shared_up_grad,
            logit_grad=logit_grad,
            gain_two_grad=gain_two_grad,
        )

    def attention_back(kept, grads, carried):
        ring_hidden = ring_rows(grads["hidden_grad"].astype(bf))
        out_grad = dot_nt(ring_hidden, output_w).astype(bf)
        results = attention_backward(
            kept["info"],
            kept["qkv"],
            out_grad.reshape(heads, block, group_width),
            kept["attended"],
            kept["logs"],
            carried,
            kept["previous"],
            kept["cache"],
        )
        carried = results[2] if len(results) > 2 else None
        query_grad = results[0].reshape(heads * block, group_width)
        query_part = lax.optimization_barrier(dot_nt(query_grad, qkv_w[:, :group_width]))
        pair_grad = jnp.sum(exchange(results[1], zy_groups).astype(f32), axis=0).astype(bf)
        qkv_grad = jnp.concatenate([query_grad, pair_grad], axis=1)
        normed_one_grad = sum_over_x(query_part + dot_nt(pair_grad, qkv_w[:, group_width:]))
        in_norm_grad, gain_one_grad = norm_back(
            kept["layer_b"].astype(f32), gain_one, normed_one_grad
        )
        grads = dict(
            grads,
            ring_hidden=ring_hidden,
            qkv_grad=qkv_grad,
            gain_one_grad=gain_one_grad,
            layer_grad=(grads["hidden_grad"] + in_norm_grad).astype(bf),
        )
        return grads, carried

    nothing = jnp.zeros((block, width), bf)
    saved = []
    received, previous, shared_pair = jnp.zeros((heads, block, width), bf), None, None
    for moment in range(micros + 1):
        kept = forward(moment, received, previous, shared_pair)
        shared_pair = kept["shared_pair"]
        saved.append(kept)
        previous = kept["cache"]
        if moment < micros:
            received = next_ring(kept["output_b"])
    backs = [None] * (micros + 1)
    received, carried = nothing, None
    for source in range(micros, -1, -1):
        own = cotangent[0, source - 1] if source > 0 else nothing
        upstream_b = jnp.where(is_first, received, own)
        grads = ffn_backward(saved[source], upstream_b)
        backs[source], carried = attention_back(saved[source], grads, carried)
        if source > 0:
            received = lax.ppermute(backs[source]["layer_grad"], "section", [(1, 0)])

    def live(name, store, axis):
        ends = jnp.where(is_first, store[0][name], store[micros][name])
        return jnp.concatenate([ends, store[1][name]], axis=axis)

    def kept_rows(name, axis=0):
        return live(name, saved, axis)

    def back_rows(name, axis=0):
        return live(name, backs, axis)

    expert_parts = [
        wide_einsum("erd,erf->edf", kept_rows("expert_in", 1), back_rows("gate_pre_grad", 1)),
        wide_einsum("erd,erf->edf", kept_rows("expert_in", 1), back_rows("up_pre_grad", 1)),
        wide_einsum("erf,erd->efd", kept_rows("activated", 1), back_rows("expert_grad", 1)),
    ]
    expert_parts = [part.astype(bf) for part in expert_parts]
    expert_others = [twin(part) for part in expert_parts]

    def both(value):
        return jnp.concatenate([value, twin(value)], axis=0)

    def both_halves(low_half, high_half):
        own, other = mine_of(low_half, high_half), mine_of(high_half, low_half)
        return jnp.concatenate([own, twin(other)], axis=0)

    normed_two = kept_rows("normed_two")
    grad_gate_up = dot_tn(
        both(normed_two), both_halves(back_rows("shared_gate_grad"), back_rows("shared_up_grad"))
    )
    grad_down = dot_tn(both(kept_rows("shared_act")), both_halves(*halves(back_rows("upstream_b"))))


    def shift_z(value, steps):
        pairs = [(p, p // ring * ring + (p % ring + 2 * steps) % ring) for p in range(shards)]
        return lax.ppermute(value, "shard", pairs)

    def shift_y(value, steps):
        return lax.ppermute(value, "shard", [(p, p ^ 1) for p in range(shards)])

    along = dict(
        x=(shift_x, position // ring), z=(shift_z, position % ring // 2), y=(shift_y, position % 2)
    )

    def reduced(value, name, axis, held_as=bf):
        shift, here = along[name]
        count = value.shape[axis]

        def piece(steps):
            return lax.dynamic_index_in_dim(value, (here + steps) % count, axis, keepdims=False)

        total = piece(0).astype(f32)
        for steps in range(1, count):
            total = total + shift(piece(steps), steps).astype(f32)
        return total.astype(held_as)

    grad_out = dot_tn(
        kept_rows("attended").reshape(micros * heads * block, group_width),
        back_rows("ring_hidden"),
    )
    grad_gate_up, grad_down, grad_out, last_grad, *expert_others = lax.optimization_barrier(
        (
            grad_gate_up.astype(bf),
            grad_down.astype(bf),
            grad_out.astype(bf),
            backs[0]["layer_grad"],
            *expert_others,
        )
    )
    backs[0]["layer_grad"] = last_grad
    expert_grads = [
        part.astype(f32) + other.astype(f32) for part, other in zip(expert_parts, expert_others)
    ]
    pieces = grad_gate_up.reshape(heads, ring // 2, 2, rows_per, shared_width)
    share_gate_up = reduced(reduced(reduced(pieces, "x", 0), "z", 0), "y", 0, f32)
    pieces = grad_down.reshape(heads, ring // 2, 2, down_rows, width // 2)
    share_down = reduced(reduced(reduced(pieces, "z", 1), "x", 0), "y", 0, f32)

    share_out = jnp.sum(
        exchange(grad_out.reshape(ring, rows_per, width), zy_groups).astype(f32), axis=0
    )
    grad_qkv = dot_tn(kept_rows("ring_one"), back_rows("qkv_grad"))
    grad_router = dot_tn(normed_two, back_rows("logit_grad"))
    gain_sums = jnp.stack(
        [sum(grads[name] for grads in backs) for name in ("gain_one_grad", "gain_two_grad")]
    )
    grad_tail = jnp.concatenate(
        [grad_router, gain_sums.T, jnp.zeros((width, 128 - experts - 2), f32)], axis=1
    )
    grad_qkv = jnp.concatenate([grad_qkv, grad_tail], axis=1)
    pieces = exchange(
        grad_qkv.astype(bf).reshape(shards, rows_per, part_width + 128)
    ).astype(f32)
    share_qkv = jnp.sum(
        pieces[:, :, :part_width].reshape(heads, ring, rows_per, part_width), axis=1
    )
    share_qkv = share_qkv.transpose(1, 0, 2)
    share_tail = jnp.sum(pieces[:, :, part_width:], axis=0)

    def total(share):
        return share + twin(share)

    out_total, qkv_total, tail_total = total(share_out), total(share_qkv), total(share_tail)
    other_gate_up = twin(share_gate_up)
    down_total = ordered(share_down, twin(share_down), 1)

    def by_micro(store, name):
        return jnp.stack(
            [jnp.where(is_first, store[m][name], store[m + 1][name]) for m in range(micros)]
        )[None, None]

    return (
        by_micro(saved, "output_b"),
        by_micro(backs, "layer_grad"),
        tail_total[:, experts][None],
        qkv_total[:, :, :group_width].reshape(1, rows_per, head_width),
        qkv_total[:, :, group_width : group_width + HD].reshape(1, rows_per, key_width),
        qkv_total[:, :, group_width + HD :].reshape(1, rows_per, key_width),
        out_total[None],
        tail_total[:, experts + 1][None],
        tail_total[:, :experts][None],
        mine_of(share_gate_up, other_gate_up)[None],
        mine_of(other_gate_up, share_gate_up)[None],
        down_total[None],
        expert_grads[0][None],
        expert_grads[1][None],
        expert_grads[2][None],
    )


def solution(mesh):
    rows = P("section", "shard", None)
    vector = P("section", "shard")
    expert = P("section", "shard", None, None)
    tokens = P("dp", None, "shard", None)
    section_tokens = P("section", "dp", None, "shard", None)
    weights = (vector, rows, rows, rows, rows, vector, rows, rows, rows, rows) + (expert,) * 3
    return jax.shard_map(
        body,
        mesh=mesh,
        in_specs=(tokens, tokens, section_tokens) + weights,
        out_specs=(section_tokens, section_tokens) + weights,
        check_vma=False,
    )
```

```python
import functools

import jax
import jax.numpy as jnp
from jax import lax
from jax.experimental import pallas as pl
from jax.experimental.pallas import tpu as pltpu
from jax.sharding import PartitionSpec as P

H = 12
KVH = 4
HD = 128
GROUP = H // KVH
TOPK = 6
CAP = 8

epsilon = 1e-05
masked_score = -1e30
scaling = HD ** (-0.5)
log2_scale = scaling * 1.4426950408889634
bf = jnp.bfloat16
f32 = jnp.float32
VMEM_LIMIT = 32 * 1024 * 1024


def inverse_rms(rows):
    return lax.rsqrt(jnp.mean(rows * rows, axis=-1, keepdims=True) + epsilon)


def norm_back(layer_in, gain, upstream):
    inverse = inverse_rms(layer_in)
    unit_rows = layer_in * inverse
    gain_grad = jnp.sum(upstream * unit_rows, axis=0)
    scaled = upstream * gain
    in_grad = inverse * (scaled - unit_rows * jnp.mean(scaled * unit_rows, axis=-1, keepdims=True))
    return (in_grad, gain_grad)


def silu_parts(argument):
    sigmoid = jax.nn.sigmoid(argument)
    return argument * sigmoid, sigmoid * (1.0 + argument * (1.0 - sigmoid))


def dot(left_side, right_side):
    return jnp.dot(left_side, right_side, preferred_element_type=f32)


def dot_nt(left_side, right_side):
    return lax.dot_general(
        left_side, right_side, (((1,), (1,)), ((), ())), preferred_element_type=f32
    )


def dot_tn(left_side, right_side):
    return lax.dot_general(
        left_side, right_side, (((0,), (0,)), ((), ())), preferred_element_type=f32
    )


def wide_einsum(formula, left_side, right_side):
    return jnp.einsum(formula, left_side, right_side, preferred_element_type=f32)


def arrival(info_ref, parts, part):
    return lax.rem(info_ref[2] + parts - part, parts)


def stacked_heads(ref, at):
    return jnp.concatenate([ref[at, :, g * HD : (g + 1) * HD] for g in range(GROUP)], axis=0)


def store_heads(ref, at, rows):
    block = ref.shape[1]
    for g in range(GROUP):
        ref[at, :, g * HD : (g + 1) * HD] = rows[g * block : (g + 1) * block]


def cached(ref, span, column):
    rows = ref[:, span, column : column + HD]
    return rows.reshape(rows.shape[0] * rows.shape[1], HD)


def block_span(at, block):
    return pl.ds(pl.multiple_of(at * block, block), block)


def diagonal_mask(rows, chunk, block, zy):
    key_at = lax.broadcasted_iota(jnp.int32, (rows, chunk), 1)
    row_at = lax.broadcasted_iota(jnp.int32, (rows, chunk), 0)
    return key_at <= zy * block + lax.rem(row_at, block)


def all_heads(ref, ats):
    return jnp.concatenate([stacked_heads(ref, at) for at in ats], axis=0)


def added_from(total, first, value):
    if first == 0:
        return total + value
    return jnp.concatenate([total[:first], total[first:] + value], axis=0)


def masked_first(mask, value, fill):
    count = mask.shape[0]
    own = jnp.where(mask, value[:count], fill)
    return own if value.shape[0] == count else jnp.concatenate([own, value[count:]], axis=0)


def attention_forward_kernel(has_prev, info_ref, q_ref, *refs):
    prev_ref = refs[0] if has_prev else None
    cur_ref, o_ref, log_ref = refs[-3:]
    parts, block, _ = q_ref.shape
    rows = GROUP * block
    mask = diagonal_mask(rows, cur_ref.shape[0] * block, block, info_ref[0])
    ats = [arrival(info_ref, parts, part) for part in range(parts)]
    queries = all_heads(q_ref, ats)
    pieces = []
    if has_prev:
        bias = jnp.where(info_ref[1] > 0, 0.0, masked_score).astype(f32)
        everything = slice(None)
        scores = dot_nt(queries, cached(prev_ref, everything, 0)) + bias
        pieces.append((scores, prev_ref, everything, 0))
    for part in range(parts):
        span, first = block_span(ats[part], block), part * rows
        scores = dot_nt(queries[first:], cached(cur_ref, span, 0))
        pieces.append((masked_first(mask, scores, masked_score), cur_ref, span, first))
    peaks = []
    for part in range(parts):
        at = part * rows
        tops = [
            jnp.max(scores[at - first : at - first + rows], axis=-1, keepdims=True)
            for scores, _, _, first in pieces
            if first <= at
        ]
        peaks.append(functools.reduce(jnp.maximum, tops))
    peak = jnp.concatenate(peaks, axis=0) * log2_scale
    total = jnp.zeros((parts * rows, 1), f32)
    mixed = jnp.zeros((parts * rows, HD), f32)
    for scores, ref, span, first in pieces:
        probs = jnp.exp2(scores * log2_scale - peak[first:])
        total = added_from(total, first, jnp.sum(probs, axis=-1, keepdims=True))
        mixed = added_from(mixed, first, dot(probs.astype(bf), cached(ref, span, HD)))
    out = (mixed / total).astype(bf)
    log_total = peak + jnp.log2(total)
    for part, at in enumerate(ats):
        store_heads(o_ref, at, out[part * rows : (part + 1) * rows])
        log_ref[at] = jnp.broadcast_to(log_total[part * rows : (part + 1) * rows], (rows, HD))


def attention_backward_kernel(has_prev, has_carry, info_ref, q_ref, do_ref, o_ref, log_ref, *refs):
    refs = list(refs)
    carry_ref = refs.pop(0) if has_carry else None
    prev_ref = refs.pop(0) if has_prev else None
    cur_ref, dq_ref, dcur_ref = refs[:3]
    dprev_ref = refs[3] if has_prev else None
    parts, block, _ = q_ref.shape
    ring = cur_ref.shape[0]
    rows = GROUP * block
    mask = diagonal_mask(rows, ring * block, block, info_ref[0])
    ats = [arrival(info_ref, parts, part) for part in range(parts)]
    queries, out_grad = all_heads(q_ref, ats), all_heads(do_ref, ats)
    out = all_heads(o_ref, ats)
    inner = jnp.sum(out_grad.astype(f32) * out.astype(f32), axis=-1, keepdims=True)
    log_total = jnp.concatenate([log_ref[at][:, :1] for at in ats], axis=0)

    def one_block(ref, span, first, log_rows, own_block):
        keys, values = cached(ref, span, 0), cached(ref, span, HD)
        some, some_grad = queries[first:], out_grad[first:]
        probs = jnp.exp2(dot_nt(some, keys) * log2_scale - log_rows[first:])
        if own_block:
            probs = masked_first(mask, probs, 0.0)
        score_grad = (probs * (dot_nt(some_grad, values) - inner[first:])).astype(bf)
        key_grad = dot_tn(score_grad, some) * scaling
        value_grad = dot_tn(probs.astype(bf), some_grad)
        shape = (ring, block, HD)
        return dot(score_grad, keys), key_grad.reshape(shape), value_grad.reshape(shape)

    query_grad = jnp.zeros((parts * rows, HD), f32)
    if has_prev:
        log_prev = log_total + jnp.where(info_ref[1] > 0, 0.0, -masked_score).astype(f32)
        for part in range(parts):
            span = slice(part * block, (part + 1) * block)
            more, key_grad, value_grad = one_block(prev_ref, span, 0, log_prev, False)
            query_grad = query_grad + more
            dprev_ref[:, span, :HD] = key_grad
            dprev_ref[:, span, HD:] = value_grad
    for part in range(parts):
        span = block_span(ats[part], block)
        more, key_grad, value_grad = one_block(cur_ref, span, part * rows, log_total, True)
        query_grad = added_from(query_grad, part * rows, more)
        if has_carry:
            key_grad = key_grad + carry_ref[:, span, :HD]
            value_grad = value_grad + carry_ref[:, span, HD:]
        dcur_ref[:, span, :HD] = key_grad.astype(bf)
        dcur_ref[:, span, HD:] = value_grad.astype(bf)
    query_grad = (query_grad * scaling).astype(bf)
    for part, at in enumerate(ats):
        store_heads(dq_ref, at, query_grad[part * rows : (part + 1) * rows])


def attention_call(kernel, factor, out_shape, info, queries, *rest):
    parts, block, _ = queries.shape
    rows = parts * GROUP * block
    keys = sum(ref.shape[0] * ref.shape[1] for ref in rest if ref.shape == rest[-1].shape)
    in_vmem = pl.BlockSpec(memory_space=pltpu.VMEM)
    return pl.pallas_call(
        kernel,
        out_shape=out_shape,
        in_specs=[pl.BlockSpec(memory_space=pltpu.SMEM)] + [in_vmem] * (1 + len(rest)),
        out_specs=(in_vmem,) * len(out_shape),
        compiler_params=pltpu.CompilerParams(vmem_limit_bytes=VMEM_LIMIT),
        cost_estimate=pl.CostEstimate(
            flops=factor * rows * keys * HD,
            bytes_accessed=factor * (keys + rows) * HD,
            transcendentals=rows * keys // 2,
        ),
    )(info, queries, *rest)


def attention_forward(info, qkv, prev, cur):
    parts, block, _ = qkv.shape
    shapes = (
        jax.ShapeDtypeStruct((parts, block, GROUP * HD), bf),
        jax.ShapeDtypeStruct((parts, GROUP * block, HD), f32),
    )
    caches = (cur,) if prev is None else (prev, cur)
    kernel = functools.partial(attention_forward_kernel, prev is not None)
    return attention_call(kernel, 2, shapes, info, qkv, *caches)


def attention_backward(info, qkv, out_grad, out, logs, carry, prev, cur):
    shapes = (jax.ShapeDtypeStruct(out.shape, bf), jax.ShapeDtypeStruct(cur.shape, bf))
    if prev is not None:
        shapes += (jax.ShapeDtypeStruct(cur.shape, f32),)
    extra = tuple(value for value in (carry, prev) if value is not None)
    kernel = functools.partial(attention_backward_kernel, prev is not None, carry is not None)
    return attention_call(kernel, 5, shapes, info, qkv, out_grad, out, logs, *extra, cur)


def body(
    inputs,
    cotangent,
    routes,
    norm_attn,
    w_query,
    w_key,
    w_value,
    w_output,
    norm_ffn,
    w_router,
    shared_gate,
    shared_up,
    shared_down,
    expert_gate,
    expert_up,
    expert_down,
):
    micros, block, width = inputs.shape[1:]
    shards = lax.axis_size("shard")
    section = lax.axis_index("section")
    core = lax.axis_index("dp")
    position = lax.axis_index("shard")
    heads = KVH
    ring = shards // heads
    local_experts = expert_gate.shape[1]
    experts = local_experts * shards
    slots = experts * CAP
    rows_per = w_query.shape[1]
    half_rows = rows_per // 2
    group_width = GROUP * HD
    head_width = H * HD
    key_width = KVH * HD
    part_width = group_width + 2 * HD
    shared_width = shared_gate.shape[2]
    down_rows = shared_down.shape[1]
    is_first = section == 0
    low_core = core == 0
    zy_groups = [[x * ring + zy for zy in range(ring)] for x in range(heads)]

    def exchange(value, groups=None):
        return lax.all_to_all(
            value, "shard", split_axis=0, concat_axis=0, tiled=True, axis_index_groups=groups
        )

    def copies(value, count):
        return jnp.broadcast_to(value[None], (count,) + value.shape)

    def twin(value):
        return lax.ppermute(value, "dp", [(0, 1), (1, 0)])

    def mine_of(low_half, high_half):
        return jnp.where(low_core, low_half, high_half)

    def ordered(own, other, axis):
        low_half, high_half = mine_of(own, other), mine_of(other, own)
        return jnp.concatenate([low_half, high_half], axis=axis)

    def ordered_by(in_order, own, other):
        return jnp.stack([jnp.where(in_order, own, other), jnp.where(in_order, other, own)])

    def halves(value):
        half = value.shape[-1] // 2
        return value[..., :half], value[..., half:]

    def my_rows(value):
        return mine_of(value[..., :half_rows, :], value[..., half_rows:, :])

    tail = jnp.concatenate(
        [
            w_router[0],
            norm_attn[0][:, None],
            norm_ffn[0][:, None],
            jnp.zeros((rows_per, 128 - experts - 2), bf),
        ],
        axis=1,
    )
    by_head = jnp.concatenate(
        [
            w_query[0].reshape(rows_per, heads, group_width),
            w_key[0].reshape(rows_per, heads, HD),
            w_value[0].reshape(rows_per, heads, HD),
            jnp.broadcast_to(tail[:, None], (rows_per, heads, 128)),
        ],
        axis=2,
    ).transpose(1, 0, 2)
    by_head = my_rows(by_head)
    by_head = jnp.broadcast_to(
        by_head[:, None], (heads, ring, half_rows, part_width + 128)
    ).reshape(shards, half_rows, part_width + 128)
    down_half = down_rows // 2
    down_flat = (half_rows, down_half * width // half_rows)
    packed = jnp.concatenate(
        [
            my_rows(jnp.concatenate([shared_gate[0], shared_up[0]], axis=1)),
            mine_of(shared_down[0][:down_half], shared_down[0][down_half:]).reshape(down_flat),
        ],
        axis=1,
    )
    by_head, packed = lax.optimization_barrier((by_head, packed))
    gathered = lax.all_gather(packed, "shard")
    own_part = exchange(by_head)
    out_rows = my_rows(w_output[0])
    out_rows = ordered_by(
        position % 2 == 0, out_rows, lax.ppermute(out_rows, "shard", [(p, p ^ 1) for p in range(shards)])
    )
    out_parts = [out_rows] + [
        lax.ppermute(
            out_rows,
            "shard",
            [(p, p // ring * ring + (p % ring - 2 * k) % ring) for p in range(shards)],
        )
        for k in range(1, ring // 2)
    ]
    own_part, *out_parts = lax.optimization_barrier((own_part, *out_parts))
    own_out = lax.dynamic_slice_in_dim(
        jnp.concatenate(out_parts + out_parts), ring - position % ring // 2 * 2, ring, axis=0
    )
    output_w = ordered(own_out, twin(own_out), 1).reshape(group_width, width)
    fetched = ordered(own_part, twin(own_part), 1).reshape(width, part_width + 128)
    qkv_w, tail = fetched[:, :part_width], fetched[:, part_width:]
    router_w = tail[:, :experts]
    gains = tail[:, experts : experts + 2].T.astype(f32)
    gain_one, gain_two = gains[0][None], gains[1][None]

    expert_g, expert_u, expert_d = expert_gate[0], expert_up[0], expert_down[0]
    slot_of = jnp.arange(slots, dtype=jnp.int32)
    expert_of = jnp.arange(experts, dtype=jnp.int32)
    row_of = jnp.arange(block, dtype=jnp.int32)
    spread = (expert_of[:, None] == slot_of[None, :] // CAP).astype(bf)
    router_slots = dot(router_w, spread).astype(bf)
    earlier = (row_of[:, None] > row_of[None, :]).astype(bf)

    def slot_table(route_rows):
        named = jnp.any(route_rows[:, :, None] == expert_of[None, None, :], axis=1).astype(bf)
        slot_ids = dot(earlier, named).astype(bf)
        return (dot(named, spread) > 0.5) & (
            dot(slot_ids, spread).astype(jnp.int32) == (slot_of % CAP)[None, :]
        )

    here = [position % ring, jnp.ones_like(position), position // ring]
    info_all = jnp.stack(here).astype(jnp.int32)
    info = jnp.stack([here[0], is_first.astype(here[0].dtype), here[2]]).astype(jnp.int32)

    def gate_values(normed_two, table):
        logits = jnp.where(table, dot(normed_two, router_slots), masked_score)
        weights = jnp.exp(logits - jnp.max(logits, axis=-1, keepdims=True))
        weights = jnp.where(table, weights, 0.0)
        return weights / jnp.sum(weights, axis=-1, keepdims=True)

    def high_low(value):
        high = value.astype(bf)
        return high, (value - high.astype(f32)).astype(bf)

    def to_experts(rows):
        wide = rows.shape[1]
        return (
            exchange(rows.reshape(shards, local_experts, CAP, wide))
            .transpose(1, 0, 2, 3)
            .reshape(local_experts, shards * CAP, wide)
        )

    def from_experts(rows):
        return exchange(
            rows.reshape(local_experts, shards, CAP, width).transpose(1, 0, 2, 3)
        ).reshape(slots, width)

    def moved(p, steps):
        return (p // ring + steps) % heads * ring + p % ring

    def shift_x(value, steps):
        return lax.ppermute(value, "shard", [(p, moved(p, steps)) for p in range(shards)])

    def next_ring(value):
        return jnp.stack(
            [
                lax.ppermute(
                    value,
                    ("section", "shard"),
                    [(p, shards + moved(p, steps)) for p in range(shards)],
                )
                for steps in range(heads)
            ]
        )

    def sum_over_x(rows):
        parts = rows.reshape(heads, block, width)
        away = [shift_x(parts[k].astype(bf), -k).astype(f32) for k in range(1, heads)]
        return sum(away, parts[0])

    def ring_rows(rows):
        return jnp.concatenate([rows] + [shift_x(rows, k) for k in range(1, heads)], axis=0)

    ring_inputs = [
        jnp.stack([inputs[0, m]] + [shift_x(inputs[0, m], k) for k in range(1, heads)])
        for m in range(micros)
    ]

    def shared_weights(gathered):
        gate_up = gathered[:, :, : 2 * shared_width]
        down = gathered[:, :, 2 * shared_width :].reshape(shards, down_half, width)
        return (
            ordered(gate_up, twin(gate_up), 1).reshape(width, 2 * shared_width),
            ordered(down, twin(down), 1).reshape(shards * down_rows, width),
        )

    def forward(moment, received, previous, shared_pair):
        first_micro = min(moment, micros - 1)
        second_micro = max(moment - 1, 0)
        ring_b = jnp.where(is_first, ring_inputs[first_micro], received)
        layer_b = ring_b[0]
        table = slot_table(
            jnp.where(is_first, routes[0, 0, first_micro], routes[0, 0, second_micro])
        )
        pick = table.astype(bf)
        layer_in = layer_b.astype(f32)
        ring_in = ring_b.reshape(heads * block, width).astype(f32)
        ring_one = (ring_in * inverse_rms(ring_in) * gain_one).astype(bf)
        qkv = dot(ring_one, qkv_w).astype(bf)
        cache = exchange(copies(qkv[:, group_width:], ring), zy_groups)
        qkv = qkv.reshape(heads, block, part_width)
        attn_info = info if moment == 1 else info_all
        early = None
        if moment == micros:
            last_rows = cotangent[0, micros - 1]
            last_rows = jnp.where(is_first, jnp.zeros_like(last_rows), last_rows)
            last_rows = dot_tn(pick, last_rows).astype(bf)
            last_rows, cache = lax.optimization_barrier((last_rows, cache))
            early = to_experts(last_rows)
        attended, logs = attention_forward(attn_info, qkv, previous, cache)
        attended_rows = attended.reshape(heads * block, group_width)
        hidden = layer_in + sum_over_x(dot(attended_rows, output_w))
        if shared_pair is None:
            arrived, hidden = lax.optimization_barrier((gathered, hidden))
            shared_pair = shared_weights(arrived)
        gate_up_w, down_w = shared_pair
        if early is not None:
            early, hidden = lax.optimization_barrier((early, hidden))
        normed_two = (hidden * inverse_rms(hidden) * gain_two).astype(bf)
        gates = gate_values(normed_two, table)
        expert_in = to_experts(dot_tn(pick, normed_two).astype(bf))
        gate_pre = wide_einsum("erd,edf->erf", expert_in, expert_g)
        up_pre = wide_einsum("erd,edf->erf", expert_in, expert_u)
        activated = (silu_parts(gate_pre)[0] * up_pre).astype(bf)
        returned = from_experts(wide_einsum("erf,efd->erd", activated, expert_d).astype(bf))
        high, low = high_low(gates)
        routed = dot(high, returned) + dot(low, returned)
        shared_gate_pre, shared_up_pre = halves(dot(normed_two, gate_up_w))
        shared_act = (silu_parts(shared_gate_pre)[0] * shared_up_pre).astype(bf)
        beside = lax.optimization_barrier(hidden + dot(shared_act, down_w))
        output_b = (beside + routed).astype(bf)
        return dict(
            layer_b=layer_b,
            pick=pick,
            ring_one=ring_one,
            qkv=qkv,
            cache=cache,
            previous=previous,
            info=attn_info,
            attended=attended,
            logs=logs,
            hidden=hidden,
            normed_two=normed_two,
            gates=gates,
            expert_in=expert_in,
            gate_pre=gate_pre,
            up_pre=up_pre,
            activated=activated,
            returned=returned,
            shared_gate_pre=shared_gate_pre,
            shared_up_pre=shared_up_pre,
            shared_act=shared_act,
            output_b=output_b,
            shared_pair=shared_pair,
            expert_grad=early,
        )

    def ffn_backward(kept, upstream_b, riders=None):
        upstream = upstream_b.astype(f32)
        gates, hidden = kept["gates"], kept["hidden"]
        gate_up_w, down_w = kept["shared_pair"]
        high, low = high_low(gates)
        expert_grad, arrived = kept["expert_grad"], None
        unscaled = expert_grad is not None
        if not unscaled:
            outgoing = (dot_tn(high, upstream_b) + dot_tn(low, upstream_b)).astype(bf)
            if riders is not None:
                outgoing = jnp.concatenate([outgoing, riders], axis=1)
            expert_grad = to_experts(outgoing)
            if riders is not None:
                expert_grad, arrived = expert_grad[..., :width], expert_grad[..., width:]
        act_silu, act_slope = silu_parts(kept["gate_pre"])
        act_grad = wide_einsum("erd,efd->erf", expert_grad, expert_d)
        gate_pre_grad = (act_grad * kept["up_pre"] * act_slope).astype(bf)
        up_pre_grad = (act_grad * act_silu).astype(bf)
        expert_in_grad = (
            wide_einsum("erf,edf->erd", gate_pre_grad, expert_g)
            + wide_einsum("erf,edf->erd", up_pre_grad, expert_u)
        ).astype(bf)
        returned_grad = from_experts(expert_in_grad)
        shared_act_grad = dot_nt(upstream_b, down_w)
        shared_silu, shared_slope = silu_parts(kept["shared_gate_pre"])
        shared_gate_grad = (shared_act_grad * kept["shared_up_pre"] * shared_slope).astype(bf)
        shared_up_grad = (shared_act_grad * shared_silu).astype(bf)
        normed_two_grad = dot_nt(
            jnp.concatenate([shared_gate_grad, shared_up_grad], axis=1), gate_up_w
        )
        gate_grad = dot_nt(upstream_b, kept["returned"])
        picked_grad = gates * (gate_grad - jnp.sum(gates * gate_grad, axis=1, keepdims=True))
        picked_b = picked_grad.astype(bf)
        normed_two_grad = normed_two_grad + dot_nt(picked_b, router_slots)
        normed_two_grad = lax.optimization_barrier(normed_two_grad)
        if unscaled:
            routed_grad = dot(high, returned_grad) + dot(low, returned_grad)
        else:
            routed_grad = dot(kept["pick"], returned_grad)
        normed_two_grad = normed_two_grad + routed_grad
        logit_grad = dot_nt(picked_b, spread).astype(bf)
        hidden_norm_grad, gain_two_grad = norm_back(hidden, gain_two, normed_two_grad)
        return dict(
            hidden_grad=upstream + hidden_norm_grad,
            upstream_b=upstream_b,
            expert_grad=expert_grad,
            gate_pre_grad=gate_pre_grad,
            up_pre_grad=up_pre_grad,
            shared_gate_grad=shared_gate_grad,
            shared_up_grad=shared_up_grad,
            logit_grad=logit_grad,
            gain_two_grad=gain_two_grad,
            arrived=arrived,
        )

    def attention_back(kept, grads, carried):
        ring_hidden = ring_rows(grads["hidden_grad"].astype(bf))
        out_grad = dot_nt(ring_hidden, output_w).astype(bf)
        results = attention_backward(
            kept["info"],
            kept["qkv"],
            out_grad.reshape(heads, block, group_width),
            kept["attended"],
            kept["logs"],
            carried,
            kept["previous"],
            kept["cache"],
        )
        carried = results[2] if len(results) > 2 else None
        query_grad = results[0].reshape(heads * block, group_width)
        query_part = lax.optimization_barrier(dot_nt(query_grad, qkv_w[:, :group_width]))
        pair_grad = jnp.sum(exchange(results[1], zy_groups).astype(f32), axis=0).astype(bf)
        qkv_grad = jnp.concatenate([query_grad, pair_grad], axis=1)
        normed_one_grad = sum_over_x(query_part + dot_nt(pair_grad, qkv_w[:, group_width:]))
        in_norm_grad, gain_one_grad = norm_back(
            kept["layer_b"].astype(f32), gain_one, normed_one_grad
        )
        grads = dict(
            grads,
            ring_hidden=ring_hidden,
            qkv_grad=qkv_grad,
            gain_one_grad=gain_one_grad,
            layer_grad=(grads["hidden_grad"] + in_norm_grad).astype(bf),
        )
        return grads, carried

    nothing = jnp.zeros((block, width), bf)
    saved = []
    received, previous, shared_pair = jnp.zeros((heads, block, width), bf), None, None
    for moment in range(micros + 1):
        kept = forward(moment, received, previous, shared_pair)
        shared_pair = kept["shared_pair"]
        saved.append(kept)
        previous = kept["cache"]
        if moment < micros:
            received = next_ring(kept["output_b"])
    backs = [None] * (micros + 1)
    received, carried = nothing, None
    for source in range(micros, -1, -1):
        own = cotangent[0, source - 1] if source > 0 else nothing
        upstream_b = jnp.where(is_first, received, own)
        riders = None
        if source == micros - 1:
            slot_gates = jnp.stack(high_low(jnp.sum(saved[micros]["gates"], axis=0)), axis=1)
            riders = jnp.pad(slot_gates, ((0, 0), (0, 126)))
        grads = ffn_backward(saved[source], upstream_b, riders)
        backs[source], carried = attention_back(saved[source], grads, carried)
        if source > 0:
            received = lax.ppermute(backs[source]["layer_grad"], "section", [(1, 0)])

    def live(name, store, axis):
        ends = jnp.where(is_first, store[0][name], store[micros][name])
        return jnp.concatenate([ends, store[1][name]], axis=axis)

    def kept_rows(name, axis=0):
        return live(name, saved, axis)

    def back_rows(name, axis=0):
        return live(name, backs, axis)

    late_gates = backs[micros - 1]["arrived"][..., :2].astype(f32)
    late_gates = jnp.sum(late_gates, axis=-1, keepdims=True)
    for name in ("expert_grad", "gate_pre_grad", "up_pre_grad"):
        rows = backs[micros][name].astype(f32) * late_gates
        backs[micros][name] = rows.astype(bf)

    expert_parts = [
        wide_einsum("erd,erf->edf", kept_rows("expert_in", 1), back_rows("gate_pre_grad", 1)),
        wide_einsum("erd,erf->edf", kept_rows("expert_in", 1), back_rows("up_pre_grad", 1)),
        wide_einsum("erf,erd->efd", kept_rows("activated", 1), back_rows("expert_grad", 1)),
    ]
    expert_parts = [part.astype(bf) for part in expert_parts]
    expert_others = [twin(part) for part in expert_parts]

    def both(value):
        return jnp.concatenate([value, twin(value)], axis=0)

    def both_halves(low_half, high_half):
        own, other = mine_of(low_half, high_half), mine_of(high_half, low_half)
        return jnp.concatenate([own, twin(other)], axis=0)

    normed_two = kept_rows("normed_two")
    grad_gate_up = dot_tn(
        both(normed_two), both_halves(back_rows("shared_gate_grad"), back_rows("shared_up_grad"))
    )
    grad_down = dot_tn(both(kept_rows("shared_act")), both_halves(*halves(back_rows("upstream_b"))))


    def shift_z(value, steps):
        pairs = [(p, p // ring * ring + (p % ring + 2 * steps) % ring) for p in range(shards)]
        return lax.ppermute(value, "shard", pairs)

    def shift_y(value, steps):
        return lax.ppermute(value, "shard", [(p, p ^ 1) for p in range(shards)])

    along = dict(
        x=(shift_x, position // ring), z=(shift_z, position % ring // 2), y=(shift_y, position % 2)
    )

    def reduced(value, name, axis, held_as=bf):
        shift, here = along[name]
        count = value.shape[axis]

        def piece(steps):
            return lax.dynamic_index_in_dim(value, (here + steps) % count, axis, keepdims=False)

        total = piece(0).astype(f32)
        for steps in range(1, count):
            total = total + shift(piece(steps), steps).astype(f32)
        return total.astype(held_as)

    grad_out = dot_tn(
        kept_rows("attended").reshape(micros * heads * block, group_width),
        back_rows("ring_hidden"),
    )
    grad_gate_up, grad_down, grad_out, last_grad, *expert_others = lax.optimization_barrier(
        (
            grad_gate_up.astype(bf),
            grad_down.astype(bf),
            grad_out.astype(bf),
            backs[0]["layer_grad"],
            *expert_others,
        )
    )
    backs[0]["layer_grad"] = last_grad
    expert_grads = [
        part.astype(f32) + other.astype(f32) for part, other in zip(expert_parts, expert_others)
    ]
    pieces = grad_gate_up.reshape(heads, ring // 2, 2, rows_per, shared_width)
    share_gate_up = reduced(reduced(reduced(pieces, "x", 0), "z", 0), "y", 0, f32)
    pieces = grad_down.reshape(heads, ring // 2, 2, down_rows, width // 2)
    share_down = reduced(reduced(reduced(pieces, "z", 1), "x", 0), "y", 0, f32)

    share_out = jnp.sum(
        exchange(grad_out.reshape(ring, rows_per, width), zy_groups).astype(f32), axis=0
    )
    grad_qkv = dot_tn(kept_rows("ring_one"), back_rows("qkv_grad"))
    grad_router = dot_tn(normed_two, back_rows("logit_grad"))
    gain_sums = jnp.stack(
        [sum(grads[name] for grads in backs) for name in ("gain_one_grad", "gain_two_grad")]
    )
    grad_tail = jnp.concatenate(
        [grad_router, gain_sums.T, jnp.zeros((width, 128 - experts - 2), f32)], axis=1
    )
    grad_qkv = jnp.concatenate([grad_qkv, grad_tail], axis=1)
    pieces = exchange(
        grad_qkv.astype(bf).reshape(shards, rows_per, part_width + 128)
    ).astype(f32)
    share_qkv = jnp.sum(
        pieces[:, :, :part_width].reshape(heads, ring, rows_per, part_width), axis=1
    )
    share_qkv = share_qkv.transpose(1, 0, 2)
    share_tail = jnp.sum(pieces[:, :, part_width:], axis=0)

    def total(share):
        return share + twin(share)

    out_total, qkv_total, tail_total = total(share_out), total(share_qkv), total(share_tail)
    other_gate_up = twin(share_gate_up)
    down_total = ordered(share_down, twin(share_down), 1)

    def by_micro(store, name):
        return jnp.stack(
            [jnp.where(is_first, store[m][name], store[m + 1][name]) for m in range(micros)]
        )[None, None]

    return (
        by_micro(saved, "output_b"),
        by_micro(backs, "layer_grad"),
        tail_total[:, experts][None],
        qkv_total[:, :, :group_width].reshape(1, rows_per, head_width),
        qkv_total[:, :, group_width : group_width + HD].reshape(1, rows_per, key_width),
        qkv_total[:, :, group_width + HD :].reshape(1, rows_per, key_width),
        out_total[None],
        tail_total[:, experts + 1][None],
        tail_total[:, :experts][None],
        mine_of(share_gate_up, other_gate_up)[None],
        mine_of(other_gate_up, share_gate_up)[None],
        down_total[None],
        expert_grads[0][None],
        expert_grads[1][None],
        expert_grads[2][None],
    )


def solution(mesh):
    rows = P("section", "shard", None)
    vector = P("section", "shard")
    expert = P("section", "shard", None, None)
    tokens = P("dp", None, "shard", None)
    section_tokens = P("section", "dp", None, "shard", None)
    weights = (vector, rows, rows, rows, rows, vector, rows, rows, rows, rows) + (expert,) * 3
    return jax.shard_map(
        body,
        mesh=mesh,
        in_specs=(tokens, tokens, section_tokens) + weights,
        out_specs=(section_tokens, section_tokens) + weights,
        check_vma=False,
    )
```

```python
import functools

import jax
import jax.numpy as jnp
from jax import lax
from jax.experimental import pallas as pl
from jax.experimental.pallas import tpu as pltpu
from jax.sharding import PartitionSpec as P

H = 12
KVH = 4
HD = 128
GROUP = H // KVH
TOPK = 6
CAP = 8

epsilon = 1e-05
masked_score = -1e30
scaling = HD ** (-0.5)
log2_scale = scaling * 1.4426950408889634
bf = jnp.bfloat16
f32 = jnp.float32
VMEM_LIMIT = 32 * 1024 * 1024


def inverse_rms(rows):
    return lax.rsqrt(jnp.mean(rows * rows, axis=-1, keepdims=True) + epsilon)


def norm_back(layer_in, gain, upstream):
    inverse = inverse_rms(layer_in)
    unit_rows = layer_in * inverse
    gain_grad = jnp.sum(upstream * unit_rows, axis=0)
    scaled = upstream * gain
    in_grad = inverse * (scaled - unit_rows * jnp.mean(scaled * unit_rows, axis=-1, keepdims=True))
    return (in_grad, gain_grad)


def silu_parts(argument):
    sigmoid = jax.nn.sigmoid(argument)
    return argument * sigmoid, sigmoid * (1.0 + argument * (1.0 - sigmoid))


def dot(left_side, right_side):
    return jnp.dot(left_side, right_side, preferred_element_type=f32)


def dot_nt(left_side, right_side):
    return lax.dot_general(
        left_side, right_side, (((1,), (1,)), ((), ())), preferred_element_type=f32
    )


def dot_tn(left_side, right_side):
    return lax.dot_general(
        left_side, right_side, (((0,), (0,)), ((), ())), preferred_element_type=f32
    )


def wide_einsum(formula, left_side, right_side):
    return jnp.einsum(formula, left_side, right_side, preferred_element_type=f32)


def arrival(info_ref, parts, part):
    return lax.rem(info_ref[2] + parts - part, parts)


def stacked_heads(ref, at):
    return jnp.concatenate([ref[at, :, g * HD : (g + 1) * HD] for g in range(GROUP)], axis=0)


def store_heads(ref, at, rows):
    block = ref.shape[1]
    for g in range(GROUP):
        ref[at, :, g * HD : (g + 1) * HD] = rows[g * block : (g + 1) * block]


def cached(ref, span, column):
    rows = ref[:, span, column : column + HD]
    return rows.reshape(rows.shape[0] * rows.shape[1], HD)


def block_span(at, block):
    return pl.ds(pl.multiple_of(at * block, block), block)


def diagonal_mask(rows, chunk, block, zy):
    key_at = lax.broadcasted_iota(jnp.int32, (rows, chunk), 1)
    row_at = lax.broadcasted_iota(jnp.int32, (rows, chunk), 0)
    return key_at <= zy * block + lax.rem(row_at, block)


def all_heads(ref, ats):
    return jnp.concatenate([stacked_heads(ref, at) for at in ats], axis=0)


def added_from(total, first, value):
    if first == 0:
        return total + value
    return jnp.concatenate([total[:first], total[first:] + value], axis=0)


def masked_first(mask, value, fill):
    count = mask.shape[0]
    own = jnp.where(mask, value[:count], fill)
    return own if value.shape[0] == count else jnp.concatenate([own, value[count:]], axis=0)


def attention_forward_kernel(has_prev, info_ref, q_ref, *refs):
    prev_ref = refs[0] if has_prev else None
    cur_ref, o_ref, log_ref = refs[-3:]
    parts, block, _ = q_ref.shape
    rows = GROUP * block
    mask = diagonal_mask(rows, cur_ref.shape[0] * block, block, info_ref[0])
    ats = [arrival(info_ref, parts, part) for part in range(parts)]
    queries = all_heads(q_ref, ats)
    pieces = []
    if has_prev:
        bias = jnp.where(info_ref[1] > 0, 0.0, masked_score).astype(f32)
        everything = slice(None)
        scores = dot_nt(queries, cached(prev_ref, everything, 0)) + bias
        pieces.append((scores, prev_ref, everything, 0))
    for part in range(parts):
        span, first = block_span(ats[part], block), part * rows
        scores = dot_nt(queries[first:], cached(cur_ref, span, 0))
        pieces.append((masked_first(mask, scores, masked_score), cur_ref, span, first))
    peaks = []
    for part in range(parts):
        at = part * rows
        tops = [
            jnp.max(scores[at - first : at - first + rows], axis=-1, keepdims=True)
            for scores, _, _, first in pieces
            if first <= at
        ]
        peaks.append(functools.reduce(jnp.maximum, tops))
    peak = jnp.concatenate(peaks, axis=0) * log2_scale
    total = jnp.zeros((parts * rows, 1), f32)
    mixed = jnp.zeros((parts * rows, HD), f32)
    for scores, ref, span, first in pieces:
        probs = jnp.exp2(scores * log2_scale - peak[first:])
        total = added_from(total, first, jnp.sum(probs, axis=-1, keepdims=True))
        mixed = added_from(mixed, first, dot(probs.astype(bf), cached(ref, span, HD)))
    out = (mixed / total).astype(bf)
    log_total = peak + jnp.log2(total)
    for part, at in enumerate(ats):
        store_heads(o_ref, at, out[part * rows : (part + 1) * rows])
        log_ref[at] = jnp.broadcast_to(log_total[part * rows : (part + 1) * rows], (rows, HD))


def attention_backward_kernel(has_prev, has_carry, info_ref, q_ref, do_ref, o_ref, log_ref, *refs):
    refs = list(refs)
    carry_ref = refs.pop(0) if has_carry else None
    prev_ref = refs.pop(0) if has_prev else None
    cur_ref, dq_ref, dcur_ref = refs[:3]
    dprev_ref = refs[3] if has_prev else None
    parts, block, _ = q_ref.shape
    ring = cur_ref.shape[0]
    rows = GROUP * block
    mask = diagonal_mask(rows, ring * block, block, info_ref[0])
    ats = [arrival(info_ref, parts, part) for part in range(parts)]
    queries, out_grad = all_heads(q_ref, ats), all_heads(do_ref, ats)
    out = all_heads(o_ref, ats)
    inner = jnp.sum(out_grad.astype(f32) * out.astype(f32), axis=-1, keepdims=True)
    log_total = jnp.concatenate([log_ref[at][:, :1] for at in ats], axis=0)

    def one_block(ref, span, first, log_rows, own_block):
        keys, values = cached(ref, span, 0), cached(ref, span, HD)
        some, some_grad = queries[first:], out_grad[first:]
        probs = jnp.exp2(dot_nt(some, keys) * log2_scale - log_rows[first:])
        if own_block:
            probs = masked_first(mask, probs, 0.0)
        score_grad = (probs * (dot_nt(some_grad, values) - inner[first:])).astype(bf)
        key_grad = dot_tn(score_grad, some) * scaling
        value_grad = dot_tn(probs.astype(bf), some_grad)
        shape = (ring, block, HD)
        return dot(score_grad, keys), key_grad.reshape(shape), value_grad.reshape(shape)

    query_grad = jnp.zeros((parts * rows, HD), f32)
    if has_prev:
        log_prev = log_total + jnp.where(info_ref[1] > 0, 0.0, -masked_score).astype(f32)
        for part in range(parts):
            span = slice(part * block, (part + 1) * block)
            more, key_grad, value_grad = one_block(prev_ref, span, 0, log_prev, False)
            query_grad = query_grad + more
            dprev_ref[:, span, :HD] = key_grad
            dprev_ref[:, span, HD:] = value_grad
    for part in range(parts):
        span = block_span(ats[part], block)
        more, key_grad, value_grad = one_block(cur_ref, span, part * rows, log_total, True)
        query_grad = added_from(query_grad, part * rows, more)
        if has_carry:
            key_grad = key_grad + carry_ref[:, span, :HD]
            value_grad = value_grad + carry_ref[:, span, HD:]
        dcur_ref[:, span, :HD] = key_grad.astype(bf)
        dcur_ref[:, span, HD:] = value_grad.astype(bf)
    query_grad = (query_grad * scaling).astype(bf)
    for part, at in enumerate(ats):
        store_heads(dq_ref, at, query_grad[part * rows : (part + 1) * rows])


def attention_call(kernel, factor, out_shape, info, queries, *rest):
    parts, block, _ = queries.shape
    rows = parts * GROUP * block
    keys = sum(ref.shape[0] * ref.shape[1] for ref in rest if ref.shape == rest[-1].shape)
    in_vmem = pl.BlockSpec(memory_space=pltpu.VMEM)
    return pl.pallas_call(
        kernel,
        out_shape=out_shape,
        in_specs=[pl.BlockSpec(memory_space=pltpu.SMEM)] + [in_vmem] * (1 + len(rest)),
        out_specs=(in_vmem,) * len(out_shape),
        compiler_params=pltpu.CompilerParams(vmem_limit_bytes=VMEM_LIMIT),
        cost_estimate=pl.CostEstimate(
            flops=factor * rows * keys * HD,
            bytes_accessed=factor * (keys + rows) * HD,
            transcendentals=rows * keys // 2,
        ),
    )(info, queries, *rest)


def attention_forward(info, qkv, prev, cur):
    parts, block, _ = qkv.shape
    shapes = (
        jax.ShapeDtypeStruct((parts, block, GROUP * HD), bf),
        jax.ShapeDtypeStruct((parts, GROUP * block, HD), f32),
    )
    caches = (cur,) if prev is None else (prev, cur)
    kernel = functools.partial(attention_forward_kernel, prev is not None)
    return attention_call(kernel, 2, shapes, info, qkv, *caches)


def attention_backward(info, qkv, out_grad, out, logs, carry, prev, cur):
    shapes = (jax.ShapeDtypeStruct(out.shape, bf), jax.ShapeDtypeStruct(cur.shape, bf))
    if prev is not None:
        shapes += (jax.ShapeDtypeStruct(cur.shape, f32),)
    extra = tuple(value for value in (carry, prev) if value is not None)
    kernel = functools.partial(attention_backward_kernel, prev is not None, carry is not None)
    return attention_call(kernel, 5, shapes, info, qkv, out_grad, out, logs, *extra, cur)


def body(
    inputs,
    cotangent,
    routes,
    norm_attn,
    w_query,
    w_key,
    w_value,
    w_output,
    norm_ffn,
    w_router,
    shared_gate,
    shared_up,
    shared_down,
    expert_gate,
    expert_up,
    expert_down,
):
    micros, block, width = inputs.shape[1:]
    shards = lax.axis_size("shard")
    section = lax.axis_index("section")
    core = lax.axis_index("dp")
    position = lax.axis_index("shard")
    heads = KVH
    ring = shards // heads
    local_experts = expert_gate.shape[1]
    experts = local_experts * shards
    slots = experts * CAP
    rows_per = w_query.shape[1]
    half_rows = rows_per // 2
    group_width = GROUP * HD
    head_width = H * HD
    key_width = KVH * HD
    part_width = group_width + 2 * HD
    shared_width = shared_gate.shape[2]
    down_rows = shared_down.shape[1]
    is_first = section == 0
    low_core = core == 0
    zy_groups = [[x * ring + zy for zy in range(ring)] for x in range(heads)]

    def exchange(value, groups=None):
        return lax.all_to_all(
            value, "shard", split_axis=0, concat_axis=0, tiled=True, axis_index_groups=groups
        )

    def copies(value, count):
        return jnp.broadcast_to(value[None], (count,) + value.shape)

    def twin(value):
        return lax.ppermute(value, "dp", [(0, 1), (1, 0)])

    def mine_of(low_half, high_half):
        return jnp.where(low_core, low_half, high_half)

    def ordered(own, other, axis):
        low_half, high_half = mine_of(own, other), mine_of(other, own)
        return jnp.concatenate([low_half, high_half], axis=axis)

    def ordered_by(in_order, own, other):
        return jnp.stack([jnp.where(in_order, own, other), jnp.where(in_order, other, own)])

    def halves(value):
        half = value.shape[-1] // 2
        return value[..., :half], value[..., half:]

    def my_rows(value):
        return mine_of(value[..., :half_rows, :], value[..., half_rows:, :])

    tail = jnp.concatenate(
        [
            w_router[0],
            norm_attn[0][:, None],
            norm_ffn[0][:, None],
            jnp.zeros((rows_per, 128 - experts - 2), bf),
        ],
        axis=1,
    )
    by_head = jnp.concatenate(
        [
            w_query[0].reshape(rows_per, heads, group_width),
            w_key[0].reshape(rows_per, heads, HD),
            w_value[0].reshape(rows_per, heads, HD),
            jnp.broadcast_to(tail[:, None], (rows_per, heads, 128)),
        ],
        axis=2,
    ).transpose(1, 0, 2)
    by_head = my_rows(by_head)
    by_head = jnp.broadcast_to(
        by_head[:, None], (heads, ring, half_rows, part_width + 128)
    ).reshape(shards, half_rows, part_width + 128)
    down_half = down_rows // 2
    down_flat = (half_rows, down_half * width // half_rows)
    packed = jnp.concatenate(
        [
            my_rows(jnp.concatenate([shared_gate[0], shared_up[0]], axis=1)),
            mine_of(shared_down[0][:down_half], shared_down[0][down_half:]).reshape(down_flat),
        ],
        axis=1,
    )
    by_head, packed = lax.optimization_barrier((by_head, packed))
    gathered = lax.all_gather(packed, "shard")
    own_part = exchange(by_head)
    out_rows = my_rows(w_output[0])
    out_rows = ordered_by(
        position % 2 == 0, out_rows, lax.ppermute(out_rows, "shard", [(p, p ^ 1) for p in range(shards)])
    )
    out_parts = [out_rows] + [
        lax.ppermute(
            out_rows,
            "shard",
            [(p, p // ring * ring + (p % ring - 2 * k) % ring) for p in range(shards)],
        )
        for k in range(1, ring // 2)
    ]
    own_part, *out_parts = lax.optimization_barrier((own_part, *out_parts))
    own_out = lax.dynamic_slice_in_dim(
        jnp.concatenate(out_parts + out_parts), ring - position % ring // 2 * 2, ring, axis=0
    )
    output_w = ordered(own_out, twin(own_out), 1).reshape(group_width, width)
    fetched = ordered(own_part, twin(own_part), 1).reshape(width, part_width + 128)
    qkv_w, tail = fetched[:, :part_width], fetched[:, part_width:]
    router_w = tail[:, :experts]
    gains = tail[:, experts : experts + 2].T.astype(f32)
    gain_one, gain_two = gains[0][None], gains[1][None]

    expert_g, expert_u, expert_d = expert_gate[0], expert_up[0], expert_down[0]
    slot_of = jnp.arange(slots, dtype=jnp.int32)
    expert_of = jnp.arange(experts, dtype=jnp.int32)
    row_of = jnp.arange(block, dtype=jnp.int32)
    spread = (expert_of[:, None] == slot_of[None, :] // CAP).astype(bf)
    router_slots = dot(router_w, spread).astype(bf)
    earlier = (row_of[:, None] > row_of[None, :]).astype(bf)

    def slot_table(route_rows):
        named = jnp.any(route_rows[:, :, None] == expert_of[None, None, :], axis=1).astype(bf)
        slot_ids = dot(earlier, named).astype(bf)
        return (dot(named, spread) > 0.5) & (
            dot(slot_ids, spread).astype(jnp.int32) == (slot_of % CAP)[None, :]
        )

    here = [position % ring, jnp.ones_like(position), position // ring]
    info_all = jnp.stack(here).astype(jnp.int32)
    info = jnp.stack([here[0], is_first.astype(here[0].dtype), here[2]]).astype(jnp.int32)

    def gate_values(normed_two, table):
        logits = jnp.where(table, dot(normed_two, router_slots), masked_score)
        weights = jnp.exp(logits - jnp.max(logits, axis=-1, keepdims=True))
        weights = jnp.where(table, weights, 0.0)
        return weights / jnp.sum(weights, axis=-1, keepdims=True)

    def high_low(value):
        high = value.astype(bf)
        return high, (value - high.astype(f32)).astype(bf)

    def to_experts(rows):
        return (
            exchange(rows.reshape(shards, local_experts, CAP, width))
            .transpose(1, 0, 2, 3)
            .reshape(local_experts, shards * CAP, width)
        )

    def from_experts(rows):
        return exchange(
            rows.reshape(local_experts, shards, CAP, width).transpose(1, 0, 2, 3)
        ).reshape(slots, width)

    def moved(p, steps):
        return (p // ring + steps) % heads * ring + p % ring

    def shift_x(value, steps):
        return lax.ppermute(value, "shard", [(p, moved(p, steps)) for p in range(shards)])

    def next_ring(value):
        return jnp.stack(
            [
                lax.ppermute(
                    value,
                    ("section", "shard"),
                    [(p, shards + moved(p, steps)) for p in range(shards)],
                )
                for steps in range(heads)
            ]
        )

    def sum_over_x(rows):
        parts = rows.reshape(heads, block, width)
        away = [shift_x(parts[k].astype(bf), -k).astype(f32) for k in range(1, heads)]
        return sum(away, parts[0])

    def ring_rows(rows):
        return jnp.concatenate([rows] + [shift_x(rows, k) for k in range(1, heads)], axis=0)

    ring_inputs = [
        jnp.stack([inputs[0, m]] + [shift_x(inputs[0, m], k) for k in range(1, heads)])
        for m in range(micros)
    ]

    def shared_weights(gathered):
        gate_up = gathered[:, :, : 2 * shared_width]
        down = gathered[:, :, 2 * shared_width :].reshape(shards, down_half, width)
        return (
            ordered(gate_up, twin(gate_up), 1).reshape(width, 2 * shared_width),
            ordered(down, twin(down), 1).reshape(shards * down_rows, width),
        )

    def forward(moment, received, previous, shared_pair):
        first_micro = min(moment, micros - 1)
        second_micro = max(moment - 1, 0)
        ring_b = jnp.where(is_first, ring_inputs[first_micro], received)
        layer_b = ring_b[0]
        table = slot_table(
            jnp.where(is_first, routes[0, 0, first_micro], routes[0, 0, second_micro])
        )
        pick = table.astype(bf)
        layer_in = layer_b.astype(f32)
        ring_in = ring_b.reshape(heads * block, width).astype(f32)
        ring_one = (ring_in * inverse_rms(ring_in) * gain_one).astype(bf)
        qkv = dot(ring_one, qkv_w).astype(bf)
        cache = exchange(copies(qkv[:, group_width:], ring), zy_groups)
        qkv = qkv.reshape(heads, block, part_width)
        attn_info = info if moment == 1 else info_all
        attended, logs = attention_forward(attn_info, qkv, previous, cache)
        attended_rows = attended.reshape(heads * block, group_width)
        hidden = layer_in + sum_over_x(dot(attended_rows, output_w))
        if shared_pair is None:
            arrived, hidden = lax.optimization_barrier((gathered, hidden))
            shared_pair = shared_weights(arrived)
        gate_up_w, down_w = shared_pair
        normed_two = (hidden * inverse_rms(hidden) * gain_two).astype(bf)
        gates = gate_values(normed_two, table)
        expert_in = to_experts(dot_tn(pick, normed_two).astype(bf))
        gate_pre = wide_einsum("erd,edf->erf", expert_in, expert_g)
        up_pre = wide_einsum("erd,edf->erf", expert_in, expert_u)
        activated = (silu_parts(gate_pre)[0] * up_pre).astype(bf)
        returned = from_experts(wide_einsum("erf,efd->erd", activated, expert_d).astype(bf))
        high, low = high_low(gates)
        routed = dot(high, returned) + dot(low, returned)
        shared_gate_pre, shared_up_pre = halves(dot(normed_two, gate_up_w))
        shared_act = (silu_parts(shared_gate_pre)[0] * shared_up_pre).astype(bf)
        beside = lax.optimization_barrier(hidden + dot(shared_act, down_w))
        output_b = (beside + routed).astype(bf)
        return dict(
            layer_b=layer_b,
            pick=pick,
            ring_one=ring_one,
            qkv=qkv,
            cache=cache,
            previous=previous,
            info=attn_info,
            attended=attended,
            logs=logs,
            hidden=hidden,
            normed_two=normed_two,
            gates=gates,
            expert_in=expert_in,
            gate_pre=gate_pre,
            up_pre=up_pre,
            activated=activated,
            returned=returned,
            shared_gate_pre=shared_gate_pre,
            shared_up_pre=shared_up_pre,
            shared_act=shared_act,
            output_b=output_b,
            shared_pair=shared_pair,
        )

    def ffn_backward(kept, upstream_b):
        upstream = upstream_b.astype(f32)
        gates, hidden = kept["gates"], kept["hidden"]
        gate_up_w, down_w = kept["shared_pair"]
        high, low = high_low(gates)
        outgoing = dot_tn(high, upstream_b) + dot_tn(low, upstream_b)
        expert_grad = to_experts(outgoing.astype(bf))
        act_silu, act_slope = silu_parts(kept["gate_pre"])
        act_grad = wide_einsum("erd,efd->erf", expert_grad, expert_d)
        gate_pre_grad = (act_grad * kept["up_pre"] * act_slope).astype(bf)
        up_pre_grad = (act_grad * act_silu).astype(bf)
        expert_in_grad = (
            wide_einsum("erf,edf->erd", gate_pre_grad, expert_g)
            + wide_einsum("erf,edf->erd", up_pre_grad, expert_u)
        ).astype(bf)
        returned_grad = from_experts(expert_in_grad)
        shared_act_grad = dot_nt(upstream_b, down_w)
        shared_silu, shared_slope = silu_parts(kept["shared_gate_pre"])
        shared_gate_grad = (shared_act_grad * kept["shared_up_pre"] * shared_slope).astype(bf)
        shared_up_grad = (shared_act_grad * shared_silu).astype(bf)
        normed_two_grad = dot_nt(
            jnp.concatenate([shared_gate_grad, shared_up_grad], axis=1), gate_up_w
        )
        gate_grad = dot_nt(upstream_b, kept["returned"])
        picked_grad = gates * (gate_grad - jnp.sum(gates * gate_grad, axis=1, keepdims=True))
        picked_b = picked_grad.astype(bf)
        normed_two_grad = normed_two_grad + dot_nt(picked_b, router_slots)
        normed_two_grad = lax.optimization_barrier(normed_two_grad)
        normed_two_grad = normed_two_grad + dot(kept["pick"], returned_grad)
        logit_grad = dot_nt(picked_b, spread).astype(bf)
        hidden_norm_grad, gain_two_grad = norm_back(hidden, gain_two, normed_two_grad)
        return dict(
            hidden_grad=upstream + hidden_norm_grad,
            upstream_b=upstream_b,
            expert_grad=expert_grad,
            gate_pre_grad=gate_pre_grad,
            up_pre_grad=up_pre_grad,
            shared_gate_grad=shared_gate_grad,
            shared_up_grad=shared_up_grad,
            logit_grad=logit_grad,
            gain_two_grad=gain_two_grad,
        )

    def attention_back(kept, grads, carried):
        ring_hidden = ring_rows(grads["hidden_grad"].astype(bf))
        out_grad = dot_nt(ring_hidden, output_w).astype(bf)
        results = attention_backward(
            kept["info"],
            kept["qkv"],
            out_grad.reshape(heads, block, group_width),
            kept["attended"],
            kept["logs"],
            carried,
            kept["previous"],
            kept["cache"],
        )
        carried = results[2] if len(results) > 2 else None
        query_grad = results[0].reshape(heads * block, group_width)
        query_part = lax.optimization_barrier(dot_nt(query_grad, qkv_w[:, :group_width]))
        pair_grad = jnp.sum(exchange(results[1], zy_groups).astype(f32), axis=0).astype(bf)
        qkv_grad = jnp.concatenate([query_grad, pair_grad], axis=1)
        normed_one_grad = sum_over_x(query_part + dot_nt(pair_grad, qkv_w[:, group_width:]))
        in_norm_grad, gain_one_grad = norm_back(
            kept["layer_b"].astype(f32), gain_one, normed_one_grad
        )
        grads = dict(
            grads,
            ring_hidden=ring_hidden,
            qkv_grad=qkv_grad,
            gain_one_grad=gain_one_grad,
            layer_grad=(grads["hidden_grad"] + in_norm_grad).astype(bf),
        )
        return grads, carried

    nothing = jnp.zeros((block, width), bf)
    saved = []
    received, previous, shared_pair = jnp.zeros((heads, block, width), bf), None, None
    for moment in range(micros + 1):
        kept = forward(moment, received, previous, shared_pair)
        shared_pair = kept["shared_pair"]
        saved.append(kept)
        previous = kept["cache"]
        if moment < micros:
            received = next_ring(kept["output_b"])
    backs = [None] * (micros + 1)
    received, carried = nothing, None
    for source in range(micros, -1, -1):
        own = cotangent[0, source - 1] if source > 0 else nothing
        upstream_b = jnp.where(is_first, received, own)
        grads = ffn_backward(saved[source], upstream_b)
        backs[source], carried = attention_back(saved[source], grads, carried)
        if source > 0:
            received = lax.ppermute(backs[source]["layer_grad"], "section", [(1, 0)])

    def live(name, store, axis):
        ends = jnp.where(is_first, store[0][name], store[micros][name])
        return jnp.concatenate([ends, store[1][name]], axis=axis)

    def kept_rows(name, axis=0):
        return live(name, saved, axis)

    def back_rows(name, axis=0):
        return live(name, backs, axis)

    expert_parts = [
        wide_einsum("erd,erf->edf", kept_rows("expert_in", 1), back_rows("gate_pre_grad", 1)),
        wide_einsum("erd,erf->edf", kept_rows("expert_in", 1), back_rows("up_pre_grad", 1)),
        wide_einsum("erf,erd->efd", kept_rows("activated", 1), back_rows("expert_grad", 1)),
    ]
    expert_parts = [part.astype(bf) for part in expert_parts]
    expert_others = [twin(part) for part in expert_parts]

    def both(value):
        return jnp.concatenate([value, twin(value)], axis=0)

    def both_halves(low_half, high_half):
        own, other = mine_of(low_half, high_half), mine_of(high_half, low_half)
        return jnp.concatenate([own, twin(other)], axis=0)

    normed_two = kept_rows("normed_two")
    grad_gate_up = dot_tn(
        both(normed_two), both_halves(back_rows("shared_gate_grad"), back_rows("shared_up_grad"))
    )
    grad_down = dot_tn(both(kept_rows("shared_act")), both_halves(*halves(back_rows("upstream_b"))))


    def shift_z(value, steps):
        pairs = [(p, p // ring * ring + (p % ring + 2 * steps) % ring) for p in range(shards)]
        return lax.ppermute(value, "shard", pairs)

    def shift_y(value, steps):
        return lax.ppermute(value, "shard", [(p, p ^ 1) for p in range(shards)])

    along = dict(
        x=(shift_x, position // ring), z=(shift_z, position % ring // 2), y=(shift_y, position % 2)
    )

    def reduced(value, name, axis, held_as=bf):
        shift, here = along[name]
        count = value.shape[axis]

        def piece(steps):
            return lax.dynamic_index_in_dim(value, (here + steps) % count, axis, keepdims=False)

        total = piece(0).astype(f32)
        for steps in range(1, count):
            total = total + shift(piece(steps), steps).astype(f32)
        return total.astype(held_as)

    grad_out = dot_tn(
        kept_rows("attended").reshape(micros * heads * block, group_width),
        back_rows("ring_hidden"),
    )
    grad_qkv = dot_tn(kept_rows("ring_one"), back_rows("qkv_grad"))
    grad_router = dot_tn(normed_two, back_rows("logit_grad"))
    gain_sums = jnp.stack(
        [sum(grads[name] for grads in backs) for name in ("gain_one_grad", "gain_two_grad")]
    )
    grad_tail = jnp.concatenate(
        [grad_router, gain_sums.T, jnp.zeros((width, 128 - experts - 2), f32)], axis=1
    )
    grad_qkv = jnp.concatenate([grad_qkv, grad_tail], axis=1)
    grad_qkv = grad_qkv.astype(bf).reshape(shards, rows_per, part_width + 128)
    (
        grad_qkv,
        grad_gate_up,
        grad_down,
        grad_out,
        last_grad,
        *expert_others,
    ) = lax.optimization_barrier(
        (
            grad_qkv,
            grad_gate_up.astype(bf),
            grad_down.astype(bf),
            grad_out.astype(bf),
            backs[0]["layer_grad"],
            *expert_others,
        )
    )
    backs[0]["layer_grad"] = last_grad
    pieces = exchange(grad_qkv)
    attention_pieces, grad_out = lax.optimization_barrier((pieces, grad_out))
    expert_grads = [
        part.astype(f32) + other.astype(f32) for part, other in zip(expert_parts, expert_others)
    ]
    pieces = grad_gate_up.reshape(heads, ring // 2, 2, rows_per, shared_width)
    share_gate_up = reduced(reduced(reduced(pieces, "x", 0), "z", 0), "y", 0, f32)
    pieces = grad_down.reshape(heads, ring // 2, 2, down_rows, width // 2)
    share_down = reduced(reduced(reduced(pieces, "z", 1), "x", 0), "y", 0, f32)

    share_out = jnp.sum(
        exchange(grad_out.reshape(ring, rows_per, width), zy_groups).astype(f32), axis=0
    )
    attention_pieces = attention_pieces.astype(f32)
    share_qkv = jnp.sum(
        attention_pieces[:, :, :part_width].reshape(heads, ring, rows_per, part_width), axis=1
    )
    share_qkv = share_qkv.transpose(1, 0, 2)
    share_tail = jnp.sum(attention_pieces[:, :, part_width:], axis=0)

    def total(share):
        return share + twin(share)

    out_total, qkv_total, tail_total = total(share_out), total(share_qkv), total(share_tail)
    other_gate_up = twin(share_gate_up)
    down_total = ordered(share_down, twin(share_down), 1)

    def by_micro(store, name):
        return jnp.stack(
            [jnp.where(is_first, store[m][name], store[m + 1][name]) for m in range(micros)]
        )[None, None]

    return (
        by_micro(saved, "output_b"),
        by_micro(backs, "layer_grad"),
        tail_total[:, experts][None],
        qkv_total[:, :, :group_width].reshape(1, rows_per, head_width),
        qkv_total[:, :, group_width : group_width + HD].reshape(1, rows_per, key_width),
        qkv_total[:, :, group_width + HD :].reshape(1, rows_per, key_width),
        out_total[None],
        tail_total[:, experts + 1][None],
        tail_total[:, :experts][None],
        mine_of(share_gate_up, other_gate_up)[None],
        mine_of(other_gate_up, share_gate_up)[None],
        down_total[None],
        expert_grads[0][None],
        expert_grads[1][None],
        expert_grads[2][None],
    )


def solution(mesh):
    rows = P("section", "shard", None)
    vector = P("section", "shard")
    expert = P("section", "shard", None, None)
    tokens = P("dp", None, "shard", None)
    section_tokens = P("section", "dp", None, "shard", None)
    weights = (vector, rows, rows, rows, rows, vector, rows, rows, rows, rows) + (expert,) * 3
    return jax.shard_map(
        body,
        mesh=mesh,
        in_specs=(tokens, tokens, section_tokens) + weights,
        out_specs=(section_tokens, section_tokens) + weights,
        check_vma=False,
    )
```

```python
import functools

import jax
import jax.numpy as jnp
from jax import lax
from jax.experimental import pallas as pl
from jax.experimental.pallas import tpu as pltpu
from jax.sharding import PartitionSpec as P

H = 12
KVH = 4
HD = 128
GROUP = H // KVH
TOPK = 6
CAP = 8

epsilon = 1e-05
masked_score = -1e30
scaling = HD ** (-0.5)
log2_scale = scaling * 1.4426950408889634
bf = jnp.bfloat16
f32 = jnp.float32
VMEM_LIMIT = 32 * 1024 * 1024


def inverse_rms(rows):
    return lax.rsqrt(jnp.mean(rows * rows, axis=-1, keepdims=True) + epsilon)


def norm_back(layer_in, gain, upstream):
    inverse = inverse_rms(layer_in)
    unit_rows = layer_in * inverse
    gain_grad = jnp.sum(upstream * unit_rows, axis=0)
    scaled = upstream * gain
    in_grad = inverse * (scaled - unit_rows * jnp.mean(scaled * unit_rows, axis=-1, keepdims=True))
    return (in_grad, gain_grad)


def silu_parts(argument):
    sigmoid = jax.nn.sigmoid(argument)
    return argument * sigmoid, sigmoid * (1.0 + argument * (1.0 - sigmoid))


def dot(left_side, right_side):
    return jnp.dot(left_side, right_side, preferred_element_type=f32)


def dot_nt(left_side, right_side):
    return lax.dot_general(
        left_side, right_side, (((1,), (1,)), ((), ())), preferred_element_type=f32
    )


def dot_tn(left_side, right_side):
    return lax.dot_general(
        left_side, right_side, (((0,), (0,)), ((), ())), preferred_element_type=f32
    )


def wide_einsum(formula, left_side, right_side):
    return jnp.einsum(formula, left_side, right_side, preferred_element_type=f32)


def arrival(info_ref, parts, part):
    return lax.rem(info_ref[2] + parts - part, parts)


def stacked_heads(ref, at):
    return jnp.concatenate([ref[at, :, g * HD : (g + 1) * HD] for g in range(GROUP)], axis=0)


def store_heads(ref, at, rows):
    block = ref.shape[1]
    for g in range(GROUP):
        ref[at, :, g * HD : (g + 1) * HD] = rows[g * block : (g + 1) * block]


def cached(ref, span, column):
    rows = ref[:, span, column : column + HD]
    return rows.reshape(rows.shape[0] * rows.shape[1], HD)


def block_span(at, block):
    return pl.ds(pl.multiple_of(at * block, block), block)


def diagonal_mask(rows, chunk, block, zy):
    key_at = lax.broadcasted_iota(jnp.int32, (rows, chunk), 1)
    row_at = lax.broadcasted_iota(jnp.int32, (rows, chunk), 0)
    return key_at <= zy * block + lax.rem(row_at, block)


def all_heads(ref, ats):
    return jnp.concatenate([stacked_heads(ref, at) for at in ats], axis=0)


def added_from(total, first, value):
    if first == 0:
        return total + value
    return jnp.concatenate([total[:first], total[first:] + value], axis=0)


def masked_first(mask, value, fill):
    count = mask.shape[0]
    own = jnp.where(mask, value[:count], fill)
    return own if value.shape[0] == count else jnp.concatenate([own, value[count:]], axis=0)


def attention_forward_kernel(has_prev, info_ref, q_ref, *refs):
    prev_ref = refs[0] if has_prev else None
    cur_ref, o_ref, log_ref = refs[-3:]
    parts, block, _ = q_ref.shape
    rows = GROUP * block
    mask = diagonal_mask(rows, cur_ref.shape[0] * block, block, info_ref[0])
    ats = [arrival(info_ref, parts, part) for part in range(parts)]
    queries = all_heads(q_ref, ats)
    pieces = []
    if has_prev:
        bias = jnp.where(info_ref[1] > 0, 0.0, masked_score).astype(f32)
        everything = slice(None)
        scores = dot_nt(queries, cached(prev_ref, everything, 0)) + bias
        pieces.append((scores, prev_ref, everything, 0))
    for part in range(parts):
        span, first = block_span(ats[part], block), part * rows
        scores = dot_nt(queries[first:], cached(cur_ref, span, 0))
        pieces.append((masked_first(mask, scores, masked_score), cur_ref, span, first))
    peaks = []
    for part in range(parts):
        at = part * rows
        tops = [
            jnp.max(scores[at - first : at - first + rows], axis=-1, keepdims=True)
            for scores, _, _, first in pieces
            if first <= at
        ]
        peaks.append(functools.reduce(jnp.maximum, tops))
    peak = jnp.concatenate(peaks, axis=0) * log2_scale
    total = jnp.zeros((parts * rows, 1), f32)
    mixed = jnp.zeros((parts * rows, HD), f32)
    for scores, ref, span, first in pieces:
        probs = jnp.exp2(scores * log2_scale - peak[first:])
        total = added_from(total, first, jnp.sum(probs, axis=-1, keepdims=True))
        mixed = added_from(mixed, first, dot(probs.astype(bf), cached(ref, span, HD)))
    out = (mixed / total).astype(bf)
    log_total = peak + jnp.log2(total)
    for part, at in enumerate(ats):
        store_heads(o_ref, at, out[part * rows : (part + 1) * rows])
        log_ref[at] = jnp.broadcast_to(log_total[part * rows : (part + 1) * rows], (rows, HD))


def attention_backward_kernel(has_prev, has_carry, info_ref, q_ref, do_ref, o_ref, log_ref, *refs):
    refs = list(refs)
    carry_ref = refs.pop(0) if has_carry else None
    prev_ref = refs.pop(0) if has_prev else None
    cur_ref, dq_ref, dcur_ref = refs[:3]
    dprev_ref = refs[3] if has_prev else None
    parts, block, _ = q_ref.shape
    ring = cur_ref.shape[0]
    rows = GROUP * block
    mask = diagonal_mask(rows, ring * block, block, info_ref[0])
    ats = [arrival(info_ref, parts, part) for part in range(parts)]
    queries, out_grad = all_heads(q_ref, ats), all_heads(do_ref, ats)
    out = all_heads(o_ref, ats)
    inner = jnp.sum(out_grad.astype(f32) * out.astype(f32), axis=-1, keepdims=True)
    log_total = jnp.concatenate([log_ref[at][:, :1] for at in ats], axis=0)

    def one_block(ref, span, first, log_rows, own_block):
        keys, values = cached(ref, span, 0), cached(ref, span, HD)
        some, some_grad = queries[first:], out_grad[first:]
        probs = jnp.exp2(dot_nt(some, keys) * log2_scale - log_rows[first:])
        if own_block:
            probs = masked_first(mask, probs, 0.0)
        score_grad = (probs * (dot_nt(some_grad, values) - inner[first:])).astype(bf)
        key_grad = dot_tn(score_grad, some) * scaling
        value_grad = dot_tn(probs.astype(bf), some_grad)
        shape = (ring, block, HD)
        return dot(score_grad, keys), key_grad.reshape(shape), value_grad.reshape(shape)

    query_grad = jnp.zeros((parts * rows, HD), f32)
    if has_prev:
        log_prev = log_total + jnp.where(info_ref[1] > 0, 0.0, -masked_score).astype(f32)
        for part in range(parts):
            span = slice(part * block, (part + 1) * block)
            more, key_grad, value_grad = one_block(prev_ref, span, 0, log_prev, False)
            query_grad = query_grad + more
            dprev_ref[:, span, :HD] = key_grad
            dprev_ref[:, span, HD:] = value_grad
    for part in range(parts):
        span = block_span(ats[part], block)
        more, key_grad, value_grad = one_block(cur_ref, span, part * rows, log_total, True)
        query_grad = added_from(query_grad, part * rows, more)
        if has_carry:
            key_grad = key_grad + carry_ref[:, span, :HD]
            value_grad = value_grad + carry_ref[:, span, HD:]
        dcur_ref[:, span, :HD] = key_grad.astype(bf)
        dcur_ref[:, span, HD:] = value_grad.astype(bf)
    query_grad = (query_grad * scaling).astype(bf)
    for part, at in enumerate(ats):
        store_heads(dq_ref, at, query_grad[part * rows : (part + 1) * rows])


def attention_call(kernel, factor, out_shape, info, queries, *rest):
    parts, block, _ = queries.shape
    rows = parts * GROUP * block
    keys = sum(ref.shape[0] * ref.shape[1] for ref in rest if ref.shape == rest[-1].shape)
    in_vmem = pl.BlockSpec(memory_space=pltpu.VMEM)
    return pl.pallas_call(
        kernel,
        out_shape=out_shape,
        in_specs=[pl.BlockSpec(memory_space=pltpu.SMEM)] + [in_vmem] * (1 + len(rest)),
        out_specs=(in_vmem,) * len(out_shape),
        compiler_params=pltpu.CompilerParams(vmem_limit_bytes=VMEM_LIMIT),
        cost_estimate=pl.CostEstimate(
            flops=factor * rows * keys * HD,
            bytes_accessed=factor * (keys + rows) * HD,
            transcendentals=rows * keys // 2,
        ),
    )(info, queries, *rest)


def attention_forward(info, qkv, prev, cur):
    parts, block, _ = qkv.shape
    shapes = (
        jax.ShapeDtypeStruct((parts, block, GROUP * HD), bf),
        jax.ShapeDtypeStruct((parts, GROUP * block, HD), f32),
    )
    caches = (cur,) if prev is None else (prev, cur)
    kernel = functools.partial(attention_forward_kernel, prev is not None)
    return attention_call(kernel, 2, shapes, info, qkv, *caches)


def attention_backward(info, qkv, out_grad, out, logs, carry, prev, cur):
    shapes = (jax.ShapeDtypeStruct(out.shape, bf), jax.ShapeDtypeStruct(cur.shape, bf))
    if prev is not None:
        shapes += (jax.ShapeDtypeStruct(cur.shape, f32),)
    extra = tuple(value for value in (carry, prev) if value is not None)
    kernel = functools.partial(attention_backward_kernel, prev is not None, carry is not None)
    return attention_call(kernel, 5, shapes, info, qkv, out_grad, out, logs, *extra, cur)


def body(
    inputs,
    cotangent,
    routes,
    norm_attn,
    w_query,
    w_key,
    w_value,
    w_output,
    norm_ffn,
    w_router,
    shared_gate,
    shared_up,
    shared_down,
    expert_gate,
    expert_up,
    expert_down,
):
    micros, block, width = inputs.shape[1:]
    shards = lax.axis_size("shard")
    section = lax.axis_index("section")
    core = lax.axis_index("dp")
    position = lax.axis_index("shard")
    heads = KVH
    ring = shards // heads
    local_experts = expert_gate.shape[1]
    experts = local_experts * shards
    slots = experts * CAP
    rows_per = w_query.shape[1]
    half_rows = rows_per // 2
    group_width = GROUP * HD
    head_width = H * HD
    key_width = KVH * HD
    part_width = group_width + 2 * HD
    shared_width = shared_gate.shape[2]
    down_rows = shared_down.shape[1]
    is_first = section == 0
    low_core = core == 0
    zy_groups = [[x * ring + zy for zy in range(ring)] for x in range(heads)]

    def exchange(value, groups=None):
        return lax.all_to_all(
            value, "shard", split_axis=0, concat_axis=0, tiled=True, axis_index_groups=groups
        )

    def copies(value, count):
        return jnp.broadcast_to(value[None], (count,) + value.shape)

    def twin(value):
        return lax.ppermute(value, "dp", [(0, 1), (1, 0)])

    def mine_of(low_half, high_half):
        return jnp.where(low_core, low_half, high_half)

    def ordered(own, other, axis):
        low_half, high_half = mine_of(own, other), mine_of(other, own)
        return jnp.concatenate([low_half, high_half], axis=axis)

    def ordered_by(in_order, own, other):
        return jnp.stack([jnp.where(in_order, own, other), jnp.where(in_order, other, own)])

    def halves(value):
        half = value.shape[-1] // 2
        return value[..., :half], value[..., half:]

    def my_rows(value):
        return mine_of(value[..., :half_rows, :], value[..., half_rows:, :])

    tail = jnp.concatenate(
        [
            w_router[0],
            norm_attn[0][:, None],
            norm_ffn[0][:, None],
            jnp.zeros((rows_per, 128 - experts - 2), bf),
        ],
        axis=1,
    )
    by_head = jnp.concatenate(
        [
            w_query[0].reshape(rows_per, heads, group_width),
            w_key[0].reshape(rows_per, heads, HD),
            w_value[0].reshape(rows_per, heads, HD),
            jnp.broadcast_to(tail[:, None], (rows_per, heads, 128)),
        ],
        axis=2,
    ).transpose(1, 0, 2)
    by_head = my_rows(by_head)
    by_head = jnp.broadcast_to(
        by_head[:, None], (heads, ring, half_rows, part_width + 128)
    ).reshape(shards, half_rows, part_width + 128)
    down_half = down_rows // 2
    down_flat = (half_rows, down_half * width // half_rows)
    packed = jnp.concatenate(
        [
            my_rows(jnp.concatenate([shared_gate[0], shared_up[0]], axis=1)),
            mine_of(shared_down[0][:down_half], shared_down[0][down_half:]).reshape(down_flat),
        ],
        axis=1,
    )
    by_head, packed = lax.optimization_barrier((by_head, packed))
    gathered = lax.all_gather(packed, "shard")
    own_part = exchange(by_head)
    out_rows = my_rows(w_output[0])
    out_rows = ordered_by(
        position % 2 == 0, out_rows, lax.ppermute(out_rows, "shard", [(p, p ^ 1) for p in range(shards)])
    )
    out_parts = [out_rows] + [
        lax.ppermute(
            out_rows,
            "shard",
            [(p, p // ring * ring + (p % ring - 2 * k) % ring) for p in range(shards)],
        )
        for k in range(1, ring // 2)
    ]
    own_part, *out_parts = lax.optimization_barrier((own_part, *out_parts))
    own_out = lax.dynamic_slice_in_dim(
        jnp.concatenate(out_parts + out_parts), ring - position % ring // 2 * 2, ring, axis=0
    )
    output_w = ordered(own_out, twin(own_out), 1).reshape(group_width, width)
    fetched = ordered(own_part, twin(own_part), 1).reshape(width, part_width + 128)
    qkv_w, tail = fetched[:, :part_width], fetched[:, part_width:]
    router_w = tail[:, :experts]
    gains = tail[:, experts : experts + 2].T.astype(f32)
    gain_one, gain_two = gains[0][None], gains[1][None]

    expert_g, expert_u, expert_d = expert_gate[0], expert_up[0], expert_down[0]
    slot_of = jnp.arange(slots, dtype=jnp.int32)
    expert_of = jnp.arange(experts, dtype=jnp.int32)
    row_of = jnp.arange(block, dtype=jnp.int32)
    spread = (expert_of[:, None] == slot_of[None, :] // CAP).astype(bf)
    router_slots = dot(router_w, spread).astype(bf)
    earlier = (row_of[:, None] > row_of[None, :]).astype(bf)

    def slot_table(route_rows):
        named = jnp.any(route_rows[:, :, None] == expert_of[None, None, :], axis=1).astype(bf)
        slot_ids = dot(earlier, named).astype(bf)
        return (dot(named, spread) > 0.5) & (
            dot(slot_ids, spread).astype(jnp.int32) == (slot_of % CAP)[None, :]
        )

    here = [position % ring, jnp.ones_like(position), position // ring]
    info_all = jnp.stack(here).astype(jnp.int32)
    info = jnp.stack([here[0], is_first.astype(here[0].dtype), here[2]]).astype(jnp.int32)

    def gate_values(normed_two, table):
        logits = jnp.where(table, dot(normed_two, router_slots), masked_score)
        weights = jnp.exp(logits - jnp.max(logits, axis=-1, keepdims=True))
        weights = jnp.where(table, weights, 0.0)
        return weights / jnp.sum(weights, axis=-1, keepdims=True)

    def high_low(value):
        high = value.astype(bf)
        return high, (value - high.astype(f32)).astype(bf)

    def to_experts(rows):
        return (
            exchange(rows.reshape(shards, local_experts, CAP, width))
            .transpose(1, 0, 2, 3)
            .reshape(local_experts, shards * CAP, width)
        )

    def from_experts(rows):
        return exchange(
            rows.reshape(local_experts, shards, CAP, width).transpose(1, 0, 2, 3)
        ).reshape(slots, width)

    def moved(p, steps):
        return (p // ring + steps) % heads * ring + p % ring

    def shift_x(value, steps):
        return lax.ppermute(value, "shard", [(p, moved(p, steps)) for p in range(shards)])

    def next_ring(value):
        return jnp.stack(
            [
                lax.ppermute(
                    value,
                    ("section", "shard"),
                    [(p, shards + moved(p, steps)) for p in range(shards)],
                )
                for steps in range(heads)
            ]
        )

    def sum_over_x(rows):
        parts = rows.reshape(heads, block, width)
        away = [shift_x(parts[k].astype(bf), -k).astype(f32) for k in range(1, heads)]
        return sum(away, parts[0])

    def ring_rows(rows):
        return jnp.concatenate([rows] + [shift_x(rows, k) for k in range(1, heads)], axis=0)

    ring_inputs = [
        jnp.stack([inputs[0, m]] + [shift_x(inputs[0, m], k) for k in range(1, heads)])
        for m in range(micros)
    ]

    def shared_weights(gathered):
        gate_up = gathered[:, :, : 2 * shared_width]
        down = gathered[:, :, 2 * shared_width :].reshape(shards, down_half, width)
        return (
            ordered(gate_up, twin(gate_up), 1).reshape(width, 2 * shared_width),
            ordered(down, twin(down), 1).reshape(shards * down_rows, width),
        )

    def forward(moment, received, previous, shared_pair):
        first_micro = min(moment, micros - 1)
        second_micro = max(moment - 1, 0)
        ring_b = jnp.where(is_first, ring_inputs[first_micro], received)
        layer_b = ring_b[0]
        table = slot_table(
            jnp.where(is_first, routes[0, 0, first_micro], routes[0, 0, second_micro])
        )
        pick = table.astype(bf)
        layer_in = layer_b.astype(f32)
        ring_in = ring_b.reshape(heads * block, width).astype(f32)
        ring_one = (ring_in * inverse_rms(ring_in) * gain_one).astype(bf)
        qkv = dot(ring_one, qkv_w).astype(bf)
        cache = exchange(copies(qkv[:, group_width:], ring), zy_groups)
        qkv = qkv.reshape(heads, block, part_width)
        attn_info = info if moment == 1 else info_all
        attended, logs = attention_forward(attn_info, qkv, previous, cache)
        attended_rows = attended.reshape(heads * block, group_width)
        hidden = layer_in + sum_over_x(dot(attended_rows, output_w))
        if shared_pair is None:
            arrived, hidden = lax.optimization_barrier((gathered, hidden))
            shared_pair = shared_weights(arrived)
        gate_up_w, down_w = shared_pair
        normed_two = (hidden * inverse_rms(hidden) * gain_two).astype(bf)
        gates = gate_values(normed_two, table)
        expert_in = to_experts(dot_tn(pick, normed_two).astype(bf))
        gate_pre = wide_einsum("erd,edf->erf", expert_in, expert_g)
        up_pre = wide_einsum("erd,edf->erf", expert_in, expert_u)
        activated = (silu_parts(gate_pre)[0] * up_pre).astype(bf)
        returned = from_experts(wide_einsum("erf,efd->erd", activated, expert_d).astype(bf))
        high, low = high_low(gates)
        routed = dot(high, returned) + dot(low, returned)
        shared_gate_pre, shared_up_pre = halves(dot(normed_two, gate_up_w))
        shared_act = (silu_parts(shared_gate_pre)[0] * shared_up_pre).astype(bf)
        beside = lax.optimization_barrier(hidden + dot(shared_act, down_w))
        output_b = (beside + routed).astype(bf)
        return dict(
            layer_b=layer_b,
            pick=pick,
            ring_one=ring_one,
            qkv=qkv,
            cache=cache,
            previous=previous,
            info=attn_info,
            attended=attended,
            logs=logs,
            hidden=hidden,
            normed_two=normed_two,
            gates=gates,
            expert_in=expert_in,
            gate_pre=gate_pre,
            up_pre=up_pre,
            activated=activated,
            returned=returned,
            shared_gate_pre=shared_gate_pre,
            shared_up_pre=shared_up_pre,
            shared_act=shared_act,
            output_b=output_b,
            shared_pair=shared_pair,
        )

    def ffn_backward(kept, upstream_b):
        upstream = upstream_b.astype(f32)
        gates, hidden = kept["gates"], kept["hidden"]
        gate_up_w, down_w = kept["shared_pair"]
        high, low = high_low(gates)
        outgoing = dot_tn(high, upstream_b) + dot_tn(low, upstream_b)
        expert_grad = to_experts(outgoing.astype(bf))
        act_silu, act_slope = silu_parts(kept["gate_pre"])
        act_grad = wide_einsum("erd,efd->erf", expert_grad, expert_d)
        gate_pre_grad = (act_grad * kept["up_pre"] * act_slope).astype(bf)
        up_pre_grad = (act_grad * act_silu).astype(bf)
        expert_in_grad = (
            wide_einsum("erf,edf->erd", gate_pre_grad, expert_g)
            + wide_einsum("erf,edf->erd", up_pre_grad, expert_u)
        ).astype(bf)
        returned_grad = from_experts(expert_in_grad)
        shared_act_grad = dot_nt(upstream_b, down_w)
        shared_silu, shared_slope = silu_parts(kept["shared_gate_pre"])
        shared_gate_grad = (shared_act_grad * kept["shared_up_pre"] * shared_slope).astype(bf)
        shared_up_grad = (shared_act_grad * shared_silu).astype(bf)
        normed_two_grad = dot_nt(
            jnp.concatenate([shared_gate_grad, shared_up_grad], axis=1), gate_up_w
        )
        gate_grad = dot_nt(upstream_b, kept["returned"])
        picked_grad = gates * (gate_grad - jnp.sum(gates * gate_grad, axis=1, keepdims=True))
        picked_b = picked_grad.astype(bf)
        normed_two_grad = normed_two_grad + dot_nt(picked_b, router_slots)
        normed_two_grad = lax.optimization_barrier(normed_two_grad)
        normed_two_grad = normed_two_grad + dot(kept["pick"], returned_grad)
        logit_grad = dot_nt(picked_b, spread).astype(bf)
        hidden_norm_grad, gain_two_grad = norm_back(hidden, gain_two, normed_two_grad)
        return dict(
            hidden_grad=upstream + hidden_norm_grad,
            upstream_b=upstream_b,
            expert_grad=expert_grad,
            gate_pre_grad=gate_pre_grad,
            up_pre_grad=up_pre_grad,
            shared_gate_grad=shared_gate_grad,
            shared_up_grad=shared_up_grad,
            logit_grad=logit_grad,
            gain_two_grad=gain_two_grad,
        )

    def attention_back(kept, grads, carried):
        ring_hidden = ring_rows(grads["hidden_grad"].astype(bf))
        out_grad = dot_nt(ring_hidden, output_w).astype(bf)
        results = attention_backward(
            kept["info"],
            kept["qkv"],
            out_grad.reshape(heads, block, group_width),
            kept["attended"],
            kept["logs"],
            carried,
            kept["previous"],
            kept["cache"],
        )
        carried = results[2] if len(results) > 2 else None
        query_grad = results[0].reshape(heads * block, group_width)
        query_part = lax.optimization_barrier(dot_nt(query_grad, qkv_w[:, :group_width]))
        pair_grad = jnp.sum(exchange(results[1], zy_groups).astype(f32), axis=0).astype(bf)
        qkv_grad = jnp.concatenate([query_grad, pair_grad], axis=1)
        normed_one_grad = sum_over_x(query_part + dot_nt(pair_grad, qkv_w[:, group_width:]))
        in_norm_grad, gain_one_grad = norm_back(
            kept["layer_b"].astype(f32), gain_one, normed_one_grad
        )
        grads = dict(
            grads,
            ring_hidden=ring_hidden,
            qkv_grad=qkv_grad,
            gain_one_grad=gain_one_grad,
            layer_grad=(grads["hidden_grad"] + in_norm_grad).astype(bf),
        )
        return grads, carried

    nothing = jnp.zeros((block, width), bf)
    saved = []
    received, previous, shared_pair = jnp.zeros((heads, block, width), bf), None, None
    for moment in range(micros + 1):
        kept = forward(moment, received, previous, shared_pair)
        shared_pair = kept["shared_pair"]
        saved.append(kept)
        previous = kept["cache"]
        if moment < micros:
            received = next_ring(kept["output_b"])
    backs = [None] * (micros + 1)
    received, carried = nothing, None
    for source in range(micros, -1, -1):
        own = cotangent[0, source - 1] if source > 0 else nothing
        upstream_b = jnp.where(is_first, received, own)
        grads = ffn_backward(saved[source], upstream_b)
        backs[source], carried = attention_back(saved[source], grads, carried)
        if source > 0:
            received = lax.ppermute(backs[source]["layer_grad"], "section", [(1, 0)])

    def live(name, store, axis):
        ends = jnp.where(is_first, store[0][name], store[micros][name])
        return jnp.concatenate([ends, store[1][name]], axis=axis)

    def kept_rows(name, axis=0):
        return live(name, saved, axis)

    def back_rows(name, axis=0):
        return live(name, backs, axis)

    expert_parts = [
        wide_einsum("erd,erf->edf", kept_rows("expert_in", 1), back_rows("gate_pre_grad", 1)),
        wide_einsum("erd,erf->edf", kept_rows("expert_in", 1), back_rows("up_pre_grad", 1)),
        wide_einsum("erf,erd->efd", kept_rows("activated", 1), back_rows("expert_grad", 1)),
    ]
    expert_parts = [part.astype(bf) for part in expert_parts]
    expert_others = [twin(part) for part in expert_parts]

    def both(value):
        return jnp.concatenate([value, twin(value)], axis=0)

    def both_halves(low_half, high_half):
        own, other = mine_of(low_half, high_half), mine_of(high_half, low_half)
        return jnp.concatenate([own, twin(other)], axis=0)

    normed_two = kept_rows("normed_two")
    grad_gate_up = dot_tn(
        both(normed_two), both_halves(back_rows("shared_gate_grad"), back_rows("shared_up_grad"))
    )
    grad_down = dot_tn(both(kept_rows("shared_act")), both_halves(*halves(back_rows("upstream_b"))))


    def shift_z(value, steps):
        pairs = [(p, p // ring * ring + (p % ring + 2 * steps) % ring) for p in range(shards)]
        return lax.ppermute(value, "shard", pairs)

    def shift_y(value, steps):
        return lax.ppermute(value, "shard", [(p, p ^ 1) for p in range(shards)])

    along = dict(
        x=(shift_x, position // ring), z=(shift_z, position % ring // 2), y=(shift_y, position % 2)
    )

    def reduced(value, name, axis, held_as=bf):
        shift, here = along[name]
        count = value.shape[axis]

        def piece(steps):
            return lax.dynamic_index_in_dim(value, (here + steps) % count, axis, keepdims=False)

        total = piece(0).astype(f32)
        for steps in range(1, count):
            total = total + shift(piece(steps), steps).astype(f32)
        return total.astype(held_as)

    grad_out = dot_tn(
        kept_rows("attended").reshape(micros * heads * block, group_width),
        back_rows("ring_hidden"),
    )
    grad_qkv = dot_tn(kept_rows("ring_one"), back_rows("qkv_grad"))
    grad_router = dot_tn(normed_two, back_rows("logit_grad"))
    gain_sums = jnp.stack(
        [sum(grads[name] for grads in backs) for name in ("gain_one_grad", "gain_two_grad")]
    )
    grad_tail = jnp.concatenate(
        [grad_router, gain_sums.T, jnp.zeros((width, 128 - experts - 2), f32)], axis=1
    )
    grad_qkv = jnp.concatenate([grad_qkv, grad_tail], axis=1)
    grad_qkv = grad_qkv.astype(bf).reshape(shards, rows_per, part_width + 128)
    (
        grad_qkv,
        grad_gate_up,
        grad_down,
        grad_out,
        last_grad,
        *expert_others,
    ) = lax.optimization_barrier(
        (
            grad_qkv,
            grad_gate_up.astype(bf),
            grad_down.astype(bf),
            grad_out.astype(bf),
            backs[0]["layer_grad"],
            *expert_others,
        )
    )
    backs[0]["layer_grad"] = last_grad
    pieces = exchange(grad_qkv)
    attention_pieces, grad_out = lax.optimization_barrier((pieces, grad_out))
    expert_grads = [
        part.astype(f32) + other.astype(f32) for part, other in zip(expert_parts, expert_others)
    ]
    pieces = grad_gate_up.reshape(heads, ring // 2, 2, rows_per, shared_width)
    pieces, out_pieces = lax.optimization_barrier(
        (reduced(pieces, "x", 0), exchange(grad_out.reshape(ring, rows_per, width), zy_groups))
    )
    share_gate_up = reduced(reduced(pieces, "z", 0), "y", 0, f32)
    pieces = grad_down.reshape(heads, ring // 2, 2, down_rows, width // 2)
    share_down = reduced(reduced(reduced(pieces, "z", 1), "x", 0), "y", 0, f32)

    share_out = jnp.sum(out_pieces.astype(f32), axis=0)
    attention_pieces = attention_pieces.astype(f32)
    share_qkv = jnp.sum(
        attention_pieces[:, :, :part_width].reshape(heads, ring, rows_per, part_width), axis=1
    )
    share_qkv = share_qkv.transpose(1, 0, 2)
    share_tail = jnp.sum(attention_pieces[:, :, part_width:], axis=0)

    def total(share):
        return share + twin(share)

    out_total, qkv_total, tail_total = total(share_out), total(share_qkv), total(share_tail)
    other_gate_up = twin(share_gate_up)
    down_total = ordered(share_down, twin(share_down), 1)

    def by_micro(store, name):
        return jnp.stack(
            [jnp.where(is_first, store[m][name], store[m + 1][name]) for m in range(micros)]
        )[None, None]

    return (
        by_micro(saved, "output_b"),
        by_micro(backs, "layer_grad"),
        tail_total[:, experts][None],
        qkv_total[:, :, :group_width].reshape(1, rows_per, head_width),
        qkv_total[:, :, group_width : group_width + HD].reshape(1, rows_per, key_width),
        qkv_total[:, :, group_width + HD :].reshape(1, rows_per, key_width),
        out_total[None],
        tail_total[:, experts + 1][None],
        tail_total[:, :experts][None],
        mine_of(share_gate_up, other_gate_up)[None],
        mine_of(other_gate_up, share_gate_up)[None],
        down_total[None],
        expert_grads[0][None],
        expert_grads[1][None],
        expert_grads[2][None],
    )


def solution(mesh):
    rows = P("section", "shard", None)
    vector = P("section", "shard")
    expert = P("section", "shard", None, None)
    tokens = P("dp", None, "shard", None)
    section_tokens = P("section", "dp", None, "shard", None)
    weights = (vector, rows, rows, rows, rows, vector, rows, rows, rows, rows) + (expert,) * 3
    return jax.shard_map(
        body,
        mesh=mesh,
        in_specs=(tokens, tokens, section_tokens) + weights,
        out_specs=(section_tokens, section_tokens) + weights,
        check_vma=False,
    )
```
